32 devices in a mesh: fsdp: 4 (over y, x), tensor: 8 (over z, core).
Axes of the slice: x: 2, y: 2, z: 4, core: 2. Of those that a mesh axis runs over, the one named last changes fastest.
Arguments:
- hidden_in: bfloat16 [16384, 1536], P(('fsdp', 'tensor')), may hold values from -6 to 6
- norm_gain: bfloat16 [1536], P('fsdp'), may hold values from 0.25 to 1.75
- in_gate: bfloat16 [1536, 3072], P('fsdp', 'tensor'), may hold values from -0.15625 to 0.15625
- in_inner: bfloat16 [1536, 3072], P('fsdp', 'tensor')
- in_state: bfloat16 [1536, 256], P('fsdp'), may hold values from -0.15625 to 0.15625
- in_step: bfloat16 [1536, 48], P('fsdp', 'tensor'), may hold values from -0.15625 to 0.15625
- conv_inner: bfloat16 [4, 48, 64], P(None, 'tensor', 'fsdp'), may hold values from -3 to 3
- conv_inner_shift: bfloat16 [48, 64], P('tensor', 'fsdp'), may hold values from -3 to 3
- conv_state: bfloat16 [4, 256], P(None, 'fsdp'), may hold values from -3 to 3
- conv_state_shift: bfloat16 [256], P('fsdp'), may hold values from -3 to 3
- step_offset: bfloat16 [48], P('fsdp'), may hold values from -6 to -2
- log_rate: bfloat16 [48], P('fsdp'), may hold values from 0 to 2.09375
- skip_gain: bfloat16 [48], P('fsdp'), may hold values from 0.5 to 2
- inner_gain: bfloat16 [48, 64], P('tensor', 'fsdp'), may hold values from 0.25 to 1.75
- out_weight: bfloat16 [3072, 1536], P('tensor', 'fsdp'), may hold values from -0.109375 to 0.109375
- segment_ids: int32 [16384], P('fsdp'), may hold values from 0 to 16, as said below
- grad_out: bfloat16 [16384, 1536], P(('fsdp', 'tensor')), may hold values from -6 to 6
Outputs:
- layer_out: bfloat16 [16384, 1536], P(('fsdp', 'tensor'))
- grad_hidden: bfloat16 [16384, 1536], P(('fsdp', 'tensor'))
- grad_norm_gain: float32 [1536], P('fsdp')
- grad_in_gate: float32 [1536, 3072], P('fsdp', 'tensor')
- grad_in_inner: float32 [1536, 3072], P('fsdp', 'tensor')
- grad_in_state: float32 [1536, 256], P('fsdp')
- grad_in_step: float32 [1536, 48], P('fsdp', 'tensor')
- grad_conv_inner: float32 [4, 48, 64], P(None, 'tensor', 'fsdp')
- grad_conv_inner_shift: float32 [48, 64], P('tensor', 'fsdp')
- grad_conv_state: float32 [4, 256], P(None, 'fsdp')
- grad_conv_state_shift: float32 [256], P('fsdp')
- grad_step_offset: float32 [48], P('fsdp')
- grad_log_rate: float32 [48], P('fsdp')
- grad_skip_gain: float32 [48], P('fsdp')
- grad_inner_gain: float32 [48, 64], P('tensor', 'fsdp')
- grad_out_weight: float32 [3072, 1536], P('tensor', 'fsdp')
The draws below stay inside these ranges and needn't reach their ends.
Inputs may be any that keep to these rules, and one draw needn't show every extreme that they name: `segment_ids`: each sequence of 1024 consecutive tokens is a pack of documents: ids start at 0 in every sequence and rise by one at each document's first token. The largest id is reached in some sequence of every draw.
All inputs are finite; a program needn't handle non-finite values.
Results may differ from the reference program's by a relative error of at most 0.025.
Values may be sent and summed in bfloat16 or wider, within the bound.
A program may use at most 256 MiB of HBM per device.

```python
import jax
import jax.numpy as jnp
from jax import lax

D = 1536
H = 48
P_SIZE = 64
N = 128
K = 4
SPAN = 256
SEQ = 1024
DI = 3072
TOKENS = 16384


def draw_in_inner(key, part):
    key = jax.random.fold_in(key, 11)
    columns = jnp.arange(H * P_SIZE) // P_SIZE
    rising = 3.0 ** (columns.astype(jnp.float32) / max(H - 1, 1))
    base = jax.random.normal(key, (D, H * P_SIZE), jnp.float32)
    return (base * rising[None, :] / D ** 0.5).astype(jnp.bfloat16)


def draw_segment_ids(key, part):
    key = jax.random.fold_in(key, 5)
    pick_key = jax.random.fold_in(key, 9)
    shortest = max(SEQ * 15 // 256, 2)
    longest = max(SEQ * 25 // 32, 4)
    count = TOKENS // SEQ
    lengths = jax.random.randint(key, (count, SEQ // shortest + 1), shortest, longest + 1)
    ends = jnp.cumsum(lengths, axis=1)
    places = jnp.arange(SEQ)
    numbers = jnp.sum((ends[:, None, :] <= places[None, :, None]).astype(jnp.int32), axis=2)
    packed = jnp.minimum(places // shortest, SEQ // shortest - 1).astype(jnp.int32)
    chosen = jax.random.randint(pick_key, (), 0, count)
    which = (jnp.arange(count) == chosen)[:, None]
    numbers = jnp.where(which, packed[None, :], numbers)
    return numbers.reshape(TOKENS).astype(jnp.int32)


def steps_of(key, shape, cuts, smallest, high):
    def one(axis_at, blocks):
        steps = jax.random.uniform(jax.random.fold_in(jax.random.fold_in(key, 6), axis_at), (blocks,), jnp.float32, smallest / len(cuts), high / len(cuts))
        return jnp.repeat(jnp.exp(steps), shape[axis_at] // blocks).reshape((-1,) + (1,) * (len(shape) - axis_at - 1))

    level = one(*cuts[0])
    for cut in cuts[1:]:
        level = level * one(*cut)
    return level


def noise(stream_key, dims, deviation, reach, shards=(), kind=jnp.bfloat16):
    values = jax.random.normal(stream_key, dims, jnp.float32) * deviation
    if len(shards) > 0:
        values = steps_of(stream_key, dims, shards, -0.22, 0.18) * values
    return jnp.clip(values, min=-reach, max=reach).astype(kind)


def setup_inputs(seed: int = 0) -> dict:
    key_list = jax.random.split(jax.random.key(seed), 18)
    hidden_in = noise(key_list[0], (TOKENS, D), 1.0, 6.0, ((0, 32),))
    norm_gain = jnp.clip(1.0 + 0.15 * jax.random.normal(key_list[1], (D,), jnp.float32), 0.25, 1.75).astype(jnp.bfloat16)
    in_gate = noise(key_list[2], (D, DI), D ** -0.5, 0.15625, ((0, 4), (1, 8)))
    in_inner = draw_in_inner(jax.random.fold_in(key_list[17], 71), 0)
    in_state = noise(key_list[4], (D, 2 * N), D ** -0.5, 0.15625, ((0, 4),))
    in_step = noise(key_list[5], (D, H), D ** -0.5, 0.15625, ((0, 4), (1, 8)))
    conv_inner = noise(key_list[6], (K, H, P_SIZE), 0.5, 3.0, ((1, 8), (2, 4)))
    conv_inner_shift = noise(key_list[7], (H, P_SIZE), 0.5, 3.0, ((0, 8), (1, 4)))
    conv_state = noise(key_list[8], (K, 2 * N), 0.5, 3.0, ((1, 4),))
    conv_state_shift = noise(key_list[9], (2 * N,), 0.5, 3.0, ((0, 4),))
    step_offset = jnp.clip(-6.0 + 4.0 * jax.random.uniform(key_list[10], (H,), jnp.float32) ** steps_of(key_list[10], (H,), ((0, 4),), -0.2, 0.2), -6.0, -2.0).astype(jnp.bfloat16)
    log_rate = jnp.clip(2.09375 * jax.random.uniform(key_list[11], (H,), jnp.float32) ** steps_of(key_list[11], (H,), ((0, 4),), -0.2, 0.2), 0.0, 2.09375).astype(jnp.bfloat16)
    skip_gain = jnp.clip(0.5 + 1.5 * jax.random.uniform(key_list[12], (H,), jnp.float32) ** steps_of(key_list[12], (H,), ((0, 4),), -0.2, 0.2), 0.5, 2.0).astype(jnp.bfloat16)
    inner_gain = jnp.clip(1.0 + 0.15 * jax.random.normal(key_list[13], (H, P_SIZE), jnp.float32), 0.25, 1.75).astype(jnp.bfloat16)
    out_weight = noise(key_list[14], (DI, D), DI ** -0.5, 0.109375, ((0, 8), (1, 4)))
    segment_ids = draw_segment_ids(jax.random.fold_in(key_list[17], 71), 0)
    grad_out = noise(key_list[16], (TOKENS, D), 1.0, 6.0, ((0, 32),))
    return {"hidden_in": hidden_in, "norm_gain": norm_gain, "in_gate": in_gate, "in_inner": in_inner, "in_state": in_state, "in_step": in_step, "conv_inner": conv_inner, "conv_inner_shift": conv_inner_shift, "conv_state": conv_state, "conv_state_shift": conv_state_shift, "step_offset": step_offset, "log_rate": log_rate, "skip_gain": skip_gain, "inner_gain": inner_gain, "out_weight": out_weight, "segment_ids": segment_ids, "grad_out": grad_out}


EPSILON = 1e-05

@jax.custom_vjp
def low(v):
    return lax.optimization_barrier(v.astype(jnp.bfloat16)).astype(jnp.float32)

@jax.custom_vjp
def low_back(v):
    return v

def low_keep(v):
    return (low(v), None)

def low_pass(kept, grad):
    return (grad,)

def back_keep(v):
    return (v, None)

def back_low(kept, grad):
    return (low(grad),)
low.defvjp(low_keep, low_pass)
low_back.defvjp(back_keep, back_low)

def product(left, right):
    return jnp.dot(left, right, precision=lax.Precision.HIGHEST, preferred_element_type=jnp.float32)

def causal_conv(values, seq_docs, kernel, shift_term):
    length_all = values.shape[0]
    taps = kernel.shape[0]
    total = shift_term[None, :] + kernel[taps - 1][None, :] * values
    for shift_by in range(1, taps):
        earlier = jnp.concatenate([jnp.zeros((shift_by, values.shape[1]), values.dtype), values[:length_all - shift_by]], 0)
        earlier_docs = jnp.concatenate([jnp.full((shift_by,), -1, seq_docs.dtype), seq_docs[:length_all - shift_by]], 0)
        total = total + kernel[taps - 1 - shift_by][None, :] * jnp.where((earlier_docs == seq_docs)[:, None], earlier, 0.0)
    return total

def state_scan(inputs, steps, decay, bmat, cmat, seq_docs):
    length_all = inputs.shape[0]
    heads = inputs.shape[1]
    width = inputs.shape[2]
    states_n = bmat.shape[1]
    blocks = length_all // SPAN
    logs = (steps * decay[None, :]).reshape(blocks, SPAN, heads)
    cumul = jnp.cumsum(logs, axis=1)
    weighted = (inputs * steps[:, :, None]).reshape(blocks, SPAN, heads, width)
    b_blocks = bmat.reshape(blocks, SPAN, states_n)
    c_blocks = cmat.reshape(blocks, SPAN, states_n)
    doc_blocks = seq_docs.reshape(blocks, SPAN)
    order = jnp.arange(SPAN)
    causal = (order[:, None] >= order[None, :])[None] & (doc_blocks[:, :, None] == doc_blocks[:, None, :])
    causal_heads = causal[:, :, :, None]
    differ = cumul[:, :, None, :] - cumul[:, None, :, :]
    kernel = jnp.where(causal_heads, jnp.exp(jnp.where(causal_heads, differ, 0.0)), 0.0)
    scores = jnp.einsum('cin,cjn->cij', c_blocks, b_blocks, precision=lax.Precision.HIGHEST)
    local_out = jnp.einsum('cijh,cjhp->cihp', kernel * scores[:, :, :, None], weighted, precision=lax.Precision.HIGHEST)
    last_log = cumul[:, -1, :]
    last_doc = doc_blocks[:, -1]
    to_end = jnp.where((doc_blocks == last_doc[:, None])[:, :, None], jnp.exp(last_log[:, None, :] - cumul), 0.0)
    block_states = jnp.einsum('cjh,cjhp,cjn->chpn', to_end, weighted, b_blocks, precision=lax.Precision.HIGHEST)
    carried = jnp.zeros((heads, width, states_n), inputs.dtype)
    prior_doc = doc_blocks[0, 0]
    outputs = []
    for block in range(blocks):
        from_start = jnp.where((doc_blocks[block] == prior_doc)[:, None], jnp.exp(cumul[block]), 0.0)
        carried_out = jnp.einsum('ih,in,hpn->ihp', from_start, c_blocks[block], carried, precision=lax.Precision.HIGHEST)
        outputs.append(local_out[block] + carried_out)
        keeping = jnp.where(last_doc[block] == prior_doc, jnp.exp(last_log[block]), 0.0)
        carried = keeping[:, None, None] * carried + block_states[block]
        prior_doc = last_doc[block]
    return jnp.concatenate(outputs, 0)

def mixer_block(gate_pre, inner_pre, state_pre, step_pre, seq_docs, kernel_inner, shift_inner, kernel_state, shift_state, offsets, rates, skips):
    heads = offsets.shape[0]
    length_all = gate_pre.shape[0]
    width = inner_pre.shape[1] // heads
    states_n = state_pre.shape[1] // 2
    inner_act = jax.nn.silu(causal_conv(inner_pre, seq_docs, kernel_inner, shift_inner))
    state_act = jax.nn.silu(causal_conv(state_pre, seq_docs, kernel_state, shift_state))
    steps = jax.nn.softplus(step_pre + offsets[None, :])
    decay = -jnp.exp(rates)
    inputs = inner_act.reshape(length_all, heads, width)
    scanned = state_scan(inputs, steps, decay, state_act[:, :states_n], state_act[:, states_n:], seq_docs)
    scanned = scanned + skips[None, :, None] * inputs
    return scanned.reshape(length_all, heads * width) * jax.nn.silu(gate_pre)

def reference(hidden_in, norm_gain, in_gate, in_inner, in_state, in_step, conv_inner, conv_inner_shift, conv_state, conv_state_shift, step_offset, log_rate, skip_gain, inner_gain, out_weight, segment_ids, grad_out):
    floats = (hidden_in.astype(jnp.float32), norm_gain.astype(jnp.float32), in_gate.astype(jnp.float32), in_inner.astype(jnp.float32), in_state.astype(jnp.float32), in_step.astype(jnp.float32), conv_inner.astype(jnp.float32), conv_inner_shift.astype(jnp.float32), conv_state.astype(jnp.float32), conv_state_shift.astype(jnp.float32), step_offset.astype(jnp.float32), log_rate.astype(jnp.float32), skip_gain.astype(jnp.float32), inner_gain.astype(jnp.float32), out_weight.astype(jnp.float32))
    rows_all = hidden_in.shape[0]
    seqs = rows_all // SEQ
    seq_docs = segment_ids.reshape(seqs, SEQ)
    inner_width = H * P_SIZE

    def layer(hidden, gain_outer, gate_cols, inner_cols, state_cols, step_cols, kernel_inner, shift_inner, kernel_state, shift_state, offsets, rates, skips, gain_inner, out_rows):
        inv_rms = lax.rsqrt(lax.optimization_barrier(jnp.mean(hidden * hidden, -1, keepdims=True)) + EPSILON)
        normed = low(hidden * inv_rms * gain_outer)
        gate_pre = low_back(product(normed, gate_cols))
        inner_pre = low_back(product(normed, inner_cols))
        state_pre = low_back(product(normed, state_cols))
        step_pre = low_back(product(normed, step_cols))
        stacked = tuple((part.reshape(seqs, SEQ, part.shape[1]) for part in (gate_pre, inner_pre, state_pre, step_pre)))
        weights = (kernel_inner.reshape(K, inner_width), shift_inner.reshape(inner_width), kernel_state, shift_state, offsets, rates, skips)

        def one_sequence(items):
            return mixer_block(items[0], items[1], items[2], items[3], items[4], *weights)
        gated = lax.map(jax.checkpoint(one_sequence), stacked + (seq_docs,)).reshape(rows_all, inner_width)
        inner_inv = lax.rsqrt(lax.optimization_barrier(jnp.mean(gated * gated, -1, keepdims=True)) + EPSILON)
        normed_inner = low(gated * inner_inv * gain_inner.reshape(inner_width))
        return hidden + product(normed_inner, out_rows)
    result, pull = jax.vjp(layer, *floats)
    grads = pull(grad_out.astype(jnp.float32))
    return (result.astype(jnp.bfloat16), grads[0].astype(jnp.bfloat16), grads[1], grads[2], grads[3], grads[4], grads[5], grads[6], grads[7], grads[8], grads[9], grads[10], grads[11], grads[12], grads[13], grads[14])
```

```python
import functools

import jax
import jax.numpy as jnp
from jax import lax
from jax.sharding import PartitionSpec as P
from jax.experimental import pallas as pl
from jax.experimental.pallas import tpu as pltpu

SEQ = 1024
L = 128
CH = SEQ // L
K = 4
GH = 6
GW = 384
EPSILON = 1e-05
LOG2E = 1.4426950408889634
F32 = jnp.float32
BF = jnp.bfloat16
ST, CU, EE, FF, SG = 0, 8, 16, 24, 32


def mm(a, b, dims=((1,), (0,))):
    return lax.dot_general(a, b, (dims, ((), ())), preferred_element_type=F32)


def split2(x):
    hi = x.astype(BF)
    return hi, (x - hi.astype(F32)).astype(BF)


def split3(x):
    hi = x.astype(BF)
    rest = x - hi.astype(F32)
    mid = rest.astype(BF)
    return hi, mid, (rest - mid.astype(F32)).astype(BF)


def sigmoid(v):
    return 1.0 / (1.0 + jnp.exp(-v))


def back_conv_input(window, k):
    return window[8 - k : 8 - k + L]


def prep_body(state_ref, step_ref, tok_ref, row_ref, convst_ref, head_ref,
              bc_ref, bct_ref, g_ref, pack_ref, cumt_ref, pad_ref):
    pad_ref[pl.ds(0, 8), :] = jnp.zeros((8, 256), F32)
    pad_ref[pl.ds(8, SEQ), :] = state_ref[...]
    lane = lax.broadcasted_iota(jnp.int32, (L, L), 1)
    sub = lax.broadcasted_iota(jnp.int32, (L, L), 0)
    tri = (sub >= lane).astype(BF)
    offset = head_ref[0:1, :]
    decay = head_ref[1:2, :]
    taps = [convst_ref[k : k + 1, :] for k in range(K)]
    shift = convst_ref[K : K + 1, :]

    def chunk(c, _):
        base = pl.multiple_of(c * L, L)
        rows = pl.ds(base, L)
        tok = tok_ref[rows, :]
        window = pad_ref[pl.ds(base, L + 8), :]
        total = shift + taps[K - 1] * back_conv_input(window, 0)
        for k in range(1, K):
            total = total + taps[K - 1 - k] * (back_conv_input(window, k) * tok[:, 2 + k : 3 + k])
        act = total * sigmoid(total)
        low = act.astype(BF)
        bc_ref[rows, :] = low
        bct_ref[c] = jnp.concatenate([act[:, :128].T, act[:, 128:].T], 0).astype(BF)
        scores = mm(low[:, 128:], low[:, :128], ((1,), (1,)))
        same = (tok[:, 0:1] == row_ref[c][0:1, :]) & (sub >= lane)
        g_ref[c] = jnp.where(same, scores, 0.0)
        v = step_ref[rows, :] + offset
        steps = jnp.maximum(v, 0.0) + jnp.log1p(jnp.exp(-jnp.abs(v)))
        logs = steps * (decay * LOG2E)
        hi, mid, lo = split3(logs)
        cum = mm(tri, hi) + mm(tri, mid) + mm(tri, lo)
        last = cum[L - 1 : L, :]
        enter = jnp.exp2(cum) * tok[:, 1:2]
        leave = jnp.exp2(last - cum) * tok[:, 2:3]
        sig = sigmoid(v)
        cumt = cum.T
        zeros = jnp.zeros((L, 2), F32)
        for g in range(4):
            part = slice(GH * g, GH * g + GH)
            pieces = []
            for values in (steps, cum, enter, leave, sig):
                pieces += [values[:, part], zeros]
            pieces.append(jnp.zeros((L, 88), F32))
            pack_ref[g, rows, :] = jnp.concatenate(pieces, 1)
            cumt_ref[g, c] = jnp.concatenate([cumt[part, :], jnp.zeros((2, L), F32)], 0)
        return 0

    lax.fori_loop(0, CH, chunk, 0)


def vm(*shape):
    return pl.BlockSpec(memory_space=pltpu.VMEM)


def prep(state_pre, step_pre, tok, row, convst, head):
    return pl.pallas_call(
        prep_body,
        out_shape=(
            jax.ShapeDtypeStruct((SEQ, 256), BF),
            jax.ShapeDtypeStruct((CH, 256, L), BF),
            jax.ShapeDtypeStruct((CH, L, L), F32),
            jax.ShapeDtypeStruct((4, SEQ, 128), F32),
            jax.ShapeDtypeStruct((4, CH, 8, L), F32),
        ),
        in_specs=[vm()] * 6,
        out_specs=[vm()] * 5,
        scratch_shapes=[pltpu.VMEM((SEQ + 8, 256), F32)],
        compiler_params=pltpu.CompilerParams(vmem_limit_bytes=56 * 2**20),
        name="prep",
    )(state_pre, step_pre, tok, row, convst, head)


def pair_lanes(pack, first, q):
    lane = lax.broadcasted_iota(jnp.int32, (pack.shape[0], 128), 1)
    a = pack[:, first + 2 * q : first + 2 * q + 1]
    b = pack[:, first + 2 * q + 1 : first + 2 * q + 2]
    return jnp.where(lane < 64, a, b)


def spread(pack, first):
    return jnp.concatenate([pair_lanes(pack, first, q) for q in range(3)], 1)


def block_diag(x):
    lane = lax.broadcasted_iota(jnp.int32, x.shape, 1)
    zero = jnp.zeros_like(x)
    return jnp.concatenate([jnp.where(lane < 64, x, zero), jnp.where(lane < 64, zero, x)], 0)


def decay_kernel(pack, cumt, h):
    return jnp.exp2(jnp.minimum(pack[:, CU + h : CU + h + 1] - cumt[h : h + 1, :], 0.0))


def conv_of(window, tok, par):
    total = par[K : K + 1, :] + par[K - 1 : K, :] * back_conv_input(window, 0)
    for k in range(1, K):
        total = total + par[K - 1 - k : K - k, :] * (back_conv_input(window, k) * tok[:, 2 + k : 3 + k])
    return total


P_SHIFT, P_SKIP, P_GAIN = 4, 5, 6


def fwd_body(inner_ref, gate_ref, par_ref, tok_ref, bc_ref, bct_ref, g_ref, pack_ref, cumt_ref,
             gated_ref, states_ref, ss_ref, pad_ref, st_ref):
    pad_ref[pl.ds(0, 8), :] = jnp.zeros((8, GW), F32)
    pad_ref[pl.ds(8, SEQ), :] = inner_ref[...]
    st_ref[...] = jnp.zeros_like(st_ref)
    par = par_ref[...]

    @pl.when(pl.program_id(0) == 0)
    def _():
        ss_ref[...] = jnp.zeros_like(ss_ref)

    def chunk(c, _):
        base = pl.multiple_of(c * L, L)
        rows = pl.ds(base, L)
        tok = tok_ref[rows, :]
        u = conv_of(pad_ref[pl.ds(base, L + 8), :], tok, par)
        act = u * sigmoid(u)
        pack = pack_ref[0, rows, :]
        cumt = cumt_ref[0, c]
        g = g_ref[c]
        weighted = act * spread(pack, ST)
        low = weighted.astype(BF)
        enter = spread(pack, EE)
        state = st_ref[...]
        low_state = state.astype(BF)
        states_ref[0, c] = low_state
        y = mm(bc_ref[rows, 128:], low_state) * enter
        locals_ = []
        for q in range(3):
            kernels = [(g * decay_kernel(pack, cumt, 2 * q + e)).astype(BF) for e in range(2)]
            locals_.append(mm(jnp.concatenate(kernels, 1), block_diag(low[:, 128 * q : 128 * q + 128])))
        y = y + jnp.concatenate(locals_, 1)
        out = weighted * spread(pack, FF)
        st_ref[...] = enter[L - 1 : L, :] * state + mm(bct_ref[c, pl.ds(0, 128), :], out.astype(BF))
        ssd = y + par[P_SKIP : P_SKIP + 1, :] * act
        gate = gate_ref[rows, :]
        gated = ssd * (gate * sigmoid(gate))
        gated_ref[rows, :] = gated
        sq = gated * gated
        ss_ref[rows, :] += sq[:, :128] + sq[:, 128:256] + sq[:, 256:]
        return 0

    lax.fori_loop(0, CH, chunk, 0)


def whole_spec(shape):
    return pl.BlockSpec(shape, lambda g: (0,) * len(shape))


def fwd(inner_pre, gate_pre, par, tok, bc, bct, gs, pack, cumt):
    cols = pl.BlockSpec((SEQ, GW), lambda g: (0, g))
    return pl.pallas_call(
        fwd_body,
        grid=(4,),
        out_shape=(
            jax.ShapeDtypeStruct((SEQ, 4 * GW), F32),
            jax.ShapeDtypeStruct((4, CH, 128, GW), BF),
            jax.ShapeDtypeStruct((SEQ, 128), F32),
        ),
        in_specs=[
            cols, cols, pl.BlockSpec((8, GW), lambda g: (0, g)),
            whole_spec((SEQ, 128)), whole_spec((SEQ, 256)), whole_spec((CH, 256, L)), whole_spec((CH, L, L)),
            pl.BlockSpec((1, SEQ, 128), lambda g: (g, 0, 0)),
            pl.BlockSpec((1, CH, 8, L), lambda g: (g, 0, 0, 0)),
        ],
        out_specs=(
            cols,
            pl.BlockSpec((1, CH, 128, GW), lambda g: (g, 0, 0, 0)),
            whole_spec((SEQ, 128)),
        ),
        scratch_shapes=[pltpu.VMEM((SEQ + 8, GW), F32), pltpu.VMEM((128, GW), F32)],
        compiler_params=pltpu.CompilerParams(vmem_limit_bytes=56 * 2**20),
        name="mixer_forward",
    )(inner_pre, gate_pre, par, tok, bc, bct, gs, pack, cumt)


def bwd_body(inner_ref, gate_ref, dinner_ref, par_ref, tok_ref, inv_ref, bc_ref, bct_ref, g_ref, pack_ref,
             cumt_ref, states_ref, decay_ref, state_pre_ref, convst_ref, row_ref,
             dgate_ref, dpre_ref, dstep_ref, dstate_ref, pgrad_ref, hgrad_ref, sgrad_ref,
             pad_ref, rt_ref, dg_ref, dbc_ref, spad_ref):
    group = pl.program_id(0)
    pad_ref[pl.ds(0, 8), :] = jnp.zeros((8, GW), F32)
    pad_ref[pl.ds(8, SEQ), :] = inner_ref[...]
    rt_ref[...] = jnp.zeros_like(rt_ref)
    pgrad_ref[...] = jnp.zeros_like(pgrad_ref)
    par = par_ref[...]
    decay = decay_ref[0]

    @pl.when(group == 0)
    def _():
        dg_ref[...] = jnp.zeros_like(dg_ref)
        dbc_ref[...] = jnp.zeros_like(dbc_ref)
        dstep_ref[...] = jnp.zeros_like(dstep_ref)
        hgrad_ref[...] = jnp.zeros_like(hgrad_ref)

    lane = lax.broadcasted_iota(jnp.int32, (L, L), 1)
    sub = lax.broadcasted_iota(jnp.int32, (L, L), 0)
    upper = (sub <= lane).astype(BF)
    per_head = (lax.broadcasted_iota(jnp.int32, (GW, 128), 0) >> 6
                == lax.broadcasted_iota(jnp.int32, (GW, 128), 1)).astype(BF)

    def head_sums(x):
        hi, lo = split2(x)
        return mm(hi, per_head) + mm(lo, per_head)

    def chunk(step, later):
        c = CH - 1 - step
        base = pl.multiple_of(c * L, L)
        rows = pl.ds(base, L)
        tok = tok_ref[rows, :]
        window = pad_ref[pl.ds(base, L + 8), :]
        u = conv_of(window, tok, par)
        su = sigmoid(u)
        act = u * su
        pack = pack_ref[0, rows, :]
        cumt = cumt_ref[0, c]
        g = g_ref[c]
        steps = spread(pack, ST)
        enter = spread(pack, EE)
        leave = spread(pack, FF)
        weighted = act * steps
        low = weighted.astype(BF)
        low_state = states_ref[0, c]
        bmat = bc_ref[rows, :128]
        cmat = bc_ref[rows, 128:]
        diags = [block_diag(low[:, 128 * q : 128 * q + 128]) for q in range(3)]
        decays = [decay_kernel(pack, cumt, h) for h in range(GH)]
        kernels = [jnp.concatenate([(g * decays[2 * q + e]).astype(BF) for e in range(2)], 1) for q in range(3)]
        y = mm(cmat, low_state) * enter + jnp.concatenate([mm(kernels[q], diags[q]) for q in range(3)], 1)
        skip = par[P_SKIP : P_SKIP + 1, :]
        ssd = y + skip * act
        gate = gate_ref[rows, :]
        sg = sigmoid(gate)
        silu = gate * sg
        scaled = dinner_ref[rows, :] * par[P_GAIN : P_GAIN + 1, :]
        inv = inv_ref[rows, :]
        d_gated = inv[:, 0:1] * scaled - (ssd * silu) * inv[:, 1:2]
        dy = d_gated * silu
        dgate_ref[rows, :] = (d_gated * ssd * sg * (1.0 + gate * (1.0 - sg))).astype(BF)
        dy_low = dy.astype(BF)
        dy_in = (dy * enter).astype(BF)
        rt = rt_ref[...]
        rt_low = rt.astype(BF)
        carried = mm(bmat, rt_low) * leave
        pieces = []
        d_scores = jnp.zeros((L, L), F32)
        for q in range(3):
            dq = dy_low[:, 128 * q : 128 * q + 128]
            dm = mm(dq, diags[q], ((1,), (1,)))
            d_scores = d_scores + dm[:, :L] * decays[2 * q] + dm[:, L:] * decays[2 * q + 1]
            both = mm(kernels[q], dq, ((0,), (0,)))
            pieces.append(jnp.where(lane < 64, both[:L], both[L:]))
        d_weighted = jnp.concatenate(pieces, 1) + carried
        dg_ref[c] += d_scores
        out = (weighted * leave).astype(BF)
        dbc_ref[rows, 128:] += mm(dy_in, low_state, ((1,), (1,)))
        dbc_ref[rows, :128] += mm(out, rt_low, ((1,), (1,)))
        keep = enter[L - 1 : L, :]
        low32 = low.astype(F32)
        d_cum = head_sums(dy_low.astype(F32) * y - low32 * d_weighted)
        at_end = jnp.sum(low32 * carried, 0, keepdims=True) + keep * jnp.sum(rt * low_state.astype(F32), 0, keepdims=True)
        d_last = head_sums(jnp.concatenate([at_end, jnp.zeros((7, GW), F32)], 0))[0:1, :]
        hi, mid, lo = split3(d_cum)
        d_log = mm(upper, hi) + mm(upper, mid) + mm(upper, lo) + d_last
        rt_ref[...] = keep * rt + mm(bct_ref[c, pl.ds(128, 128), :], dy_in)
        d_step = head_sums(act * d_weighted) + decay[0:1, :] * d_log
        heads = lane < GH
        d_step_pre = jnp.where(heads, d_step * jnp.roll(pack, -SG, 1), 0.0)
        dstep_ref[rows, :] += pltpu.roll(d_step_pre, GH * group, 1)
        rate = jnp.sum(jnp.where(heads, pack, 0.0) * d_log, 0, keepdims=True) * decay[0:1, :]
        offs = jnp.sum(d_step_pre, 0, keepdims=True)
        hgrad_ref[0:1, :] += pltpu.roll(jnp.concatenate([rate, jnp.zeros((7, 128), F32)], 0), GH * group, 1)[0:1]
        hgrad_ref[1:2, :] += pltpu.roll(jnp.concatenate([offs, jnp.zeros((7, 128), F32)], 0), GH * group, 1)[0:1]
        d_act = skip * dy + steps * d_weighted
        du = d_act * su * (1.0 + u * (1.0 - su))
        pgrad_ref[K : K + 1, :] += jnp.sum(du, 0, keepdims=True)
        pgrad_ref[P_SKIP : P_SKIP + 1, :] += jnp.sum(dy * act, 0, keepdims=True)
        for k in range(K):
            moved = back_conv_input(window, k)
            if k:
                moved = moved * tok[:, 2 + k : 3 + k]
            pgrad_ref[K - 1 - k : K - k, :] += jnp.sum(du * moved, 0, keepdims=True)
        ahead = jnp.concatenate([du, later], 0)
        d_pre = par[K - 1 : K, :] * du
        for k in range(1, K):
            d_pre = d_pre + par[K - 1 - k : K - k, :] * (ahead[k : k + L] * tok[:, 5 + k : 6 + k])
        dpre_ref[rows, :] = d_pre.astype(BF)
        return du[:8]

    lax.fori_loop(0, CH, chunk, jnp.zeros((8, GW), F32))

    @pl.when(group == pl.num_programs(0) - 1)
    def _():
        spad_ref[pl.ds(0, 8), :] = jnp.zeros((8, 256), F32)
        spad_ref[pl.ds(8, SEQ), :] = state_pre_ref[...]
        sgrad_ref[...] = jnp.zeros_like(sgrad_ref)
        cst = convst_ref[...]

        def last(step, later):
            c = CH - 1 - step
            base = pl.multiple_of(c * L, L)
            rows = pl.ds(base, L)
            tok = tok_ref[rows, :]
            same = (tok[:, 0:1] == row_ref[c][0:1, :]) & (sub >= lane)
            ds = jnp.where(same, dg_ref[c], 0.0).astype(BF)
            d_c = dbc_ref[rows, 128:] + mm(ds, bc_ref[rows, :128])
            d_b = dbc_ref[rows, :128] + mm(ds, bc_ref[rows, 128:], ((0,), (0,)))
            window = spad_ref[pl.ds(base, L + 8), :]
            w = conv_of(window, tok, cst)
            sw = sigmoid(w)
            dw = jnp.concatenate([d_b, d_c], 1) * (sw * (1.0 + w * (1.0 - sw)))
            sgrad_ref[K : K + 1, :] += jnp.sum(dw, 0, keepdims=True)
            for k in range(K):
                moved = back_conv_input(window, k)
                if k:
                    moved = moved * tok[:, 2 + k : 3 + k]
                sgrad_ref[K - 1 - k : K - k, :] += jnp.sum(dw * moved, 0, keepdims=True)
            ahead = jnp.concatenate([dw, later], 0)
            d_pre = cst[K - 1 : K, :] * dw
            for k in range(1, K):
                d_pre = d_pre + cst[K - 1 - k : K - k, :] * (ahead[k : k + L] * tok[:, 5 + k : 6 + k])
            dstate_ref[rows, :] = d_pre.astype(BF)
            return dw[:8]

        lax.fori_loop(0, CH, last, jnp.zeros((8, 256), F32))


def bwd(inner_pre, gate_pre, d_inner, par, tok, inv, bc, bct, gs, pack, cumt, states, decay, state_pre, convst, row):
    cols = pl.BlockSpec((SEQ, GW), lambda g: (0, g))
    pcol = pl.BlockSpec((8, GW), lambda g: (0, g))
    return pl.pallas_call(
        bwd_body,
        grid=(4,),
        out_shape=(
            jax.ShapeDtypeStruct((SEQ, 4 * GW), BF),
            jax.ShapeDtypeStruct((SEQ, 4 * GW), BF),
            jax.ShapeDtypeStruct((SEQ, 128), F32),
            jax.ShapeDtypeStruct((SEQ, 256), BF),
            jax.ShapeDtypeStruct((8, 4 * GW), F32),
            jax.ShapeDtypeStruct((8, 128), F32),
            jax.ShapeDtypeStruct((8, 256), F32),
        ),
        in_specs=[
            cols, cols, cols, pcol,
            whole_spec((SEQ, 128)), whole_spec((SEQ, 128)), whole_spec((SEQ, 256)), whole_spec((CH, 256, L)),
            whole_spec((CH, L, L)),
            pl.BlockSpec((1, SEQ, 128), lambda g: (g, 0, 0)),
            pl.BlockSpec((1, CH, 8, L), lambda g: (g, 0, 0, 0)),
            pl.BlockSpec((1, CH, 128, GW), lambda g: (g, 0, 0, 0)),
            pl.BlockSpec((1, 8, 128), lambda g: (g, 0, 0)),
            whole_spec((SEQ, 256)), whole_spec((8, 256)), whole_spec((CH, 8, L)),
        ],
        out_specs=(
            cols, cols, whole_spec((SEQ, 128)), whole_spec((SEQ, 256)), pcol, whole_spec((8, 128)), whole_spec((8, 256)),
        ),
        scratch_shapes=[
            pltpu.VMEM((SEQ + 8, GW), F32),
            pltpu.VMEM((128, GW), F32),
            pltpu.VMEM((CH, L, L), F32),
            pltpu.VMEM((SEQ, 256), F32),
            pltpu.VMEM((SEQ + 8, 256), F32),
        ],
        compiler_params=pltpu.CompilerParams(vmem_limit_bytes=56 * 2**20),
        name="mixer_backward",
    )(inner_pre, gate_pre, d_inner, par, tok, inv, bc, bct, gs, pack, cumt, states, decay, state_pre, convst, row)


def on_device(fsdp, halves, hidden_in, norm_gain, in_gate, in_inner, in_state, in_step, conv_inner, conv_inner_shift,
              conv_state, conv_state_shift, step_offset, log_rate, skip_gain, inner_gain, out_weight, segment_ids,
              grad_out):
    both = ("fsdp", "zz")
    depth, width = in_gate.shape
    model = depth * fsdp
    inner = width * halves
    heads_dev = in_step.shape[1]
    heads = heads_dev * halves
    heads_all = 2 * heads
    unit = conv_inner.shape[2] * fsdp
    inner_all = 2 * inner
    core = lax.axis_index("core")
    zz = lax.axis_index("zz")
    rows = hidden_in.shape[0]

    def swap(x):
        return lax.ppermute(x, "core", [(0, 1), (1, 0)])

    def both_cores(own, other):
        return jnp.where(core == 0, jnp.concatenate([own, other], 0), jnp.concatenate([other, own], 0))

    small = [norm_gain, in_step, conv_inner, conv_inner_shift, conv_state, conv_state_shift, step_offset, log_rate,
             skip_gain, inner_gain]
    flat = jnp.concatenate([v.reshape(-1) for v in small])
    got = lax.all_gather(flat, both, axis=0).reshape(fsdp, halves, -1)
    parts = []
    at = 0
    for v in small:
        parts.append(got[:, :, at : at + v.size].reshape((fsdp, halves) + v.shape))
        at += v.size
    gain_outer = parts[0][:, 0].reshape(model).astype(F32)
    step_cols = parts[1].transpose(0, 2, 1, 3).reshape(model, heads)
    conv_in = parts[2].transpose(2, 1, 3, 0, 4).reshape(K, inner).astype(F32)
    shift_in = parts[3].transpose(1, 2, 0, 3).reshape(1, inner).astype(F32)
    conv_st = parts[4][:, 0].transpose(1, 0, 2).reshape(K, -1).astype(F32)
    shift_st = parts[5][:, 0].reshape(1, -1).astype(F32)
    gain_in = parts[9].transpose(1, 2, 0, 3).reshape(1, inner).astype(F32)

    def my_heads(v):
        return v.reshape(halves, 2, heads_dev)[:, core].reshape(heads).astype(F32)

    offset = my_heads(parts[6][:, 0].reshape(heads_all))
    decay = -jnp.exp(my_heads(parts[7][:, 0].reshape(heads_all)))
    skip = my_heads(parts[8][:, 0].reshape(heads_all))
    state_cols = lax.all_gather(in_state, "fsdp", axis=0, tiled=True)

    def columns(w):
        return lax.all_gather(w, both, axis=0).reshape(fsdp, halves, depth, width).transpose(0, 2, 1, 3).reshape(model, inner)

    inner_cols = columns(in_inner)
    gate_cols = columns(in_gate)
    out_rows = lax.all_gather(out_weight, both, axis=0).reshape(fsdp, halves, width, depth).transpose(1, 2, 0, 3).reshape(inner, model)

    par = jnp.concatenate([conv_in, shift_in, jnp.repeat(skip, unit)[None], gain_in, jnp.zeros((1, inner), F32)], 0)
    convst = jnp.concatenate([conv_st, shift_st, jnp.zeros((3, 256), F32)], 0)
    head = jnp.pad(jnp.stack([offset, decay]), ((0, 6), (0, 128 - heads)))
    decay_g = jnp.pad(decay.reshape(heads // GH, 1, GH), ((0, 0), (0, 7), (0, 128 - GH)))

    docs = lax.dynamic_slice_in_dim(segment_ids, zz * SEQ, SEQ)
    blocks = docs.reshape(CH, L)
    prior = jnp.concatenate([jnp.full((1,), -1, docs.dtype), blocks[:-1, -1]])
    masks = [docs, (blocks == prior[:, None]).reshape(SEQ), (blocks == blocks[:, -1:]).reshape(SEQ)]
    for k in range(1, K):
        masks.append(jnp.concatenate([jnp.zeros((k,), bool), docs[k:] == docs[:-k]]))
    for k in range(1, K):
        masks.append(jnp.concatenate([docs[k:] == docs[:-k], jnp.zeros((k,), bool)]))
    tok = jnp.pad(jnp.stack([m.astype(F32) for m in masks], 1), ((0, 0), (0, 128 - len(masks))))
    row = jnp.broadcast_to(blocks.astype(F32)[:, None, :], (CH, 8, L))

    hidden_all = both_cores(hidden_in, swap(hidden_in)).astype(F32)
    cot_all = both_cores(grad_out, swap(grad_out))
    inv_rms = lax.rsqrt(jnp.mean(hidden_all * hidden_all, -1, keepdims=True) + EPSILON)
    normed = (hidden_all * inv_rms * gain_outer).astype(BF)
    small_cols = jnp.concatenate([state_cols, jnp.pad(step_cols, ((0, 0), (0, 128 - heads)))], 1)
    pre_small = mm(normed, small_cols)
    state_pre = pre_small[:, :256]
    step_pre = pre_small[:, 256:]
    inner_pre = mm(normed, inner_cols)
    gate_pre = mm(normed, gate_cols)
    bc, bct, gs, pack, cumt = prep(state_pre, step_pre, tok, row, convst, head)
    gated, states, ss = fwd(inner_pre, gate_pre, par, tok, bc, bct, gs, pack, cumt)
    ss_own = jnp.sum(ss, -1)
    squares = ss_own + swap(ss_own)
    inner_inv = lax.rsqrt(squares / inner_all + EPSILON)[:, None]
    normed_inner = (gated * inner_inv * gain_in).astype(BF)
    mixed = mm(normed_inner, out_rows)

    def to_own(x):
        own = lax.dynamic_slice_in_dim(x, core * rows, rows)
        other = lax.dynamic_slice_in_dim(x, (1 - core) * rows, rows)
        return own + swap(other.astype(BF)).astype(F32)

    layer_out = (hidden_in.astype(F32) + to_own(mixed)).astype(BF)
    grad_out_part = mm(normed_inner, cot_all, ((0,), (0,)))
    d_inner = mm(cot_all, out_rows, ((1,), (1,)))
    grad_gain_in = jnp.sum(d_inner * gated * inner_inv, 0)
    prod_own = jnp.sum(gated * d_inner * gain_in, -1)
    products = prod_own + swap(prod_own)
    inv_pack = jnp.pad(
        jnp.stack([inner_inv[:, 0], inner_inv[:, 0] ** 3 * products / inner_all], 1), ((0, 0), (0, 126))
    )
    d_gate, d_pre, d_step, d_state, pgrad, hgrad, sgrad = bwd(
        inner_pre, gate_pre, d_inner, par, tok, inv_pack, bc, bct, gs, pack, cumt, states, decay_g, state_pre, convst, row
    )
    d_step = d_step.astype(BF)
    d_small = jnp.concatenate([d_state, d_step], 1)
    d_normed = to_own(
        mm(d_gate, gate_cols, ((1,), (1,))) + mm(d_pre, inner_cols, ((1,), (1,))) + mm(d_small, small_cols, ((1,), (1,)))
    )
    hidden = hidden_in.astype(F32)
    inv_own = lax.dynamic_slice_in_dim(inv_rms, core * rows, rows)
    grad_gain_outer = jnp.sum(d_normed * hidden * inv_own, 0)
    weighted_back = d_normed * gain_outer
    d_hidden = inv_own * weighted_back - hidden * inv_own**3 * jnp.mean(hidden * weighted_back, -1, keepdims=True)
    grad_hidden = (grad_out.astype(F32) + d_hidden).astype(BF)

    def scatter_columns(g):
        g = g.astype(BF).reshape(fsdp, depth, halves, width).transpose(0, 2, 1, 3).reshape(fsdp * halves, depth, width)
        return lax.psum_scatter(g, both, scatter_dimension=0).astype(F32)

    grad_gate = scatter_columns(mm(normed, d_gate, ((0,), (0,))))
    grad_inner = scatter_columns(mm(normed, d_pre, ((0,), (0,))))
    grad_small = mm(normed, d_small, ((0,), (0,)))
    grad_out_weight = grad_out_part.astype(BF).reshape(halves, width, fsdp, depth).transpose(2, 0, 1, 3)
    grad_out_weight = lax.psum_scatter(
        grad_out_weight.reshape(fsdp * halves, width, depth), both, scatter_dimension=0
    ).astype(F32)
    grad_state = lax.psum_scatter(grad_small[:, :256].astype(BF), "fsdp", scatter_dimension=0, tiled=True)
    grad_state = lax.psum(grad_state, ("zz", "core")).astype(F32)

    own_heads = [
        grad_small[:, 256 : 256 + heads].reshape(fsdp, depth, halves, heads_dev).transpose(0, 2, 1, 3),
        pgrad[:K].reshape(K, halves, heads_dev, fsdp, -1).transpose(3, 1, 0, 2, 4),
        pgrad[K].reshape(halves, heads_dev, fsdp, -1).transpose(2, 0, 1, 3),
        grad_gain_in.reshape(halves, heads_dev, fsdp, -1).transpose(2, 0, 1, 3),
    ]
    sizes = [v.shape[2:] for v in own_heads]
    stacked = jnp.concatenate([v.reshape(fsdp * halves, -1) for v in own_heads], 1)
    mine = lax.psum_scatter(stacked, both, scatter_dimension=0)
    outs = []
    at = 0
    for s in sizes:
        n = 1
        for d in s:
            n *= d
        outs.append(mine[at : at + n].reshape(s))
        at += n
    grad_step, grad_conv_in, grad_conv_in_shift, grad_gain_inner = outs

    def place(v):
        v = v.reshape(halves, 1, heads_dev)
        zero = jnp.zeros_like(v)
        return jnp.where(core == 0, jnp.concatenate([v, zero], 1), jnp.concatenate([zero, v], 1)).reshape(heads_all)

    skip_sum = jnp.sum(pgrad[P_SKIP].reshape(heads, unit), 1)
    shared = [grad_gain_outer.reshape(fsdp, depth), sgrad[:K].reshape(K, fsdp, -1).transpose(1, 0, 2), sgrad[K].reshape(fsdp, -1)]
    shared += [place(v).reshape(fsdp, -1) for v in (hgrad[1, :heads], hgrad[0, :heads], skip_sum)]
    sizes = [v.shape[1:] for v in shared]
    stacked = jnp.concatenate([v.reshape(fsdp, -1) for v in shared], 1)
    mine = lax.psum(stacked, ("fsdp", "zz", "core"))
    mine = lax.dynamic_index_in_dim(mine, lax.axis_index("fsdp"), keepdims=False)
    outs = []
    at = 0
    for s in sizes:
        n = 1
        for d in s:
            n *= d
        outs.append(mine[at : at + n].reshape(s))
        at += n
    grad_norm_gain, grad_conv_st, grad_conv_st_shift, grad_offset, grad_rate, grad_skip = outs
    return (layer_out, grad_hidden, grad_norm_gain, grad_gate, grad_inner, grad_state, grad_step, grad_conv_in,
            grad_conv_in_shift, grad_conv_st, grad_conv_st_shift, grad_offset, grad_rate, grad_skip, grad_gain_inner,
            grad_out_weight)


def solution(mesh):
    fsdp = mesh.shape["fsdp"]
    halves = mesh.shape["tensor"] // 2
    fine = jax.sharding.Mesh(mesh.devices.reshape(fsdp, halves, 2), ("fsdp", "zz", "core"))
    tensor = ("zz", "core")
    tokens = P(("fsdp", "zz", "core"), None)
    grid = P("fsdp", tensor)
    heads = P(tensor, "fsdp")
    return jax.shard_map(
        functools.partial(on_device, fsdp, halves),
        mesh=fine,
        in_specs=(
            tokens, P("fsdp"), grid, grid, P("fsdp", None), grid, P(None, tensor, "fsdp"), heads, P(None, "fsdp"),
            P("fsdp"), P("fsdp"), P("fsdp"), P("fsdp"), heads, heads, P("fsdp"), tokens,
        ),
        out_specs=(
            tokens, tokens, P("fsdp"), grid, grid, P("fsdp", None), grid, P(None, tensor, "fsdp"), heads,
            P(None, "fsdp"), P("fsdp"), P("fsdp"), P("fsdp"), P("fsdp"), heads, heads,
        ),
        check_vma=False,
    )
```

```python
import functools

import jax
import jax.numpy as jnp
from jax import lax
from jax.sharding import PartitionSpec as P
from jax.experimental import pallas as pl
from jax.experimental.pallas import tpu as pltpu

SEQ = 1024
L = 128
CH = SEQ // L
K = 4
GH = 6
GW = 384
EPSILON = 1e-05
LOG2E = 1.4426950408889634
F32 = jnp.float32
BF = jnp.bfloat16
ST, CU, EE, FF, SG = 0, 8, 16, 24, 32


def mm(a, b, dims=((1,), (0,))):
    return lax.dot_general(a, b, (dims, ((), ())), preferred_element_type=F32)


def split2(x):
    hi = x.astype(BF)
    return hi, (x - hi.astype(F32)).astype(BF)


def split3(x):
    hi = x.astype(BF)
    rest = x - hi.astype(F32)
    mid = rest.astype(BF)
    return hi, mid, (rest - mid.astype(F32)).astype(BF)


def sigmoid(v):
    return 1.0 / (1.0 + jnp.exp(-v))


def back_conv_input(window, k):
    return window[8 - k : 8 - k + L]


def prep_body(state_ref, step_ref, tok_ref, row_ref, convst_ref, head_ref,
              bc_ref, bct_ref, g_ref, pack_ref, cumt_ref, pad_ref):
    pad_ref[pl.ds(0, 8), :] = jnp.zeros((8, 256), F32)
    pad_ref[pl.ds(8, SEQ), :] = state_ref[...]
    lane = lax.broadcasted_iota(jnp.int32, (L, L), 1)
    sub = lax.broadcasted_iota(jnp.int32, (L, L), 0)
    tri = (sub >= lane).astype(BF)
    offset = head_ref[0:1, :]
    decay = head_ref[1:2, :]
    taps = [convst_ref[k : k + 1, :] for k in range(K)]
    shift = convst_ref[K : K + 1, :]

    def chunk(c, _):
        base = pl.multiple_of(c * L, L)
        rows = pl.ds(base, L)
        tok = tok_ref[rows, :]
        window = pad_ref[pl.ds(base, L + 8), :]
        total = shift + taps[K - 1] * back_conv_input(window, 0)
        for k in range(1, K):
            total = total + taps[K - 1 - k] * (back_conv_input(window, k) * tok[:, 2 + k : 3 + k])
        act = total * sigmoid(total)
        low = act.astype(BF)
        bc_ref[rows, :] = low
        bct_ref[c] = jnp.concatenate([act[:, :128].T, act[:, 128:].T], 0).astype(BF)
        scores = mm(low[:, 128:], low[:, :128], ((1,), (1,)))
        same = (tok[:, 0:1] == row_ref[c][0:1, :]) & (sub >= lane)
        g_ref[c] = jnp.where(same, scores, 0.0)
        v = step_ref[rows, :] + offset
        steps = jnp.maximum(v, 0.0) + jnp.log1p(jnp.exp(-jnp.abs(v)))
        logs = steps * (decay * LOG2E)
        hi, mid, lo = split3(logs)
        cum = mm(tri, hi) + mm(tri, mid) + mm(tri, lo)
        last = cum[L - 1 : L, :]
        enter = jnp.exp2(cum) * tok[:, 1:2]
        leave = jnp.exp2(last - cum) * tok[:, 2:3]
        sig = sigmoid(v)
        cumt = cum.T
        zeros = jnp.zeros((L, 2), F32)
        for g in range(4):
            part = slice(GH * g, GH * g + GH)
            pieces = []
            for values in (steps, cum, enter, leave, sig):
                pieces += [values[:, part], zeros]
            pieces.append(jnp.zeros((L, 88), F32))
            pack_ref[g, rows, :] = jnp.concatenate(pieces, 1)
            cumt_ref[g, c] = jnp.concatenate([cumt[part, :], jnp.zeros((2, L), F32)], 0)
        return 0

    lax.fori_loop(0, CH, chunk, 0)


def vm(*shape):
    return pl.BlockSpec(memory_space=pltpu.VMEM)


def prep(state_pre, step_pre, tok, row, convst, head):
    return pl.pallas_call(
        prep_body,
        out_shape=(
            jax.ShapeDtypeStruct((SEQ, 256), BF),
            jax.ShapeDtypeStruct((CH, 256, L), BF),
            jax.ShapeDtypeStruct((CH, L, L), F32),
            jax.ShapeDtypeStruct((4, SEQ, 128), F32),
            jax.ShapeDtypeStruct((4, CH, 8, L), F32),
        ),
        in_specs=[vm()] * 6,
        out_specs=[vm()] * 5,
        scratch_shapes=[pltpu.VMEM((SEQ + 8, 256), F32)],
        compiler_params=pltpu.CompilerParams(vmem_limit_bytes=56 * 2**20),
        name="prep",
    )(state_pre, step_pre, tok, row, convst, head)


def pair_lanes(pack, first, q):
    lane = lax.broadcasted_iota(jnp.int32, (pack.shape[0], 128), 1)
    a = pack[:, first + 2 * q : first + 2 * q + 1]
    b = pack[:, first + 2 * q + 1 : first + 2 * q + 2]
    return jnp.where(lane < 64, a, b)


def spread(pack, first):
    return jnp.concatenate([pair_lanes(pack, first, q) for q in range(3)], 1)


def block_diag(x):
    lane = lax.broadcasted_iota(jnp.int32, x.shape, 1)
    zero = jnp.zeros_like(x)
    return jnp.concatenate([jnp.where(lane < 64, x, zero), jnp.where(lane < 64, zero, x)], 0)


def decay_kernel(pack, cumt, h):
    return jnp.exp2(jnp.minimum(pack[:, CU + h : CU + h + 1] - cumt[h : h + 1, :], 0.0))


def conv_of(window, tok, par):
    total = par[K : K + 1, :] + par[K - 1 : K, :] * back_conv_input(window, 0)
    for k in range(1, K):
        total = total + par[K - 1 - k : K - k, :] * (back_conv_input(window, k) * tok[:, 2 + k : 3 + k])
    return total


P_SHIFT, P_SKIP, P_GAIN = 4, 5, 6


def fwd_body(inner_ref, gate_ref, par_ref, tok_ref, bc_ref, bct_ref, g_ref, pack_ref, cumt_ref,
             gated_ref, states_ref, ss_ref, pad_ref, st_ref):
    pad_ref[pl.ds(0, 8), :] = jnp.zeros((8, GW), F32)
    pad_ref[pl.ds(8, SEQ), :] = inner_ref[...]
    st_ref[...] = jnp.zeros_like(st_ref)
    par = par_ref[...]

    @pl.when(pl.program_id(0) == 0)
    def _():
        ss_ref[...] = jnp.zeros_like(ss_ref)

    def chunk(c, _):
        base = pl.multiple_of(c * L, L)
        rows = pl.ds(base, L)
        tok = tok_ref[rows, :]
        u = conv_of(pad_ref[pl.ds(base, L + 8), :], tok, par)
        act = u * sigmoid(u)
        pack = pack_ref[0, rows, :]
        cumt = cumt_ref[0, c]
        g = g_ref[c]
        weighted = act * spread(pack, ST)
        low = weighted.astype(BF)
        enter = spread(pack, EE)
        state = st_ref[...]
        low_state = state.astype(BF)
        states_ref[0, c] = low_state
        y = mm(bc_ref[rows, 128:], low_state) * enter
        locals_ = []
        for q in range(3):
            kernels = [(g * decay_kernel(pack, cumt, 2 * q + e)).astype(BF) for e in range(2)]
            locals_.append(mm(jnp.concatenate(kernels, 1), block_diag(low[:, 128 * q : 128 * q + 128])))
        y = y + jnp.concatenate(locals_, 1)
        out = weighted * spread(pack, FF)
        st_ref[...] = enter[L - 1 : L, :] * state + mm(bct_ref[c, pl.ds(0, 128), :], out.astype(BF))
        ssd = y + par[P_SKIP : P_SKIP + 1, :] * act
        gate = gate_ref[rows, :]
        gated = ssd * (gate * sigmoid(gate))
        gated_ref[rows, :] = gated
        sq = gated * gated
        ss_ref[rows, :] += sq[:, :128] + sq[:, 128:256] + sq[:, 256:]
        return 0

    lax.fori_loop(0, CH, chunk, 0)


def whole_spec(shape):
    return pl.BlockSpec(shape, lambda g: (0,) * len(shape))


def fwd(inner_pre, gate_pre, par, tok, bc, bct, gs, pack, cumt):
    cols = pl.BlockSpec((SEQ, GW), lambda g: (0, g))
    return pl.pallas_call(
        fwd_body,
        grid=(4,),
        out_shape=(
            jax.ShapeDtypeStruct((SEQ, 4 * GW), F32),
            jax.ShapeDtypeStruct((4, CH, 128, GW), BF),
            jax.ShapeDtypeStruct((SEQ, 128), F32),
        ),
        in_specs=[
            cols, cols, pl.BlockSpec((8, GW), lambda g: (0, g)),
            whole_spec((SEQ, 128)), whole_spec((SEQ, 256)), whole_spec((CH, 256, L)), whole_spec((CH, L, L)),
            pl.BlockSpec((1, SEQ, 128), lambda g: (g, 0, 0)),
            pl.BlockSpec((1, CH, 8, L), lambda g: (g, 0, 0, 0)),
        ],
        out_specs=(
            cols,
            pl.BlockSpec((1, CH, 128, GW), lambda g: (g, 0, 0, 0)),
            whole_spec((SEQ, 128)),
        ),
        scratch_shapes=[pltpu.VMEM((SEQ + 8, GW), F32), pltpu.VMEM((128, GW), F32)],
        compiler_params=pltpu.CompilerParams(vmem_limit_bytes=56 * 2**20),
        name="mixer_forward",
    )(inner_pre, gate_pre, par, tok, bc, bct, gs, pack, cumt)


def bwd_body(inner_ref, gate_ref, dinner_ref, par_ref, tok_ref, inv_ref, bc_ref, bct_ref, g_ref, pack_ref,
             cumt_ref, states_ref, decay_ref, state_pre_ref, convst_ref, row_ref,
             dgate_ref, dpre_ref, dstep_ref, dstate_ref, pgrad_ref, hgrad_ref, sgrad_ref,
             pad_ref, rt_ref, dg_ref, dbc_ref, spad_ref):
    group = pl.program_id(0)
    pad_ref[pl.ds(0, 8), :] = jnp.zeros((8, GW), F32)
    pad_ref[pl.ds(8, SEQ), :] = inner_ref[...]
    rt_ref[...] = jnp.zeros_like(rt_ref)
    pgrad_ref[...] = jnp.zeros_like(pgrad_ref)
    par = par_ref[...]
    decay = decay_ref[0]

    @pl.when(group == 0)
    def _():
        dg_ref[...] = jnp.zeros_like(dg_ref)
        dbc_ref[...] = jnp.zeros_like(dbc_ref)
        dstep_ref[...] = jnp.zeros_like(dstep_ref)
        hgrad_ref[...] = jnp.zeros_like(hgrad_ref)

    lane = lax.broadcasted_iota(jnp.int32, (L, L), 1)
    sub = lax.broadcasted_iota(jnp.int32, (L, L), 0)
    upper = (sub <= lane).astype(BF)
    per_head = (lax.broadcasted_iota(jnp.int32, (GW, 128), 0) >> 6
                == lax.broadcasted_iota(jnp.int32, (GW, 128), 1)).astype(BF)

    def head_sums(x):
        hi, lo = split2(x)
        return mm(hi, per_head) + mm(lo, per_head)

    def chunk(step, later):
        c = CH - 1 - step
        base = pl.multiple_of(c * L, L)
        rows = pl.ds(base, L)
        tok = tok_ref[rows, :]
        window = pad_ref[pl.ds(base, L + 8), :]
        u = conv_of(window, tok, par)
        su = sigmoid(u)
        act = u * su
        pack = pack_ref[0, rows, :]
        cumt = cumt_ref[0, c]
        g = g_ref[c]
        steps = spread(pack, ST)
        enter = spread(pack, EE)
        leave = spread(pack, FF)
        weighted = act * steps
        low = weighted.astype(BF)
        low_state = states_ref[0, c]
        bmat = bc_ref[rows, :128]
        cmat = bc_ref[rows, 128:]
        diags = [block_diag(low[:, 128 * q : 128 * q + 128]) for q in range(3)]
        decays = [decay_kernel(pack, cumt, h) for h in range(GH)]
        kernels = [jnp.concatenate([(g * decays[2 * q + e]).astype(BF) for e in range(2)], 1) for q in range(3)]
        y = mm(cmat, low_state) * enter + jnp.concatenate([mm(kernels[q], diags[q]) for q in range(3)], 1)
        skip = par[P_SKIP : P_SKIP + 1, :]
        ssd = y + skip * act
        gate = gate_ref[rows, :]
        sg = sigmoid(gate)
        silu = gate * sg
        scaled = dinner_ref[rows, :] * par[P_GAIN : P_GAIN + 1, :]
        inv = inv_ref[rows, :]
        d_gated = inv[:, 0:1] * scaled - (ssd * silu) * inv[:, 1:2]
        dy = d_gated * silu
        dgate_ref[rows, :] = (d_gated * ssd * sg * (1.0 + gate * (1.0 - sg))).astype(BF)
        dy_low = dy.astype(BF)
        dy_in = (dy * enter).astype(BF)
        rt = rt_ref[...]
        rt_low = rt.astype(BF)
        carried = mm(bmat, rt_low) * leave
        pieces = []
        d_scores = jnp.zeros((L, L), F32)
        for q in range(3):
            dq = dy_low[:, 128 * q : 128 * q + 128]
            dm = mm(dq, diags[q], ((1,), (1,)))
            d_scores = d_scores + dm[:, :L] * decays[2 * q] + dm[:, L:] * decays[2 * q + 1]
            both = mm(kernels[q], dq, ((0,), (0,)))
            pieces.append(jnp.where(lane < 64, both[:L], both[L:]))
        d_weighted = jnp.concatenate(pieces, 1) + carried
        dg_ref[c] += d_scores
        out = (weighted * leave).astype(BF)
        dbc_ref[rows, 128:] += mm(dy_in, low_state, ((1,), (1,)))
        dbc_ref[rows, :128] += mm(out, rt_low, ((1,), (1,)))
        keep = enter[L - 1 : L, :]
        low32 = low.astype(F32)
        d_cum = head_sums(dy_low.astype(F32) * y - low32 * d_weighted)
        at_end = jnp.sum(low32 * carried, 0, keepdims=True) + keep * jnp.sum(rt * low_state.astype(F32), 0, keepdims=True)
        d_last = head_sums(jnp.concatenate([at_end, jnp.zeros((7, GW), F32)], 0))[0:1, :]
        hi, mid, lo = split3(d_cum)
        d_log = mm(upper, hi) + mm(upper, mid) + mm(upper, lo) + d_last
        rt_ref[...] = keep * rt + mm(bct_ref[c, pl.ds(128, 128), :], dy_in)
        d_step = head_sums(act * d_weighted) + decay[0:1, :] * d_log
        heads = lane < GH
        d_step_pre = jnp.where(heads, d_step * jnp.roll(pack, -SG, 1), 0.0)
        dstep_ref[rows, :] += pltpu.roll(d_step_pre, GH * group, 1)
        rate = jnp.sum(jnp.where(heads, pack, 0.0) * d_log, 0, keepdims=True) * decay[0:1, :]
        offs = jnp.sum(d_step_pre, 0, keepdims=True)
        hgrad_ref[0:1, :] += pltpu.roll(jnp.concatenate([rate, jnp.zeros((7, 128), F32)], 0), GH * group, 1)[0:1]
        hgrad_ref[1:2, :] += pltpu.roll(jnp.concatenate([offs, jnp.zeros((7, 128), F32)], 0), GH * group, 1)[0:1]
        d_act = skip * dy + steps * d_weighted
        du = d_act * su * (1.0 + u * (1.0 - su))
        pgrad_ref[K : K + 1, :] += jnp.sum(du, 0, keepdims=True)
        pgrad_ref[P_SKIP : P_SKIP + 1, :] += jnp.sum(dy * act, 0, keepdims=True)
        for k in range(K):
            moved = back_conv_input(window, k)
            if k:
                moved = moved * tok[:, 2 + k : 3 + k]
            pgrad_ref[K - 1 - k : K - k, :] += jnp.sum(du * moved, 0, keepdims=True)
        ahead = jnp.concatenate([du, later], 0)
        d_pre = par[K - 1 : K, :] * du
        for k in range(1, K):
            d_pre = d_pre + par[K - 1 - k : K - k, :] * (ahead[k : k + L] * tok[:, 5 + k : 6 + k])
        dpre_ref[rows, :] = d_pre.astype(BF)
        return du[:8]

    lax.fori_loop(0, CH, chunk, jnp.zeros((8, GW), F32))

    @pl.when(group == pl.num_programs(0) - 1)
    def _():
        spad_ref[pl.ds(0, 8), :] = jnp.zeros((8, 256), F32)
        spad_ref[pl.ds(8, SEQ), :] = state_pre_ref[...]
        sgrad_ref[...] = jnp.zeros_like(sgrad_ref)
        cst = convst_ref[...]

        def last(step, later):
            c = CH - 1 - step
            base = pl.multiple_of(c * L, L)
            rows = pl.ds(base, L)
            tok = tok_ref[rows, :]
            same = (tok[:, 0:1] == row_ref[c][0:1, :]) & (sub >= lane)
            ds = jnp.where(same, dg_ref[c], 0.0).astype(BF)
            d_c = dbc_ref[rows, 128:] + mm(ds, bc_ref[rows, :128])
            d_b = dbc_ref[rows, :128] + mm(ds, bc_ref[rows, 128:], ((0,), (0,)))
            window = spad_ref[pl.ds(base, L + 8), :]
            w = conv_of(window, tok, cst)
            sw = sigmoid(w)
            dw = jnp.concatenate([d_b, d_c], 1) * (sw * (1.0 + w * (1.0 - sw)))
            sgrad_ref[K : K + 1, :] += jnp.sum(dw, 0, keepdims=True)
            for k in range(K):
                moved = back_conv_input(window, k)
                if k:
                    moved = moved * tok[:, 2 + k : 3 + k]
                sgrad_ref[K - 1 - k : K - k, :] += jnp.sum(dw * moved, 0, keepdims=True)
            ahead = jnp.concatenate([dw, later], 0)
            d_pre = cst[K - 1 : K, :] * dw
            for k in range(1, K):
                d_pre = d_pre + cst[K - 1 - k : K - k, :] * (ahead[k : k + L] * tok[:, 5 + k : 6 + k])
            dstate_ref[rows, :] = d_pre.astype(BF)
            return dw[:8]

        lax.fori_loop(0, CH, last, jnp.zeros((8, 256), F32))


def bwd(inner_pre, gate_pre, d_inner, par, tok, inv, bc, bct, gs, pack, cumt, states, decay, state_pre, convst, row):
    cols = pl.BlockSpec((SEQ, GW), lambda g: (0, g))
    pcol = pl.BlockSpec((8, GW), lambda g: (0, g))
    return pl.pallas_call(
        bwd_body,
        grid=(4,),
        out_shape=(
            jax.ShapeDtypeStruct((SEQ, 4 * GW), BF),
            jax.ShapeDtypeStruct((SEQ, 4 * GW), BF),
            jax.ShapeDtypeStruct((SEQ, 128), F32),
            jax.ShapeDtypeStruct((SEQ, 256), BF),
            jax.ShapeDtypeStruct((8, 4 * GW), F32),
            jax.ShapeDtypeStruct((8, 128), F32),
            jax.ShapeDtypeStruct((8, 256), F32),
        ),
        in_specs=[
            cols, cols, cols, pcol,
            whole_spec((SEQ, 128)), whole_spec((SEQ, 128)), whole_spec((SEQ, 256)), whole_spec((CH, 256, L)),
            whole_spec((CH, L, L)),
            pl.BlockSpec((1, SEQ, 128), lambda g: (g, 0, 0)),
            pl.BlockSpec((1, CH, 8, L), lambda g: (g, 0, 0, 0)),
            pl.BlockSpec((1, CH, 128, GW), lambda g: (g, 0, 0, 0)),
            pl.BlockSpec((1, 8, 128), lambda g: (g, 0, 0)),
            whole_spec((SEQ, 256)), whole_spec((8, 256)), whole_spec((CH, 8, L)),
        ],
        out_specs=(
            cols, cols, whole_spec((SEQ, 128)), whole_spec((SEQ, 256)), pcol, whole_spec((8, 128)), whole_spec((8, 256)),
        ),
        scratch_shapes=[
            pltpu.VMEM((SEQ + 8, GW), F32),
            pltpu.VMEM((128, GW), F32),
            pltpu.VMEM((CH, L, L), F32),
            pltpu.VMEM((SEQ, 256), F32),
            pltpu.VMEM((SEQ + 8, 256), F32),
        ],
        compiler_params=pltpu.CompilerParams(vmem_limit_bytes=56 * 2**20),
        name="mixer_backward",
    )(inner_pre, gate_pre, d_inner, par, tok, inv, bc, bct, gs, pack, cumt, states, decay, state_pre, convst, row)


def prep_chunks(state_ref, step_ref, tok_ref, row_ref, convst_ref, head_ref,
                bc_ref, bct_ref, g_ref, pack_ref, cumt_ref, pad_ref):
    pad_ref[pl.ds(0, 8), :] = jnp.zeros((8, 256), F32)
    pad_ref[pl.ds(8, SEQ), :] = state_ref[...]
    lane = lax.broadcasted_iota(jnp.int32, (L, L), 1)
    sub = lax.broadcasted_iota(jnp.int32, (L, L), 0)
    tri = (sub >= lane).astype(BF)
    offset = head_ref[0:1, :]
    decay = head_ref[1:2, :]
    convst = convst_ref[...]

    def chunk(c, _):
        base = pl.multiple_of(c * L, L)
        rows = pl.ds(base, L)
        tok = tok_ref[rows, :]
        total = conv_of(pad_ref[pl.ds(base, L + 8), :], tok, convst)
        act = total * sigmoid(total)
        low = act.astype(BF)
        bc_ref[rows, :] = low
        bct_ref[c] = jnp.concatenate([act[:, :128].T, act[:, 128:].T], 0).astype(BF)
        scores = mm(low[:, 128:], low[:, :128], ((1,), (1,)))
        same = (tok[:, 0:1] == row_ref[pl.ds(c, 1), :]) & (sub >= lane)
        g_ref[c] = jnp.where(same, scores, 0.0)
        v = step_ref[rows, :] + offset
        steps = jnp.maximum(v, 0.0) + jnp.log1p(jnp.exp(-jnp.abs(v)))
        logs = steps * (decay * LOG2E)
        hi, mid, lo = split3(logs)
        cum = mm(tri, hi) + mm(tri, mid) + mm(tri, lo)
        last = cum[L - 1 : L, :]
        enter = jnp.exp2(cum) * tok[:, 1:2]
        leave = jnp.exp2(last - cum) * tok[:, 2:3]
        sig = sigmoid(v)
        cumt = cum.T
        for g in range(4):
            part = slice(16 * g, 16 * g + 8)
            pieces = [values[:, part] for values in (steps, cum, enter, leave, sig)]
            pieces.append(jnp.zeros((L, 88), F32))
            pack_ref[g, rows, :] = jnp.concatenate(pieces, 1)
            cumt_ref[g, c] = cumt[part, :]
        return 0

    lax.fori_loop(0, CH, chunk, 0)


def fwd_chunks(pre_ref, par_ref, tok_ref, bc_ref, bct_ref, g_ref, pack_ref, cumt_ref,
               gated_ref, states_ref, ss_ref, st_ref):
    st_ref[...] = jnp.zeros_like(st_ref)
    par = par_ref[...]

    def chunk(c, _):
        base = pl.multiple_of(c * L, L)
        rows = pl.ds(base, L)
        tok = tok_ref[rows, :]
        u = conv_of(pre_ref[pl.ds(base, L + 8), :GW], tok, par)
        act = u * sigmoid(u)
        pack = pack_ref[rows, :]
        cumt = cumt_ref[c]
        g = g_ref[c]
        weighted = act * spread(pack, ST)
        low = weighted.astype(BF)
        enter = spread(pack, EE)
        state = st_ref[...]
        low_state = state.astype(BF)
        states_ref[c] = low_state
        y = mm(bc_ref[rows, 128:], low_state) * enter
        locals_ = []
        for q in range(3):
            kernels = [(g * decay_kernel(pack, cumt, 2 * q + e)).astype(BF) for e in range(2)]
            locals_.append(mm(jnp.concatenate(kernels, 1), block_diag(low[:, 128 * q : 128 * q + 128])))
        y = y + jnp.concatenate(locals_, 1)
        out = weighted * spread(pack, FF)
        st_ref[...] = enter[L - 1 : L, :] * state + mm(bct_ref[c, pl.ds(0, 128), :], out.astype(BF))
        ssd = y + par[P_SKIP : P_SKIP + 1, :] * act
        gate = pre_ref[pl.ds(base + 8, L), GW:]
        gated = ssd * (gate * sigmoid(gate))
        gated_ref[rows, :] = gated.astype(BF)
        sq = gated * gated
        ss_ref[rows, :] += sq[:, :128] + sq[:, 128:256] + sq[:, 256:]
        return 0

    lax.fori_loop(0, CH, chunk, 0)


def bwd_chunks(group, z_k, tick, pre_ref, dinner_ref, par_ref, tok_ref, inv_ref, bc_ref, bct_ref, g_ref, pack_ref,
               cumt_ref, states_ref, hpar_ref, dcat_ref, dstep_ref, pgrad_ref, hgrad_ref, rt_ref, dg_ref, dbc_ref):
    rt_ref[...] = jnp.zeros_like(rt_ref)
    pgrad_ref[...] = jnp.zeros_like(pgrad_ref)
    par = par_ref[...]
    decay = pltpu.roll(hpar_ref[...], (128 - 16 * group) % 128, 1)[1:2, :]
    lane = lax.broadcasted_iota(jnp.int32, (L, L), 1)
    sub = lax.broadcasted_iota(jnp.int32, (L, L), 0)
    upper = (sub <= lane).astype(BF)
    per_head = (lax.broadcasted_iota(jnp.int32, (GW, 128), 0) >> 6
                == lax.broadcasted_iota(jnp.int32, (GW, 128), 1)).astype(BF)

    def head_sums(x):
        hi, lo = split2(x)
        return mm(hi, per_head) + mm(lo, per_head)

    def chunk(step, later):
        tick(step)
        c = CH - 1 - step
        base = pl.multiple_of(c * L, L)
        rows = pl.ds(base, L)
        tok = tok_ref[rows, :]
        window = pre_ref[pl.ds(base, L + 8), :GW]
        u = conv_of(window, tok, par)
        su = sigmoid(u)
        act = u * su
        pack = pack_ref[rows, :]
        cumt = cumt_ref[c]
        g = g_ref[c]
        steps = spread(pack, ST)
        enter = spread(pack, EE)
        leave = spread(pack, FF)
        weighted = act * steps
        low = weighted.astype(BF)
        low_state = states_ref[c]
        bmat = bc_ref[rows, :128]
        cmat = bc_ref[rows, 128:]
        diags = [block_diag(low[:, 128 * q : 128 * q + 128]) for q in range(3)]
        decays = [decay_kernel(pack, cumt, h) for h in range(GH)]
        kernels = [jnp.concatenate([(g * decays[2 * q + e]).astype(BF) for e in range(2)], 1) for q in range(3)]
        y = mm(cmat, low_state) * enter + jnp.concatenate([mm(kernels[q], diags[q]) for q in range(3)], 1)
        skip = par[P_SKIP : P_SKIP + 1, :]
        ssd = y + skip * act
        gate = pre_ref[pl.ds(base + 8, L), GW:]
        sg = sigmoid(gate)
        silu = gate * sg
        scaled = dinner_ref[rows, :] * par[P_GAIN : P_GAIN + 1, :]
        inv = inv_ref[rows, :]
        d_gated = inv[:, 0:1] * scaled - (ssd * silu) * inv[:, 1:2]
        dy = d_gated * silu
        dcat_ref[rows, GW:] = (d_gated * ssd * sg * (1.0 + gate * (1.0 - sg))).astype(BF)
        dy_low = dy.astype(BF)
        dy_in = (dy * enter).astype(BF)
        rt = rt_ref[...]
        rt_low = rt.astype(BF)
        carried = mm(bmat, rt_low) * leave
        pieces = []
        d_scores = jnp.zeros((L, L), F32)
        for q in range(3):
            dq = dy_low[:, 128 * q : 128 * q + 128]
            dm = mm(dq, diags[q], ((1,), (1,)))
            d_scores = d_scores + dm[:, :L] * decays[2 * q] + dm[:, L:] * decays[2 * q + 1]
            both = mm(kernels[q], dq, ((0,), (0,)))
            pieces.append(jnp.where(lane < 64, both[:L], both[L:]))
        d_weighted = jnp.concatenate(pieces, 1) + carried
        dg_ref[c] += d_scores
        out = (weighted * leave).astype(BF)
        dbc_ref[rows, 128:] += mm(dy_in, low_state, ((1,), (1,)))
        dbc_ref[rows, :128] += mm(out, rt_low, ((1,), (1,)))
        keep = enter[L - 1 : L, :]
        low32 = low.astype(F32)
        d_cum = head_sums(dy_low.astype(F32) * y - low32 * d_weighted)
        at_end = jnp.sum(low32 * carried, 0, keepdims=True) + keep * jnp.sum(rt * low_state.astype(F32), 0, keepdims=True)
        d_last = head_sums(jnp.concatenate([at_end, jnp.zeros((7, GW), F32)], 0))[0:1, :]
        hi, mid, lo = split3(d_cum)
        d_log = mm(upper, hi) + mm(upper, mid) + mm(upper, lo) + d_last
        rt_ref[...] = keep * rt + mm(bct_ref[c, pl.ds(128, 128), :], dy_in)
        d_step = head_sums(act * d_weighted) + decay * d_log
        heads = lane < GH
        d_step_pre = jnp.where(heads, d_step * pltpu.roll(pack, 128 - SG, 1), 0.0)
        dstep_ref[rows, :] += pltpu.roll(d_step_pre, 16 * group, 1).astype(BF)
        rate = jnp.sum(jnp.where(heads, pack, 0.0) * d_log, 0, keepdims=True) * decay
        offs = jnp.sum(d_step_pre, 0, keepdims=True)
        hgrad_ref[0:1, :] += pltpu.roll(jnp.concatenate([rate, jnp.zeros((7, 128), F32)], 0), 16 * z_k, 1)[0:1]
        hgrad_ref[1:2, :] += pltpu.roll(jnp.concatenate([offs, jnp.zeros((7, 128), F32)], 0), 16 * z_k, 1)[0:1]
        d_act = skip * dy + steps * d_weighted
        du = d_act * su * (1.0 + u * (1.0 - su))
        pgrad_ref[K : K + 1, :] += jnp.sum(du, 0, keepdims=True)
        pgrad_ref[P_SKIP : P_SKIP + 1, :] += jnp.sum(dy * act, 0, keepdims=True)
        for k in range(K):
            moved = back_conv_input(window, k)
            if k:
                moved = moved * tok[:, 2 + k : 3 + k]
            pgrad_ref[K - 1 - k : K - k, :] += jnp.sum(du * moved, 0, keepdims=True)
        ahead = jnp.concatenate([du, later], 0)
        d_pre = par[K - 1 : K, :] * du
        for k in range(1, K):
            d_pre = d_pre + par[K - 1 - k : K - k, :] * (ahead[k : k + L] * tok[:, 5 + k : 6 + k])
        dcat_ref[rows, :GW] = d_pre.astype(BF)
        return du[:8]

    lax.fori_loop(0, CH, chunk, jnp.zeros((8, GW), F32))


def state_chunks(statepre_ref, cst_ref, tok_ref, row_ref, bc_ref, dg_ref, dbc_ref, dstate_ref, sgrad_ref, spad_ref):
    spad_ref[pl.ds(0, 8), :] = jnp.zeros((8, 256), F32)
    spad_ref[pl.ds(8, SEQ), :] = statepre_ref[...]
    sgrad_ref[...] = jnp.zeros_like(sgrad_ref)
    cst = cst_ref[...]
    lane = lax.broadcasted_iota(jnp.int32, (L, L), 1)
    sub = lax.broadcasted_iota(jnp.int32, (L, L), 0)

    def last(step, later):
        c = CH - 1 - step
        base = pl.multiple_of(c * L, L)
        rows = pl.ds(base, L)
        tok = tok_ref[rows, :]
        same = (tok[:, 0:1] == row_ref[pl.ds(c, 1), :]) & (sub >= lane)
        ds = jnp.where(same, dg_ref[c], 0.0).astype(BF)
        d_c = dbc_ref[rows, 128:] + mm(ds, bc_ref[rows, :128])
        d_b = dbc_ref[rows, :128] + mm(ds, bc_ref[rows, 128:], ((0,), (0,)))
        window = spad_ref[pl.ds(base, L + 8), :]
        w = conv_of(window, tok, cst)
        sw = sigmoid(w)
        dw = jnp.concatenate([d_b, d_c], 1) * (sw * (1.0 + w * (1.0 - sw)))
        sgrad_ref[K : K + 1, :] += jnp.sum(dw, 0, keepdims=True)
        for k in range(K):
            moved = back_conv_input(window, k)
            if k:
                moved = moved * tok[:, 2 + k : 3 + k]
            sgrad_ref[K - 1 - k : K - k, :] += jnp.sum(dw * moved, 0, keepdims=True)
        ahead = jnp.concatenate([dw, later], 0)
        d_pre = cst[K - 1 : K, :] * dw
        for k in range(1, K):
            d_pre = d_pre + cst[K - 1 - k : K - k, :] * (ahead[k : k + L] * tok[:, 5 + k : 6 + k])
        dstate_ref[rows, :] = d_pre.astype(BF)
        return dw[:8]

    lax.fori_loop(0, CH, last, jnp.zeros((8, 256), F32))


MESH = pl.DeviceIdType.MESH
VMEM_LIMIT = 63 * 2**20
R_GAIN, R_CONV, R_SHIFT, R_INNER, R_OFF, R_RATE, R_SKIP, R_CST = 6, 7, 11, 12, 13, 14, 15, 16
SMALL = 32


class Links:
    def __init__(self, send_sems):
        self.send_sems = send_sems
        self.number = {}
        self.like = {}
        self.ended = set()

    def send(self, name, src, dst, recv_sem, device, like=None):
        at = self.number.setdefault(name, len(self.number))
        self.like[name] = src if like is None else like
        pltpu.make_async_remote_copy(
            src_ref=src, dst_ref=dst, send_sem=self.send_sems.at[at], recv_sem=recv_sem,
            device_id=device, device_id_type=MESH,
        ).start()

    def arrived(self, dst, recv_sem, device):
        pltpu.make_async_remote_copy(
            src_ref=dst, dst_ref=dst, send_sem=self.send_sems.at[0], recv_sem=recv_sem,
            device_id=device, device_id_type=MESH,
        ).wait_recv()

    def left(self, name, recv_sem, device):
        self.ended.add(name)
        like = self.like[name]
        pltpu.make_async_remote_copy(
            src_ref=like, dst_ref=like, send_sem=self.send_sems.at[self.number[name]], recv_sem=recv_sem,
            device_id=device, device_id_type=MESH,
        ).wait_send()

    def finish(self, recv_sem, device):
        for name in self.number:
            if name not in self.ended:
                self.left(name, recv_sem, device)


class Place:
    def __init__(self):
        self.f = lax.axis_index("fsdp")
        self.z = lax.axis_index("zz")
        self.c = lax.axis_index("core")
        f, c = self.f, self.c
        y, x = f // 2, f % 2
        by_x = y * 2 + 1 - x
        by_y = (1 - y) * 2 + x
        self.f2 = by_x * (1 - c) + by_y * c
        self.f3 = by_y * (1 - c) + by_x * c
        self.f4 = 3 - f
        z_low, z_high = self.z % 2, self.z // 2
        self.zk = [((z_high + k // 2) % 2) * 2 + (z_low + k % 2) % 2 for k in range(4)]

    def at(self, f=None, z=None, c=None):
        return (self.f if f is None else f, self.z if z is None else z, self.c if c is None else c)

    def near(self):
        devices = [self.at(z=self.zk[k]) for k in (1, 2, 3)]
        return devices + [self.at(f=self.f2), self.at(f=self.f3), self.at(f=self.f4), self.at(c=1 - self.c)]

    def greet(self):
        for device in self.near():
            pl.semaphore_signal(pltpu.get_barrier_semaphore(), inc=1, device_id=device, device_id_type=MESH)

    def greeted(self):
        pl.semaphore_wait(pltpu.get_barrier_semaphore(), len(self.near()))


def piece(inout_ref, out_ref, m, f, z):
    depth = out_ref.shape[2] // 4
    at = pl.ds(pl.multiple_of(f * depth, depth), depth)
    if m == 2:
        return out_ref.at[z, :, at]
    return inout_ref.at[z, at, pl.ds(m * GW, GW)]


def iota(shape, dim):
    return lax.broadcasted_iota(jnp.int32, shape, dim)


def own_block(f, rows, unit):
    return ((iota((rows, GW), 1) & 63) == f * unit + iota((rows, GW), 0)).astype(BF)


def at_block(f, rows, size):
    row = iota((rows, GW), 0)
    return ((iota((rows, GW), 1) == f * size + row) & (row < size)).astype(BF)


def spread_units(values, place):
    rows = mm(values, place)
    return jnp.sum(jnp.where((iota(rows.shape, 1) >> 6) == iota(rows.shape, 0), rows, 0.0), 0, keepdims=True)


def small_block(f, vec_ref, step_ref, conv_ref, shift_ref, gain_ref, cst_ref):
    units = own_block(f, conv_ref.shape[2], conv_ref.shape[2])
    states = at_block(f, cst_ref.shape[1], cst_ref.shape[1])
    heads = at_block(f, 16, 12)
    steps = jnp.concatenate([step_ref[...].astype(F32), jnp.zeros((step_ref.shape[0], 128 - GH), F32)], 1).T
    rows = [steps[:GH], vec_ref[0:1, :]]
    rows += [spread_units(conv_ref[k], units) for k in range(K)]
    rows += [spread_units(shift_ref[...], units), spread_units(gain_ref[...], units)]
    rows.append(mm(vec_ref[2:5, :16].astype(BF), heads))
    rows.append(mm(cst_ref[...], states))
    rows.append(mm(vec_ref[1:2, :64].astype(BF), states))
    rows.append(jnp.zeros((SMALL - 21, GW), F32))
    return jnp.concatenate(rows, 0).astype(BF)


def token_masks(docs, tok_ref):
    lane, sub = iota((CH, L), 1), iota((CH, L), 0)
    masks = [docs, jnp.where((sub > 0) & (docs == pltpu.roll(docs, 1, 0)[:, L - 1 : L]), 1.0, 0.0)]
    masks.append(jnp.where(docs == docs[:, L - 1 : L], 1.0, 0.0))
    for k in range(1, K):
        moved = pltpu.roll(docs, k, 1)
        before = jnp.where(lane < k, pltpu.roll(moved, 1, 0), moved)
        masks.append(jnp.where((before == docs) & ((sub > 0) | (lane >= k)), 1.0, 0.0))
    for k in range(1, K):
        moved = pltpu.roll(docs, L - k, 1)
        after = jnp.where(lane >= L - k, pltpu.roll(moved, CH - 1, 0), moved)
        masks.append(jnp.where((after == docs) & ((sub < CH - 1) | (lane < L - k)), 1.0, 0.0))
    for c in range(CH):
        rows = [m[c : c + 1, :] for m in masks] + [jnp.zeros((128 - len(masks), L), F32)]
        tok_ref[pl.ds(c * L, L), :] = jnp.concatenate(rows, 0).T


def forward_kernel(model, hid_ref, cot_ref, w0_ref, w1_ref, w2_ref, wst_ref, vec_ref, step_ref, conv_ref, shift_ref, gain_ref,
                   cvst_ref, seg_ref,
                   normt_out, cot_out, win_out, wout_out, pre_out, dinner_out, nin_out, nint_out, states_out,
                   bc_ref, bct_ref, g_ref, pack_ref, cumt_ref, par_ref, hpar_ref, cst_ref, stw_ref, stbuf, gains_ref,
                   statepre_ref, invp_ref, gaingrad_ref, tok_ref, docs_ref,
                   small_ref, hall, call, win, wout, sbuf, pre, flip, ninner, gated, states, dinner, ss_ref, ssr_ref, pr_ref, prr_ref,
                   spad_ref, st_ref, stepre_ref,
                   sends, recvs, small_recvs, state_recvs, core_recvs, outs_sem, pre_sem, back_sem):
    here = Place()
    z, zk = here.z, here.zk
    rows_own = hid_ref.shape[0]
    depth = model // 4
    links = Links(sends)
    shards = [w0_ref, w1_ref, w2_ref]
    outs = []

    def put(src, dst):
        copy = pltpu.make_async_copy(src, dst, outs_sem.at[len(outs)])
        copy.start()
        outs.append(copy)

    here.greet()
    small_ref[...] = small_block(here.f, vec_ref, step_ref, conv_ref, shift_ref, gain_ref, cvst_ref)
    here.greeted()
    for k in (1, 2, 3):
        links.send(("small", k), small_ref, sbuf.at[here.f, z], small_recvs.at[k], here.at(z=zk[k]))
    mine = pl.ds(pl.multiple_of(here.c * rows_own, rows_own), rows_own)
    links.send("hidden", hid_ref, hall.at[mine], core_recvs.at[0], here.at(c=1 - here.c))
    sbuf[here.f, z] = small_ref[...]

    def recv_sem(m, f, z_):
        return recvs.at[m, f, z_]

    def push_z(m):
        for k in (1, 2, 3):
            links.send(("z", m, k), shards[m], piece(win, wout, m, here.f, z), recv_sem(m, here.f, z), here.at(z=zk[k]))

    def first(m, k):
        src = shards[m] if k == 0 else piece(win, wout, m, here.f, zk[k])
        if k:
            links.arrived(src, recv_sem(m, here.f, zk[k]), here.at(z=zk[k]))
        dst = piece(win, wout, m, here.f, zk[k])
        links.send(("first", m, k, 2), src, dst, recv_sem(m, here.f, zk[k]), here.at(f=here.f2))
        links.send(("first", m, k, 3), src, dst, recv_sem(m, here.f, zk[k]), here.at(f=here.f3))

    def second(m, k):
        src = piece(win, wout, m, here.f2, zk[k])
        links.arrived(src, recv_sem(m, here.f2, zk[k]), here.at(f=here.f2))
        links.send(("second", m, k), src, src, recv_sem(m, here.f2, zk[k]), here.at(f=here.f3))

    def third(m, k):
        for f in (here.f3, here.f4):
            src = piece(win, wout, m, f, zk[k])
            links.arrived(src, recv_sem(m, f, zk[k]), here.at(f=here.f3))

    push_z(0)
    push_z(1)
    first(0, 0)
    first(1, 0)
    first(2, 0)
    half_state = pl.ds(pl.multiple_of(here.c * 128, 128), 128)
    rest_state = pl.ds(pl.multiple_of(128 - here.c * 128, 128), 128)
    links.send(("state", 0), wst_ref.at[:, half_state], stbuf.at[here.f, :, half_state], state_recvs.at[0], here.at(f=here.f2))
    links.send(("state", 1), wst_ref.at[:, half_state], stbuf.at[here.f, :, half_state], state_recvs.at[1], here.at(f=here.f3))
    links.send("cot", cot_ref, call.at[mine], core_recvs.at[1], here.at(c=1 - here.c))
    win[z, pl.ds(pl.multiple_of(here.f * depth, depth), depth), pl.ds(0, GW)] = w0_ref[...]
    win[z, pl.ds(pl.multiple_of(here.f * depth, depth), depth), pl.ds(GW, GW)] = w1_ref[...]
    wout[z, :, pl.ds(pl.multiple_of(here.f * depth, depth), depth)] = w2_ref[...]
    stbuf[here.f] = wst_ref[...]
    hall[mine] = hid_ref[...]
    call[mine] = cot_ref[...]
    docs = seg_ref[pl.ds(pl.multiple_of(z * CH, CH), CH), :].astype(F32)
    docs_ref[...] = docs
    token_masks(docs, tok_ref)
    for k in (1, 2, 3):
        links.arrived(sbuf.at[here.f, zk[k]], small_recvs.at[k], here.at(z=zk[k]))
    links.send(("small", 4), sbuf.at[here.f], sbuf.at[here.f], small_recvs.at[4], here.at(f=here.f2))
    links.send(("small", 5), sbuf.at[here.f], sbuf.at[here.f], small_recvs.at[5], here.at(f=here.f3))
    links.arrived(sbuf.at[here.f2], small_recvs.at[4], here.at(f=here.f2))
    links.send(("small", 6), sbuf.at[here.f2], sbuf.at[here.f2], small_recvs.at[6], here.at(f=here.f3))
    def state_of(f, part):
        return stbuf.at[f, :, part]

    links.arrived(state_of(here.f2, half_state), state_recvs.at[0], here.at(f=here.f2))
    links.send(("state", 2), state_of(here.f2, half_state), state_of(here.f2, half_state), state_recvs.at[2], here.at(f=here.f3))
    links.send(("state", 3), state_of(here.f2, half_state), state_of(here.f2, half_state), state_recvs.at[3], here.at(c=1 - here.c))
    other = pl.ds(pl.multiple_of((1 - here.c) * rows_own, rows_own), rows_own)
    links.arrived(hall.at[other], core_recvs.at[0], here.at(c=1 - here.c))
    push_z(2)
    first(0, 1)
    second(0, 0)
    links.arrived(sbuf.at[here.f3], small_recvs.at[5], here.at(f=here.f3))
    links.arrived(sbuf.at[here.f4], small_recvs.at[6], here.at(f=here.f3))

    shared = sum(sbuf[f, 0].astype(F32) for f in range(4))
    gain_outer = jnp.concatenate([sbuf[f, 0][R_GAIN : R_GAIN + 1, :].astype(F32) for f in range(4)], 1)
    gains_ref[...] = jnp.broadcast_to(gain_outer, (8, model))
    cst_ref[...] = jnp.concatenate([shared[R_CST : R_CST + 5, :256], jnp.zeros((3, 256), F32)], 0)
    lane8 = lax.broadcasted_iota(jnp.int32, (8, 128), 1)
    heads8 = jnp.concatenate([shared[R_OFF : R_SKIP + 1, :128], jnp.zeros((5, 128), F32)], 0)
    own_heads = jnp.zeros((8, 128), F32)
    spread_heads = (lax.broadcasted_iota(jnp.int32, (128, GW), 1) >> 6
                    == lax.broadcasted_iota(jnp.int32, (128, GW), 0)).astype(BF)
    stw_ref[...] = jnp.zeros_like(stw_ref)
    for k in range(4):
        turned = pltpu.roll(heads8, 128 - (2 * zk[k] + here.c) * GH, 1)
        own_heads = own_heads + pltpu.roll(jnp.where(lane8 < GH, turned, 0.0), 16 * k, 1)
        group = sum(sbuf[f, zk[k]].astype(F32) for f in range(4))
        skips = mm(turned.astype(BF), spread_heads)[2:3, :]
        par_ref[k] = jnp.concatenate(
            [group[R_CONV : R_CONV + 5], skips, group[R_INNER : R_INNER + 1], jnp.zeros((1, GW), F32)], 0
        )
        for f in range(4):
            block = sbuf[f, zk[k]][:16].astype(F32)
            keep = lax.broadcasted_iota(jnp.int32, block.shape, 0) < GH
            stw_ref[pl.ds(16 * k, 16), pl.ds(depth * f, depth)] = jnp.where(keep, block, 0.0).astype(BF)
    decay = -jnp.exp(own_heads[1:2, :])
    hpar_ref[...] = jnp.concatenate([own_heads[0:1], decay, own_heads[2:3], jnp.zeros((5, 128), F32)], 0)

    def norm(i, _):
        rows = pl.ds(pl.multiple_of(i * L, L), L)
        x = hall[rows, :].astype(F32)
        inv = lax.rsqrt(jnp.sum(x * x, 1, keepdims=True) / model + EPSILON)
        hall[rows, :] = (x * inv * gain_outer).astype(BF)
        return 0

    lax.fori_loop(0, SEQ // L, norm, 0)
    first(1, 1)
    second(1, 0)
    links.arrived(state_of(here.f3, half_state), state_recvs.at[1], here.at(f=here.f3))
    links.send(("state", 4), state_of(here.f3, half_state), state_of(here.f3, half_state), state_recvs.at[4], here.at(c=1 - here.c))
    links.arrived(state_of(here.f4, half_state), state_recvs.at[2], here.at(f=here.f3))
    links.send(("state", 5), state_of(here.f4, half_state), state_of(here.f4, half_state), state_recvs.at[5], here.at(c=1 - here.c))
    for n, f in ((3, here.f3), (4, here.f2), (5, here.f4)):
        links.arrived(state_of(f, rest_state), state_recvs.at[n], here.at(c=1 - here.c))

    TILE = 256

    def project_small(i, _):
        rows = pl.ds(pl.multiple_of(i * TILE, TILE), TILE)
        total = jnp.zeros((TILE, 256), F32)
        for f in range(4):
            total = total + mm(hall[rows, pl.ds(depth * f, depth)], stbuf[f])
        statepre_ref[rows, :] = total
        steps = mm(hall[rows, :], stw_ref[...], ((1,), (1,)))
        stepre_ref[rows, :] = jnp.concatenate([steps, jnp.zeros((TILE, 64), F32)], 1)
        return 0

    lax.fori_loop(0, SEQ // TILE, project_small, 0)

    def turn(i, _):
        for half in range(2):
            lanes = pl.ds(pl.multiple_of(i * 256 + half * 128, 128), 128)
            flip[lanes, :] = hall[:, lanes].T
        return 0

    lax.fori_loop(0, model // 256, turn, 0)
    TURNED = len(outs)
    put(flip, normt_out)
    prep_chunks(statepre_ref, stepre_ref, tok_ref, docs_ref, cst_ref, hpar_ref, bc_ref, bct_ref, g_ref, pack_ref, cumt_ref,
                spad_ref)
    units = [(k, m) for k in range(4) for m in (0, 1)] + [(k, 2) for k in range(4)]
    done = [3, 1]

    def advance(i):
        while done[0] < min(i + 3, len(units) - 1) or done[1] < min(i + 1, len(units) - 1):
            if done[0] < min(i + 3, len(units) - 1):
                done[0] += 1
                k, m = units[done[0]]
                if (k, m) != (0, 2):
                    first(m, k)
            if done[1] < min(i + 1, len(units) - 1):
                done[1] += 1
                k, m = units[done[1]]
                second(m, k)

    links.arrived(call.at[other], core_recvs.at[1], here.at(c=1 - here.c))
    put(call, cot_out)
    ss_ref[...] = jnp.zeros_like(ss_ref)
    for slot in range(2):
        pre[slot, pl.ds(0, 8), :] = jnp.zeros((8, 2 * GW), F32)
    pre_copies = []
    for k in range(4):
        advance(2 * k)
        third(0, k)
        advance(2 * k + 1)
        third(1, k)
        slot = k % 2
        if k >= 2:
            pre_copies[k - 2].wait()

        def project(i, _, slot=slot, k=k):
            rows = pl.ds(pl.multiple_of(i * TILE, TILE), TILE)
            to = pl.ds(pl.multiple_of(i * TILE + 8, 8), TILE)
            pre[slot, to, :] = mm(hall[rows, :], win[zk[k]])
            return 0

        lax.fori_loop(0, SEQ // TILE, project, 0)
        copy = pltpu.make_async_copy(pre.at[slot, pl.ds(8, SEQ)], pre_out.at[k], pre_sem.at[k])
        copy.start()
        pre_copies.append(copy)
        put(win.at[zk[k]], win_out.at[k])
        advance(2 * k + 2)
        fwd_chunks(pre.at[slot], par_ref.at[k], tok_ref, bc_ref, bct_ref, g_ref, pack_ref.at[k], cumt_ref.at[k],
                   gated.at[k], states.at[k], ss_ref, st_ref)
        put(states.at[k], states_out.at[k])
    pre_copies[2].wait()
    pre_copies[3].wait()

    links.send("squares", ss_ref, ssr_ref, core_recvs.at[2], here.at(c=1 - here.c))
    advance(8)
    links.arrived(ssr_ref, core_recvs.at[2], here.at(c=1 - here.c))
    inner_all = 2 * 4 * GW

    def inner_norm(i, _):
        rows = pl.ds(pl.multiple_of(i * L, L), L)
        total = jnp.sum(ss_ref[rows, :] + ssr_ref[rows, :], 1, keepdims=True)
        inv = lax.rsqrt(total / inner_all + EPSILON)
        invp_ref[rows, :] = jnp.broadcast_to(inv, (L, 128))
        for k in range(4):
            gain = par_ref[k, P_GAIN : P_GAIN + 1, :]
            low = (gated[k, rows, :].astype(F32) * inv * gain).astype(BF)
            ninner[k, rows, :] = low
            flip[pl.ds(k * GW, GW), rows] = low.T
        pr_ref[rows, :] = jnp.zeros((L, 128), F32)
        return 0

    outs[TURNED].wait()
    outs[TURNED] = None
    lax.fori_loop(0, SEQ // L, inner_norm, 0)
    put(ninner, nin_out)
    put(flip, nint_out)
    back_copies = []
    for k in range(4):
        advance(8 + k)
        third(2, k)
        slot = k % 2
        if k >= 2:
            back_copies[k - 2].wait()
        gaingrad_ref[k] = jnp.zeros((8, GW), F32)

        def back(i, _, slot=slot, k=k):
            rows = pl.ds(pl.multiple_of(i * TILE, TILE), TILE)
            d = mm(call[rows, :], wout[zk[k]], ((1,), (1,)))
            dinner[slot, rows, :] = d
            both = d * gated[k, rows, :].astype(F32)
            gaingrad_ref[k, 0:1, :] += jnp.sum(both * invp_ref[rows, 0:1], 0, keepdims=True)
            both = both * par_ref[k, P_GAIN : P_GAIN + 1, :]
            pr_ref[rows, :] += both[:, :128] + both[:, 128:256] + both[:, 256:]
            return 0

        lax.fori_loop(0, SEQ // TILE, back, 0)
        copy = pltpu.make_async_copy(dinner.at[slot], dinner_out.at[k], back_sem.at[k])
        copy.start()
        back_copies.append(copy)
        put(wout.at[zk[k]], wout_out.at[k])
    links.send("products", pr_ref, prr_ref, core_recvs.at[3], here.at(c=1 - here.c))
    links.arrived(prr_ref, core_recvs.at[3], here.at(c=1 - here.c))

    def scale(i, _):
        rows = pl.ds(pl.multiple_of(i * L, L), L)
        total = jnp.sum(pr_ref[rows, :] + prr_ref[rows, :], 1, keepdims=True)
        inv = invp_ref[rows, :]
        lane = lax.broadcasted_iota(jnp.int32, (L, 128), 1)
        invp_ref[rows, :] = jnp.where(lane == 0, inv, inv * inv * inv * (total / inner_all))
        return 0

    lax.fori_loop(0, SEQ // L, scale, 0)
    back_copies[2].wait()
    back_copies[3].wait()
    for copy in outs:
        if copy is not None:
            copy.wait()
    links.finish(core_recvs.at[0], here.at(c=1 - here.c))


def forward_call(model, hidden, cot, *args):
    rows = hidden.shape[0]
    any_ = pl.BlockSpec(memory_space=pl.ANY)
    sds = jax.ShapeDtypeStruct
    inner = 4 * GW
    depth = model // 4
    return pl.pallas_call(
        functools.partial(forward_kernel, model),
        out_shape=(
            sds((model, SEQ), BF), sds((SEQ, model), BF), sds((4, model, 2 * GW), BF), sds((4, GW, model), BF),
            sds((4, SEQ, 2 * GW), F32), sds((4, SEQ, GW), F32), sds((4, SEQ, GW), BF),
            sds((4 * GW, SEQ), BF), sds((4, CH, 128, GW), BF),
            sds((SEQ, 256), BF), sds((CH, 256, L), BF), sds((CH, L, L), F32), sds((4, SEQ, 128), F32),
            sds((4, CH, 8, L), F32), sds((4, 8, GW), F32), sds((8, 128), F32), sds((8, 256), F32),
            sds((64, model), BF), sds((4, depth, 256), BF), sds((8, model), F32), sds((SEQ, 256), F32), sds((SEQ, 128), F32),
            sds((4, 8, GW), F32), sds((SEQ, 128), F32), sds((CH, L), F32),
        ),
        in_specs=[vm()] * (2 + len(args)),
        out_specs=tuple([any_] * 9 + [vm()] * 16),
        scratch_shapes=[
            pltpu.VMEM((SMALL, GW), BF),
            pltpu.VMEM((SEQ, model), BF),
            pltpu.VMEM((SEQ, model), BF),
            pltpu.VMEM((4, model, 2 * GW), BF),
            pltpu.VMEM((4, GW, model), BF),
            pltpu.VMEM((4, 4, SMALL, GW), BF),
            pltpu.VMEM((2, SEQ + 8, 2 * GW), F32),
            pltpu.VMEM((model, SEQ), BF),
            pltpu.VMEM((4, SEQ, GW), BF),
            pltpu.VMEM((4, SEQ, GW), BF),
            pltpu.VMEM((4, CH, 128, GW), BF),
            pltpu.VMEM((2, SEQ, GW), F32),
            pltpu.VMEM((SEQ, 128), F32),
            pltpu.VMEM((SEQ, 128), F32),
            pltpu.VMEM((SEQ, 128), F32),
            pltpu.VMEM((SEQ, 128), F32),
            pltpu.VMEM((SEQ + 8, 256), F32),
            pltpu.VMEM((128, GW), F32),
            pltpu.VMEM((SEQ, 128), F32),
            pltpu.SemaphoreType.DMA((64,)),
            pltpu.SemaphoreType.DMA((3, 4, 4)),
            pltpu.SemaphoreType.DMA((7,)),
            pltpu.SemaphoreType.DMA((6,)),
            pltpu.SemaphoreType.DMA((4,)),
            pltpu.SemaphoreType.DMA((16,)),
            pltpu.SemaphoreType.DMA((4,)),
            pltpu.SemaphoreType.DMA((4,)),
        ],
        compiler_params=pltpu.CompilerParams(vmem_limit_bytes=VMEM_LIMIT, collective_id=1, has_side_effects=True),
        name="gather_and_forward",
    )(hidden, cot, *args)


ORDER = (3, 2, 1, 0)


def backward_kernel(model, hid_ref, tok_ref, row_ref, inv_ref, bc_ref, bct_ref, g_ref, cumt_ref, par_ref,
                    hpar_ref, cst_ref, stw_ref, stbuf_ref, statepre_ref, gaingrad_ref, gains_ref,
                    normt_in, cot_in, win_in, wout_in, pre_in, dinner_in, nin_in, nint_in, states_in, pack_in,
                    layer_out, hidden_out, ginner_ref, ggate_ref, gout_ref, gstate_ref, gsmall_ref, gother_ref,
                    normt, cot, win, pre, dinner, states, pack, acc, half, halfr, dcat, parts, recv1, recv2, recv3,
                    sparts, ssend, srecv, srecv1, srecv2, srecv3, srecvc, qparts, qrecv1, qrecv3, qsend, qrecvc,
                    dstep, dstate, pgrad, hgrad, sgrad, rt_ref, dg_ref, dbc_ref, spad_ref,
                    sends, recv_sems, core_sems, load_sems, credit1, credit2):
    here = Place()
    zk = here.zk
    f, f2, f3, f4 = here.f, here.f2, here.f3, here.f4
    links = Links(sends)
    depth = model // 4
    rows_own = hid_ref.shape[0]
    mine = pl.ds(pl.multiple_of(here.c * rows_own, rows_own), rows_own)
    across = pl.ds(pl.multiple_of((1 - here.c) * rows_own, rows_own), rows_own)
    units = [(k, 2) for k in ORDER] + [(k, m) for k in ORDER for m in (0, 1)]
    ROWS = 128

    loads = {}

    def load(name, src, dst, sem):
        copy = pltpu.make_async_copy(src, dst, load_sems.at[sem])
        copy.start()
        loads[name] = copy

    wouts = [halfr.at[1, pl.ds(0, GW)], half.at[pl.ds(0, GW)]]

    def nin(i):
        return dcat.at[:, pl.ds(GW * (i % 2), GW)]

    def load_out(i):
        k = ORDER[i]
        load(("nin", i), nin_in.at[k], nin(i), 2 * (i % 2))
        load(("wout", i), wout_in.at[k], wouts[i % 2], 2 * (i % 2) + 1)

    def load_group(i):
        k = ORDER[i]
        load(("pre", i), pre_in.at[k], pre.at[pl.ds(8, SEQ)], 8)
        load(("dinner", i), dinner_in.at[k], dinner, 9)
        load(("states", i), states_in.at[k], states, 10)
        load(("pack", i), pack_in.at[k], pack, 5)

    def load_win(i):
        load(("win", i), win_in.at[ORDER[i]], win, 11)

    load("nint", nint_in, normt, 4)
    load("cot", cot_in, cot, 6)
    load_out(0)
    load_out(1)
    load_group(0)
    load_win(0)
    pre[pl.ds(0, 8), :] = jnp.zeros((8, 2 * GW), F32)
    hgrad[...] = jnp.zeros_like(hgrad)
    dg_ref[...] = jnp.zeros_like(dg_ref)
    dbc_ref[...] = jnp.zeros_like(dbc_ref)
    dstep[...] = jnp.zeros_like(dstep)
    here.greet()
    here.greeted()

    one_block = parts.at[0, 0]

    def part(u, f_):
        return parts.at[u % 6, f_]

    def add_into(dst, src):
        rows, width = dst.shape

        def body(i, _):
            at = pl.ds(pl.multiple_of(i * ROWS, ROWS), ROWS)
            dst[at, :] = (dst[at, :].astype(F32) + src[at, :].astype(F32)).astype(dst.dtype)
            return 0

        lax.fori_loop(0, rows // ROWS, body, 0)

    def s1(u):
        if u >= 8:
            pl.semaphore_wait(credit1, 1)
        for n, f_ in enumerate((f3, f4)):
            links.send(("s1", u, n), part(u, f_), recv1.at[u % 8, n], recv_sems.at[u, n], here.at(f=f3), one_block)

    def s2(u):
        links.arrived(recv1.at[u % 8, 1], recv_sems.at[u, 1], here.at(f=f3))
        add_into(part(u, f2), recv1.at[u % 8, 1])
        if u >= 8:
            pl.semaphore_wait(credit2, 1)
        links.send(("s2", u), part(u, f2), recv2.at[u % 8], recv_sems.at[u, 2], here.at(f=f2), one_block)
        links.arrived(recv1.at[u % 8, 0], recv_sems.at[u, 0], here.at(f=f3))
        add_into(part(u, f), recv1.at[u % 8, 0])
        if u < 4:
            pl.semaphore_signal(credit1, inc=1, device_id=here.at(f=f3), device_id_type=MESH)

    def give_credit(u):
        if u < 4:
            pl.semaphore_signal(credit2, inc=1, device_id=here.at(f=f2), device_id_type=MESH)

    outs = {0: ginner_ref, 1: ggate_ref, 2: gout_ref}

    def s3(u):
        k, m = units[u]
        links.arrived(recv2.at[u % 8], recv_sems.at[u, 2], here.at(f=f2))
        add_into(part(u, f), recv2.at[u % 8])
        give_credit(u)
        links.send(("s3", u), part(u, f), recv3.at[m, k - 1], recv_sems.at[12 + m, k - 1], here.at(z=zk[k]), one_block)

    def last_sum(u):
        k, m = units[u]
        links.arrived(recv2.at[u % 8], recv_sems.at[u, 2], here.at(f=f2))
        for j in (1, 2, 3):
            links.arrived(recv3.at[m, j - 1], recv_sems.at[12 + m, j - 1], here.at(z=zk[j]))
        own = part(u, f)

        def body(i, _):
            at = pl.ds(pl.multiple_of(i * ROWS, ROWS), ROWS)
            total = own[at, :].astype(F32) + recv2[u % 8, at, :].astype(F32)
            for j in range(3):
                total = total + recv3[m, j, at, :].astype(F32)
            outs[m][at, :] = total
            return 0

        lax.fori_loop(0, GW // ROWS, body, 0)
        give_credit(u)

    loads["nint"].wait()
    loads["cot"].wait()
    for i, k in enumerate(ORDER):

        def grad_out(j, _, i=i, k=k):
            at = pl.ds(pl.multiple_of(j * ROWS, ROWS), ROWS)
            src = pl.ds(pl.multiple_of(k * GW + j * ROWS, ROWS), ROWS)
            total = mm(normt[src, :], cot[...])
            for f_ in range(4):
                parts[i, f_, at, :] = total[:, f_ * depth : (f_ + 1) * depth].astype(BF)
            return 0

        lax.fori_loop(0, GW // ROWS, grad_out, 0)
        s1(i)
        loads["nin", i].wait()
        loads["wout", i].wait()

        def mix_rows(j, _, i=i):
            at = pl.ds(pl.multiple_of(j * 256, 256), 256)
            total = mm(nin(i)[at, :], wouts[i % 2][...])
            acc[at, :] = total if i == 0 else acc[at, :] + total
            return 0

        lax.fori_loop(0, SEQ // 256, mix_rows, 0)
        if i + 2 < 4:
            load_out(i + 2)

    load("normt", normt_in, normt, 7)

    def exchange(n):
        if n:
            links.left(("half", 0), core_sems.at[0], here.at(c=1 - here.c))

        def body(j, _):
            at = pl.ds(pl.multiple_of(j * ROWS, ROWS), ROWS)
            src = pl.ds(pl.multiple_of((1 - here.c) * rows_own + j * ROWS, ROWS), ROWS)
            half[at, :] = acc[src, :].astype(BF)
            return 0

        lax.fori_loop(0, rows_own // ROWS, body, 0)
        links.send(("half", n), half, halfr.at[n], core_sems.at[n], here.at(c=1 - here.c))

    def received(n):
        links.arrived(halfr.at[n], core_sems.at[n], here.at(c=1 - here.c))

    exchange(0)
    received(0)

    def layer(j, _):
        at = pl.ds(pl.multiple_of(j * ROWS, ROWS), ROWS)
        src = pl.ds(pl.multiple_of(here.c * rows_own + j * ROWS, ROWS), ROWS)
        halfr[0, at, :] = (hid_ref[at, :].astype(F32) + acc[src, :] + halfr[0, at, :].astype(F32)).astype(BF)
        return 0

    lax.fori_loop(0, rows_own // ROWS, layer, 0)
    load("layer", halfr.at[0], layer_out, 12)
    loads["normt"].wait()

    due = {
        0: {0: [(s2, 0)], 1: [(s2, 1)], 2: [(s3, 0)], 4: [(s2, 2)], 5: [(s3, 1)], 7: [(s2, 3)]},
        1: {0: [(s3, 2)], 5: [(s2, 4)], 7: [(s2, 5)]},
        2: {0: [(s3, 4)], 1: [(s3, 5)], 3: [(s2, 6)], 4: [(last_sum, 3)], 5: [(s3, 6)], 6: [(s2, 7)]},
        3: {0: [(s3, 7)], 3: [(s2, 8)], 5: [(s3, 8)], 6: [(s2, 9)], 7: [(s3, 9)]},
    }
    for i, k in enumerate(ORDER):
        for name in ("pre", "dinner", "states", "pack"):
            loads[name, i].wait()

        def tick(step, i=i):
            for at, events in due[i].items():
                @pl.when(step == at)
                def _(events=events):
                    for event, u in events:
                        event(u)

        bwd_chunks(k, zk[k], tick, pre, dinner, par_ref.at[k], tok_ref, inv_ref, bc_ref, bct_ref, g_ref, pack,
                   cumt_ref.at[k], states, hpar_ref, dcat, dstep, pgrad.at[k], hgrad, rt_ref, dg_ref, dbc_ref)
        if i < 3:
            load_group(i + 1)
        u = 4 + 2 * i
        if u >= 6:
            for n in (u - 6, u - 5):
                for name in (("s1", n, 0), ("s1", n, 1), ("s2", n), ("s3", n)):
                    if name in links.number:
                        links.left(name, core_sems.at[0], here.at(c=1 - here.c))

        def grads(j, _, u=u):
            at = pl.ds(pl.multiple_of(j * ROWS, ROWS), ROWS)
            for f_ in range(4):
                src = pl.ds(pl.multiple_of(f_ * depth + j * ROWS, ROWS), ROWS)
                total = mm(normt[src, :], dcat[...])
                parts[u % 6, f_, at, :] = total[:, :GW].astype(BF)
                parts[(u + 1) % 6, f_, at, :] = total[:, GW:].astype(BF)
            return 0

        lax.fori_loop(0, depth // ROWS, grads, 0)
        s1(u)
        s1(u + 1)
        loads["win", i].wait()

        def to_normed(j, _, i=i):
            at = pl.ds(pl.multiple_of(j * 256, 256), 256)
            total = mm(dcat[at, :], win[...], ((1,), (1,)))
            acc[at, :] = total if i == 0 else acc[at, :] + total
            return 0

        lax.fori_loop(0, SEQ // 256, to_normed, 0)
        if i < 3:
            load_win(i + 1)

    state_chunks(statepre_ref, cst_ref, tok_ref, row_ref, bc_ref, dg_ref, dbc_ref, dstate, sgrad, spad_ref)
    half_state = pl.ds(pl.multiple_of(here.c * 128, 128), 128)
    rest_state = pl.ds(pl.multiple_of(128 - here.c * 128, 128), 128)
    core = here.at(c=1 - here.c)
    for f_ in range(4):
        sums = mm(normt[pl.ds(f_ * depth, depth), :], dstate[...])
        lower, upper = sums[:, :128], sums[:, 128:]
        sparts[f_] = jnp.where(here.c == 0, lower, upper).astype(BF)
        ssend[f_] = jnp.where(here.c == 0, upper, lower).astype(BF)
    links.send("state_core", ssend, srecv, core_sems.at[2], core)

    def finish_normed(j, _):
        at = pl.ds(pl.multiple_of(j * 256, 256), 256)
        total = mm(dstep[at, :64], stw_ref[...])
        total = total + jnp.concatenate([mm(dstate[at, :], stbuf_ref[f_], ((1,), (1,))) for f_ in range(4)], 1)
        acc[at, :] = acc[at, :] + total
        return 0

    lax.fori_loop(0, SEQ // 256, finish_normed, 0)
    exchange(1)
    links.arrived(srecv, core_sems.at[2], core)
    for f_ in range(4):
        sparts[f_] = (sparts[f_].astype(F32) + srecv[f_].astype(F32)).astype(BF)
    links.send("state3", sparts.at[f3], srecv1.at[0], recv_sems.at[15, 0], here.at(f=f3))
    links.send("state4", sparts.at[f4], srecv1.at[1], recv_sems.at[15, 1], here.at(f=f3))
    step_rows = mm(dstep[:, :64], normt[...], ((0,), (1,)))
    received(1)
    gain = gains_ref[0:1, :]

    def last(j, gain_grad):
        at = pl.ds(pl.multiple_of(j * ROWS, ROWS), ROWS)
        src = pl.ds(pl.multiple_of(here.c * rows_own + j * ROWS, ROWS), ROWS)
        d = acc[src, :] + halfr[1, at, :].astype(F32)
        x = hid_ref[at, :].astype(F32)
        inv = lax.rsqrt(jnp.sum(x * x, 1, keepdims=True) / model + EPSILON)
        weighted = d * gain
        mean = jnp.sum(x * weighted, 1, keepdims=True) / model
        d_hidden = inv * weighted - x * (inv * inv * inv * mean)
        halfr[1, at, :] = (cot[src, :].astype(F32) + d_hidden).astype(BF)
        return gain_grad + jnp.sum(d * x * inv, 0, keepdims=True)

    gain_grad = lax.fori_loop(0, rows_own // ROWS, last, jnp.zeros((1, model), F32))
    load("hidden", halfr.at[1], hidden_out, 13)
    zeros = jnp.zeros((1, GW - 256), F32)
    skips = jnp.zeros((8, 128), F32)
    heads_of = (iota((GW, 128), 0) >> 6 == iota((GW, 128), 1)).astype(BF)
    for k in range(4):
        hi, lo = split2(pgrad[k])
        skips = skips + pltpu.roll(mm(hi, heads_of) + mm(lo, heads_of), 16 * zk[k], 1)
    head_rows = jnp.concatenate([hgrad[0:2, :], skips[P_SKIP : P_SKIP + 1, :]], 0)
    head_rows = jnp.concatenate([head_rows, jnp.zeros((3, GW - 128), F32)], 1)
    for f_ in range(4):
        common = [gain_grad[:, f_ * depth : (f_ + 1) * depth]]
        common += [jnp.concatenate([sgrad[r : r + 1, :], zeros], 1) for r in range(5)]
        common.append(head_rows)
        for k in range(4):
            own = jnp.concatenate([pgrad[k, 0:5, :], gaingrad_ref[k, 0:1, :], jnp.zeros((1, GW), F32)], 0)
            qparts[f_, k] = jnp.concatenate(
                [step_rows[16 * k : 16 * k + 16, f_ * depth : (f_ + 1) * depth], own] + common, 0
            ).astype(BF)
    for n, f_ in enumerate((f2, f3, f4)):
        links.send(("small", n), qparts.at[f_], qrecv1.at[n], recv_sems.at[16, n], here.at(f=f_))
    links.arrived(srecv1.at[1], recv_sems.at[15, 1], here.at(f=f3))
    sparts[f2] = (sparts[f2].astype(F32) + srecv1[1].astype(F32)).astype(BF)
    links.send("state2", sparts.at[f2], srecv2, recv_sems.at[15, 2], here.at(f=f2))
    links.arrived(srecv1.at[0], recv_sems.at[15, 0], here.at(f=f3))
    s2(10)
    for n, f_ in enumerate((f2, f3, f4)):
        links.arrived(qrecv1.at[n], recv_sems.at[16, n], here.at(f=f_))
    for k in range(4):
        total = qparts[f, k].astype(F32)
        for n in range(3):
            total = total + qrecv1[n, k].astype(F32)
        qsend[k] = total.astype(BF)
        if k:
            links.send(("small_z", k), qsend.at[k], qrecv3.at[k - 1], recv_sems.at[18, k - 1], here.at(z=zk[k]))
    s2(11)
    links.arrived(srecv2, recv_sems.at[15, 2], here.at(f=f2))
    sparts[f] = (sparts[f].astype(F32) + srecv1[0].astype(F32) + srecv2[...].astype(F32)).astype(BF)
    for k in (1, 2, 3):
        links.send(("state", k), sparts.at[f], srecv3.at[k - 1], recv_sems.at[17, k - 1], here.at(z=zk[k]))
    for k in (1, 2, 3):
        links.arrived(qrecv3.at[k - 1], recv_sems.at[18, k - 1], here.at(z=zk[k]))
    total = qsend[0].astype(F32)
    for k in range(3):
        total = total + qrecv3[k].astype(F32)
    gsmall_ref[...] = total
    qsend[0] = total.astype(BF)
    links.send("small_core", qsend.at[0], qrecvc, core_sems.at[3], core)
    last_sum(10)
    last_sum(11)
    for k in (1, 2, 3):
        links.arrived(srecv3.at[k - 1], recv_sems.at[17, k - 1], here.at(z=zk[k]))
    total = sparts[f].astype(F32)
    for k in range(3):
        total = total + srecv3[k].astype(F32)
    links.left("state_core", core_sems.at[0], core)
    ssend[0] = total.astype(BF)
    links.send("state_back", ssend.at[0], srecvc, core_sems.at[4], core)
    links.arrived(qrecvc, core_sems.at[3], core)
    gother_ref[...] = qrecvc[...].astype(F32)
    links.arrived(srecvc, core_sems.at[4], core)
    rest = srecvc[...].astype(F32)
    gstate_ref[...] = jnp.concatenate([jnp.where(here.c == 0, total, rest), jnp.where(here.c == 0, rest, total)], 1)
    loads["layer"].wait()
    loads["hidden"].wait()
    links.finish(core_sems.at[0], core)


def backward_call(model, hidden, saved):
    (normt, cot, win, wout, pre, dinner, nin, nint, states, bc, bct, gs, pack, cumt, par, hpar, cst, stw, stbuf, gains,
     statepre, invp, gaingrad, tok, row) = saved
    rows = hidden.shape[0]
    depth = model // 4
    any_ = pl.BlockSpec(memory_space=pl.ANY)
    sds = jax.ShapeDtypeStruct
    block = (GW, GW)
    state = (depth, 256)
    part = (depth, 128)
    small = (SMALL, GW)
    return pl.pallas_call(
        functools.partial(backward_kernel, model),
        out_shape=(
            sds((rows, model), BF), sds((rows, model), BF), sds(block, F32), sds(block, F32), sds(block, F32),
            sds(state, F32), sds(small, F32), sds(small, F32),
        ),
        in_specs=[vm()] * 16 + [any_] * 10,
        out_specs=tuple([any_] * 2 + [vm()] * 6),
        scratch_shapes=[
            pltpu.VMEM((model, SEQ), BF),
            pltpu.VMEM((SEQ, model), BF),
            pltpu.VMEM((model, 2 * GW), BF),
            pltpu.VMEM((SEQ + 8, 2 * GW), F32),
            pltpu.VMEM((SEQ, GW), F32),
            pltpu.VMEM((CH, 128, GW), BF),
            pltpu.VMEM((SEQ, 128), F32),
            pltpu.VMEM((SEQ, model), F32),
            pltpu.VMEM((rows, model), BF),
            pltpu.VMEM((2, rows, model), BF),
            pltpu.VMEM((SEQ, 2 * GW), BF),
            pltpu.VMEM((6, 4) + block, BF),
            pltpu.VMEM((8, 2) + block, BF),
            pltpu.VMEM((8,) + block, BF),
            pltpu.VMEM((3, 3) + block, BF),
            pltpu.VMEM((4,) + part, BF),
            pltpu.VMEM((4,) + part, BF),
            pltpu.VMEM((4,) + part, BF),
            pltpu.VMEM((2,) + part, BF),
            pltpu.VMEM(part, BF),
            pltpu.VMEM((3,) + part, BF),
            pltpu.VMEM(part, BF),
            pltpu.VMEM((4, 4) + small, BF),
            pltpu.VMEM((3, 4) + small, BF),
            pltpu.VMEM((3,) + small, BF),
            pltpu.VMEM((4,) + small, BF),
            pltpu.VMEM(small, BF),
            pltpu.VMEM((SEQ, 128), BF),
            pltpu.VMEM((SEQ, 256), BF),
            pltpu.VMEM((4, 8, GW), F32),
            pltpu.VMEM((8, 128), F32),
            pltpu.VMEM((8, 256), F32),
            pltpu.VMEM((128, GW), F32),
            pltpu.VMEM((CH, L, L), F32),
            pltpu.VMEM((SEQ, 256), F32),
            pltpu.VMEM((SEQ + 8, 256), F32),
            pltpu.SemaphoreType.DMA((72,)),
            pltpu.SemaphoreType.DMA((19, 4)),
            pltpu.SemaphoreType.DMA((5,)),
            pltpu.SemaphoreType.DMA((14,)),
            pltpu.SemaphoreType.REGULAR,
            pltpu.SemaphoreType.REGULAR,
        ],
        compiler_params=pltpu.CompilerParams(vmem_limit_bytes=VMEM_LIMIT, collective_id=2, has_side_effects=True),
        name="backward_and_scatter",
    )(hidden, tok, row, invp, bc, bct, gs, cumt, par, hpar, cst, stw, stbuf, statepre, gaingrad, gains,
      normt, cot, win, wout, pre, dinner, nin, nint, states, pack)


def on_device(fsdp, halves, hidden_in, norm_gain, in_gate, in_inner, in_state, in_step, conv_inner, conv_inner_shift,
              conv_state, conv_state_shift, step_offset, log_rate, skip_gain, inner_gain, out_weight, segment_ids,
              grad_out):
    both = ("fsdp", "zz")
    depth, width = in_gate.shape
    model = depth * fsdp
    inner = width * halves
    heads_dev = in_step.shape[1]
    heads = heads_dev * halves
    heads_all = 2 * heads
    unit = conv_inner.shape[2] * fsdp
    inner_all = 2 * inner
    core = lax.axis_index("core")
    zz = lax.axis_index("zz")
    rows = hidden_in.shape[0]

    def swap(x):
        return lax.ppermute(x, "core", [(0, 1), (1, 0)])

    def both_cores(own, other):
        return jnp.where(core == 0, jnp.concatenate([own, other], 0), jnp.concatenate([other, own], 0))

    small = [norm_gain, in_step, conv_inner, conv_inner_shift, conv_state, conv_state_shift, step_offset, log_rate,
             skip_gain, inner_gain]
    flat = jnp.concatenate([v.reshape(-1) for v in small])
    got = lax.all_gather(flat, both, axis=0).reshape(fsdp, halves, -1)
    parts = []
    at = 0
    for v in small:
        parts.append(got[:, :, at : at + v.size].reshape((fsdp, halves) + v.shape))
        at += v.size
    gain_outer = parts[0][:, 0].reshape(model).astype(F32)
    step_cols = parts[1].transpose(0, 2, 1, 3).reshape(model, heads)
    conv_in = parts[2].transpose(2, 1, 3, 0, 4).reshape(K, inner).astype(F32)
    shift_in = parts[3].transpose(1, 2, 0, 3).reshape(1, inner).astype(F32)
    conv_st = parts[4][:, 0].transpose(1, 0, 2).reshape(K, -1).astype(F32)
    shift_st = parts[5][:, 0].reshape(1, -1).astype(F32)
    gain_in = parts[9].transpose(1, 2, 0, 3).reshape(1, inner).astype(F32)

    def my_heads(v):
        return v.reshape(halves, 2, heads_dev)[:, core].reshape(heads).astype(F32)

    offset = my_heads(parts[6][:, 0].reshape(heads_all))
    decay = -jnp.exp(my_heads(parts[7][:, 0].reshape(heads_all)))
    skip = my_heads(parts[8][:, 0].reshape(heads_all))
    state_cols = lax.all_gather(in_state, "fsdp", axis=0, tiled=True)

    def columns(w):
        return lax.all_gather(w, both, axis=0).reshape(fsdp, halves, depth, width).transpose(0, 2, 1, 3).reshape(model, inner)

    inner_cols = columns(in_inner)
    gate_cols = columns(in_gate)
    out_rows = lax.all_gather(out_weight, both, axis=0).reshape(fsdp, halves, width, depth).transpose(1, 2, 0, 3).reshape(inner, model)

    par = jnp.concatenate([conv_in, shift_in, jnp.repeat(skip, unit)[None], gain_in, jnp.zeros((1, inner), F32)], 0)
    convst = jnp.concatenate([conv_st, shift_st, jnp.zeros((3, 256), F32)], 0)
    head = jnp.pad(jnp.stack([offset, decay]), ((0, 6), (0, 128 - heads)))
    decay_g = jnp.pad(decay.reshape(heads // GH, 1, GH), ((0, 0), (0, 7), (0, 128 - GH)))

    docs = lax.dynamic_slice_in_dim(segment_ids, zz * SEQ, SEQ)
    blocks = docs.reshape(CH, L)
    prior = jnp.concatenate([jnp.full((1,), -1, docs.dtype), blocks[:-1, -1]])
    masks = [docs, (blocks == prior[:, None]).reshape(SEQ), (blocks == blocks[:, -1:]).reshape(SEQ)]
    for k in range(1, K):
        masks.append(jnp.concatenate([jnp.zeros((k,), bool), docs[k:] == docs[:-k]]))
    for k in range(1, K):
        masks.append(jnp.concatenate([docs[k:] == docs[:-k], jnp.zeros((k,), bool)]))
    tok = jnp.pad(jnp.stack([m.astype(F32) for m in masks], 1), ((0, 0), (0, 128 - len(masks))))
    row = jnp.broadcast_to(blocks.astype(F32)[:, None, :], (CH, 8, L))

    hidden_all = both_cores(hidden_in, swap(hidden_in)).astype(F32)
    cot_all = both_cores(grad_out, swap(grad_out))
    inv_rms = lax.rsqrt(jnp.mean(hidden_all * hidden_all, -1, keepdims=True) + EPSILON)
    normed = (hidden_all * inv_rms * gain_outer).astype(BF)
    small_cols = jnp.concatenate([state_cols, jnp.pad(step_cols, ((0, 0), (0, 128 - heads)))], 1)
    pre_small = mm(normed, small_cols)
    state_pre = pre_small[:, :256]
    step_pre = pre_small[:, 256:]
    inner_pre = mm(normed, inner_cols)
    gate_pre = mm(normed, gate_cols)
    bc, bct, gs, pack, cumt = prep(state_pre, step_pre, tok, row, convst, head)
    gated, states, ss = fwd(inner_pre, gate_pre, par, tok, bc, bct, gs, pack, cumt)
    ss_own = jnp.sum(ss, -1)
    squares = ss_own + swap(ss_own)
    inner_inv = lax.rsqrt(squares / inner_all + EPSILON)[:, None]
    normed_inner = (gated * inner_inv * gain_in).astype(BF)
    mixed = mm(normed_inner, out_rows)

    def to_own(x):
        own = lax.dynamic_slice_in_dim(x, core * rows, rows)
        other = lax.dynamic_slice_in_dim(x, (1 - core) * rows, rows)
        return own + swap(other.astype(BF)).astype(F32)

    layer_out = (hidden_in.astype(F32) + to_own(mixed)).astype(BF)
    grad_out_part = mm(normed_inner, cot_all, ((0,), (0,)))
    d_inner = mm(cot_all, out_rows, ((1,), (1,)))
    grad_gain_in = jnp.sum(d_inner * gated * inner_inv, 0)
    prod_own = jnp.sum(gated * d_inner * gain_in, -1)
    products = prod_own + swap(prod_own)
    inv_pack = jnp.pad(
        jnp.stack([inner_inv[:, 0], inner_inv[:, 0] ** 3 * products / inner_all], 1), ((0, 0), (0, 126))
    )
    d_gate, d_pre, d_step, d_state, pgrad, hgrad, sgrad = bwd(
        inner_pre, gate_pre, d_inner, par, tok, inv_pack, bc, bct, gs, pack, cumt, states, decay_g, state_pre, convst, row
    )
    d_step = d_step.astype(BF)
    d_small = jnp.concatenate([d_state, d_step], 1)
    d_normed = to_own(
        mm(d_gate, gate_cols, ((1,), (1,))) + mm(d_pre, inner_cols, ((1,), (1,))) + mm(d_small, small_cols, ((1,), (1,)))
    )
    hidden = hidden_in.astype(F32)
    inv_own = lax.dynamic_slice_in_dim(inv_rms, core * rows, rows)
    grad_gain_outer = jnp.sum(d_normed * hidden * inv_own, 0)
    weighted_back = d_normed * gain_outer
    d_hidden = inv_own * weighted_back - hidden * inv_own**3 * jnp.mean(hidden * weighted_back, -1, keepdims=True)
    grad_hidden = (grad_out.astype(F32) + d_hidden).astype(BF)

    def scatter_columns(g):
        g = g.astype(BF).reshape(fsdp, depth, halves, width).transpose(0, 2, 1, 3).reshape(fsdp * halves, depth, width)
        return lax.psum_scatter(g, both, scatter_dimension=0).astype(F32)

    grad_gate = scatter_columns(mm(normed, d_gate, ((0,), (0,))))
    grad_inner = scatter_columns(mm(normed, d_pre, ((0,), (0,))))
    grad_small = mm(normed, d_small, ((0,), (0,)))
    grad_out_weight = grad_out_part.astype(BF).reshape(halves, width, fsdp, depth).transpose(2, 0, 1, 3)
    grad_out_weight = lax.psum_scatter(
        grad_out_weight.reshape(fsdp * halves, width, depth), both, scatter_dimension=0
    ).astype(F32)
    grad_state = lax.psum_scatter(grad_small[:, :256].astype(BF), "fsdp", scatter_dimension=0, tiled=True)
    grad_state = lax.psum(grad_state, ("zz", "core")).astype(F32)

    own_heads = [
        grad_small[:, 256 : 256 + heads].reshape(fsdp, depth, halves, heads_dev).transpose(0, 2, 1, 3),
        pgrad[:K].reshape(K, halves, heads_dev, fsdp, -1).transpose(3, 1, 0, 2, 4),
        pgrad[K].reshape(halves, heads_dev, fsdp, -1).transpose(2, 0, 1, 3),
        grad_gain_in.reshape(halves, heads_dev, fsdp, -1).transpose(2, 0, 1, 3),
    ]
    sizes = [v.shape[2:] for v in own_heads]
    stacked = jnp.concatenate([v.reshape(fsdp * halves, -1) for v in own_heads], 1)
    mine = lax.psum_scatter(stacked, both, scatter_dimension=0)
    outs = []
    at = 0
    for s in sizes:
        n = 1
        for d in s:
            n *= d
        outs.append(mine[at : at + n].reshape(s))
        at += n
    grad_step, grad_conv_in, grad_conv_in_shift, grad_gain_inner = outs

    def place(v):
        v = v.reshape(halves, 1, heads_dev)
        zero = jnp.zeros_like(v)
        return jnp.where(core == 0, jnp.concatenate([v, zero], 1), jnp.concatenate([zero, v], 1)).reshape(heads_all)

    skip_sum = jnp.sum(pgrad[P_SKIP].reshape(heads, unit), 1)
    shared = [grad_gain_outer.reshape(fsdp, depth), sgrad[:K].reshape(K, fsdp, -1).transpose(1, 0, 2), sgrad[K].reshape(fsdp, -1)]
    shared += [place(v).reshape(fsdp, -1) for v in (hgrad[1, :heads], hgrad[0, :heads], skip_sum)]
    sizes = [v.shape[1:] for v in shared]
    stacked = jnp.concatenate([v.reshape(fsdp, -1) for v in shared], 1)
    mine = lax.psum(stacked, ("fsdp", "zz", "core"))
    mine = lax.dynamic_index_in_dim(mine, lax.axis_index("fsdp"), keepdims=False)
    outs = []
    at = 0
    for s in sizes:
        n = 1
        for d in s:
            n *= d
        outs.append(mine[at : at + n].reshape(s))
        at += n
    grad_norm_gain, grad_conv_st, grad_conv_st_shift, grad_offset, grad_rate, grad_skip = outs
    return (layer_out, grad_hidden, grad_norm_gain, grad_gate, grad_inner, grad_state, grad_step, grad_conv_in,
            grad_conv_in_shift, grad_conv_st, grad_conv_st_shift, grad_offset, grad_rate, grad_skip, grad_gain_inner,
            grad_out_weight)


def on_chip(hidden_in, norm_gain, in_gate, in_inner, in_state, in_step, conv_inner, conv_inner_shift, conv_state,
            conv_state_shift, step_offset, log_rate, skip_gain, inner_gain, out_weight, segment_ids, grad_out):
    depth = in_gate.shape[0]
    model = depth * 4
    f = lax.axis_index("fsdp")
    core = lax.axis_index("core")

    vec = [jnp.pad(v, (0, GW - v.shape[0])) for v in (norm_gain, conv_state_shift, step_offset, log_rate, skip_gain)]
    vec = jnp.concatenate(vec + [jnp.zeros((3 * GW,), BF)]).reshape(8, GW).astype(F32)
    saved = forward_call(model, hidden_in, grad_out, in_inner, in_gate, out_weight, in_state, vec, in_step, conv_inner,
                         conv_inner_shift, inner_gain, conv_state, segment_ids.reshape(-1, L))
    layer_out, grad_hidden, g_inner, g_gate, g_out, g_state, own, other = backward_call(model, hidden_in, saved)
    shared = own[23:] + other[23:]

    def my_part(v):
        r, n = v.shape
        return lax.dynamic_index_in_dim(v.reshape(r, n // (4 * 16), 4, 16), f, 2, False)

    def heads(r):
        mine = jnp.where(core == 0, own[r], other[r])[:64].reshape(4, 16)[:, :GH]
        theirs = jnp.where(core == 0, other[r], own[r])[:64].reshape(4, 16)[:, :GH]
        every = jnp.concatenate([mine, theirs], 1)
        return lax.dynamic_index_in_dim(every, f, 0, False)

    conv = my_part(own[16:20])
    grad_state_conv = lax.dynamic_slice_in_dim(shared[1:6, :256], f * 64, 64, 1)
    return (
        layer_out, grad_hidden, shared[0], g_gate, g_inner, g_state, own[:GH].T, conv, my_part(own[20:21])[0],
        grad_state_conv[:4], grad_state_conv[4], heads(30), heads(29), heads(31), my_part(own[21:22])[0], g_out,
    )


def solution(mesh):
    fsdp = mesh.shape["fsdp"]
    halves = mesh.shape["tensor"] // 2
    fine = jax.sharding.Mesh(mesh.devices.reshape(fsdp, halves, 2), ("fsdp", "zz", "core"))
    tensor = ("zz", "core")
    tokens = P(("fsdp", "zz", "core"), None)
    grid = P("fsdp", tensor)
    heads = P(tensor, "fsdp")
    return jax.shard_map(
        on_chip if (fsdp, halves) == (4, 4) else functools.partial(on_device, fsdp, halves),
        mesh=fine,
        in_specs=(
            tokens, P("fsdp"), grid, grid, P("fsdp", None), grid, P(None, tensor, "fsdp"), heads, P(None, "fsdp"),
            P("fsdp"), P("fsdp"), P("fsdp"), P("fsdp"), heads, heads, P("fsdp"), tokens,
        ),
        out_specs=(
            tokens, tokens, P("fsdp"), grid, grid, P("fsdp", None), grid, P(None, tensor, "fsdp"), heads,
            P(None, "fsdp"), P("fsdp"), P("fsdp"), P("fsdp"), P("fsdp"), heads, heads,
        ),
        check_vma=False,
    )
```

```python
import functools

import jax
import jax.numpy as jnp
from jax import lax
from jax.sharding import PartitionSpec as P
from jax.experimental import pallas as pl
from jax.experimental.pallas import tpu as pltpu

SEQ = 1024
L = 128
CH = SEQ // L
K = 4
GH = 6
GW = 384
EPSILON = 1e-05
LOG2E = 1.4426950408889634
F32 = jnp.float32
BF = jnp.bfloat16
ST, CU, EE, FF, SG = 0, 8, 16, 24, 32


def mm(a, b, dims=((1,), (0,))):
    return lax.dot_general(a, b, (dims, ((), ())), preferred_element_type=F32)


def split2(x):
    hi = x.astype(BF)
    return hi, (x - hi.astype(F32)).astype(BF)


def split3(x):
    hi = x.astype(BF)
    rest = x - hi.astype(F32)
    mid = rest.astype(BF)
    return hi, mid, (rest - mid.astype(F32)).astype(BF)


def sigmoid(v):
    return 1.0 / (1.0 + jnp.exp(-v))


def back_conv_input(window, k):
    return window[8 - k : 8 - k + L]


def prep_body(state_ref, step_ref, tok_ref, row_ref, convst_ref, head_ref,
              bc_ref, bct_ref, g_ref, pack_ref, cumt_ref, pad_ref):
    pad_ref[pl.ds(0, 8), :] = jnp.zeros((8, 256), F32)
    pad_ref[pl.ds(8, SEQ), :] = state_ref[...]
    lane = lax.broadcasted_iota(jnp.int32, (L, L), 1)
    sub = lax.broadcasted_iota(jnp.int32, (L, L), 0)
    tri = (sub >= lane).astype(BF)
    offset = head_ref[0:1, :]
    decay = head_ref[1:2, :]
    taps = [convst_ref[k : k + 1, :] for k in range(K)]
    shift = convst_ref[K : K + 1, :]

    def chunk(c, _):
        base = pl.multiple_of(c * L, L)
        rows = pl.ds(base, L)
        tok = tok_ref[rows, :]
        window = pad_ref[pl.ds(base, L + 8), :]
        total = shift + taps[K - 1] * back_conv_input(window, 0)
        for k in range(1, K):
            total = total + taps[K - 1 - k] * (back_conv_input(window, k) * tok[:, 2 + k : 3 + k])
        act = total * sigmoid(total)
        low = act.astype(BF)
        bc_ref[rows, :] = low
        bct_ref[c] = jnp.concatenate([act[:, :128].T, act[:, 128:].T], 0).astype(BF)
        scores = mm(low[:, 128:], low[:, :128], ((1,), (1,)))
        same = (tok[:, 0:1] == row_ref[c][0:1, :]) & (sub >= lane)
        g_ref[c] = jnp.where(same, scores, 0.0)
        v = step_ref[rows, :] + offset
        steps = jnp.maximum(v, 0.0) + jnp.log1p(jnp.exp(-jnp.abs(v)))
        logs = steps * (decay * LOG2E)
        hi, mid, lo = split3(logs)
        cum = mm(tri, hi) + mm(tri, mid) + mm(tri, lo)
        last = cum[L - 1 : L, :]
        enter = jnp.exp2(cum) * tok[:, 1:2]
        leave = jnp.exp2(last - cum) * tok[:, 2:3]
        sig = sigmoid(v)
        cumt = cum.T
        zeros = jnp.zeros((L, 2), F32)
        for g in range(4):
            part = slice(GH * g, GH * g + GH)
            pieces = []
            for values in (steps, cum, enter, leave, sig):
                pieces += [values[:, part], zeros]
            pieces.append(jnp.zeros((L, 88), F32))
            pack_ref[g, rows, :] = jnp.concatenate(pieces, 1)
            cumt_ref[g, c] = jnp.concatenate([cumt[part, :], jnp.zeros((2, L), F32)], 0)
        return 0

    lax.fori_loop(0, CH, chunk, 0)


def vm(*shape):
    return pl.BlockSpec(memory_space=pltpu.VMEM)


def prep(state_pre, step_pre, tok, row, convst, head):
    return pl.pallas_call(
        prep_body,
        out_shape=(
            jax.ShapeDtypeStruct((SEQ, 256), BF),
            jax.ShapeDtypeStruct((CH, 256, L), BF),
            jax.ShapeDtypeStruct((CH, L, L), F32),
            jax.ShapeDtypeStruct((4, SEQ, 128), F32),
            jax.ShapeDtypeStruct((4, CH, 8, L), F32),
        ),
        in_specs=[vm()] * 6,
        out_specs=[vm()] * 5,
        scratch_shapes=[pltpu.VMEM((SEQ + 8, 256), F32)],
        compiler_params=pltpu.CompilerParams(vmem_limit_bytes=56 * 2**20),
        name="prep",
    )(state_pre, step_pre, tok, row, convst, head)


def pair_lanes(pack, first, q):
    lane = lax.broadcasted_iota(jnp.int32, (pack.shape[0], 128), 1)
    a = pack[:, first + 2 * q : first + 2 * q + 1]
    b = pack[:, first + 2 * q + 1 : first + 2 * q + 2]
    return jnp.where(lane < 64, a, b)


def spread(pack, first):
    return jnp.concatenate([pair_lanes(pack, first, q) for q in range(3)], 1)


def block_diag(x):
    lane = lax.broadcasted_iota(jnp.int32, x.shape, 1)
    zero = jnp.zeros_like(x)
    return jnp.concatenate([jnp.where(lane < 64, x, zero), jnp.where(lane < 64, zero, x)], 0)


def decay_kernel(pack, cumt, h):
    return jnp.exp2(jnp.minimum(pack[:, CU + h : CU + h + 1] - cumt[h : h + 1, :], 0.0))


def conv_of(window, tok, par):
    total = par[K : K + 1, :] + par[K - 1 : K, :] * back_conv_input(window, 0)
    for k in range(1, K):
        total = total + par[K - 1 - k : K - k, :] * (back_conv_input(window, k) * tok[:, 2 + k : 3 + k])
    return total


P_SHIFT, P_SKIP, P_GAIN = 4, 5, 6


def fwd_body(inner_ref, gate_ref, par_ref, tok_ref, bc_ref, bct_ref, g_ref, pack_ref, cumt_ref,
             gated_ref, states_ref, ss_ref, pad_ref, st_ref):
    pad_ref[pl.ds(0, 8), :] = jnp.zeros((8, GW), F32)
    pad_ref[pl.ds(8, SEQ), :] = inner_ref[...]
    st_ref[...] = jnp.zeros_like(st_ref)
    par = par_ref[...]

    @pl.when(pl.program_id(0) == 0)
    def _():
        ss_ref[...] = jnp.zeros_like(ss_ref)

    def chunk(c, _):
        base = pl.multiple_of(c * L, L)
        rows = pl.ds(base, L)
        tok = tok_ref[rows, :]
        u = conv_of(pad_ref[pl.ds(base, L + 8), :], tok, par)
        act = u * sigmoid(u)
        pack = pack_ref[0, rows, :]
        cumt = cumt_ref[0, c]
        g = g_ref[c]
        weighted = act * spread(pack, ST)
        low = weighted.astype(BF)
        enter = spread(pack, EE)
        state = st_ref[...]
        low_state = state.astype(BF)
        states_ref[0, c] = low_state
        y = mm(bc_ref[rows, 128:], low_state) * enter
        locals_ = []
        for q in range(3):
            kernels = [(g * decay_kernel(pack, cumt, 2 * q + e)).astype(BF) for e in range(2)]
            locals_.append(mm(jnp.concatenate(kernels, 1), block_diag(low[:, 128 * q : 128 * q + 128])))
        y = y + jnp.concatenate(locals_, 1)
        out = weighted * spread(pack, FF)
        st_ref[...] = enter[L - 1 : L, :] * state + mm(bct_ref[c, pl.ds(0, 128), :], out.astype(BF))
        ssd = y + par[P_SKIP : P_SKIP + 1, :] * act
        gate = gate_ref[rows, :]
        gated = ssd * (gate * sigmoid(gate))
        gated_ref[rows, :] = gated
        sq = gated * gated
        ss_ref[rows, :] += sq[:, :128] + sq[:, 128:256] + sq[:, 256:]
        return 0

    lax.fori_loop(0, CH, chunk, 0)


def whole_spec(shape):
    return pl.BlockSpec(shape, lambda g: (0,) * len(shape))


def fwd(inner_pre, gate_pre, par, tok, bc, bct, gs, pack, cumt):
    cols = pl.BlockSpec((SEQ, GW), lambda g: (0, g))
    return pl.pallas_call(
        fwd_body,
        grid=(4,),
        out_shape=(
            jax.ShapeDtypeStruct((SEQ, 4 * GW), F32),
            jax.ShapeDtypeStruct((4, CH, 128, GW), BF),
            jax.ShapeDtypeStruct((SEQ, 128), F32),
        ),
        in_specs=[
            cols, cols, pl.BlockSpec((8, GW), lambda g: (0, g)),
            whole_spec((SEQ, 128)), whole_spec((SEQ, 256)), whole_spec((CH, 256, L)), whole_spec((CH, L, L)),
            pl.BlockSpec((1, SEQ, 128), lambda g: (g, 0, 0)),
            pl.BlockSpec((1, CH, 8, L), lambda g: (g, 0, 0, 0)),
        ],
        out_specs=(
            cols,
            pl.BlockSpec((1, CH, 128, GW), lambda g: (g, 0, 0, 0)),
            whole_spec((SEQ, 128)),
        ),
        scratch_shapes=[pltpu.VMEM((SEQ + 8, GW), F32), pltpu.VMEM((128, GW), F32)],
        compiler_params=pltpu.CompilerParams(vmem_limit_bytes=56 * 2**20),
        name="mixer_forward",
    )(inner_pre, gate_pre, par, tok, bc, bct, gs, pack, cumt)


def bwd_body(inner_ref, gate_ref, dinner_ref, par_ref, tok_ref, inv_ref, bc_ref, bct_ref, g_ref, pack_ref,
             cumt_ref, states_ref, decay_ref, state_pre_ref, convst_ref, row_ref,
             dgate_ref, dpre_ref, dstep_ref, dstate_ref, pgrad_ref, hgrad_ref, sgrad_ref,
             pad_ref, rt_ref, dg_ref, dbc_ref, spad_ref):
    group = pl.program_id(0)
    pad_ref[pl.ds(0, 8), :] = jnp.zeros((8, GW), F32)
    pad_ref[pl.ds(8, SEQ), :] = inner_ref[...]
    rt_ref[...] = jnp.zeros_like(rt_ref)
    pgrad_ref[...] = jnp.zeros_like(pgrad_ref)
    par = par_ref[...]
    decay = decay_ref[0]

    @pl.when(group == 0)
    def _():
        dg_ref[...] = jnp.zeros_like(dg_ref)
        dbc_ref[...] = jnp.zeros_like(dbc_ref)
        dstep_ref[...] = jnp.zeros_like(dstep_ref)
        hgrad_ref[...] = jnp.zeros_like(hgrad_ref)

    lane = lax.broadcasted_iota(jnp.int32, (L, L), 1)
    sub = lax.broadcasted_iota(jnp.int32, (L, L), 0)
    upper = (sub <= lane).astype(BF)
    per_head = (lax.broadcasted_iota(jnp.int32, (GW, 128), 0) >> 6
                == lax.broadcasted_iota(jnp.int32, (GW, 128), 1)).astype(BF)

    def head_sums(x):
        hi, lo = split2(x)
        return mm(hi, per_head) + mm(lo, per_head)

    def chunk(step, later):
        c = CH - 1 - step
        base = pl.multiple_of(c * L, L)
        rows = pl.ds(base, L)
        tok = tok_ref[rows, :]
        window = pad_ref[pl.ds(base, L + 8), :]
        u = conv_of(window, tok, par)
        su = sigmoid(u)
        act = u * su
        pack = pack_ref[0, rows, :]
        cumt = cumt_ref[0, c]
        g = g_ref[c]
        steps = spread(pack, ST)
        enter = spread(pack, EE)
        leave = spread(pack, FF)
        weighted = act * steps
        low = weighted.astype(BF)
        low_state = states_ref[0, c]
        bmat = bc_ref[rows, :128]
        cmat = bc_ref[rows, 128:]
        diags = [block_diag(low[:, 128 * q : 128 * q + 128]) for q in range(3)]
        decays = [decay_kernel(pack, cumt, h) for h in range(GH)]
        kernels = [jnp.concatenate([(g * decays[2 * q + e]).astype(BF) for e in range(2)], 1) for q in range(3)]
        y = mm(cmat, low_state) * enter + jnp.concatenate([mm(kernels[q], diags[q]) for q in range(3)], 1)
        skip = par[P_SKIP : P_SKIP + 1, :]
        ssd = y + skip * act
        gate = gate_ref[rows, :]
        sg = sigmoid(gate)
        silu = gate * sg
        scaled = dinner_ref[rows, :] * par[P_GAIN : P_GAIN + 1, :]
        inv = inv_ref[rows, :]
        d_gated = inv[:, 0:1] * scaled - (ssd * silu) * inv[:, 1:2]
        dy = d_gated * silu
        dgate_ref[rows, :] = (d_gated * ssd * sg * (1.0 + gate * (1.0 - sg))).astype(BF)
        dy_low = dy.astype(BF)
        dy_in = (dy * enter).astype(BF)
        rt = rt_ref[...]
        rt_low = rt.astype(BF)
        carried = mm(bmat, rt_low) * leave
        pieces = []
        d_scores = jnp.zeros((L, L), F32)
        for q in range(3):
            dq = dy_low[:, 128 * q : 128 * q + 128]
            dm = mm(dq, diags[q], ((1,), (1,)))
            d_scores = d_scores + dm[:, :L] * decays[2 * q] + dm[:, L:] * decays[2 * q + 1]
            both = mm(kernels[q], dq, ((0,), (0,)))
            pieces.append(jnp.where(lane < 64, both[:L], both[L:]))
        d_weighted = jnp.concatenate(pieces, 1) + carried
        dg_ref[c] += d_scores
        out = (weighted * leave).astype(BF)
        dbc_ref[rows, 128:] += mm(dy_in, low_state, ((1,), (1,)))
        dbc_ref[rows, :128] += mm(out, rt_low, ((1,), (1,)))
        keep = enter[L - 1 : L, :]
        low32 = low.astype(F32)
        d_cum = head_sums(dy_low.astype(F32) * y - low32 * d_weighted)
        at_end = jnp.sum(low32 * carried, 0, keepdims=True) + keep * jnp.sum(rt * low_state.astype(F32), 0, keepdims=True)
        d_last = head_sums(jnp.concatenate([at_end, jnp.zeros((7, GW), F32)], 0))[0:1, :]
        hi, mid, lo = split3(d_cum)
        d_log = mm(upper, hi) + mm(upper, mid) + mm(upper, lo) + d_last
        rt_ref[...] = keep * rt + mm(bct_ref[c, pl.ds(128, 128), :], dy_in)
        d_step = head_sums(act * d_weighted) + decay[0:1, :] * d_log
        heads = lane < GH
        d_step_pre = jnp.where(heads, d_step * jnp.roll(pack, -SG, 1), 0.0)
        dstep_ref[rows, :] += pltpu.roll(d_step_pre, GH * group, 1)
        rate = jnp.sum(jnp.where(heads, pack, 0.0) * d_log, 0, keepdims=True) * decay[0:1, :]
        offs = jnp.sum(d_step_pre, 0, keepdims=True)
        hgrad_ref[0:1, :] += pltpu.roll(jnp.concatenate([rate, jnp.zeros((7, 128), F32)], 0), GH * group, 1)[0:1]
        hgrad_ref[1:2, :] += pltpu.roll(jnp.concatenate([offs, jnp.zeros((7, 128), F32)], 0), GH * group, 1)[0:1]
        d_act = skip * dy + steps * d_weighted
        du = d_act * su * (1.0 + u * (1.0 - su))
        pgrad_ref[K : K + 1, :] += jnp.sum(du, 0, keepdims=True)
        pgrad_ref[P_SKIP : P_SKIP + 1, :] += jnp.sum(dy * act, 0, keepdims=True)
        for k in range(K):
            moved = back_conv_input(window, k)
            if k:
                moved = moved * tok[:, 2 + k : 3 + k]
            pgrad_ref[K - 1 - k : K - k, :] += jnp.sum(du * moved, 0, keepdims=True)
        ahead = jnp.concatenate([du, later], 0)
        d_pre = par[K - 1 : K, :] * du
        for k in range(1, K):
            d_pre = d_pre + par[K - 1 - k : K - k, :] * (ahead[k : k + L] * tok[:, 5 + k : 6 + k])
        dpre_ref[rows, :] = d_pre.astype(BF)
        return du[:8]

    lax.fori_loop(0, CH, chunk, jnp.zeros((8, GW), F32))

    @pl.when(group == pl.num_programs(0) - 1)
    def _():
        spad_ref[pl.ds(0, 8), :] = jnp.zeros((8, 256), F32)
        spad_ref[pl.ds(8, SEQ), :] = state_pre_ref[...]
        sgrad_ref[...] = jnp.zeros_like(sgrad_ref)
        cst = convst_ref[...]

        def last(step, later):
            c = CH - 1 - step
            base = pl.multiple_of(c * L, L)
            rows = pl.ds(base, L)
            tok = tok_ref[rows, :]
            same = (tok[:, 0:1] == row_ref[c][0:1, :]) & (sub >= lane)
            ds = jnp.where(same, dg_ref[c], 0.0).astype(BF)
            d_c = dbc_ref[rows, 128:] + mm(ds, bc_ref[rows, :128])
            d_b = dbc_ref[rows, :128] + mm(ds, bc_ref[rows, 128:], ((0,), (0,)))
            window = spad_ref[pl.ds(base, L + 8), :]
            w = conv_of(window, tok, cst)
            sw = sigmoid(w)
            dw = jnp.concatenate([d_b, d_c], 1) * (sw * (1.0 + w * (1.0 - sw)))
            sgrad_ref[K : K + 1, :] += jnp.sum(dw, 0, keepdims=True)
            for k in range(K):
                moved = back_conv_input(window, k)
                if k:
                    moved = moved * tok[:, 2 + k : 3 + k]
                sgrad_ref[K - 1 - k : K - k, :] += jnp.sum(dw * moved, 0, keepdims=True)
            ahead = jnp.concatenate([dw, later], 0)
            d_pre = cst[K - 1 : K, :] * dw
            for k in range(1, K):
                d_pre = d_pre + cst[K - 1 - k : K - k, :] * (ahead[k : k + L] * tok[:, 5 + k : 6 + k])
            dstate_ref[rows, :] = d_pre.astype(BF)
            return dw[:8]

        lax.fori_loop(0, CH, last, jnp.zeros((8, 256), F32))


def bwd(inner_pre, gate_pre, d_inner, par, tok, inv, bc, bct, gs, pack, cumt, states, decay, state_pre, convst, row):
    cols = pl.BlockSpec((SEQ, GW), lambda g: (0, g))
    pcol = pl.BlockSpec((8, GW), lambda g: (0, g))
    return pl.pallas_call(
        bwd_body,
        grid=(4,),
        out_shape=(
            jax.ShapeDtypeStruct((SEQ, 4 * GW), BF),
            jax.ShapeDtypeStruct((SEQ, 4 * GW), BF),
            jax.ShapeDtypeStruct((SEQ, 128), F32),
            jax.ShapeDtypeStruct((SEQ, 256), BF),
            jax.ShapeDtypeStruct((8, 4 * GW), F32),
            jax.ShapeDtypeStruct((8, 128), F32),
            jax.ShapeDtypeStruct((8, 256), F32),
        ),
        in_specs=[
            cols, cols, cols, pcol,
            whole_spec((SEQ, 128)), whole_spec((SEQ, 128)), whole_spec((SEQ, 256)), whole_spec((CH, 256, L)),
            whole_spec((CH, L, L)),
            pl.BlockSpec((1, SEQ, 128), lambda g: (g, 0, 0)),
            pl.BlockSpec((1, CH, 8, L), lambda g: (g, 0, 0, 0)),
            pl.BlockSpec((1, CH, 128, GW), lambda g: (g, 0, 0, 0)),
            pl.BlockSpec((1, 8, 128), lambda g: (g, 0, 0)),
            whole_spec((SEQ, 256)), whole_spec((8, 256)), whole_spec((CH, 8, L)),
        ],
        out_specs=(
            cols, cols, whole_spec((SEQ, 128)), whole_spec((SEQ, 256)), pcol, whole_spec((8, 128)), whole_spec((8, 256)),
        ),
        scratch_shapes=[
            pltpu.VMEM((SEQ + 8, GW), F32),
            pltpu.VMEM((128, GW), F32),
            pltpu.VMEM((CH, L, L), F32),
            pltpu.VMEM((SEQ, 256), F32),
            pltpu.VMEM((SEQ + 8, 256), F32),
        ],
        compiler_params=pltpu.CompilerParams(vmem_limit_bytes=56 * 2**20),
        name="mixer_backward",
    )(inner_pre, gate_pre, d_inner, par, tok, inv, bc, bct, gs, pack, cumt, states, decay, state_pre, convst, row)


def prep_chunks(state_ref, step_ref, tok_ref, row_ref, convst_ref, head_ref,
                bc_ref, bct_ref, g_ref, pack_ref, cumt_ref):
    lane = lax.broadcasted_iota(jnp.int32, (L, L), 1)
    sub = lax.broadcasted_iota(jnp.int32, (L, L), 0)
    tri = (sub >= lane).astype(BF)
    offset = head_ref[0:1, :]
    decay = head_ref[1:2, :]
    convst = convst_ref[...]

    def chunk(c, _):
        base = pl.multiple_of(c * L, L)
        rows = pl.ds(base, L)
        tok = tok_ref[rows, :]
        total = conv_of(state_ref[pl.ds(base, L + 8), :], tok, convst)
        act = total * sigmoid(total)
        low = act.astype(BF)
        bc_ref[rows, :] = low
        bct_ref[c] = jnp.concatenate([act[:, :128].T, act[:, 128:].T], 0).astype(BF)
        scores = mm(low[:, 128:], low[:, :128], ((1,), (1,)))
        same = (tok[:, 0:1] == row_ref[pl.ds(c, 1), :]) & (sub >= lane)
        g_ref[c] = jnp.where(same, scores, 0.0)
        v = step_ref[rows, :] + offset
        steps = jnp.maximum(v, 0.0) + jnp.log1p(jnp.exp(-jnp.abs(v)))
        logs = steps * (decay * LOG2E)
        hi, mid, lo = split3(logs)
        cum = mm(tri, hi) + mm(tri, mid) + mm(tri, lo)
        last = cum[L - 1 : L, :]
        enter = jnp.exp2(cum) * tok[:, 1:2]
        leave = jnp.exp2(last - cum) * tok[:, 2:3]
        sig = sigmoid(v)
        cumt = cum.T
        for g in range(4):
            cumt_ref[g, c] = cumt[16 * g : 16 * g + 8, :]
        for g in range(2):
            pieces = []
            for part in (slice(32 * g, 32 * g + 8), slice(32 * g + 16, 32 * g + 24)):
                pieces += [values[:, part] for values in (steps, cum, enter, leave, sig)] + [jnp.zeros((L, 24), F32)]
            pack_ref[g, rows, :] = jnp.concatenate(pieces, 1)
        return 0

    lax.fori_loop(0, CH, chunk, 0)


def fwd_chunks(group, tick, pre_ref, par_ref, tok_ref, bc_ref, bct_ref, g_ref, pack_ref, cumt_ref,
               gated_ref, states_ref, ss_ref, st_ref):
    st_ref[...] = jnp.zeros_like(st_ref)
    par = par_ref[...]

    def chunk(c, _):
        tick(c)
        base = pl.multiple_of(c * L, L)
        rows = pl.ds(base, L)
        tok = tok_ref[rows, :]
        u = conv_of(pre_ref[pl.ds(base, L + 8), :GW], tok, par)
        act = u * sigmoid(u)
        pack = pack_ref[rows, :]
        if group % 2:
            pack = pltpu.roll(pack, 64, 1)
        cumt = cumt_ref[c]
        g = g_ref[c]
        weighted = act * spread(pack, ST)
        low = weighted.astype(BF)
        enter = spread(pack, EE)
        state = st_ref[...]
        low_state = state.astype(BF)
        states_ref[c] = low_state
        y = mm(bc_ref[rows, 128:], low_state) * enter
        locals_ = []
        for q in range(3):
            kernels = [(g * decay_kernel(pack, cumt, 2 * q + e)).astype(BF) for e in range(2)]
            locals_.append(mm(jnp.concatenate(kernels, 1), block_diag(low[:, 128 * q : 128 * q + 128])))
        y = y + jnp.concatenate(locals_, 1)
        out = weighted * spread(pack, FF)
        st_ref[...] = enter[L - 1 : L, :] * state + mm(bct_ref[c, pl.ds(0, 128), :], out.astype(BF))
        ssd = y + par[P_SKIP : P_SKIP + 1, :] * act
        gate = pre_ref[pl.ds(base + 8, L), GW:]
        gated = ssd * (gate * sigmoid(gate))
        gated_ref[rows, :] = gated.astype(BF)
        sq = gated * gated
        ss_ref[rows, :] += sq[:, :128] + sq[:, 128:256] + sq[:, 256:]
        return 0

    lax.fori_loop(0, CH, chunk, 0)


def bwd_chunks(group, z_k, tick, pre_ref, dinner_ref, par_ref, tok_ref, bc_ref, bct_ref, g_ref, pack_ref,
               cumt_ref, states_ref, hpar_ref, dcat_ref, dstep_ref, pgrad_ref, hgrad_ref, rt_ref, dg_ref, dbc_ref):
    rt_ref[...] = jnp.zeros_like(rt_ref)
    pgrad_ref[...] = jnp.zeros_like(pgrad_ref)
    par = par_ref[...]
    decay = pltpu.roll(hpar_ref[...], (128 - 16 * group) % 128, 1)[1:2, :]
    lane = lax.broadcasted_iota(jnp.int32, (L, L), 1)
    sub = lax.broadcasted_iota(jnp.int32, (L, L), 0)
    upper = (sub <= lane).astype(BF)
    per_head = (lax.broadcasted_iota(jnp.int32, (GW, 128), 0) >> 6
                == lax.broadcasted_iota(jnp.int32, (GW, 128), 1)).astype(BF)

    def head_sums(x):
        hi, lo = split2(x)
        return mm(hi, per_head) + mm(lo, per_head)

    def chunk(step, later):
        tick(step)
        c = CH - 1 - step
        base = pl.multiple_of(c * L, L)
        rows = pl.ds(base, L)
        tok = tok_ref[rows, :]
        window = pre_ref[pl.ds(base, L + 8), :GW]
        u = conv_of(window, tok, par)
        su = sigmoid(u)
        act = u * su
        pack = pack_ref[rows, :]
        if group % 2:
            pack = pltpu.roll(pack, 64, 1)
        cumt = cumt_ref[c]
        g = g_ref[c]
        steps = spread(pack, ST)
        enter = spread(pack, EE)
        leave = spread(pack, FF)
        weighted = act * steps
        low = weighted.astype(BF)
        low_state = states_ref[c]
        bmat = bc_ref[rows, :128]
        cmat = bc_ref[rows, 128:]
        diags = [block_diag(low[:, 128 * q : 128 * q + 128]) for q in range(3)]
        decays = [decay_kernel(pack, cumt, h) for h in range(GH)]
        kernels = [jnp.concatenate([(g * decays[2 * q + e]).astype(BF) for e in range(2)], 1) for q in range(3)]
        y = mm(cmat, low_state) * enter + jnp.concatenate([mm(kernels[q], diags[q]) for q in range(3)], 1)
        skip = par[P_SKIP : P_SKIP + 1, :]
        ssd = y + skip * act
        gate = pre_ref[pl.ds(base + 8, L), GW:]
        sg = sigmoid(gate)
        silu = gate * sg
        scaled = dinner_ref[rows, :].astype(F32) * par[P_GAIN : P_GAIN + 1, :]
        d_gated = tok[:, T_INV : T_INV + 1] * scaled - (ssd * silu) * tok[:, T_BACK : T_BACK + 1]
        dy = d_gated * silu
        dcat_ref[rows, GW:] = (d_gated * ssd * sg * (1.0 + gate * (1.0 - sg))).astype(BF)
        dy_low = dy.astype(BF)
        dy_in = (dy * enter).astype(BF)
        rt = rt_ref[...]
        rt_low = rt.astype(BF)
        carried = mm(bmat, rt_low) * leave
        pieces = []
        d_scores = jnp.zeros((L, L), F32)
        for q in range(3):
            dq = dy_low[:, 128 * q : 128 * q + 128]
            dm = mm(dq, diags[q], ((1,), (1,)))
            d_scores = d_scores + dm[:, :L] * decays[2 * q] + dm[:, L:] * decays[2 * q + 1]
            both = mm(kernels[q], dq, ((0,), (0,)))
            pieces.append(jnp.where(lane < 64, both[:L], both[L:]))
        d_weighted = jnp.concatenate(pieces, 1) + carried
        dg_ref[c] += d_scores
        out = (weighted * leave).astype(BF)
        dbc_ref[rows, 128:] += mm(dy_in, low_state, ((1,), (1,)))
        dbc_ref[rows, :128] += mm(out, rt_low, ((1,), (1,)))
        keep = enter[L - 1 : L, :]
        low32 = low.astype(F32)
        d_cum = head_sums(dy_low.astype(F32) * y - low32 * d_weighted)
        at_end = jnp.sum(low32 * carried, 0, keepdims=True) + keep * jnp.sum(rt * low_state.astype(F32), 0, keepdims=True)
        d_last = head_sums(jnp.concatenate([at_end, jnp.zeros((7, GW), F32)], 0))[0:1, :]
        hi, mid, lo = split3(d_cum)
        d_log = mm(upper, hi) + mm(upper, mid) + mm(upper, lo) + d_last
        rt_ref[...] = keep * rt + mm(bct_ref[c, pl.ds(128, 128), :], dy_in)
        d_step = head_sums(act * d_weighted) + decay * d_log
        heads = lane < GH
        d_step_pre = jnp.where(heads, d_step * pltpu.roll(pack, 128 - SG, 1), 0.0)
        dstep_ref[rows, :] += pltpu.roll(d_step_pre, 16 * group, 1).astype(BF)
        rate = jnp.sum(jnp.where(heads, pack, 0.0) * d_log, 0, keepdims=True) * decay
        offs = jnp.sum(d_step_pre, 0, keepdims=True)
        hgrad_ref[0:1, :] += pltpu.roll(jnp.concatenate([rate, jnp.zeros((7, 128), F32)], 0), 16 * z_k, 1)[0:1]
        hgrad_ref[1:2, :] += pltpu.roll(jnp.concatenate([offs, jnp.zeros((7, 128), F32)], 0), 16 * z_k, 1)[0:1]
        d_act = skip * dy + steps * d_weighted
        du = d_act * su * (1.0 + u * (1.0 - su))
        pgrad_ref[K : K + 1, :] += jnp.sum(du, 0, keepdims=True)
        pgrad_ref[P_SKIP : P_SKIP + 1, :] += jnp.sum(dy * act, 0, keepdims=True)
        for k in range(K):
            moved = back_conv_input(window, k)
            if k:
                moved = moved * tok[:, 2 + k : 3 + k]
            pgrad_ref[K - 1 - k : K - k, :] += jnp.sum(du * moved, 0, keepdims=True)
        ahead = jnp.concatenate([du, later], 0)
        d_pre = par[K - 1 : K, :] * du
        for k in range(1, K):
            d_pre = d_pre + par[K - 1 - k : K - k, :] * (ahead[k : k + L] * tok[:, 5 + k : 6 + k])
        dcat_ref[rows, :GW] = d_pre.astype(BF)
        return du[:8]

    lax.fori_loop(0, CH, chunk, jnp.zeros((8, GW), F32))


def state_chunks(statepre_ref, cst_ref, tok_ref, row_ref, bc_ref, dg_ref, dbc_ref, dstate_ref, sgrad_ref):
    sgrad_ref[...] = jnp.zeros_like(sgrad_ref)
    cst = cst_ref[...]
    lane = lax.broadcasted_iota(jnp.int32, (L, L), 1)
    sub = lax.broadcasted_iota(jnp.int32, (L, L), 0)

    def last(step, later):
        c = CH - 1 - step
        base = pl.multiple_of(c * L, L)
        rows = pl.ds(base, L)
        tok = tok_ref[rows, :]
        same = (tok[:, 0:1] == row_ref[pl.ds(c, 1), :]) & (sub >= lane)
        ds = jnp.where(same, dg_ref[c], 0.0).astype(BF)
        d_c = dbc_ref[rows, 128:] + mm(ds, bc_ref[rows, :128])
        d_b = dbc_ref[rows, :128] + mm(ds, bc_ref[rows, 128:], ((0,), (0,)))
        window = statepre_ref[pl.ds(base, L + 8), :]
        w = conv_of(window, tok, cst)
        sw = sigmoid(w)
        dw = jnp.concatenate([d_b, d_c], 1) * (sw * (1.0 + w * (1.0 - sw)))
        sgrad_ref[K : K + 1, :] += jnp.sum(dw, 0, keepdims=True)
        for k in range(K):
            moved = back_conv_input(window, k)
            if k:
                moved = moved * tok[:, 2 + k : 3 + k]
            sgrad_ref[K - 1 - k : K - k, :] += jnp.sum(dw * moved, 0, keepdims=True)
        ahead = jnp.concatenate([dw, later], 0)
        d_pre = cst[K - 1 : K, :] * dw
        for k in range(1, K):
            d_pre = d_pre + cst[K - 1 - k : K - k, :] * (ahead[k : k + L] * tok[:, 5 + k : 6 + k])
        dstate_ref[rows, :] = d_pre.astype(BF)
        return dw[:8]

    lax.fori_loop(0, CH, last, jnp.zeros((8, 256), F32))


MESH = pl.DeviceIdType.MESH
VMEM_LIMIT = 63 * 2**20
R_GAIN, R_CONV, R_SHIFT, R_INNER, R_OFF, R_RATE, R_SKIP, R_CST = 6, 7, 11, 12, 13, 14, 15, 16
SMALL = 32


class Links:
    def __init__(self, send_sems):
        self.send_sems = send_sems
        self.number = {}
        self.like = {}
        self.ended = set()

    def send(self, name, src, dst, recv_sem, device, like=None):
        at = self.number.setdefault(name, len(self.number))
        self.like[name] = src if like is None else like
        pltpu.make_async_remote_copy(
            src_ref=src, dst_ref=dst, send_sem=self.send_sems.at[at], recv_sem=recv_sem,
            device_id=device, device_id_type=MESH,
        ).start()

    def arrived(self, dst, recv_sem, device):
        pltpu.make_async_remote_copy(
            src_ref=dst, dst_ref=dst, send_sem=self.send_sems.at[0], recv_sem=recv_sem,
            device_id=device, device_id_type=MESH,
        ).wait_recv()

    def left(self, name, recv_sem, device):
        self.ended.add(name)
        like = self.like[name]
        pltpu.make_async_remote_copy(
            src_ref=like, dst_ref=like, send_sem=self.send_sems.at[self.number[name]], recv_sem=recv_sem,
            device_id=device, device_id_type=MESH,
        ).wait_send()

    def finish(self, recv_sem, device):
        for name in self.number:
            if name not in self.ended:
                self.left(name, recv_sem, device)


class Place:
    def __init__(self):
        self.f = lax.axis_index("fsdp")
        self.z = lax.axis_index("zz")
        self.c = lax.axis_index("core")
        f, c = self.f, self.c
        y, x = f // 2, f % 2
        by_x = y * 2 + 1 - x
        by_y = (1 - y) * 2 + x
        self.f2 = by_x * (1 - c) + by_y * c
        self.f3 = by_y * (1 - c) + by_x * c
        self.f4 = 3 - f
        z_low, z_high = self.z % 2, self.z // 2
        self.zk = [((z_high + k // 2) % 2) * 2 + (z_low + k % 2) % 2 for k in range(4)]

    def at(self, f=None, z=None, c=None):
        return (self.f if f is None else f, self.z if z is None else z, self.c if c is None else c)

    def near(self):
        devices = [self.at(z=self.zk[k]) for k in (1, 2, 3)]
        return devices + [self.at(f=self.f2), self.at(f=self.f3), self.at(f=self.f4), self.at(c=1 - self.c)]

    def greet(self):
        for device in self.near():
            pl.semaphore_signal(pltpu.get_barrier_semaphore(), inc=1, device_id=device, device_id_type=MESH)

    def greeted(self):
        pl.semaphore_wait(pltpu.get_barrier_semaphore(), len(self.near()))


def piece(inout_ref, out_ref, m, f, z):
    depth = out_ref.shape[2] // 4
    at = pl.ds(pl.multiple_of(f * depth, depth), depth)
    if m == 2:
        return out_ref.at[z, :, at]
    return inout_ref.at[z, at, pl.ds(m * GW, GW)]


def iota(shape, dim):
    return lax.broadcasted_iota(jnp.int32, shape, dim)


def own_block(f, rows, unit):
    return ((iota((rows, GW), 1) & 63) == f * unit + iota((rows, GW), 0)).astype(BF)


def at_block(f, rows, size):
    row = iota((rows, GW), 0)
    return ((iota((rows, GW), 1) == f * size + row) & (row < size)).astype(BF)


def spread_units(values, place):
    rows = mm(values, place)
    return jnp.sum(jnp.where((iota(rows.shape, 1) >> 6) == iota(rows.shape, 0), rows, 0.0), 0, keepdims=True)


def small_block(f, vec_ref, step_ref, conv_ref, shift_ref, gain_ref, cst_ref):
    units = own_block(f, conv_ref.shape[2], conv_ref.shape[2])
    states = at_block(f, cst_ref.shape[1], cst_ref.shape[1])
    heads = at_block(f, 16, 12)
    steps = jnp.concatenate([step_ref[...].astype(F32), jnp.zeros((step_ref.shape[0], 128 - GH), F32)], 1).T
    rows = [steps[:GH], vec_ref[0:1, :]]
    rows += [spread_units(conv_ref[k], units) for k in range(K)]
    rows += [spread_units(shift_ref[...], units), spread_units(gain_ref[...], units)]
    rows.append(mm(vec_ref[2:5, :16].astype(BF), heads))
    rows.append(mm(cst_ref[...], states))
    rows.append(mm(vec_ref[1:2, :64].astype(BF), states))
    rows.append(jnp.zeros((SMALL - 21, GW), F32))
    return jnp.concatenate(rows, 0).astype(BF)


def token_masks(docs, tok_ref):
    lane, sub = iota((CH, L), 1), iota((CH, L), 0)
    masks = [docs, jnp.where((sub > 0) & (docs == pltpu.roll(docs, 1, 0)[:, L - 1 : L]), 1.0, 0.0)]
    masks.append(jnp.where(docs == docs[:, L - 1 : L], 1.0, 0.0))
    for k in range(1, K):
        moved = pltpu.roll(docs, k, 1)
        before = jnp.where(lane < k, pltpu.roll(moved, 1, 0), moved)
        masks.append(jnp.where((before == docs) & ((sub > 0) | (lane >= k)), 1.0, 0.0))
    for k in range(1, K):
        moved = pltpu.roll(docs, L - k, 1)
        after = jnp.where(lane >= L - k, pltpu.roll(moved, CH - 1, 0), moved)
        masks.append(jnp.where((after == docs) & ((sub < CH - 1) | (lane < L - k)), 1.0, 0.0))
    for c in range(CH):
        rows = [m[c : c + 1, :] for m in masks] + [jnp.zeros((128 - len(masks), L), F32)]
        tok_ref[pl.ds(c * L, L), :] = jnp.concatenate(rows, 0).T


ORDER = (3, 2, 1, 0)
ROWS = 128
SCHEDULE = {
    "s1": [("second", 0, 0)],
    "s2": [("second", 1, 0), ("first", 0, 1)],
    "s5": [("second", 0, 1), ("first", 1, 1)],
    "m05": [("second", 1, 1), ("first", 0, 2)],
    "m10": [("second", 0, 2), ("first", 1, 2)],
    "p2": [("second", 1, 2), ("first", 0, 3)],
    "m20": [("second", 0, 3), ("first", 1, 3)],
    "p3": [("second", 1, 3), ("first", 2, 0)],
    "m30": [("second", 2, 0), ("first", 2, 1)],
    "n1": [("second", 2, 1), ("first", 2, 2)],
    "b10": [("second", 2, 2), ("first", 2, 3)],
    "b30": [("second", 2, 3), ("s1", 0), ("s1", 1), ("s1", 2)],
    "b31": [("s1", 3)],
    "x2": [("s2", 0)],
    "g02": [("s3", 0), ("s2", 1)],
    "g06": [("s3", 1)],
    "g07": [("s2", 2)],
    "h01": [("s3", 2)],
    "h02": [("s2", 3)],
    "g14": [("last", 3), ("s2", 4)],
    "h10": [("s3", 4)],
    "h11": [("s2", 5)],
    "g23": [("s3", 5)],
    "g24": [("s2", 6)],
    "h20": [("s3", 6)],
    "h21": [("s2", 7)],
    "g33": [("s3", 7)],
    "g34": [("s2", 8)],
    "h30": [("s3", 8)],
    "h31": [("s2", 9)],
    "t1": [("s3", 9)],
    "t2": [("s2", 10)],
    "t4": [("s2", 11), ("last", 10)],
    "t5": [("last", 11)],
}
T_INV, T_BACK = 16, 17


def block_kernel(model, hid_ref, cot_ref, w0_ref, w1_ref, w2_ref, wst_ref, vec_ref, step_ref, conv_ref, shift_ref, gain_ref,
                 cvst_ref, seg_ref,
                 layer_out, hidden_out, normt_hbm, win_hbm, pre_hbm, states_hbm,
                 ginner_out, ggate_out, gout_out, gstate_ref, gsmall_ref, gother_ref,
                 hall, call, win, wout, pre, accr, flip, gated, states, halfr, recv1, recv2, recv3, stage,
                 small_ref, sbuf, stbuf, statepre_ref, ss_ref, ssr_ref, tok_ref, docs_ref,
                 bc_ref, bct_ref, g_ref, pack_ref, cumt_ref, par_ref, hpar_ref, cst_ref, stw_ref, gains_ref, gaingrad_ref, st_ref,
                 srecv, srecv1, srecv3, srecvc, qrecv1, qrecv3, qsend, qrecvc, nparts, nrecv, nback,
                 dstep, dstate, pgrad, hgrad, sgrad, rt_ref, dg_ref, dbc_ref,
                 sends, recvs, small_recvs, state_recvs, core_recvs, recv_sems, core_sems, state_sems, gain_sems,
                 outs_sem, pre_sem, state_sem, own_sem, load_sems, stage_sem, hid_sem, credit, free_out, free_core, free_half):
    stepre_ref = pr_ref = ss_ref
    dcat = hall.at[:, pl.ds(0, 2 * GW)]
    here = Place()
    z, zk = here.z, here.zk
    rows_own = hid_ref.shape[0]
    wide = 2 * GW
    depth = model // 4
    links = Links(sends)
    shards = [w0_ref, w1_ref, w2_ref]
    outs = []

    def put(src, dst):
        copy = pltpu.make_async_copy(src, dst, outs_sem.at[len(outs)])
        copy.start()
        outs.append(copy)

    here.greet()
    small_ref[...] = small_block(here.f, vec_ref, step_ref, conv_ref, shift_ref, gain_ref, cvst_ref)
    here.greeted()
    mine = pl.ds(pl.multiple_of(here.c * rows_own, rows_own), rows_own)
    other = pl.ds(pl.multiple_of((1 - here.c) * rows_own, rows_own), rows_own)
    core = here.at(c=1 - here.c)
    one_block = recv2.at[0]
    for k in (1, 2, 3):
        links.send(("small", k), small_ref, sbuf.at[here.f, z], small_recvs.at[k], here.at(z=zk[k]))
    links.send("hidden", hid_ref, hall.at[mine], core_recvs.at[0], core)

    def recv_sem(m, f, z_):
        return recvs.at[m, f, z_]

    def push_z(m):
        for k in (1, 2, 3):
            links.send(("z", m, k), shards[m], piece(win, wout, m, here.f, z), recv_sem(m, here.f, z), here.at(z=zk[k]))

    def first(m, k):
        dst = piece(win, wout, m, here.f, zk[k])
        src = shards[m] if k == 0 else dst
        if k:
            links.arrived(dst, recv_sem(m, here.f, zk[k]), here.at(z=zk[k]))
        links.send(("first", m, k, 2), src, dst, recv_sem(m, here.f, zk[k]), here.at(f=here.f2), one_block)
        links.send(("first", m, k, 3), src, dst, recv_sem(m, here.f, zk[k]), here.at(f=here.f3), one_block)

    def second(m, k):
        src = piece(win, wout, m, here.f2, zk[k])
        links.arrived(src, recv_sem(m, here.f2, zk[k]), here.at(f=here.f2))
        links.send(("second", m, k), src, src, recv_sem(m, here.f2, zk[k]), here.at(f=here.f3), one_block)

    def third(m, k):
        for f in (here.f3, here.f4):
            src = piece(win, wout, m, f, zk[k])
            links.arrived(src, recv_sem(m, f, zk[k]), here.at(f=here.f3))

    events = {"first": first, "second": second}

    def due(slot):
        for name, *what in SCHEDULE.get(slot, ()):
            events[name](*what)

    def ticker(prefix):
        def tick(step):
            for at in range(CH):
                if prefix + str(at) in SCHEDULE:
                    pl.when(step == at)(functools.partial(due, prefix + str(at)))

        return tick

    def state_of(f, part):
        return stbuf.at[f, :, part]

    push_z(0)
    links.send("cot", cot_ref, call.at[mine], core_recvs.at[1], core)
    own_copies = [pltpu.make_async_copy(shards[m], piece(win, wout, m, here.f, z), own_sem.at[m]) for m in range(3)]
    own_copies.append(pltpu.make_async_copy(cot_ref, call.at[mine], own_sem.at[3]))
    own_copies.append(pltpu.make_async_copy(hid_ref, hall.at[mine], hid_sem.at[4]))
    for copy in own_copies:
        copy.start()
    sbuf[here.f, z] = small_ref[...]
    stbuf[here.f] = wst_ref[...]
    docs = seg_ref[pl.ds(pl.multiple_of(z * CH, CH), CH), :].astype(F32)
    docs_ref[...] = docs
    token_masks(docs, tok_ref)
    for k in (1, 2, 3):
        links.arrived(sbuf.at[here.f, zk[k]], small_recvs.at[k], here.at(z=zk[k]))
    links.send(("small", 4), sbuf.at[here.f], sbuf.at[here.f], small_recvs.at[4], here.at(f=here.f2))
    links.send(("small", 5), sbuf.at[here.f], sbuf.at[here.f], small_recvs.at[5], here.at(f=here.f3))
    half_state = pl.ds(pl.multiple_of(here.c * 128, 128), 128)
    rest_state = pl.ds(pl.multiple_of(128 - here.c * 128, 128), 128)
    links.send(("state", 0), wst_ref.at[:, half_state], state_of(here.f, half_state), state_recvs.at[0], here.at(f=here.f2))
    links.send(("state", 1), wst_ref.at[:, half_state], state_of(here.f, half_state), state_recvs.at[1], here.at(f=here.f3))
    first(0, 0)
    push_z(1)
    links.arrived(sbuf.at[here.f2], small_recvs.at[4], here.at(f=here.f2))
    links.send(("small", 6), sbuf.at[here.f2], sbuf.at[here.f2], small_recvs.at[6], here.at(f=here.f3))
    links.arrived(state_of(here.f2, half_state), state_recvs.at[0], here.at(f=here.f2))
    links.send(("state", 2), state_of(here.f2, half_state), state_of(here.f2, half_state), state_recvs.at[2], here.at(f=here.f3))
    links.send(("state", 3), state_of(here.f2, half_state), state_of(here.f2, half_state), state_recvs.at[3], core)
    first(1, 0)
    push_z(2)
    due("s0")
    links.arrived(sbuf.at[here.f3], small_recvs.at[5], here.at(f=here.f3))
    links.arrived(sbuf.at[here.f4], small_recvs.at[6], here.at(f=here.f3))

    shared = sum(sbuf[f, 0].astype(F32) for f in range(4))
    gain_outer = jnp.concatenate([sbuf[f, 0][R_GAIN : R_GAIN + 1, :].astype(F32) for f in range(4)], 1)
    gains_ref[...] = jnp.broadcast_to(gain_outer, (8, model))
    cst_ref[...] = jnp.concatenate([shared[R_CST : R_CST + 5, :256], jnp.zeros((3, 256), F32)], 0)
    lane8 = lax.broadcasted_iota(jnp.int32, (8, 128), 1)
    heads8 = jnp.concatenate([shared[R_OFF : R_SKIP + 1, :128], jnp.zeros((5, 128), F32)], 0)
    own_heads = jnp.zeros((8, 128), F32)
    spread_heads = (lax.broadcasted_iota(jnp.int32, (128, GW), 1) >> 6
                    == lax.broadcasted_iota(jnp.int32, (128, GW), 0)).astype(BF)
    stw_ref[...] = jnp.zeros_like(stw_ref)
    for k in range(4):
        turned = pltpu.roll(heads8, 128 - (2 * zk[k] + here.c) * GH, 1)
        own_heads = own_heads + pltpu.roll(jnp.where(lane8 < GH, turned, 0.0), 16 * k, 1)
        group = sum(sbuf[f, zk[k]].astype(F32) for f in range(4))
        skips = mm(turned.astype(BF), spread_heads)[2:3, :]
        par_ref[k] = jnp.concatenate(
            [group[R_CONV : R_CONV + 5], skips, group[R_INNER : R_INNER + 1], jnp.zeros((1, GW), F32)], 0
        )
        for f in range(4):
            block = sbuf[f, zk[k]][:16].astype(F32)
            keep = lax.broadcasted_iota(jnp.int32, block.shape, 0) < GH
            stw_ref[pl.ds(16 * k, 16), pl.ds(depth * f, depth)] = jnp.where(keep, block, 0.0).astype(BF)
    decay = -jnp.exp(own_heads[1:2, :])
    hpar_ref[...] = jnp.concatenate([own_heads[0:1], decay, own_heads[2:3], jnp.zeros((5, 128), F32)], 0)

    due("s1")
    own_copies[4].wait()
    links.arrived(hall.at[other], core_recvs.at[0], core)

    def norm(i, _):
        rows = pl.ds(pl.multiple_of(i * L, L), L)
        x = hall[rows, :].astype(F32)
        inv = lax.rsqrt(jnp.sum(x * x, 1, keepdims=True) / model + EPSILON)
        hall[rows, :] = (x * inv * gain_outer).astype(BF)
        return 0

    lax.fori_loop(0, SEQ // L, norm, 0)
    due("s2")
    links.arrived(state_of(here.f3, half_state), state_recvs.at[1], here.at(f=here.f3))
    links.send(("state", 4), state_of(here.f3, half_state), state_of(here.f3, half_state), state_recvs.at[4], core)
    links.arrived(state_of(here.f4, half_state), state_recvs.at[2], here.at(f=here.f3))
    links.send(("state", 5), state_of(here.f4, half_state), state_of(here.f4, half_state), state_recvs.at[5], core)
    for n, f in ((3, here.f3), (4, here.f2), (5, here.f4)):
        links.arrived(state_of(f, rest_state), state_recvs.at[n], core)

    TILE = 256

    def project_small(i, _):
        rows = pl.ds(pl.multiple_of(i * TILE, TILE), TILE)
        total = jnp.zeros((TILE, 256), F32)
        for f in range(4):
            total = total + mm(hall[rows, pl.ds(depth * f, depth)], stbuf[f])
        statepre_ref[pl.ds(pl.multiple_of(i * TILE + 8, 8), TILE), :] = total
        steps = mm(hall[rows, :], stw_ref[...], ((1,), (1,)))
        stepre_ref[rows, :] = jnp.concatenate([steps, jnp.zeros((TILE, 64), F32)], 1)
        return 0

    statepre_ref[pl.ds(0, 8), :] = jnp.zeros((8, 256), F32)
    lax.fori_loop(0, SEQ // TILE, project_small, 0)

    due("s3")

    def turn(i, _):
        for half in range(2):
            lanes = pl.ds(pl.multiple_of(i * 256 + half * 128, 128), 128)
            flip[lanes, :] = hall[:, lanes].T
        return 0

    lax.fori_loop(0, model // 256, turn, 0)
    TURNED = len(outs)
    put(flip, normt_hbm)
    due("s4")
    prep_chunks(statepre_ref, stepre_ref, tok_ref, docs_ref, cst_ref, hpar_ref, bc_ref, bct_ref, g_ref, pack_ref, cumt_ref)
    due("s5")
    links.arrived(call.at[other], core_recvs.at[1], core)
    for copy in own_copies[:4]:
        copy.wait()
    ss_ref[...] = jnp.zeros_like(ss_ref)
    for slot in range(2):
        pre[slot, pl.ds(0, 8), :] = jnp.zeros((8, 2 * GW), F32)
    pre_copies = []
    state_copies = []
    for k in range(4):
        due("p%d" % k)
        third(0, k)
        third(1, k)
        slot = k % 2
        if k >= 2:
            pre_copies[k - 2].wait()

        def project(i, _, slot=slot, k=k):
            rows = pl.ds(pl.multiple_of(i * TILE, TILE), TILE)
            to = pl.ds(pl.multiple_of(i * TILE + 8, 8), TILE)
            pre[slot, to, :] = mm(hall[rows, :], win[zk[k]])
            return 0

        lax.fori_loop(0, SEQ // TILE, project, 0)
        copy = pltpu.make_async_copy(pre.at[slot, pl.ds(8, SEQ)], pre_hbm.at[k], pre_sem.at[k])
        copy.start()
        pre_copies.append(copy)
        put(win.at[zk[k]], win_hbm.at[k])
        if k:
            state_copies[k - 1].wait()
        fwd_chunks(k, ticker("m%d" % k), pre.at[slot], par_ref.at[k], tok_ref, bc_ref, bct_ref, g_ref, pack_ref.at[k // 2], cumt_ref.at[k],
                   gated.at[k], states, ss_ref, st_ref)
        copy = pltpu.make_async_copy(states, states_hbm.at[k], state_sem.at[k])
        copy.start()
        state_copies.append(copy)
    for copy in pre_copies[2:] + state_copies[3:]:
        copy.wait()

    links.send("squares", ss_ref, ssr_ref, core_recvs.at[2], core)
    due("n0")
    links.arrived(ssr_ref, core_recvs.at[2], core)
    inner_all = 2 * 4 * GW

    def inner_norm(i, _):
        rows = pl.ds(pl.multiple_of(i * L, L), L)
        total = jnp.sum(ss_ref[rows, :] + ssr_ref[rows, :], 1, keepdims=True)
        inv = lax.rsqrt(total / inner_all + EPSILON)
        tok_ref[rows, :] = jnp.where(iota((L, 128), 1) == T_INV, inv, tok_ref[rows, :])
        for k in range(4):
            gain = par_ref[k, P_GAIN : P_GAIN + 1, :]
            low = (gated[k, rows, :].astype(F32) * inv * gain).astype(BF)
            hall[rows, pl.ds(k * GW, GW)] = low
            flip[pl.ds(k * GW, GW), rows] = low.T
        pr_ref[rows, :] = jnp.zeros((L, 128), F32)
        return 0

    links.left("squares", core_recvs.at[0], core)
    for copy in outs:
        copy.wait()
    lax.fori_loop(0, SEQ // L, inner_norm, 0)
    pl.semaphore_signal(free_core, inc=1, device_id=core, device_id_type=MESH)
    f, f2, f3, f4 = here.f, here.f2, here.f3, here.f4
    for m in (0, 1):
        for k in range(4):
            for name in (("first", m, k, 2), ("first", m, k, 3), ("second", m, k)):
                links.left(name, core_recvs.at[0], core)
    loads = {}

    def load(name, src, dst, sem):
        copy = pltpu.make_async_copy(src, dst, load_sems.at[sem])
        copy.start()
        loads[name] = copy

    accl = pre.at[0, pl.ds(8, SEQ)]

    def slot_of(u):
        return (u % 6) // 2, u % 2

    def part(u, f_):
        at, side = slot_of(u)
        return win.at[at, pl.ds(pl.multiple_of(f_ * depth, depth), depth), pl.ds(side * GW, GW)]

    def landing(u, n):
        if u < 4:
            return recv1.at[u, n]
        n += 2 * (u - 4)
        return wout.at[n // 4, :, pl.ds((n % 4) * GW, GW)]

    def s1(u):
        for n, f_ in enumerate((f3, f4)):
            links.send(("s1", u, n), part(u, f_), landing(u, n), recv_sems.at[u, n], here.at(f=f3), one_block)

    units = [(k, 2) for k in ORDER] + [(k, m) for k in ORDER for m in (0, 1)]

    def add_into(dst, src):
        rows, width = dst.shape

        def body(i, _):
            at = pl.ds(pl.multiple_of(i * ROWS, ROWS), ROWS)
            dst[at, :] = (dst[at, :].astype(F32) + src[at, :].astype(F32)).astype(dst.dtype)
            return 0

        lax.fori_loop(0, rows // ROWS, body, 0)

    def s2(u):
        links.arrived(landing(u, 1), recv_sems.at[u, 1], here.at(f=f3))
        add_into(part(u, f2), landing(u, 1))
        if u >= 4:
            pl.semaphore_wait(credit, 1)
        links.send(("s2", u), part(u, f2), recv2.at[u % 4], recv_sems.at[u, 2], here.at(f=f2), one_block)
        links.arrived(landing(u, 0), recv_sems.at[u, 0], here.at(f=f3))
        add_into(part(u, f), landing(u, 0))

    def give_credit(u):
        if u < 8:
            pl.semaphore_signal(credit, inc=1, device_id=here.at(f=f2), device_id_type=MESH)

    outs = {0: ginner_out, 1: ggate_out, 2: gout_out}
    results = [pltpu.make_async_copy(stage, outs[m], stage_sem.at[m]) for m in range(3)]
    staged = []

    def s3(u):
        k, m = units[u]
        links.arrived(recv2.at[u % 4], recv_sems.at[u, 2], here.at(f=f2))
        add_into(part(u, f), recv2.at[u % 4])
        give_credit(u)
        links.send(("s3", u), part(u, f), recv3.at[m, k - 1], recv_sems.at[12 + m, k - 1], here.at(z=zk[k]), one_block)

    def last_sum(u):
        k, m = units[u]
        links.arrived(recv2.at[u % 4], recv_sems.at[u, 2], here.at(f=f2))
        for j in (1, 2, 3):
            links.arrived(recv3.at[m, j - 1], recv_sems.at[12 + m, j - 1], here.at(z=zk[j]))
        own = part(u, f)
        if staged:
            results[staged[-1]].wait()

        def body(i, _):
            at = pl.ds(pl.multiple_of(i * ROWS, ROWS), ROWS)
            total = own[at, :].astype(F32) + recv2[u % 4, at, :].astype(F32)
            for j in range(3):
                total = total + recv3[m, j, at, :].astype(F32)
            stage[at, :] = total
            return 0

        lax.fori_loop(0, GW // ROWS, body, 0)
        give_credit(u)
        staged.append(m)
        results[m].start()

    events.update({"s1": s1, "s2": s2, "s3": s3, "last": last_sum})

    def grad_out(i):
        k = ORDER[i]
        at, side = slot_of(i)

        def rows_of(j, _):
            src = pl.ds(pl.multiple_of(k * GW + j * ROWS, ROWS), ROWS)
            total = mm(flip[src, :], call[...])
            for f_ in range(4):
                to = pl.ds(pl.multiple_of(f_ * depth + j * ROWS, ROWS), ROWS)
                win[at, to, pl.ds(side * GW, GW)] = total[:, f_ * depth : (f_ + 1) * depth].astype(BF)
            return 0

        lax.fori_loop(0, GW // ROWS, rows_of, 0)

    hid_copies = []
    for side in range(2):
        src = hid_ref.at[:, pl.ds(side * wide, wide)]
        hid_copies.append(pltpu.make_async_copy(src, halfr.at[pl.ds(side * rows_own, rows_own)], hid_sem.at[side]))
        hid_copies[-1].start()
    due("n1")
    for k in range(4):
        due("b%d0" % k)
        grad_out(k)
        due("b%d1" % k)
        third(2, k)
        gaingrad_ref[k] = jnp.zeros((8, GW), F32)

        def back(i, _, k=k):
            rows = pl.ds(pl.multiple_of(i * TILE, TILE), TILE)
            d = mm(call[rows, :], wout[zk[k]], ((1,), (1,)))
            both = d * gated[k, rows, :].astype(F32)
            gated[k, rows, :] = d.astype(BF)
            gaingrad_ref[k, 0:1, :] += jnp.sum(both * tok_ref[rows, T_INV : T_INV + 1], 0, keepdims=True)
            both = both * par_ref[k, P_GAIN : P_GAIN + 1, :]
            pr_ref[rows, :] += both[:, :128] + both[:, 128:256] + both[:, 256:]
            return 0

        lax.fori_loop(0, SEQ // TILE, back, 0)
    pl.semaphore_wait(free_core, 1)
    links.send("products", pr_ref, ssr_ref, core_recvs.at[3], core)
    due("x0")
    load("normt", normt_hbm, flip, 0)
    load(("win", 0), win_hbm.at[ORDER[0]], win.at[3], 1)

    def mix_rows(i, _):
        rows = pl.ds(pl.multiple_of(i * TILE, TILE), TILE)
        for k in range(4):
            mixed = mm(hall[rows, pl.ds(k * GW, GW)], wout[zk[k]])
            accl[rows, :] = mixed[:, :wide] if k == 0 else accl[rows, :] + mixed[:, :wide]
            accr[rows, :] = mixed[:, wide:] if k == 0 else accr[rows, :] + mixed[:, wide:]
        return 0

    lax.fori_loop(0, SEQ // TILE, mix_rows, 0)
    due("x1")
    half = hall.at[:, pl.ds(0, wide)]
    halves = [halfr, hall.at[:, pl.ds(wide, wide)]]

    def exchange(n):
        def body(j, _):
            src = pl.ds(pl.multiple_of((1 - here.c) * rows_own + j * ROWS, ROWS), ROWS)
            half[pl.ds(pl.multiple_of(j * ROWS, ROWS), ROWS), :] = accl[src, :].astype(BF)
            half[pl.ds(pl.multiple_of(rows_own + j * ROWS, ROWS), ROWS), :] = accr[src, :].astype(BF)
            return 0

        lax.fori_loop(0, rows_own // ROWS, body, 0)
        links.send(("half", n), half, halves[n], core_sems.at[n], core)

    def received(n):
        links.arrived(halves[n], core_sems.at[n], core)

    def places(j):
        own = pl.ds(pl.multiple_of(here.c * rows_own + j * ROWS, ROWS), ROWS)
        at = pl.ds(pl.multiple_of(j * ROWS, ROWS), ROWS)
        below = pl.ds(pl.multiple_of(rows_own + j * ROWS, ROWS), ROWS)
        return own, at, below

    def summed(n, j):
        own, at, below = places(j)
        left = accl[own, :] + halves[n][at, :].astype(F32)
        right = accr[own, :] + halves[n][below, :].astype(F32)
        return own, at, below, jnp.concatenate([left, right], 1)

    def store(n, at, below, values):
        halves[n][at, :] = values[:, :wide].astype(BF)
        halves[n][below, :] = values[:, wide:].astype(BF)

    def give(n, out, sem):
        for side in range(2):
            load((n, side), halves[n].at[pl.ds(side * rows_own, rows_own)], out.at[:, pl.ds(side * wide, wide)], sem + side)

    def add_hidden(j, _):
        own, at, below = places(j)
        accl[own, :] = accl[own, :] + halfr[at, :].astype(F32)
        accr[own, :] = accr[own, :] + halfr[below, :].astype(F32)
        return 0

    for copy in hid_copies:
        copy.wait()
    lax.fori_loop(0, rows_own // ROWS, add_hidden, 0)
    pl.semaphore_signal(free_half, inc=1, device_id=core, device_id_type=MESH)
    pl.semaphore_wait(free_half, 1)
    exchange(0)
    due("x2")
    links.arrived(ssr_ref, core_recvs.at[3], core)

    def scale(i, _):
        rows = pl.ds(pl.multiple_of(i * L, L), L)
        total = jnp.sum(pr_ref[rows, :] + ssr_ref[rows, :], 1, keepdims=True)
        tok = tok_ref[rows, :]
        inv = tok[:, T_INV : T_INV + 1]
        tok_ref[rows, :] = jnp.where(iota((L, 128), 1) == T_BACK, inv * inv * inv * (total / inner_all), tok)
        return 0

    lax.fori_loop(0, SEQ // L, scale, 0)
    for k in range(4):
        for name in (("first", 2, k, 2), ("first", 2, k, 3), ("second", 2, k)):
            links.left(name, core_recvs.at[0], core)
    pl.semaphore_signal(free_out, inc=1, device_id=here.at(f=f3), device_id_type=MESH)
    links.left(("half", 0), core_sems.at[0], core)
    hgrad[...] = jnp.zeros_like(hgrad)
    dg_ref[...] = jnp.zeros_like(dg_ref)
    dbc_ref[...] = jnp.zeros_like(dbc_ref)
    dstep[...] = jnp.zeros_like(dstep)
    def to_normed(fresh, j, _):
        at = pl.ds(pl.multiple_of(j * 256, 256), 256)
        total = mm(dcat[at, :], win[3], ((1,), (1,)))
        accl[at, :] = total[:, :wide] if fresh else accl[at, :] + total[:, :wide]
        accr[at, :] = total[:, wide:] if fresh else accr[at, :] + total[:, wide:]
        return 0

    for i, k in enumerate(ORDER):
        if i:
            for name in ("pre", "states"):
                loads[name, i].wait()

        bwd_chunks(k, zk[k], ticker("g%d" % i), pre.at[1], gated.at[k], par_ref.at[k], tok_ref, bc_ref, bct_ref, g_ref,
                   pack_ref.at[k // 2], cumt_ref.at[k], states, hpar_ref, dcat, dstep, pgrad.at[k], hgrad, rt_ref, dg_ref, dbc_ref)
        if i < 3:
            load(("pre", i + 1), pre_hbm.at[ORDER[i + 1]], pre.at[1, pl.ds(8, SEQ)], 2)
            load(("states", i + 1), states_hbm.at[ORDER[i + 1]], states, 3)
        else:
            loads[0, 0].wait()
            loads[0, 1].wait()
        u = 4 + 2 * i
        due("h%d0" % i)
        if u >= 6:
            for n in (u - 6, u - 5):
                for name in (("s1", n, 0), ("s1", n, 1), ("s2", n), ("s3", n)):
                    if name in links.number:
                        links.left(name, core_sems.at[0], here.at(c=1 - here.c))

        if i == 0:
            loads["normt"].wait()
            pl.semaphore_wait(free_out, 1)

        def grads(j, _, u=u):
            at = pl.ds(pl.multiple_of(j * ROWS, ROWS), ROWS)
            win[slot_of(u)[0], at, :] = mm(flip[at, :], dcat[...]).astype(BF)
            return 0

        lax.fori_loop(0, model // ROWS, grads, 0)
        s1(u)
        s1(u + 1)
        if i == 0:
            received(0)

            def layer(j, _):
                own, at, below, total = summed(0, j)
                store(0, at, below, total)
                return 0

            lax.fori_loop(0, rows_own // ROWS, layer, 0)
            give(0, layer_out, 4)
        due("h%d1" % i)
        if i < 3:
            loads["win", i].wait()
            lax.fori_loop(0, SEQ // 256, functools.partial(to_normed, i == 0), 0)
            load(("win", i + 1), win_hbm.at[ORDER[i + 1]], win.at[3], 1)
            due("h%d2" % i)

    last_tokens = []
    for k in range(4):
        src = hid_ref.at[:, pl.ds(k * GW, GW)]
        last_tokens.append(pltpu.make_async_copy(src, gated.at[k, pl.ds(0, rows_own)], hid_sem.at[k]))
        last_tokens[-1].start()
    state_chunks(statepre_ref, cst_ref, tok_ref, docs_ref, bc_ref, dg_ref, dbc_ref, dstate, sgrad)
    due("t0")

    def state_part(f_, n=0):
        at = pl.ds(pl.multiple_of((f_ % 2) * depth, depth), depth)
        return halfr.at[at, pl.ds(pl.multiple_of((f_ // 2) * 256 + n * 128, 128), 128)]

    def small_part(f_):
        at = pl.ds(pl.multiple_of(2 * depth + (f_ // 2) * 4 * SMALL, 4 * SMALL), 4 * SMALL)
        return halfr.at[at, pl.ds(pl.multiple_of((f_ % 2) * GW, GW), GW)]

    def add_to(ref, *others):
        total = ref[...].astype(F32)
        for other in others:
            total = total + other.astype(F32)
        ref[...] = total.astype(BF)
        return total

    for f_ in range(4):
        sums = mm(flip[pl.ds(f_ * depth, depth), :], dstate[...])
        lower, upper = sums[:, :128], sums[:, 128:]
        state_part(f_)[...] = jnp.where(here.c == 0, lower, upper).astype(BF)
        state_part(f_, 1)[...] = jnp.where(here.c == 0, upper, lower).astype(BF)
        links.send(("state_core", f_), state_part(f_, 1), srecv.at[f_], state_sems.at[f_], core)
    due("t1")
    step_rows = mm(dstep[:, :64], flip[...], ((0,), (1,)))
    zeros = jnp.zeros((1, GW - 256), F32)
    skips = jnp.zeros((8, 128), F32)
    heads_of = (iota((GW, 128), 0) >> 6 == iota((GW, 128), 1)).astype(BF)
    for k in range(4):
        hi, lo = split2(pgrad[k])
        skips = skips + pltpu.roll(mm(hi, heads_of) + mm(lo, heads_of), 16 * zk[k], 1)
    head_rows = jnp.concatenate([hgrad[0:2, :], skips[P_SKIP : P_SKIP + 1, :]], 0)
    head_rows = jnp.concatenate([head_rows, jnp.zeros((3, GW - 128), F32)], 1)
    common = [jnp.zeros((1, GW), F32)]
    common += [jnp.concatenate([sgrad[r : r + 1, :], zeros], 1) for r in range(5)]
    common.append(head_rows)
    for f_ in range(4):
        blocks = []
        for k in range(4):
            own = jnp.concatenate([pgrad[k, 0:5, :], gaingrad_ref[k, 0:1, :], jnp.zeros((1, GW), F32)], 0)
            blocks += [step_rows[16 * k : 16 * k + 16, f_ * depth : (f_ + 1) * depth], own] + common
        small_part(f_)[...] = jnp.concatenate(blocks, 0).astype(BF)
    for n, f_ in enumerate((f2, f3, f4)):
        links.send(("sums", n), small_part(f_), qrecv1.at[n], recv_sems.at[16, n], here.at(f=f_))
    loads["win", 3].wait()
    lax.fori_loop(0, SEQ // 256, functools.partial(to_normed, False), 0)

    def finish_normed(j, _):
        at = pl.ds(pl.multiple_of(j * 256, 256), 256)
        total = mm(dstep[at, :64], stw_ref[...])
        total = total + jnp.concatenate([mm(dstate[at, :], stbuf[f_], ((1,), (1,))) for f_ in range(4)], 1)
        accl[at, :] = accl[at, :] + total[:, :wide]
        accr[at, :] = accr[at, :] + total[:, wide:]
        return 0

    lax.fori_loop(0, SEQ // 256, finish_normed, 0)
    due("t2")
    exchange(1)
    for f_ in range(4):
        links.arrived(srecv.at[f_], state_sems.at[f_], core)
        add_to(state_part(f_), srecv[f_])
    for n, f_ in enumerate((f2, f3, f4)):
        links.send(("state", f"f{n}"), state_part(f_), srecv1.at[n], recv_sems.at[15, n], here.at(f=f_))
    due("t3")
    received(1)
    gain = gains_ref[0:1, :]
    for copy in last_tokens:
        copy.wait()

    def last(j, gain_grad):
        own, at, below, d = summed(1, j)
        x = jnp.concatenate([gated[k, at, :] for k in range(4)], 1).astype(F32)
        inv = lax.rsqrt(jnp.sum(x * x, 1, keepdims=True) / model + EPSILON)
        weighted = d * gain
        mean = jnp.sum(x * weighted, 1, keepdims=True) / model
        d_hidden = inv * weighted - x * (inv * inv * inv * mean)
        store(1, at, below, call[own, :].astype(F32) + d_hidden)
        return gain_grad + jnp.sum(d * x * inv, 0, keepdims=True)

    gain_grad = lax.fori_loop(0, rows_own // ROWS, last, jnp.zeros((1, model), F32))
    give(1, hidden_out, 6)
    for f_ in range(4):
        nparts[f_] = jnp.broadcast_to(gain_grad[:, f_ * depth : (f_ + 1) * depth], (16, GW)).astype(BF)
    for n, f_ in enumerate((f2, f3, f4)):
        links.send(("gain", n), nparts.at[f_], nrecv.at[n], gain_sems.at[n], here.at(f=f_))
    due("t4")
    for n, f_ in enumerate((f2, f3, f4)):
        links.arrived(qrecv1.at[n], recv_sems.at[16, n], here.at(f=f_))
    sums = add_to(small_part(f), qrecv1[0], qrecv1[1], qrecv1[2])
    for k in range(4):
        qsend[k] = sums[k * SMALL : (k + 1) * SMALL].astype(BF)
        if k:
            links.send(("small_z", k), qsend.at[k], qrecv3.at[k - 1], recv_sems.at[18, k - 1], here.at(z=zk[k]))
    for n, f_ in enumerate((f2, f3, f4)):
        links.arrived(srecv1.at[n], recv_sems.at[15, n], here.at(f=f_))
    add_to(state_part(f), srecv1[0], srecv1[1], srecv1[2])
    for k in (1, 2, 3):
        links.send(("state_z", k), state_part(f), srecv3.at[k - 1], recv_sems.at[17, k - 1], here.at(z=zk[k]))
    for n, f_ in enumerate((f2, f3, f4)):
        links.arrived(nrecv.at[n], gain_sems.at[n], here.at(f=f_))
    add_to(nparts.at[f], nrecv[0], nrecv[1], nrecv[2])
    for k in (1, 2, 3):
        links.send(("gain_z", k), nparts.at[f], nrecv.at[k + 2], gain_sems.at[k + 2], here.at(z=zk[k]))
    due("t5")
    for k in (1, 2, 3):
        links.arrived(qrecv3.at[k - 1], recv_sems.at[18, k - 1], here.at(z=zk[k]))
    small_total = qsend[0].astype(F32)
    for k in range(3):
        small_total = small_total + qrecv3[k].astype(F32)
    qsend[0] = small_total.astype(BF)
    links.send("small_core", qsend.at[0], qrecvc, core_sems.at[3], core)
    due("t6")
    for k in (1, 2, 3):
        links.arrived(nrecv.at[k + 2], gain_sems.at[k + 2], here.at(z=zk[k]))
    gain_total = nparts[f].astype(F32)
    for k in (3, 4, 5):
        gain_total = gain_total + nrecv[k].astype(F32)
    nback[...] = gain_total.astype(BF)
    links.send("gain_core", nback, nrecv.at[6], gain_sems.at[6], core)
    for k in (1, 2, 3):
        links.arrived(srecv3.at[k - 1], recv_sems.at[17, k - 1], here.at(z=zk[k]))
    total = state_part(f)[...].astype(F32)
    for k in range(3):
        total = total + srecv3[k].astype(F32)
    back = halfr.at[pl.ds(0, depth), pl.ds(512, 128)]
    back[...] = total.astype(BF)
    links.send("state_back", back, srecvc, core_sems.at[4], core)
    due("t7")
    gain_row = iota((SMALL, GW), 0) == 23
    links.arrived(qrecvc, core_sems.at[3], core)
    links.arrived(nrecv.at[6], gain_sems.at[6], core)
    gsmall_ref[...] = jnp.where(gain_row, gain_total[0:1, :], small_total)
    gother_ref[...] = jnp.where(gain_row, nrecv[6][0:1, :].astype(F32), qrecvc[...].astype(F32))
    links.arrived(srecvc, core_sems.at[4], core)
    rest = srecvc[...].astype(F32)
    gstate_ref[...] = jnp.concatenate([jnp.where(here.c == 0, total, rest), jnp.where(here.c == 0, rest, total)], 1)
    for side in range(2):
        loads[1, side].wait()
    results[staged[-1]].wait()
    links.finish(core_sems.at[0], core)


def block_call(model, hidden, *args):
    rows = hidden.shape[0]
    depth = model // 4
    any_ = pl.BlockSpec(memory_space=pl.ANY)
    sds = jax.ShapeDtypeStruct
    block = (GW, GW)
    part = (depth, 128)
    small = (SMALL, GW)

    def v(kind, *shape):
        return pltpu.VMEM(shape, kind)

    return pl.pallas_call(
        functools.partial(block_kernel, model),
        out_shape=(
            sds((rows, model), BF), sds((rows, model), BF),
            sds((model, SEQ), BF), sds((4, model, 2 * GW), BF), sds((4, SEQ, 2 * GW), F32), sds((4, CH, 128, GW), BF),
            sds(block, F32), sds(block, F32), sds(block, F32), sds((depth, 256), F32), sds(small, F32), sds(small, F32),
        ),
        in_specs=[any_] * 5 + [vm()] * (len(args) - 4),
        out_specs=tuple([any_] * 9 + [vm()] * 3),
        scratch_shapes=[
            v(BF, SEQ, model), v(BF, SEQ, model), v(BF, 4, model, 2 * GW), v(BF, 4, GW, model),
            v(F32, 2, SEQ + 8, 2 * GW), v(F32, SEQ, 2 * GW), v(BF, model, SEQ), v(BF, 4, SEQ, GW), v(BF, CH, 128, GW),
            v(BF, SEQ, 2 * GW), v(BF, 4, 2, GW, GW), v(BF, 4, GW, GW), v(BF, 3, 3, GW, GW), v(F32, GW, GW),
            v(BF, *small), v(BF, 4, 4, *small), v(BF, 4, depth, 256), v(F32, SEQ + 8, 256),
            v(F32, SEQ, 128), v(F32, SEQ, 128), v(F32, SEQ, 128), v(F32, CH, L),
            v(BF, SEQ, 256), v(BF, CH, 256, L), v(F32, CH, L, L), v(F32, 2, SEQ, 128), v(F32, 4, CH, 8, L),
            v(F32, 4, 8, GW), v(F32, 8, 128), v(F32, 8, 256), v(BF, 64, model), v(F32, 8, model), v(F32, 4, 8, GW),
            v(F32, 128, GW),
            v(BF, 4, *part), v(BF, 3, *part), v(BF, 3, *part), v(BF, *part),
            v(BF, 3, 4 * SMALL, GW), v(BF, 3, *small), v(BF, 4, *small), v(BF, *small),
            v(BF, 4, 16, GW), v(BF, 7, 16, GW), v(BF, 16, GW),
            v(BF, SEQ, 128), v(BF, SEQ, 256), v(F32, 4, 8, GW), v(F32, 8, 128), v(F32, 8, 256), v(F32, 128, GW),
            v(F32, CH, L, L), v(F32, SEQ, 256),
            pltpu.SemaphoreType.DMA((144,)),
            pltpu.SemaphoreType.DMA((3, 4, 4)),
            pltpu.SemaphoreType.DMA((7,)),
            pltpu.SemaphoreType.DMA((6,)),
            pltpu.SemaphoreType.DMA((4,)),
            pltpu.SemaphoreType.DMA((19, 4)),
            pltpu.SemaphoreType.DMA((5,)),
            pltpu.SemaphoreType.DMA((4,)),
            pltpu.SemaphoreType.DMA((7,)),
            pltpu.SemaphoreType.DMA((16,)),
            pltpu.SemaphoreType.DMA((4,)),
            pltpu.SemaphoreType.DMA((4,)),
            pltpu.SemaphoreType.DMA((4,)),
            pltpu.SemaphoreType.DMA((8,)),
            pltpu.SemaphoreType.DMA((3,)),
            pltpu.SemaphoreType.DMA((5,)),
            pltpu.SemaphoreType.REGULAR,
            pltpu.SemaphoreType.REGULAR,
            pltpu.SemaphoreType.REGULAR,
            pltpu.SemaphoreType.REGULAR,
        ],
        compiler_params=pltpu.CompilerParams(vmem_limit_bytes=VMEM_LIMIT, collective_id=1, has_side_effects=True),
        name="whole_block",
    )(hidden, *args)


def on_device(fsdp, halves, hidden_in, norm_gain, in_gate, in_inner, in_state, in_step, conv_inner, conv_inner_shift,
              conv_state, conv_state_shift, step_offset, log_rate, skip_gain, inner_gain, out_weight, segment_ids,
              grad_out):
    both = ("fsdp", "zz")
    depth, width = in_gate.shape
    model = depth * fsdp
    inner = width * halves
    heads_dev = in_step.shape[1]
    heads = heads_dev * halves
    heads_all = 2 * heads
    unit = conv_inner.shape[2] * fsdp
    inner_all = 2 * inner
    core = lax.axis_index("core")
    zz = lax.axis_index("zz")
    rows = hidden_in.shape[0]

    def swap(x):
        return lax.ppermute(x, "core", [(0, 1), (1, 0)])

    def both_cores(own, other):
        return jnp.where(core == 0, jnp.concatenate([own, other], 0), jnp.concatenate([other, own], 0))

    small = [norm_gain, in_step, conv_inner, conv_inner_shift, conv_state, conv_state_shift, step_offset, log_rate,
             skip_gain, inner_gain]
    flat = jnp.concatenate([v.reshape(-1) for v in small])
    got = lax.all_gather(flat, both, axis=0).reshape(fsdp, halves, -1)
    parts = []
    at = 0
    for v in small:
        parts.append(got[:, :, at : at + v.size].reshape((fsdp, halves) + v.shape))
        at += v.size
    gain_outer = parts[0][:, 0].reshape(model).astype(F32)
    step_cols = parts[1].transpose(0, 2, 1, 3).reshape(model, heads)
    conv_in = parts[2].transpose(2, 1, 3, 0, 4).reshape(K, inner).astype(F32)
    shift_in = parts[3].transpose(1, 2, 0, 3).reshape(1, inner).astype(F32)
    conv_st = parts[4][:, 0].transpose(1, 0, 2).reshape(K, -1).astype(F32)
    shift_st = parts[5][:, 0].reshape(1, -1).astype(F32)
    gain_in = parts[9].transpose(1, 2, 0, 3).reshape(1, inner).astype(F32)

    def my_heads(v):
        return v.reshape(halves, 2, heads_dev)[:, core].reshape(heads).astype(F32)

    offset = my_heads(parts[6][:, 0].reshape(heads_all))
    decay = -jnp.exp(my_heads(parts[7][:, 0].reshape(heads_all)))
    skip = my_heads(parts[8][:, 0].reshape(heads_all))
    state_cols = lax.all_gather(in_state, "fsdp", axis=0, tiled=True)

    def columns(w):
        return lax.all_gather(w, both, axis=0).reshape(fsdp, halves, depth, width).transpose(0, 2, 1, 3).reshape(model, inner)

    inner_cols = columns(in_inner)
    gate_cols = columns(in_gate)
    out_rows = lax.all_gather(out_weight, both, axis=0).reshape(fsdp, halves, width, depth).transpose(1, 2, 0, 3).reshape(inner, model)

    par = jnp.concatenate([conv_in, shift_in, jnp.repeat(skip, unit)[None], gain_in, jnp.zeros((1, inner), F32)], 0)
    convst = jnp.concatenate([conv_st, shift_st, jnp.zeros((3, 256), F32)], 0)
    head = jnp.pad(jnp.stack([offset, decay]), ((0, 6), (0, 128 - heads)))
    decay_g = jnp.pad(decay.reshape(heads // GH, 1, GH), ((0, 0), (0, 7), (0, 128 - GH)))

    docs = lax.dynamic_slice_in_dim(segment_ids, zz * SEQ, SEQ)
    blocks = docs.reshape(CH, L)
    prior = jnp.concatenate([jnp.full((1,), -1, docs.dtype), blocks[:-1, -1]])
    masks = [docs, (blocks == prior[:, None]).reshape(SEQ), (blocks == blocks[:, -1:]).reshape(SEQ)]
    for k in range(1, K):
        masks.append(jnp.concatenate([jnp.zeros((k,), bool), docs[k:] == docs[:-k]]))
    for k in range(1, K):
        masks.append(jnp.concatenate([docs[k:] == docs[:-k], jnp.zeros((k,), bool)]))
    tok = jnp.pad(jnp.stack([m.astype(F32) for m in masks], 1), ((0, 0), (0, 128 - len(masks))))
    row = jnp.broadcast_to(blocks.astype(F32)[:, None, :], (CH, 8, L))

    hidden_all = both_cores(hidden_in, swap(hidden_in)).astype(F32)
    cot_all = both_cores(grad_out, swap(grad_out))
    inv_rms = lax.rsqrt(jnp.mean(hidden_all * hidden_all, -1, keepdims=True) + EPSILON)
    normed = (hidden_all * inv_rms * gain_outer).astype(BF)
    small_cols = jnp.concatenate([state_cols, jnp.pad(step_cols, ((0, 0), (0, 128 - heads)))], 1)
    pre_small = mm(normed, small_cols)
    state_pre = pre_small[:, :256]
    step_pre = pre_small[:, 256:]
    inner_pre = mm(normed, inner_cols)
    gate_pre = mm(normed, gate_cols)
    bc, bct, gs, pack, cumt = prep(state_pre, step_pre, tok, row, convst, head)
    gated, states, ss = fwd(inner_pre, gate_pre, par, tok, bc, bct, gs, pack, cumt)
    ss_own = jnp.sum(ss, -1)
    squares = ss_own + swap(ss_own)
    inner_inv = lax.rsqrt(squares / inner_all + EPSILON)[:, None]
    normed_inner = (gated * inner_inv * gain_in).astype(BF)
    mixed = mm(normed_inner, out_rows)

    def to_own(x):
        own = lax.dynamic_slice_in_dim(x, core * rows, rows)
        other = lax.dynamic_slice_in_dim(x, (1 - core) * rows, rows)
        return own + swap(other.astype(BF)).astype(F32)

    layer_out = (hidden_in.astype(F32) + to_own(mixed)).astype(BF)
    grad_out_part = mm(normed_inner, cot_all, ((0,), (0,)))
    d_inner = mm(cot_all, out_rows, ((1,), (1,)))
    grad_gain_in = jnp.sum(d_inner * gated * inner_inv, 0)
    prod_own = jnp.sum(gated * d_inner * gain_in, -1)
    products = prod_own + swap(prod_own)
    inv_pack = jnp.pad(
        jnp.stack([inner_inv[:, 0], inner_inv[:, 0] ** 3 * products / inner_all], 1), ((0, 0), (0, 126))
    )
    d_gate, d_pre, d_step, d_state, pgrad, hgrad, sgrad = bwd(
        inner_pre, gate_pre, d_inner, par, tok, inv_pack, bc, bct, gs, pack, cumt, states, decay_g, state_pre, convst, row
    )
    d_step = d_step.astype(BF)
    d_small = jnp.concatenate([d_state, d_step], 1)
    d_normed = to_own(
        mm(d_gate, gate_cols, ((1,), (1,))) + mm(d_pre, inner_cols, ((1,), (1,))) + mm(d_small, small_cols, ((1,), (1,)))
    )
    hidden = hidden_in.astype(F32)
    inv_own = lax.dynamic_slice_in_dim(inv_rms, core * rows, rows)
    grad_gain_outer = jnp.sum(d_normed * hidden * inv_own, 0)
    weighted_back = d_normed * gain_outer
    d_hidden = inv_own * weighted_back - hidden * inv_own**3 * jnp.mean(hidden * weighted_back, -1, keepdims=True)
    grad_hidden = (grad_out.astype(F32) + d_hidden).astype(BF)

    def scatter_columns(g):
        g = g.astype(BF).reshape(fsdp, depth, halves, width).transpose(0, 2, 1, 3).reshape(fsdp * halves, depth, width)
        return lax.psum_scatter(g, both, scatter_dimension=0).astype(F32)

    grad_gate = scatter_columns(mm(normed, d_gate, ((0,), (0,))))
    grad_inner = scatter_columns(mm(normed, d_pre, ((0,), (0,))))
    grad_small = mm(normed, d_small, ((0,), (0,)))
    grad_out_weight = grad_out_part.astype(BF).reshape(halves, width, fsdp, depth).transpose(2, 0, 1, 3)
    grad_out_weight = lax.psum_scatter(
        grad_out_weight.reshape(fsdp * halves, width, depth), both, scatter_dimension=0
    ).astype(F32)
    grad_state = lax.psum_scatter(grad_small[:, :256].astype(BF), "fsdp", scatter_dimension=0, tiled=True)
    grad_state = lax.psum(grad_state, ("zz", "core")).astype(F32)

    own_heads = [
        grad_small[:, 256 : 256 + heads].reshape(fsdp, depth, halves, heads_dev).transpose(0, 2, 1, 3),
        pgrad[:K].reshape(K, halves, heads_dev, fsdp, -1).transpose(3, 1, 0, 2, 4),
        pgrad[K].reshape(halves, heads_dev, fsdp, -1).transpose(2, 0, 1, 3),
        grad_gain_in.reshape(halves, heads_dev, fsdp, -1).transpose(2, 0, 1, 3),
    ]
    sizes = [v.shape[2:] for v in own_heads]
    stacked = jnp.concatenate([v.reshape(fsdp * halves, -1) for v in own_heads], 1)
    mine = lax.psum_scatter(stacked, both, scatter_dimension=0)
    outs = []
    at = 0
    for s in sizes:
        n = 1
        for d in s:
            n *= d
        outs.append(mine[at : at + n].reshape(s))
        at += n
    grad_step, grad_conv_in, grad_conv_in_shift, grad_gain_inner = outs

    def place(v):
        v = v.reshape(halves, 1, heads_dev)
        zero = jnp.zeros_like(v)
        return jnp.where(core == 0, jnp.concatenate([v, zero], 1), jnp.concatenate([zero, v], 1)).reshape(heads_all)

    skip_sum = jnp.sum(pgrad[P_SKIP].reshape(heads, unit), 1)
    shared = [grad_gain_outer.reshape(fsdp, depth), sgrad[:K].reshape(K, fsdp, -1).transpose(1, 0, 2), sgrad[K].reshape(fsdp, -1)]
    shared += [place(v).reshape(fsdp, -1) for v in (hgrad[1, :heads], hgrad[0, :heads], skip_sum)]
    sizes = [v.shape[1:] for v in shared]
    stacked = jnp.concatenate([v.reshape(fsdp, -1) for v in shared], 1)
    mine = lax.psum(stacked, ("fsdp", "zz", "core"))
    mine = lax.dynamic_index_in_dim(mine, lax.axis_index("fsdp"), keepdims=False)
    outs = []
    at = 0
    for s in sizes:
        n = 1
        for d in s:
            n *= d
        outs.append(mine[at : at + n].reshape(s))
        at += n
    grad_norm_gain, grad_conv_st, grad_conv_st_shift, grad_offset, grad_rate, grad_skip = outs
    return (layer_out, grad_hidden, grad_norm_gain, grad_gate, grad_inner, grad_state, grad_step, grad_conv_in,
            grad_conv_in_shift, grad_conv_st, grad_conv_st_shift, grad_offset, grad_rate, grad_skip, grad_gain_inner,
            grad_out_weight)


def on_chip(hidden_in, norm_gain, in_gate, in_inner, in_state, in_step, conv_inner, conv_inner_shift, conv_state,
            conv_state_shift, step_offset, log_rate, skip_gain, inner_gain, out_weight, segment_ids, grad_out):
    depth = in_gate.shape[0]
    model = depth * 4
    f = lax.axis_index("fsdp")
    core = lax.axis_index("core")

    vec = [jnp.pad(v, (0, GW - v.shape[0])) for v in (norm_gain, conv_state_shift, step_offset, log_rate, skip_gain)]
    vec = jnp.concatenate(vec + [jnp.zeros((3 * GW,), BF)]).reshape(8, GW).astype(F32)
    result = block_call(model, hidden_in, grad_out, in_inner, in_gate, out_weight, in_state, vec, in_step, conv_inner,
                        conv_inner_shift, inner_gain, conv_state, segment_ids.reshape(-1, L))
    layer_out, grad_hidden, g_inner, g_gate, g_out, g_state, own, other = result[:2] + result[6:]
    shared = own[23:] + other[23:]

    def my_part(v):
        r, n = v.shape
        return lax.dynamic_index_in_dim(v.reshape(r, n // (4 * 16), 4, 16), f, 2, False)

    def heads(r):
        mine = jnp.where(core == 0, own[r], other[r])[:64].reshape(4, 16)[:, :GH]
        theirs = jnp.where(core == 0, other[r], own[r])[:64].reshape(4, 16)[:, :GH]
        every = jnp.concatenate([mine, theirs], 1)
        return lax.dynamic_index_in_dim(every, f, 0, False)

    conv = my_part(own[16:20])
    grad_state_conv = lax.dynamic_slice_in_dim(shared[1:6, :256], f * 64, 64, 1)
    return (
        layer_out, grad_hidden, shared[0], g_gate, g_inner, g_state, own[:GH].T, conv, my_part(own[20:21])[0],
        grad_state_conv[:4], grad_state_conv[4], heads(30), heads(29), heads(31), my_part(own[21:22])[0], g_out,
    )


def solution(mesh):
    fsdp = mesh.shape["fsdp"]
    halves = mesh.shape["tensor"] // 2
    fine = jax.sharding.Mesh(mesh.devices.reshape(fsdp, halves, 2), ("fsdp", "zz", "core"))
    tensor = ("zz", "core")
    tokens = P(("fsdp", "zz", "core"), None)
    grid = P("fsdp", tensor)
    heads = P(tensor, "fsdp")
    return jax.shard_map(
        on_chip if (fsdp, halves) == (4, 4) else functools.partial(on_device, fsdp, halves),
        mesh=fine,
        in_specs=(
            tokens, P("fsdp"), grid, grid, P("fsdp", None), grid, P(None, tensor, "fsdp"), heads, P(None, "fsdp"),
            P("fsdp"), P("fsdp"), P("fsdp"), P("fsdp"), heads, heads, P("fsdp"), tokens,
        ),
        out_specs=(
            tokens, tokens, P("fsdp"), grid, grid, P("fsdp", None), grid, P(None, tensor, "fsdp"), heads,
            P(None, "fsdp"), P("fsdp"), P("fsdp"), P("fsdp"), P("fsdp"), heads, heads,
        ),
        check_vma=False,
    )
```

```python
import functools

import jax
import jax.numpy as jnp
from jax import lax
from jax.sharding import PartitionSpec as P
from jax.experimental import pallas as pl
from jax.experimental.pallas import tpu as pltpu

SEQ = 1024
L = 128
CH = SEQ // L
K = 4
GH = 6
GW = 384
EPSILON = 1e-05
LOG2E = 1.4426950408889634
F32 = jnp.float32
BF = jnp.bfloat16
ST, CU, EE, FF, SG = 0, 8, 16, 24, 32


def mm(a, b, dims=((1,), (0,))):
    return lax.dot_general(a, b, (dims, ((), ())), preferred_element_type=F32)


def split2(x):
    hi = x.astype(BF)
    return hi, (x - hi.astype(F32)).astype(BF)


def split3(x):
    hi = x.astype(BF)
    rest = x - hi.astype(F32)
    mid = rest.astype(BF)
    return hi, mid, (rest - mid.astype(F32)).astype(BF)


def sigmoid(v):
    return 1.0 / (1.0 + jnp.exp(-v))


def back_conv_input(window, k):
    return window[8 - k : 8 - k + L]


def prep_body(state_ref, step_ref, tok_ref, row_ref, convst_ref, head_ref,
              bc_ref, bct_ref, g_ref, pack_ref, cumt_ref, pad_ref):
    pad_ref[pl.ds(0, 8), :] = jnp.zeros((8, 256), F32)
    pad_ref[pl.ds(8, SEQ), :] = state_ref[...]
    lane = lax.broadcasted_iota(jnp.int32, (L, L), 1)
    sub = lax.broadcasted_iota(jnp.int32, (L, L), 0)
    tri = (sub >= lane).astype(BF)
    offset = head_ref[0:1, :]
    decay = head_ref[1:2, :]
    taps = [convst_ref[k : k + 1, :] for k in range(K)]
    shift = convst_ref[K : K + 1, :]

    def chunk(c, _):
        base = pl.multiple_of(c * L, L)
        rows = pl.ds(base, L)
        tok = tok_ref[rows, :]
        window = pad_ref[pl.ds(base, L + 8), :]
        total = shift + taps[K - 1] * back_conv_input(window, 0)
        for k in range(1, K):
            total = total + taps[K - 1 - k] * (back_conv_input(window, k) * tok[:, 2 + k : 3 + k])
        act = total * sigmoid(total)
        low = act.astype(BF)
        bc_ref[rows, :] = low
        bct_ref[c] = jnp.concatenate([act[:, :128].T, act[:, 128:].T], 0).astype(BF)
        scores = mm(low[:, 128:], low[:, :128], ((1,), (1,)))
        same = (tok[:, 0:1] == row_ref[c][0:1, :]) & (sub >= lane)
        g_ref[c] = jnp.where(same, scores, 0.0)
        v = step_ref[rows, :] + offset
        steps = jnp.maximum(v, 0.0) + jnp.log1p(jnp.exp(-jnp.abs(v)))
        logs = steps * (decay * LOG2E)
        hi, mid, lo = split3(logs)
        cum = mm(tri, hi) + mm(tri, mid) + mm(tri, lo)
        last = cum[L - 1 : L, :]
        enter = jnp.exp2(cum) * tok[:, 1:2]
        leave = jnp.exp2(last - cum) * tok[:, 2:3]
        sig = sigmoid(v)
        cumt = cum.T
        zeros = jnp.zeros((L, 2), F32)
        for g in range(4):
            part = slice(GH * g, GH * g + GH)
            pieces = []
            for values in (steps, cum, enter, leave, sig):
                pieces += [values[:, part], zeros]
            pieces.append(jnp.zeros((L, 88), F32))
            pack_ref[g, rows, :] = jnp.concatenate(pieces, 1)
            cumt_ref[g, c] = jnp.concatenate([cumt[part, :], jnp.zeros((2, L), F32)], 0)
        return 0

    lax.fori_loop(0, CH, chunk, 0)


def vm(*shape):
    return pl.BlockSpec(memory_space=pltpu.VMEM)


def prep(state_pre, step_pre, tok, row, convst, head):
    return pl.pallas_call(
        prep_body,
        out_shape=(
            jax.ShapeDtypeStruct((SEQ, 256), BF),
            jax.ShapeDtypeStruct((CH, 256, L), BF),
            jax.ShapeDtypeStruct((CH, L, L), F32),
            jax.ShapeDtypeStruct((4, SEQ, 128), F32),
            jax.ShapeDtypeStruct((4, CH, 8, L), F32),
        ),
        in_specs=[vm()] * 6,
        out_specs=[vm()] * 5,
        scratch_shapes=[pltpu.VMEM((SEQ + 8, 256), F32)],
        compiler_params=pltpu.CompilerParams(vmem_limit_bytes=56 * 2**20),
        name="prep",
    )(state_pre, step_pre, tok, row, convst, head)


def pair_lanes(pack, first, q):
    lane = lax.broadcasted_iota(jnp.int32, (pack.shape[0], 128), 1)
    a = pack[:, first + 2 * q : first + 2 * q + 1]
    b = pack[:, first + 2 * q + 1 : first + 2 * q + 2]
    return jnp.where(lane < 64, a, b)


def spread(pack, first):
    return jnp.concatenate([pair_lanes(pack, first, q) for q in range(3)], 1)


def block_diag(x):
    lane = lax.broadcasted_iota(jnp.int32, x.shape, 1)
    zero = jnp.zeros_like(x)
    return jnp.concatenate([jnp.where(lane < 64, x, zero), jnp.where(lane < 64, zero, x)], 0)


def decay_kernel(pack, cumt, h):
    return jnp.exp2(jnp.minimum(pack[:, CU + h : CU + h + 1] - cumt[h : h + 1, :], 0.0))


def conv_of(window, tok, par):
    total = par[K : K + 1, :] + par[K - 1 : K, :] * back_conv_input(window, 0)
    for k in range(1, K):
        total = total + par[K - 1 - k : K - k, :] * (back_conv_input(window, k) * tok[:, 2 + k : 3 + k])
    return total


P_SHIFT, P_SKIP, P_GAIN = 4, 5, 6


def fwd_body(inner_ref, gate_ref, par_ref, tok_ref, bc_ref, bct_ref, g_ref, pack_ref, cumt_ref,
             gated_ref, states_ref, ss_ref, pad_ref, st_ref):
    pad_ref[pl.ds(0, 8), :] = jnp.zeros((8, GW), F32)
    pad_ref[pl.ds(8, SEQ), :] = inner_ref[...]
    st_ref[...] = jnp.zeros_like(st_ref)
    par = par_ref[...]

    @pl.when(pl.program_id(0) == 0)
    def _():
        ss_ref[...] = jnp.zeros_like(ss_ref)

    def chunk(c, _):
        base = pl.multiple_of(c * L, L)
        rows = pl.ds(base, L)
        tok = tok_ref[rows, :]
        u = conv_of(pad_ref[pl.ds(base, L + 8), :], tok, par)
        act = u * sigmoid(u)
        pack = pack_ref[0, rows, :]
        cumt = cumt_ref[0, c]
        g = g_ref[c]
        weighted = act * spread(pack, ST)
        low = weighted.astype(BF)
        enter = spread(pack, EE)
        state = st_ref[...]
        low_state = state.astype(BF)
        states_ref[0, c] = low_state
        y = mm(bc_ref[rows, 128:], low_state) * enter
        locals_ = []
        for q in range(3):
            kernels = [(g * decay_kernel(pack, cumt, 2 * q + e)).astype(BF) for e in range(2)]
            locals_.append(mm(jnp.concatenate(kernels, 1), block_diag(low[:, 128 * q : 128 * q + 128])))
        y = y + jnp.concatenate(locals_, 1)
        out = weighted * spread(pack, FF)
        st_ref[...] = enter[L - 1 : L, :] * state + mm(bct_ref[c, pl.ds(0, 128), :], out.astype(BF))
        ssd = y + par[P_SKIP : P_SKIP + 1, :] * act
        gate = gate_ref[rows, :]
        gated = ssd * (gate * sigmoid(gate))
        gated_ref[rows, :] = gated
        sq = gated * gated
        ss_ref[rows, :] += sq[:, :128] + sq[:, 128:256] + sq[:, 256:]
        return 0

    lax.fori_loop(0, CH, chunk, 0)


def whole_spec(shape):
    return pl.BlockSpec(shape, lambda g: (0,) * len(shape))


def fwd(inner_pre, gate_pre, par, tok, bc, bct, gs, pack, cumt):
    cols = pl.BlockSpec((SEQ, GW), lambda g: (0, g))
    return pl.pallas_call(
        fwd_body,
        grid=(4,),
        out_shape=(
            jax.ShapeDtypeStruct((SEQ, 4 * GW), F32),
            jax.ShapeDtypeStruct((4, CH, 128, GW), BF),
            jax.ShapeDtypeStruct((SEQ, 128), F32),
        ),
        in_specs=[
            cols, cols, pl.BlockSpec((8, GW), lambda g: (0, g)),
            whole_spec((SEQ, 128)), whole_spec((SEQ, 256)), whole_spec((CH, 256, L)), whole_spec((CH, L, L)),
            pl.BlockSpec((1, SEQ, 128), lambda g: (g, 0, 0)),
            pl.BlockSpec((1, CH, 8, L), lambda g: (g, 0, 0, 0)),
        ],
        out_specs=(
            cols,
            pl.BlockSpec((1, CH, 128, GW), lambda g: (g, 0, 0, 0)),
            whole_spec((SEQ, 128)),
        ),
        scratch_shapes=[pltpu.VMEM((SEQ + 8, GW), F32), pltpu.VMEM((128, GW), F32)],
        compiler_params=pltpu.CompilerParams(vmem_limit_bytes=56 * 2**20),
        name="mixer_forward",
    )(inner_pre, gate_pre, par, tok, bc, bct, gs, pack, cumt)


def bwd_body(inner_ref, gate_ref, dinner_ref, par_ref, tok_ref, inv_ref, bc_ref, bct_ref, g_ref, pack_ref,
             cumt_ref, states_ref, decay_ref, state_pre_ref, convst_ref, row_ref,
             dgate_ref, dpre_ref, dstep_ref, dstate_ref, pgrad_ref, hgrad_ref, sgrad_ref,
             pad_ref, rt_ref, dg_ref, dbc_ref, spad_ref):
    group = pl.program_id(0)
    pad_ref[pl.ds(0, 8), :] = jnp.zeros((8, GW), F32)
    pad_ref[pl.ds(8, SEQ), :] = inner_ref[...]
    rt_ref[...] = jnp.zeros_like(rt_ref)
    pgrad_ref[...] = jnp.zeros_like(pgrad_ref)
    par = par_ref[...]
    decay = decay_ref[0]

    @pl.when(group == 0)
    def _():
        dg_ref[...] = jnp.zeros_like(dg_ref)
        dbc_ref[...] = jnp.zeros_like(dbc_ref)
        dstep_ref[...] = jnp.zeros_like(dstep_ref)
        hgrad_ref[...] = jnp.zeros_like(hgrad_ref)

    lane = lax.broadcasted_iota(jnp.int32, (L, L), 1)
    sub = lax.broadcasted_iota(jnp.int32, (L, L), 0)
    upper = (sub <= lane).astype(BF)
    per_head = (lax.broadcasted_iota(jnp.int32, (GW, 128), 0) >> 6
                == lax.broadcasted_iota(jnp.int32, (GW, 128), 1)).astype(BF)

    def head_sums(x):
        hi, lo = split2(x)
        return mm(hi, per_head) + mm(lo, per_head)

    def chunk(step, later):
        c = CH - 1 - step
        base = pl.multiple_of(c * L, L)
        rows = pl.ds(base, L)
        tok = tok_ref[rows, :]
        window = pad_ref[pl.ds(base, L + 8), :]
        u = conv_of(window, tok, par)
        su = sigmoid(u)
        act = u * su
        pack = pack_ref[0, rows, :]
        cumt = cumt_ref[0, c]
        g = g_ref[c]
        steps = spread(pack, ST)
        enter = spread(pack, EE)
        leave = spread(pack, FF)
        weighted = act * steps
        low = weighted.astype(BF)
        low_state = states_ref[0, c]
        bmat = bc_ref[rows, :128]
        cmat = bc_ref[rows, 128:]
        diags = [block_diag(low[:, 128 * q : 128 * q + 128]) for q in range(3)]
        decays = [decay_kernel(pack, cumt, h) for h in range(GH)]
        kernels = [jnp.concatenate([(g * decays[2 * q + e]).astype(BF) for e in range(2)], 1) for q in range(3)]
        y = mm(cmat, low_state) * enter + jnp.concatenate([mm(kernels[q], diags[q]) for q in range(3)], 1)
        skip = par[P_SKIP : P_SKIP + 1, :]
        ssd = y + skip * act
        gate = gate_ref[rows, :]
        sg = sigmoid(gate)
        silu = gate * sg
        scaled = dinner_ref[rows, :] * par[P_GAIN : P_GAIN + 1, :]
        inv = inv_ref[rows, :]
        d_gated = inv[:, 0:1] * scaled - (ssd * silu) * inv[:, 1:2]
        dy = d_gated * silu
        dgate_ref[rows, :] = (d_gated * ssd * sg * (1.0 + gate * (1.0 - sg))).astype(BF)
        dy_low = dy.astype(BF)
        dy_in = (dy * enter).astype(BF)
        rt = rt_ref[...]
        rt_low = rt.astype(BF)
        carried = mm(bmat, rt_low) * leave
        pieces = []
        d_scores = jnp.zeros((L, L), F32)
        for q in range(3):
            dq = dy_low[:, 128 * q : 128 * q + 128]
            dm = mm(dq, diags[q], ((1,), (1,)))
            d_scores = d_scores + dm[:, :L] * decays[2 * q] + dm[:, L:] * decays[2 * q + 1]
            both = mm(kernels[q], dq, ((0,), (0,)))
            pieces.append(jnp.where(lane < 64, both[:L], both[L:]))
        d_weighted = jnp.concatenate(pieces, 1) + carried
        dg_ref[c] += d_scores
        out = (weighted * leave).astype(BF)
        dbc_ref[rows, 128:] += mm(dy_in, low_state, ((1,), (1,)))
        dbc_ref[rows, :128] += mm(out, rt_low, ((1,), (1,)))
        keep = enter[L - 1 : L, :]
        low32 = low.astype(F32)
        d_cum = head_sums(dy_low.astype(F32) * y - low32 * d_weighted)
        at_end = jnp.sum(low32 * carried, 0, keepdims=True) + keep * jnp.sum(rt * low_state.astype(F32), 0, keepdims=True)
        d_last = head_sums(jnp.concatenate([at_end, jnp.zeros((7, GW), F32)], 0))[0:1, :]
        hi, mid, lo = split3(d_cum)
        d_log = mm(upper, hi) + mm(upper, mid) + mm(upper, lo) + d_last
        rt_ref[...] = keep * rt + mm(bct_ref[c, pl.ds(128, 128), :], dy_in)
        d_step = head_sums(act * d_weighted) + decay[0:1, :] * d_log
        heads = lane < GH
        d_step_pre = jnp.where(heads, d_step * jnp.roll(pack, -SG, 1), 0.0)
        dstep_ref[rows, :] += pltpu.roll(d_step_pre, GH * group, 1)
        rate = jnp.sum(jnp.where(heads, pack, 0.0) * d_log, 0, keepdims=True) * decay[0:1, :]
        offs = jnp.sum(d_step_pre, 0, keepdims=True)
        hgrad_ref[0:1, :] += pltpu.roll(jnp.concatenate([rate, jnp.zeros((7, 128), F32)], 0), GH * group, 1)[0:1]
        hgrad_ref[1:2, :] += pltpu.roll(jnp.concatenate([offs, jnp.zeros((7, 128), F32)], 0), GH * group, 1)[0:1]
        d_act = skip * dy + steps * d_weighted
        du = d_act * su * (1.0 + u * (1.0 - su))
        pgrad_ref[K : K + 1, :] += jnp.sum(du, 0, keepdims=True)
        pgrad_ref[P_SKIP : P_SKIP + 1, :] += jnp.sum(dy * act, 0, keepdims=True)
        for k in range(K):
            moved = back_conv_input(window, k)
            if k:
                moved = moved * tok[:, 2 + k : 3 + k]
            pgrad_ref[K - 1 - k : K - k, :] += jnp.sum(du * moved, 0, keepdims=True)
        ahead = jnp.concatenate([du, later], 0)
        d_pre = par[K - 1 : K, :] * du
        for k in range(1, K):
            d_pre = d_pre + par[K - 1 - k : K - k, :] * (ahead[k : k + L] * tok[:, 5 + k : 6 + k])
        dpre_ref[rows, :] = d_pre.astype(BF)
        return du[:8]

    lax.fori_loop(0, CH, chunk, jnp.zeros((8, GW), F32))

    @pl.when(group == pl.num_programs(0) - 1)
    def _():
        spad_ref[pl.ds(0, 8), :] = jnp.zeros((8, 256), F32)
        spad_ref[pl.ds(8, SEQ), :] = state_pre_ref[...]
        sgrad_ref[...] = jnp.zeros_like(sgrad_ref)
        cst = convst_ref[...]

        def last(step, later):
            c = CH - 1 - step
            base = pl.multiple_of(c * L, L)
            rows = pl.ds(base, L)
            tok = tok_ref[rows, :]
            same = (tok[:, 0:1] == row_ref[c][0:1, :]) & (sub >= lane)
            ds = jnp.where(same, dg_ref[c], 0.0).astype(BF)
            d_c = dbc_ref[rows, 128:] + mm(ds, bc_ref[rows, :128])
            d_b = dbc_ref[rows, :128] + mm(ds, bc_ref[rows, 128:], ((0,), (0,)))
            window = spad_ref[pl.ds(base, L + 8), :]
            w = conv_of(window, tok, cst)
            sw = sigmoid(w)
            dw = jnp.concatenate([d_b, d_c], 1) * (sw * (1.0 + w * (1.0 - sw)))
            sgrad_ref[K : K + 1, :] += jnp.sum(dw, 0, keepdims=True)
            for k in range(K):
                moved = back_conv_input(window, k)
                if k:
                    moved = moved * tok[:, 2 + k : 3 + k]
                sgrad_ref[K - 1 - k : K - k, :] += jnp.sum(dw * moved, 0, keepdims=True)
            ahead = jnp.concatenate([dw, later], 0)
            d_pre = cst[K - 1 : K, :] * dw
            for k in range(1, K):
                d_pre = d_pre + cst[K - 1 - k : K - k, :] * (ahead[k : k + L] * tok[:, 5 + k : 6 + k])
            dstate_ref[rows, :] = d_pre.astype(BF)
            return dw[:8]

        lax.fori_loop(0, CH, last, jnp.zeros((8, 256), F32))


def bwd(inner_pre, gate_pre, d_inner, par, tok, inv, bc, bct, gs, pack, cumt, states, decay, state_pre, convst, row):
    cols = pl.BlockSpec((SEQ, GW), lambda g: (0, g))
    pcol = pl.BlockSpec((8, GW), lambda g: (0, g))
    return pl.pallas_call(
        bwd_body,
        grid=(4,),
        out_shape=(
            jax.ShapeDtypeStruct((SEQ, 4 * GW), BF),
            jax.ShapeDtypeStruct((SEQ, 4 * GW), BF),
            jax.ShapeDtypeStruct((SEQ, 128), F32),
            jax.ShapeDtypeStruct((SEQ, 256), BF),
            jax.ShapeDtypeStruct((8, 4 * GW), F32),
            jax.ShapeDtypeStruct((8, 128), F32),
            jax.ShapeDtypeStruct((8, 256), F32),
        ),
        in_specs=[
            cols, cols, cols, pcol,
            whole_spec((SEQ, 128)), whole_spec((SEQ, 128)), whole_spec((SEQ, 256)), whole_spec((CH, 256, L)),
            whole_spec((CH, L, L)),
            pl.BlockSpec((1, SEQ, 128), lambda g: (g, 0, 0)),
            pl.BlockSpec((1, CH, 8, L), lambda g: (g, 0, 0, 0)),
            pl.BlockSpec((1, CH, 128, GW), lambda g: (g, 0, 0, 0)),
            pl.BlockSpec((1, 8, 128), lambda g: (g, 0, 0)),
            whole_spec((SEQ, 256)), whole_spec((8, 256)), whole_spec((CH, 8, L)),
        ],
        out_specs=(
            cols, cols, whole_spec((SEQ, 128)), whole_spec((SEQ, 256)), pcol, whole_spec((8, 128)), whole_spec((8, 256)),
        ),
        scratch_shapes=[
            pltpu.VMEM((SEQ + 8, GW), F32),
            pltpu.VMEM((128, GW), F32),
            pltpu.VMEM((CH, L, L), F32),
            pltpu.VMEM((SEQ, 256), F32),
            pltpu.VMEM((SEQ + 8, 256), F32),
        ],
        compiler_params=pltpu.CompilerParams(vmem_limit_bytes=56 * 2**20),
        name="mixer_backward",
    )(inner_pre, gate_pre, d_inner, par, tok, inv, bc, bct, gs, pack, cumt, states, decay, state_pre, convst, row)


def prep_chunks(state_ref, step_ref, tok_ref, row_ref, convst_ref, head_ref,
                bc_ref, bct_ref, g_ref, pack_ref, cumt_ref):
    lane = lax.broadcasted_iota(jnp.int32, (L, L), 1)
    sub = lax.broadcasted_iota(jnp.int32, (L, L), 0)
    tri = (sub >= lane).astype(BF)
    offset = head_ref[0:1, :]
    decay = head_ref[1:2, :]
    convst = convst_ref[...]

    def chunk(c, _):
        base = pl.multiple_of(c * L, L)
        rows = pl.ds(base, L)
        tok = tok_ref[rows, :]
        total = conv_of(state_ref[pl.ds(base, L + 8), :], tok, convst)
        act = total * sigmoid(total)
        low = act.astype(BF)
        bc_ref[rows, :] = low
        bct_ref[c] = jnp.concatenate([act[:, :128].T, act[:, 128:].T], 0).astype(BF)
        scores = mm(low[:, 128:], low[:, :128], ((1,), (1,)))
        same = (tok[:, 0:1] == row_ref[pl.ds(c, 1), :]) & (sub >= lane)
        g_ref[c] = jnp.where(same, scores, 0.0)
        v = step_ref[rows, :] + offset
        steps = jnp.maximum(v, 0.0) + jnp.log1p(jnp.exp(-jnp.abs(v)))
        logs = steps * (decay * LOG2E)
        hi, mid, lo = split3(logs)
        cum = mm(tri, hi) + mm(tri, mid) + mm(tri, lo)
        last = cum[L - 1 : L, :]
        enter = jnp.exp2(cum) * tok[:, 1:2]
        leave = jnp.exp2(last - cum) * tok[:, 2:3]
        sig = sigmoid(v)
        cumt = cum.T
        for g in range(4):
            cumt_ref[g, c] = cumt[16 * g : 16 * g + 8, :]
        for g in range(2):
            pieces = []
            for part in (slice(32 * g, 32 * g + 8), slice(32 * g + 16, 32 * g + 24)):
                pieces += [values[:, part] for values in (steps, cum, enter, leave, sig)] + [jnp.zeros((L, 24), F32)]
            pack_ref[g, rows, :] = jnp.concatenate(pieces, 1)
        return 0

    lax.fori_loop(0, CH, chunk, 0)


def spread_masks(tok):
    return [jnp.broadcast_to(tok[:, i : i + 1], (L, 128)) for i in range(3, 9)]


def pair_conv(window, masks, par):
    total = par[K : K + 1, :] + par[K - 1 : K, :] * back_conv_input(window, 0)
    moved = [back_conv_input(window, 0)]
    for k in range(1, K):
        moved.append(back_conv_input(window, k) * masks[k - 1])
        total = total + par[K - 1 - k : K - k, :] * moved[k]
    return total, moved


def fwd_chunks(group, tick, pre_ref, par_ref, tok_ref, bc_ref, bct_ref, g_ref, pack_ref, cumt_ref,
               gated_ref, states_ref, ss_ref, st_ref):
    st_ref[...] = jnp.zeros_like(st_ref)

    def chunk(c, _):
        tick(c)
        base = pl.multiple_of(c * L, L)
        rows = pl.ds(base, L)
        masks = spread_masks(tok_ref[rows, :])
        pack = pack_ref[rows, :]
        if group % 2:
            pack = pltpu.roll(pack, 64, 1)
        cumt = cumt_ref[c]
        g = g_ref[c]
        squares = jnp.zeros((L, 128), F32)
        for q in range(3):
            lanes = pl.ds(128 * q, 128)
            par = par_ref[:, lanes]
            u, _ = pair_conv(pre_ref[pl.ds(base, L + 8), lanes], masks, par)
            act = u * sigmoid(u)
            weighted = act * pair_lanes(pack, ST, q)
            kernels = [(g * decay_kernel(pack, cumt, 2 * q + e)).astype(BF) for e in range(2)]
            y = mm(jnp.concatenate(kernels, 1), block_diag(weighted.astype(BF)))
            enter = pair_lanes(pack, EE, q)
            state = st_ref[:, lanes]
            low_state = state.astype(BF)
            states_ref[c, :, lanes] = low_state
            y = y + mm(bc_ref[rows, 128:], low_state) * enter
            out = (weighted * pair_lanes(pack, FF, q)).astype(BF)
            st_ref[:, lanes] = enter[L - 1 : L, :] * state + mm(bct_ref[c, pl.ds(0, 128), :], out)
            ssd = y + par[P_SKIP : P_SKIP + 1, :] * act
            gate = pre_ref[pl.ds(base + 8, L), pl.ds(GW + 128 * q, 128)]
            gated = ssd * (gate * sigmoid(gate))
            gated_ref[rows, lanes] = gated.astype(BF)
            squares = squares + gated * gated
        ss_ref[rows, :] += squares
        return 0

    lax.fori_loop(0, CH, chunk, 0)


def bwd_chunks(group, z_k, tick, pre_ref, dinner_ref, par_ref, tok_ref, bc_ref, bct_ref, g_ref, pack_ref,
               cumt_ref, states_ref, hpar_ref, dcat_ref, dstep_ref, pgrad_ref, hgrad_ref, rt_ref, dg_ref, dbc_ref):
    rt_ref[...] = jnp.zeros_like(rt_ref)
    pgrad_ref[...] = jnp.zeros_like(pgrad_ref)
    decay = pltpu.roll(hpar_ref[...], (128 - 16 * group) % 128, 1)[1:2, :]
    lane = lax.broadcasted_iota(jnp.int32, (L, L), 1)
    sub = lax.broadcasted_iota(jnp.int32, (L, L), 0)
    upper = (sub <= lane).astype(BF)
    heads = lane < GH

    def chunk(step, later):
        tick(step)
        c = CH - 1 - step
        base = pl.multiple_of(c * L, L)
        rows = pl.ds(base, L)
        tok = tok_ref[rows, :]
        masks = spread_masks(tok)
        inv = jnp.broadcast_to(tok[:, T_INV : T_INV + 1], (L, 128))
        inv_back = jnp.broadcast_to(tok[:, T_BACK : T_BACK + 1], (L, 128))
        pack = pack_ref[rows, :]
        if group % 2:
            pack = pltpu.roll(pack, 64, 1)
        cumt = cumt_ref[c]
        g = g_ref[c]
        d_scores = jnp.zeros((L, L), F32)
        sums = jnp.zeros((3 * L + 16, 128), F32)
        d_c = dbc_ref[rows, 128:]
        d_b = dbc_ref[rows, :128]
        heads_of_pair = []
        for q in range(3):
            lanes = pl.ds(128 * q, 128)
            gate_lanes = pl.ds(GW + 128 * q, 128)
            par = par_ref[:, lanes]
            u, moved = pair_conv(pre_ref[pl.ds(base, L + 8), lanes], masks, par)
            su = sigmoid(u)
            act = u * su
            steps = pair_lanes(pack, ST, q)
            weighted = act * steps
            low = weighted.astype(BF)
            diag = block_diag(low)
            decays = [decay_kernel(pack, cumt, 2 * q + e) for e in range(2)]
            kernels = jnp.concatenate([(g * d).astype(BF) for d in decays], 1)
            enter = pair_lanes(pack, EE, q)
            low_state = states_ref[c, :, lanes]
            y = mm(bc_ref[rows, 128:], low_state) * enter + mm(kernels, diag)
            skip = par[P_SKIP : P_SKIP + 1, :]
            ssd = y + skip * act
            gate = pre_ref[pl.ds(base + 8, L), gate_lanes]
            sg = sigmoid(gate)
            silu = gate * sg
            scaled = dinner_ref[rows, lanes].astype(F32) * par[P_GAIN : P_GAIN + 1, :]
            d_gated = inv * scaled - (ssd * silu) * inv_back
            dy = d_gated * silu
            dcat_ref[rows, gate_lanes] = (d_gated * ssd * (sg + silu * (1.0 - sg))).astype(BF)
            dy_low = dy.astype(BF)
            dy_in = (dy * enter).astype(BF)
            d_c = d_c + mm(dy_in, low_state, ((1,), (1,)))
            dm = mm(dy_low, diag, ((1,), (1,)))
            d_scores = d_scores + dm[:, :L] * decays[0] + dm[:, L:] * decays[1]
            both = mm(kernels, dy_low, ((0,), (0,)))
            rt = rt_ref[:, lanes]
            rt_low = rt.astype(BF)
            leave = pair_lanes(pack, FF, q)
            carried = mm(bc_ref[rows, :128], rt_low) * leave
            d_weighted = jnp.where(lane < 64, both[:L], both[L:]) + carried
            d_b = d_b + mm((weighted * leave).astype(BF), rt_low, ((1,), (1,)))
            keep = enter[L - 1 : L, :]
            rt_ref[:, lanes] = keep * rt + mm(bct_ref[c, pl.ds(128, 128), :], dy_in)
            low32 = low.astype(F32)
            at_end = jnp.sum(low32 * carried, 0, keepdims=True)
            at_end = at_end + keep * jnp.sum(rt * low_state.astype(F32), 0, keepdims=True)
            cum_high, cum_low = split2(dy_low.astype(F32) * y - low32 * d_weighted)
            end_high, end_low = split2(jnp.concatenate([at_end, jnp.zeros((7, 128), F32)], 0))
            ends = jnp.concatenate([end_high, end_low], 0)
            per_head = ((sub >> 6) + 2 * q == lane).astype(BF)
            sums = sums + mm(jnp.concatenate([cum_high, cum_low, (act * d_weighted).astype(BF), ends], 0), per_head)
            d_act = skip * dy + steps * d_weighted
            du = d_act * (su + act * (1.0 - su))
            pgrad_ref[K : K + 1, lanes] += jnp.sum(du, 0, keepdims=True)
            pgrad_ref[P_SKIP : P_SKIP + 1, lanes] += jnp.sum(dy * act, 0, keepdims=True)
            ahead = jnp.concatenate([du, later[:, 128 * q : 128 * q + 128]], 0)
            d_pre = par[K - 1 : K, :] * du
            for k in range(K):
                pgrad_ref[K - 1 - k : K - k, lanes] += jnp.sum(du * moved[k], 0, keepdims=True)
                if k:
                    d_pre = d_pre + par[K - 1 - k : K - k, :] * (ahead[k : k + L] * masks[2 + k])
            dcat_ref[rows, lanes] = d_pre.astype(BF)
            heads_of_pair.append(du[:8])
        dg_ref[c] += d_scores
        dbc_ref[rows, 128:] = d_c
        dbc_ref[rows, :128] = d_b
        d_last = sums[3 * L : 3 * L + 1] + sums[3 * L + 8 : 3 * L + 9]
        hi, mid, lo = split3(sums[:L] + sums[L : 2 * L])
        parts = hi.astype(F32) + pltpu.roll(mid.astype(F32), 8, 1) + pltpu.roll(lo.astype(F32), 16, 1)
        d_log = mm(upper, parts.astype(BF))
        d_log = d_log + pltpu.roll(d_log, 120, 1) + pltpu.roll(d_log, 112, 1) + d_last
        d_step = sums[2 * L : 3 * L] + decay * d_log
        d_step_pre = jnp.where(heads, d_step * pltpu.roll(pack, 128 - SG, 1), 0.0)
        dstep_ref[rows, :] += pltpu.roll(d_step_pre, 16 * group, 1).astype(BF)
        rate = jnp.sum(jnp.where(heads, pack, 0.0) * d_log, 0, keepdims=True) * decay
        offs = jnp.sum(d_step_pre, 0, keepdims=True)
        hgrad_ref[0:1, :] += pltpu.roll(jnp.concatenate([rate, jnp.zeros((7, 128), F32)], 0), 16 * z_k, 1)[0:1]
        hgrad_ref[1:2, :] += pltpu.roll(jnp.concatenate([offs, jnp.zeros((7, 128), F32)], 0), 16 * z_k, 1)[0:1]
        return jnp.concatenate(heads_of_pair, 1)

    lax.fori_loop(0, CH, chunk, jnp.zeros((8, GW), F32))


def state_chunks(statepre_ref, cst_ref, tok_ref, row_ref, bc_ref, dg_ref, dbc_ref, dstate_ref, sgrad_ref):
    sgrad_ref[...] = jnp.zeros_like(sgrad_ref)
    cst = cst_ref[...]
    lane = lax.broadcasted_iota(jnp.int32, (L, L), 1)
    sub = lax.broadcasted_iota(jnp.int32, (L, L), 0)

    def last(step, later):
        c = CH - 1 - step
        base = pl.multiple_of(c * L, L)
        rows = pl.ds(base, L)
        tok = tok_ref[rows, :]
        same = (tok[:, 0:1] == row_ref[pl.ds(c, 1), :]) & (sub >= lane)
        ds = jnp.where(same, dg_ref[c], 0.0).astype(BF)
        d_c = dbc_ref[rows, 128:] + mm(ds, bc_ref[rows, :128])
        d_b = dbc_ref[rows, :128] + mm(ds, bc_ref[rows, 128:], ((0,), (0,)))
        window = statepre_ref[pl.ds(base, L + 8), :]
        w = conv_of(window, tok, cst)
        sw = sigmoid(w)
        dw = jnp.concatenate([d_b, d_c], 1) * (sw * (1.0 + w * (1.0 - sw)))
        sgrad_ref[K : K + 1, :] += jnp.sum(dw, 0, keepdims=True)
        for k in range(K):
            moved = back_conv_input(window, k)
            if k:
                moved = moved * tok[:, 2 + k : 3 + k]
            sgrad_ref[K - 1 - k : K - k, :] += jnp.sum(dw * moved, 0, keepdims=True)
        ahead = jnp.concatenate([dw, later], 0)
        d_pre = cst[K - 1 : K, :] * dw
        for k in range(1, K):
            d_pre = d_pre + cst[K - 1 - k : K - k, :] * (ahead[k : k + L] * tok[:, 5 + k : 6 + k])
        dstate_ref[rows, :] = d_pre.astype(BF)
        return dw[:8]

    lax.fori_loop(0, CH, last, jnp.zeros((8, 256), F32))


MESH = pl.DeviceIdType.MESH
VMEM_LIMIT = 63 * 2**20
R_GAIN, R_CONV, R_SHIFT, R_INNER, R_OFF, R_RATE, R_SKIP, R_CST = 6, 7, 11, 12, 13, 14, 15, 16
SMALL = 32


class Links:
    def __init__(self, send_sems):
        self.send_sems = send_sems
        self.number = {}
        self.like = {}
        self.ended = set()

    def send(self, name, src, dst, recv_sem, device, like=None):
        at = self.number.setdefault(name, len(self.number))
        self.like[name] = src if like is None else like
        pltpu.make_async_remote_copy(
            src_ref=src, dst_ref=dst, send_sem=self.send_sems.at[at], recv_sem=recv_sem,
            device_id=device, device_id_type=MESH,
        ).start()

    def arrived(self, dst, recv_sem, device):
        pltpu.make_async_remote_copy(
            src_ref=dst, dst_ref=dst, send_sem=self.send_sems.at[0], recv_sem=recv_sem,
            device_id=device, device_id_type=MESH,
        ).wait_recv()

    def left(self, name, recv_sem, device):
        self.ended.add(name)
        like = self.like[name]
        pltpu.make_async_remote_copy(
            src_ref=like, dst_ref=like, send_sem=self.send_sems.at[self.number[name]], recv_sem=recv_sem,
            device_id=device, device_id_type=MESH,
        ).wait_send()

    def finish(self, recv_sem, device):
        for name in self.number:
            if name not in self.ended:
                self.left(name, recv_sem, device)


class Place:
    def __init__(self):
        self.f = lax.axis_index("fsdp")
        self.z = lax.axis_index("zz")
        self.c = lax.axis_index("core")
        f, c = self.f, self.c
        y, x = f // 2, f % 2
        by_x = y * 2 + 1 - x
        by_y = (1 - y) * 2 + x
        self.f2 = by_x * (1 - c) + by_y * c
        self.f3 = by_y * (1 - c) + by_x * c
        self.f4 = 3 - f
        z_low, z_high = self.z % 2, self.z // 2
        self.zk = [((z_high + k // 2) % 2) * 2 + (z_low + k % 2) % 2 for k in range(4)]

    def at(self, f=None, z=None, c=None):
        return (self.f if f is None else f, self.z if z is None else z, self.c if c is None else c)

    def near(self):
        devices = [self.at(z=self.zk[k]) for k in (1, 2, 3)]
        return devices + [self.at(f=self.f2), self.at(f=self.f3), self.at(f=self.f4), self.at(c=1 - self.c)]

    def greet(self):
        for device in self.near():
            pl.semaphore_signal(pltpu.get_barrier_semaphore(), inc=1, device_id=device, device_id_type=MESH)

    def greeted(self):
        pl.semaphore_wait(pltpu.get_barrier_semaphore(), len(self.near()))


def piece(inout_ref, out_ref, m, f, z):
    depth = out_ref.shape[2] // 4
    at = pl.ds(pl.multiple_of(f * depth, depth), depth)
    if m == 2:
        return out_ref.at[z, :, at]
    return inout_ref.at[z, at, pl.ds(m * GW, GW)]


def iota(shape, dim):
    return lax.broadcasted_iota(jnp.int32, shape, dim)


def own_block(f, rows, unit):
    return ((iota((rows, GW), 1) & 63) == f * unit + iota((rows, GW), 0)).astype(BF)


def at_block(f, rows, size):
    row = iota((rows, GW), 0)
    return ((iota((rows, GW), 1) == f * size + row) & (row < size)).astype(BF)


def spread_units(values, place):
    rows = mm(values, place)
    return jnp.sum(jnp.where((iota(rows.shape, 1) >> 6) == iota(rows.shape, 0), rows, 0.0), 0, keepdims=True)


def small_block(f, refs):
    norm, step, conv, shift, gain, cst, cst_shift, offset, rate, skip = [r[...].astype(F32) for r in refs]
    units = own_block(f, conv.shape[2], conv.shape[2])
    states = at_block(f, cst.shape[1], cst.shape[1])
    heads = at_block(f, 16, 12)
    rows = [step, norm.reshape(1, -1)]
    rows += [spread_units(conv[:, k].astype(BF), units) for k in range(K)]
    rows += [spread_units(shift.astype(BF), units), spread_units(gain.astype(BF), units)]
    per_head = jnp.concatenate([v.reshape(1, -1) for v in (offset, rate, skip)], 0)
    per_head = jnp.concatenate([per_head, jnp.zeros((3, 16 - per_head.shape[1]), F32)], 1)
    rows.append(mm(per_head.astype(BF), heads))
    rows.append(mm(cst.astype(BF), states))
    rows.append(mm(cst_shift.reshape(1, -1).astype(BF), states))
    rows.append(jnp.zeros((SMALL - 21, GW), F32))
    return jnp.concatenate(rows, 0).astype(BF)


def token_masks(docs, tok_ref):
    lane, sub = iota((CH, L), 1), iota((CH, L), 0)
    masks = [docs, jnp.where((sub > 0) & (docs == pltpu.roll(docs, 1, 0)[:, L - 1 : L]), 1.0, 0.0)]
    masks.append(jnp.where(docs == docs[:, L - 1 : L], 1.0, 0.0))
    for k in range(1, K):
        moved = pltpu.roll(docs, k, 1)
        before = jnp.where(lane < k, pltpu.roll(moved, 1, 0), moved)
        masks.append(jnp.where((before == docs) & ((sub > 0) | (lane >= k)), 1.0, 0.0))
    for k in range(1, K):
        moved = pltpu.roll(docs, L - k, 1)
        after = jnp.where(lane >= L - k, pltpu.roll(moved, CH - 1, 0), moved)
        masks.append(jnp.where((after == docs) & ((sub < CH - 1) | (lane < L - k)), 1.0, 0.0))
    for c in range(CH):
        rows = [m[c : c + 1, :] for m in masks] + [jnp.zeros((128 - len(masks), L), F32)]
        tok_ref[pl.ds(c * L, L), :] = jnp.concatenate(rows, 0).T


ORDER = (3, 2, 1, 0)
ROWS = 128
SCHEDULE = {
    "s1": [("second", 0, 0), ("first", 0, 1)],
    "s2": [("second", 1, 0), ("first", 1, 1)],
    "s5": [("second", 0, 1), ("first", 0, 2)],
    "m00": [("second", 1, 1), ("first", 1, 2), ("second", 0, 2), ("first", 0, 3)],
    "m10": [("second", 1, 2), ("first", 1, 3), ("second", 0, 3), ("first", 2, 0)],
    "m20": [("second", 1, 3), ("first", 2, 1), ("second", 2, 0), ("first", 2, 2)],
    "m30": [("second", 2, 1), ("first", 2, 3), ("second", 2, 2)],
    "n1": [("second", 2, 3)],
    "b01": [("s1", 0)],
    "b11": [("s1", 1)],
    "b21": [("s1", 2)],
    "b31": [("s1", 3)],
    "x1": [("s2", 0)],
    "g01": [("s3", 0)],
    "g02": [("s2", 1)],
    "g06": [("s3", 1)],
    "g07": [("s2", 2)],
    "h01": [("s3", 2)],
    "h02": [("s2", 3)],
    "g14": [("s2", 4), ("last", 3)],
    "h10": [("s3", 4)],
    "h11": [("s2", 5)],
    "g23": [("s3", 5)],
    "g24": [("s2", 6)],
    "h20": [("s3", 6)],
    "h21": [("s2", 7)],
    "g33": [("s3", 7)],
    "g34": [("s2", 8)],
    "h30": [("s3", 8)],
    "h31": [("s2", 9)],
    "t2": [("s3", 9), ("s2", 10)],
    "t4": [("s2", 11), ("last", 10)],
    "t5": [("last", 11)],
}
T_INV, T_BACK = 16, 17


def block_kernel(model, hid_ref, cot_ref, w0_ref, w1_ref, w2_ref, wst_ref, norm_ref, step_ref, conv_ref, shift_ref, gain_ref,
                 cvst_ref, cvst_shift_ref, offset_ref, rate_ref, skip_ref, seg_ref,
                 layer_out, hidden_out, normt_hbm, win_hbm, pre_hbm, states_hbm,
                 ginner_out, ggate_out, gout_out, gstate_ref, gsmall_ref, gother_ref,
                 hall, call, win, wout, pre, accr, flip, gated, states, halfr, recv1, recv2, recv3, stage,
                 small_ref, sbuf, stbuf, statepre_ref, ss_ref, ssr_ref, tok_ref, docs_ref,
                 bc_ref, bct_ref, g_ref, pack_ref, cumt_ref, par_ref, hpar_ref, cst_ref, stw_ref, gains_ref, gaingrad_ref, st_ref,
                 srecv, srecv1, srecv3, srecvc, qrecv1, qrecv3, qsend, qrecvc, nparts, nrecv, nback,
                 dstep, dstate, pgrad, hgrad, sgrad, rt_ref, dg_ref, dbc_ref,
                 sends, recvs, small_recvs, state_recvs, core_recvs, recv_sems, core_sems, state_sems, gain_sems,
                 outs_sem, pre_sem, state_sem, own_sem, load_sems, stage_sem, hid_sem, credit, free_out, free_core, free_half):
    stepre_ref = pr_ref = ss_ref
    dcat = hall.at[:, pl.ds(0, 2 * GW)]
    here = Place()
    z, zk = here.z, here.zk
    rows_own = hid_ref.shape[0]
    wide = 2 * GW
    depth = model // 4
    links = Links(sends)
    shards = [w0_ref, w1_ref, w2_ref]
    outs = []

    def put(src, dst):
        copy = pltpu.make_async_copy(src, dst, outs_sem.at[len(outs)])
        copy.start()
        outs.append(copy)

    here.greet()
    small_ref[...] = small_block(
        here.f, (norm_ref, step_ref, conv_ref, shift_ref, gain_ref, cvst_ref, cvst_shift_ref, offset_ref, rate_ref, skip_ref)
    )
    here.greeted()
    mine = pl.ds(pl.multiple_of(here.c * rows_own, rows_own), rows_own)
    other = pl.ds(pl.multiple_of((1 - here.c) * rows_own, rows_own), rows_own)
    core = here.at(c=1 - here.c)
    one_block = recv2.at[0]
    for k in (1, 2, 3):
        links.send(("small", k), small_ref, sbuf.at[here.f, z], small_recvs.at[k], here.at(z=zk[k]))
    links.send("hidden", hid_ref, hall.at[mine], core_recvs.at[0], core)

    def recv_sem(m, f, z_):
        return recvs.at[m, f, z_]

    def push_z(m):
        for k in (1, 2, 3):
            links.send(("z", m, k), shards[m], piece(win, wout, m, here.f, z), recv_sem(m, here.f, z), here.at(z=zk[k]))

    def first(m, k):
        dst = piece(win, wout, m, here.f, zk[k])
        src = shards[m] if k == 0 else dst
        if k:
            links.arrived(dst, recv_sem(m, here.f, zk[k]), here.at(z=zk[k]))
        links.send(("first", m, k, 2), src, dst, recv_sem(m, here.f, zk[k]), here.at(f=here.f2), one_block)
        links.send(("first", m, k, 3), src, dst, recv_sem(m, here.f, zk[k]), here.at(f=here.f3), one_block)

    def second(m, k):
        src = piece(win, wout, m, here.f2, zk[k])
        links.arrived(src, recv_sem(m, here.f2, zk[k]), here.at(f=here.f2))
        links.send(("second", m, k), src, src, recv_sem(m, here.f2, zk[k]), here.at(f=here.f3), one_block)

    def third(m, k):
        for f in (here.f3, here.f4):
            src = piece(win, wout, m, f, zk[k])
            links.arrived(src, recv_sem(m, f, zk[k]), here.at(f=here.f3))

    events = {"first": first, "second": second}

    def due(slot):
        for name, *what in SCHEDULE.get(slot, ()):
            events[name](*what)

    def ticker(prefix):
        def tick(step):
            for at in range(CH):
                if prefix + str(at) in SCHEDULE:
                    pl.when(step == at)(functools.partial(due, prefix + str(at)))

        return tick

    def state_of(f, part):
        return stbuf.at[f, :, part]

    push_z(0)
    links.send("cot", cot_ref, call.at[mine], core_recvs.at[1], core)
    own_copies = [pltpu.make_async_copy(shards[m], piece(win, wout, m, here.f, z), own_sem.at[m]) for m in range(3)]
    own_copies.append(pltpu.make_async_copy(cot_ref, call.at[mine], own_sem.at[3]))
    own_copies.append(pltpu.make_async_copy(hid_ref, hall.at[mine], hid_sem.at[4]))
    for copy in own_copies:
        copy.start()
    sbuf[here.f, z] = small_ref[...]
    stbuf[here.f] = wst_ref[...]
    docs = seg_ref[pl.ds(pl.multiple_of(z * CH, CH), CH), :].astype(F32)
    docs_ref[...] = docs
    token_masks(docs, tok_ref)
    for k in (1, 2, 3):
        links.arrived(sbuf.at[here.f, zk[k]], small_recvs.at[k], here.at(z=zk[k]))
    links.send(("small", 4), sbuf.at[here.f], sbuf.at[here.f], small_recvs.at[4], here.at(f=here.f2))
    links.send(("small", 5), sbuf.at[here.f], sbuf.at[here.f], small_recvs.at[5], here.at(f=here.f3))
    half_state = pl.ds(pl.multiple_of(here.c * 128, 128), 128)
    rest_state = pl.ds(pl.multiple_of(128 - here.c * 128, 128), 128)
    links.send(("state", 0), wst_ref.at[:, half_state], state_of(here.f, half_state), state_recvs.at[0], here.at(f=here.f2))
    links.send(("state", 1), wst_ref.at[:, half_state], state_of(here.f, half_state), state_recvs.at[1], here.at(f=here.f3))
    first(0, 0)
    push_z(1)
    links.arrived(sbuf.at[here.f2], small_recvs.at[4], here.at(f=here.f2))
    links.send(("small", 6), sbuf.at[here.f2], sbuf.at[here.f2], small_recvs.at[6], here.at(f=here.f3))
    links.arrived(state_of(here.f2, half_state), state_recvs.at[0], here.at(f=here.f2))
    links.send(("state", 2), state_of(here.f2, half_state), state_of(here.f2, half_state), state_recvs.at[2], here.at(f=here.f3))
    links.send(("state", 3), state_of(here.f2, half_state), state_of(here.f2, half_state), state_recvs.at[3], core)
    first(1, 0)
    push_z(2)
    due("s0")
    links.arrived(sbuf.at[here.f3], small_recvs.at[5], here.at(f=here.f3))
    links.arrived(sbuf.at[here.f4], small_recvs.at[6], here.at(f=here.f3))

    shared = sum(sbuf[f, 0].astype(F32) for f in range(4))
    gain_outer = jnp.concatenate([sbuf[f, 0][R_GAIN : R_GAIN + 1, :].astype(F32) for f in range(4)], 1)
    gains_ref[...] = jnp.broadcast_to(gain_outer, (8, model))
    cst_ref[...] = jnp.concatenate([shared[R_CST : R_CST + 5, :256], jnp.zeros((3, 256), F32)], 0)
    lane8 = lax.broadcasted_iota(jnp.int32, (8, 128), 1)
    heads8 = jnp.concatenate([shared[R_OFF : R_SKIP + 1, :128], jnp.zeros((5, 128), F32)], 0)
    own_heads = jnp.zeros((8, 128), F32)
    spread_heads = (lax.broadcasted_iota(jnp.int32, (128, GW), 1) >> 6
                    == lax.broadcasted_iota(jnp.int32, (128, GW), 0)).astype(BF)
    stw_ref[...] = jnp.zeros_like(stw_ref)
    for k in range(4):
        turned = pltpu.roll(heads8, 128 - (2 * zk[k] + here.c) * GH, 1)
        own_heads = own_heads + pltpu.roll(jnp.where(lane8 < GH, turned, 0.0), 16 * k, 1)
        group = sum(sbuf[f, zk[k]].astype(F32) for f in range(4))
        skips = mm(turned.astype(BF), spread_heads)[2:3, :]
        par_ref[k] = jnp.concatenate(
            [group[R_CONV : R_CONV + 5], skips, group[R_INNER : R_INNER + 1], jnp.zeros((1, GW), F32)], 0
        )
        for f in range(4):
            block = sbuf[f, zk[k]][:16].astype(F32)
            keep = lax.broadcasted_iota(jnp.int32, block.shape, 0) < GH
            stw_ref[pl.ds(16 * k, 16), pl.ds(depth * f, depth)] = jnp.where(keep, block, 0.0).astype(BF)
    decay = -jnp.exp(own_heads[1:2, :])
    hpar_ref[...] = jnp.concatenate([own_heads[0:1], decay, own_heads[2:3], jnp.zeros((5, 128), F32)], 0)

    due("s1")
    own_copies[4].wait()
    links.arrived(hall.at[other], core_recvs.at[0], core)

    def norm(i, _):
        rows = pl.ds(pl.multiple_of(i * L, L), L)
        x = hall[rows, :].astype(F32)
        inv = lax.rsqrt(jnp.sum(x * x, 1, keepdims=True) / model + EPSILON)
        hall[rows, :] = (x * inv * gain_outer).astype(BF)
        return 0

    lax.fori_loop(0, SEQ // L, norm, 0)
    due("s2")
    links.arrived(state_of(here.f3, half_state), state_recvs.at[1], here.at(f=here.f3))
    links.send(("state", 4), state_of(here.f3, half_state), state_of(here.f3, half_state), state_recvs.at[4], core)
    links.arrived(state_of(here.f4, half_state), state_recvs.at[2], here.at(f=here.f3))
    links.send(("state", 5), state_of(here.f4, half_state), state_of(here.f4, half_state), state_recvs.at[5], core)
    for n, f in ((3, here.f3), (4, here.f2), (5, here.f4)):
        links.arrived(state_of(f, rest_state), state_recvs.at[n], core)

    TILE = 256
    WIDE_TILE = 512

    def project_small(i, _):
        rows = pl.ds(pl.multiple_of(i * TILE, TILE), TILE)
        total = jnp.zeros((TILE, 256), F32)
        for f in range(4):
            total = total + mm(hall[rows, pl.ds(depth * f, depth)], stbuf[f])
        statepre_ref[pl.ds(pl.multiple_of(i * TILE + 8, 8), TILE), :] = total
        steps = mm(hall[rows, :], stw_ref[...], ((1,), (1,)))
        stepre_ref[rows, :] = jnp.concatenate([steps, jnp.zeros((TILE, 64), F32)], 1)
        return 0

    statepre_ref[pl.ds(0, 8), :] = jnp.zeros((8, 256), F32)
    lax.fori_loop(0, SEQ // TILE, project_small, 0)

    due("s3")

    def turn(i, _):
        for half in range(2):
            lanes = pl.ds(pl.multiple_of(i * 256 + half * 128, 128), 128)
            flip[lanes, :] = hall[:, lanes].T
        return 0

    lax.fori_loop(0, model // 256, turn, 0)
    TURNED = len(outs)
    put(flip, normt_hbm)
    due("s4")
    prep_chunks(statepre_ref, stepre_ref, tok_ref, docs_ref, cst_ref, hpar_ref, bc_ref, bct_ref, g_ref, pack_ref, cumt_ref)
    due("s5")
    links.arrived(call.at[other], core_recvs.at[1], core)
    for copy in own_copies[:4]:
        copy.wait()
    ss_ref[...] = jnp.zeros_like(ss_ref)
    for slot in range(2):
        pre[slot, pl.ds(0, 8), :] = jnp.zeros((8, 2 * GW), F32)
    pre_copies = []
    state_copies = []
    for k in range(4):
        due("p%d" % k)
        third(0, k)
        third(1, k)
        slot = k % 2
        if k >= 2:
            pre_copies[k - 2].wait()

        def project(i, _, slot=slot, k=k):
            rows = pl.ds(pl.multiple_of(i * WIDE_TILE, WIDE_TILE), WIDE_TILE)
            to = pl.ds(pl.multiple_of(i * WIDE_TILE + 8, 8), WIDE_TILE)
            pre[slot, to, :] = mm(hall[rows, :], win[zk[k]])
            return 0

        lax.fori_loop(0, SEQ // WIDE_TILE, project, 0)
        copy = pltpu.make_async_copy(pre.at[slot, pl.ds(8, SEQ)], pre_hbm.at[k], pre_sem.at[k])
        copy.start()
        pre_copies.append(copy)
        put(win.at[zk[k]], win_hbm.at[k])
        if k:
            state_copies[k - 1].wait()
        fwd_chunks(k, ticker("m%d" % k), pre.at[slot], par_ref.at[k], tok_ref, bc_ref, bct_ref, g_ref, pack_ref.at[k // 2], cumt_ref.at[k],
                   gated.at[k], states, ss_ref, st_ref)
        copy = pltpu.make_async_copy(states, states_hbm.at[k], state_sem.at[k])
        copy.start()
        state_copies.append(copy)
    for copy in pre_copies[2:] + state_copies[3:]:
        copy.wait()

    links.send("squares", ss_ref, ssr_ref, core_recvs.at[2], core)
    due("n0")
    links.arrived(ssr_ref, core_recvs.at[2], core)
    inner_all = 2 * 4 * GW

    def inner_norm(i, _):
        rows = pl.ds(pl.multiple_of(i * L, L), L)
        total = jnp.sum(ss_ref[rows, :] + ssr_ref[rows, :], 1, keepdims=True)
        inv = lax.rsqrt(total / inner_all + EPSILON)
        tok_ref[rows, :] = jnp.where(iota((L, 128), 1) == T_INV, inv, tok_ref[rows, :])
        for k in range(4):
            gain = par_ref[k, P_GAIN : P_GAIN + 1, :]
            low = (gated[k, rows, :].astype(F32) * inv * gain).astype(BF)
            hall[rows, pl.ds(k * GW, GW)] = low
            flip[pl.ds(k * GW, GW), rows] = low.T
        pr_ref[rows, :] = jnp.zeros((L, 128), F32)
        return 0

    links.left("squares", core_recvs.at[0], core)
    for copy in outs:
        copy.wait()
    lax.fori_loop(0, SEQ // L, inner_norm, 0)
    pl.semaphore_signal(free_core, inc=1, device_id=core, device_id_type=MESH)
    f, f2, f3, f4 = here.f, here.f2, here.f3, here.f4
    for m in (0, 1):
        for k in range(4):
            for name in (("first", m, k, 2), ("first", m, k, 3), ("second", m, k)):
                links.left(name, core_recvs.at[0], core)
    loads = {}

    def load(name, src, dst, sem):
        copy = pltpu.make_async_copy(src, dst, load_sems.at[sem])
        copy.start()
        loads[name] = copy

    accl = pre.at[0, pl.ds(8, SEQ)]

    def slot_of(u):
        return (u % 6) // 2, u % 2

    def part(u, f_):
        at, side = slot_of(u)
        return win.at[at, pl.ds(pl.multiple_of(f_ * depth, depth), depth), pl.ds(side * GW, GW)]

    def landing(u, n):
        if u < 4:
            return recv1.at[u, n]
        n += 2 * (u - 4)
        return wout.at[n // 4, :, pl.ds((n % 4) * GW, GW)]

    def s1(u):
        for n, f_ in enumerate((f3, f4)):
            links.send(("s1", u, n), part(u, f_), landing(u, n), recv_sems.at[u, n], here.at(f=f3), one_block)

    units = [(k, 2) for k in ORDER] + [(k, m) for k in ORDER for m in (0, 1)]

    def add_into(dst, src):
        rows, width = dst.shape

        def body(i, _):
            at = pl.ds(pl.multiple_of(i * ROWS, ROWS), ROWS)
            dst[at, :] = (dst[at, :].astype(F32) + src[at, :].astype(F32)).astype(dst.dtype)
            return 0

        lax.fori_loop(0, rows // ROWS, body, 0)

    def s2(u):
        links.arrived(landing(u, 1), recv_sems.at[u, 1], here.at(f=f3))
        add_into(part(u, f2), landing(u, 1))
        if u >= 4:
            pl.semaphore_wait(credit, 1)
        links.send(("s2", u), part(u, f2), recv2.at[u % 4], recv_sems.at[u, 2], here.at(f=f2), one_block)
        links.arrived(landing(u, 0), recv_sems.at[u, 0], here.at(f=f3))
        add_into(part(u, f), landing(u, 0))

    def give_credit(u):
        if u < 8:
            pl.semaphore_signal(credit, inc=1, device_id=here.at(f=f2), device_id_type=MESH)

    outs = {0: ginner_out, 1: ggate_out, 2: gout_out}
    results = [pltpu.make_async_copy(stage, outs[m], stage_sem.at[m]) for m in range(3)]
    staged = []

    def s3(u):
        k, m = units[u]
        links.arrived(recv2.at[u % 4], recv_sems.at[u, 2], here.at(f=f2))
        add_into(part(u, f), recv2.at[u % 4])
        give_credit(u)
        links.send(("s3", u), part(u, f), recv3.at[m, k - 1], recv_sems.at[12 + m, k - 1], here.at(z=zk[k]), one_block)

    def last_sum(u):
        k, m = units[u]
        links.arrived(recv2.at[u % 4], recv_sems.at[u, 2], here.at(f=f2))
        for j in (1, 2, 3):
            links.arrived(recv3.at[m, j - 1], recv_sems.at[12 + m, j - 1], here.at(z=zk[j]))
        own = part(u, f)
        if staged:
            results[staged[-1]].wait()

        def body(i, _):
            at = pl.ds(pl.multiple_of(i * ROWS, ROWS), ROWS)
            total = own[at, :].astype(F32) + recv2[u % 4, at, :].astype(F32)
            for j in range(3):
                total = total + recv3[m, j, at, :].astype(F32)
            stage[at, :] = total
            return 0

        lax.fori_loop(0, GW // ROWS, body, 0)
        give_credit(u)
        staged.append(m)
        results[m].start()

    events.update({"s1": s1, "s2": s2, "s3": s3, "last": last_sum})

    def grad_out(i):
        k = ORDER[i]
        at, side = slot_of(i)

        def columns_of(f_, _):
            lanes = pl.ds(pl.multiple_of(f_ * depth, depth), depth)
            total = mm(flip[pl.ds(k * GW, GW), :], call[:, lanes])
            win[at, lanes, pl.ds(side * GW, GW)] = total.astype(BF)
            return 0

        lax.fori_loop(0, 4, columns_of, 0)

    hid_copies = []
    for side in range(2):
        src = hid_ref.at[:, pl.ds(side * wide, wide)]
        hid_copies.append(pltpu.make_async_copy(src, halfr.at[pl.ds(side * rows_own, rows_own)], hid_sem.at[side]))
        hid_copies[-1].start()
    due("n1")
    for k in range(4):
        due("b%d0" % k)
        grad_out(k)
        due("b%d1" % k)
        third(2, k)
        gaingrad_ref[k] = jnp.zeros((8, GW), F32)

        def back(i, _, k=k):
            rows = pl.ds(pl.multiple_of(i * WIDE_TILE, WIDE_TILE), WIDE_TILE)
            d = mm(call[rows, :], wout[zk[k]], ((1,), (1,)))
            both = d * gated[k, rows, :].astype(F32)
            gated[k, rows, :] = d.astype(BF)
            gaingrad_ref[k, 0:1, :] += jnp.sum(both * tok_ref[rows, T_INV : T_INV + 1], 0, keepdims=True)
            both = both * par_ref[k, P_GAIN : P_GAIN + 1, :]
            pr_ref[rows, :] += both[:, :128] + both[:, 128:256] + both[:, 256:]
            return 0

        lax.fori_loop(0, SEQ // WIDE_TILE, back, 0)
    pl.semaphore_wait(free_core, 1)
    links.send("products", pr_ref, ssr_ref, core_recvs.at[3], core)
    due("x0")
    load("normt", normt_hbm, flip, 0)
    load(("win", 0), win_hbm.at[ORDER[0]], win.at[3], 1)

    def mix_rows(i, _):
        rows = pl.ds(pl.multiple_of(i * WIDE_TILE, WIDE_TILE), WIDE_TILE)
        for acc, first_lane in ((accl, 0), (accr, wide)):
            acc[rows, :] = sum(mm(hall[rows, pl.ds(k * GW, GW)], wout[zk[k], :, pl.ds(first_lane, wide)]) for k in range(4))
        return 0

    lax.fori_loop(0, SEQ // WIDE_TILE, mix_rows, 0)
    due("x1")
    half = hall.at[:, pl.ds(0, wide)]
    halves = [halfr, hall.at[:, pl.ds(wide, wide)]]

    def exchange(n):
        def body(j, _):
            src = pl.ds(pl.multiple_of((1 - here.c) * rows_own + j * ROWS, ROWS), ROWS)
            half[pl.ds(pl.multiple_of(j * ROWS, ROWS), ROWS), :] = accl[src, :].astype(BF)
            half[pl.ds(pl.multiple_of(rows_own + j * ROWS, ROWS), ROWS), :] = accr[src, :].astype(BF)
            return 0

        lax.fori_loop(0, rows_own // ROWS, body, 0)
        links.send(("half", n), half, halves[n], core_sems.at[n], core)

    def received(n):
        links.arrived(halves[n], core_sems.at[n], core)

    def places(j):
        own = pl.ds(pl.multiple_of(here.c * rows_own + j * ROWS, ROWS), ROWS)
        at = pl.ds(pl.multiple_of(j * ROWS, ROWS), ROWS)
        below = pl.ds(pl.multiple_of(rows_own + j * ROWS, ROWS), ROWS)
        return own, at, below

    def summed(n, j):
        own, at, below = places(j)
        left = accl[own, :] + halves[n][at, :].astype(F32)
        right = accr[own, :] + halves[n][below, :].astype(F32)
        return own, at, below, jnp.concatenate([left, right], 1)

    def store(n, at, below, values):
        halves[n][at, :] = values[:, :wide].astype(BF)
        halves[n][below, :] = values[:, wide:].astype(BF)

    def give(n, out, sem):
        for side in range(2):
            load((n, side), halves[n].at[pl.ds(side * rows_own, rows_own)], out.at[:, pl.ds(side * wide, wide)], sem + side)

    def add_hidden(j, _):
        own, at, below = places(j)
        accl[own, :] = accl[own, :] + halfr[at, :].astype(F32)
        accr[own, :] = accr[own, :] + halfr[below, :].astype(F32)
        return 0

    for copy in hid_copies:
        copy.wait()
    lax.fori_loop(0, rows_own // ROWS, add_hidden, 0)
    pl.semaphore_signal(free_half, inc=1, device_id=core, device_id_type=MESH)
    pl.semaphore_wait(free_half, 1)
    exchange(0)
    due("x2")
    links.arrived(ssr_ref, core_recvs.at[3], core)

    def scale(i, _):
        rows = pl.ds(pl.multiple_of(i * L, L), L)
        total = jnp.sum(pr_ref[rows, :] + ssr_ref[rows, :], 1, keepdims=True)
        tok = tok_ref[rows, :]
        inv = tok[:, T_INV : T_INV + 1]
        tok_ref[rows, :] = jnp.where(iota((L, 128), 1) == T_BACK, inv * inv * inv * (total / inner_all), tok)
        return 0

    lax.fori_loop(0, SEQ // L, scale, 0)
    for k in range(4):
        for name in (("first", 2, k, 2), ("first", 2, k, 3), ("second", 2, k)):
            links.left(name, core_recvs.at[0], core)
    pl.semaphore_signal(free_out, inc=1, device_id=here.at(f=f3), device_id_type=MESH)
    links.left(("half", 0), core_sems.at[0], core)
    hgrad[...] = jnp.zeros_like(hgrad)
    dg_ref[...] = jnp.zeros_like(dg_ref)
    dbc_ref[...] = jnp.zeros_like(dbc_ref)
    dstep[...] = jnp.zeros_like(dstep)
    def to_normed(fresh, j, _):
        at = pl.ds(pl.multiple_of(j * WIDE_TILE, WIDE_TILE), WIDE_TILE)
        for acc, first_row in ((accl, 0), (accr, wide)):
            total = mm(dcat[at, :], win[3, pl.ds(first_row, wide), :], ((1,), (1,)))
            acc[at, :] = total if fresh else acc[at, :] + total
        return 0

    for i, k in enumerate(ORDER):
        if i:
            for name in ("pre", "states"):
                loads[name, i].wait()

        bwd_chunks(k, zk[k], ticker("g%d" % i), pre.at[1], gated.at[k], par_ref.at[k], tok_ref, bc_ref, bct_ref, g_ref,
                   pack_ref.at[k // 2], cumt_ref.at[k], states, hpar_ref, dcat, dstep, pgrad.at[k], hgrad, rt_ref, dg_ref, dbc_ref)
        if i < 3:
            load(("pre", i + 1), pre_hbm.at[ORDER[i + 1]], pre.at[1, pl.ds(8, SEQ)], 2)
            load(("states", i + 1), states_hbm.at[ORDER[i + 1]], states, 3)
        else:
            loads[0, 0].wait()
            loads[0, 1].wait()
        u = 4 + 2 * i
        due("h%d0" % i)
        if u >= 6:
            for n in (u - 6, u - 5):
                for name in (("s1", n, 0), ("s1", n, 1), ("s2", n), ("s3", n)):
                    if name in links.number:
                        links.left(name, core_sems.at[0], here.at(c=1 - here.c))

        if i == 0:
            loads["normt"].wait()
            pl.semaphore_wait(free_out, 1)

        def grads(j, _, u=u):
            at = pl.ds(pl.multiple_of(j * depth, depth), depth)
            win[slot_of(u)[0], at, :] = mm(flip[at, :], dcat[...]).astype(BF)
            return 0

        lax.fori_loop(0, 4, grads, 0)
        s1(u)
        s1(u + 1)
        if i == 0:
            received(0)

            def layer(j, _):
                own, at, below, total = summed(0, j)
                store(0, at, below, total)
                return 0

            lax.fori_loop(0, rows_own // ROWS, layer, 0)
            give(0, layer_out, 4)
        due("h%d1" % i)
        if i < 3:
            loads["win", i].wait()
            lax.fori_loop(0, SEQ // WIDE_TILE, functools.partial(to_normed, i == 0), 0)
            load(("win", i + 1), win_hbm.at[ORDER[i + 1]], win.at[3], 1)
            due("h%d2" % i)

    last_tokens = []
    for k in range(4):
        src = hid_ref.at[:, pl.ds(k * GW, GW)]
        last_tokens.append(pltpu.make_async_copy(src, gated.at[k, pl.ds(0, rows_own)], hid_sem.at[k]))
        last_tokens[-1].start()
    state_chunks(statepre_ref, cst_ref, tok_ref, docs_ref, bc_ref, dg_ref, dbc_ref, dstate, sgrad)
    due("t0")

    def state_part(f_, n=0):
        at = pl.ds(pl.multiple_of((f_ % 2) * depth, depth), depth)
        return halfr.at[at, pl.ds(pl.multiple_of((f_ // 2) * 256 + n * 128, 128), 128)]

    def small_part(f_):
        at = pl.ds(pl.multiple_of(2 * depth + (f_ // 2) * 4 * SMALL, 4 * SMALL), 4 * SMALL)
        return halfr.at[at, pl.ds(pl.multiple_of((f_ % 2) * GW, GW), GW)]

    def add_to(ref, *others):
        total = ref[...].astype(F32)
        for other in others:
            total = total + other.astype(F32)
        ref[...] = total.astype(BF)
        return total

    for f_ in range(4):
        sums = mm(flip[pl.ds(f_ * depth, depth), :], dstate[...])
        lower, upper = sums[:, :128], sums[:, 128:]
        state_part(f_)[...] = jnp.where(here.c == 0, lower, upper).astype(BF)
        state_part(f_, 1)[...] = jnp.where(here.c == 0, upper, lower).astype(BF)
        links.send(("state_core", f_), state_part(f_, 1), srecv.at[f_], state_sems.at[f_], core)
    due("t1")
    step_rows = mm(dstep[:, :64], flip[...], ((0,), (1,)))
    zeros = jnp.zeros((1, GW - 256), F32)
    skips = jnp.zeros((8, 128), F32)
    heads_of = (iota((GW, 128), 0) >> 6 == iota((GW, 128), 1)).astype(BF)
    for k in range(4):
        hi, lo = split2(pgrad[k])
        skips = skips + pltpu.roll(mm(hi, heads_of) + mm(lo, heads_of), 16 * zk[k], 1)
    head_rows = jnp.concatenate([hgrad[0:2, :], skips[P_SKIP : P_SKIP + 1, :]], 0)
    head_rows = jnp.concatenate([head_rows, jnp.zeros((3, GW - 128), F32)], 1)
    common = [jnp.zeros((1, GW), F32)]
    common += [jnp.concatenate([sgrad[r : r + 1, :], zeros], 1) for r in range(5)]
    common.append(head_rows)
    for f_ in range(4):
        blocks = []
        for k in range(4):
            own = jnp.concatenate([pgrad[k, 0:5, :], gaingrad_ref[k, 0:1, :], jnp.zeros((1, GW), F32)], 0)
            blocks += [step_rows[16 * k : 16 * k + 16, f_ * depth : (f_ + 1) * depth], own] + common
        small_part(f_)[...] = jnp.concatenate(blocks, 0).astype(BF)
    for n, f_ in enumerate((f2, f3, f4)):
        links.send(("sums", n), small_part(f_), qrecv1.at[n], recv_sems.at[16, n], here.at(f=f_))
    loads["win", 3].wait()
    lax.fori_loop(0, SEQ // WIDE_TILE, functools.partial(to_normed, False), 0)

    def finish_normed(j, _):
        at = pl.ds(pl.multiple_of(j * 256, 256), 256)
        total = mm(dstep[at, :64], stw_ref[...])
        total = total + jnp.concatenate([mm(dstate[at, :], stbuf[f_], ((1,), (1,))) for f_ in range(4)], 1)
        accl[at, :] = accl[at, :] + total[:, :wide]
        accr[at, :] = accr[at, :] + total[:, wide:]
        return 0

    lax.fori_loop(0, SEQ // 256, finish_normed, 0)
    due("t2")
    exchange(1)
    for f_ in range(4):
        links.arrived(srecv.at[f_], state_sems.at[f_], core)
        add_to(state_part(f_), srecv[f_])
    for n, f_ in enumerate((f2, f3, f4)):
        links.send(("state", f"f{n}"), state_part(f_), srecv1.at[n], recv_sems.at[15, n], here.at(f=f_))
    due("t3")
    received(1)
    gain = gains_ref[0:1, :]
    for copy in last_tokens:
        copy.wait()

    def last(j, gain_grad):
        own, at, below, d = summed(1, j)
        x = jnp.concatenate([gated[k, at, :] for k in range(4)], 1).astype(F32)
        inv = lax.rsqrt(jnp.sum(x * x, 1, keepdims=True) / model + EPSILON)
        weighted = d * gain
        mean = jnp.sum(x * weighted, 1, keepdims=True) / model
        d_hidden = inv * weighted - x * (inv * inv * inv * mean)
        store(1, at, below, call[own, :].astype(F32) + d_hidden)
        return gain_grad + jnp.sum(d * x * inv, 0, keepdims=True)

    gain_grad = lax.fori_loop(0, rows_own // ROWS, last, jnp.zeros((1, model), F32))
    give(1, hidden_out, 6)
    for f_ in range(4):
        nparts[f_] = jnp.broadcast_to(gain_grad[:, f_ * depth : (f_ + 1) * depth], (16, GW)).astype(BF)
    for n, f_ in enumerate((f2, f3, f4)):
        links.send(("gain", n), nparts.at[f_], nrecv.at[n], gain_sems.at[n], here.at(f=f_))
    due("t4")
    for n, f_ in enumerate((f2, f3, f4)):
        links.arrived(qrecv1.at[n], recv_sems.at[16, n], here.at(f=f_))
    sums = add_to(small_part(f), qrecv1[0], qrecv1[1], qrecv1[2])
    for k in range(4):
        qsend[k] = sums[k * SMALL : (k + 1) * SMALL].astype(BF)
        if k:
            links.send(("small_z", k), qsend.at[k], qrecv3.at[k - 1], recv_sems.at[18, k - 1], here.at(z=zk[k]))
    for n, f_ in enumerate((f2, f3, f4)):
        links.arrived(srecv1.at[n], recv_sems.at[15, n], here.at(f=f_))
    add_to(state_part(f), srecv1[0], srecv1[1], srecv1[2])
    for k in (1, 2, 3):
        links.send(("state_z", k), state_part(f), srecv3.at[k - 1], recv_sems.at[17, k - 1], here.at(z=zk[k]))
    for n, f_ in enumerate((f2, f3, f4)):
        links.arrived(nrecv.at[n], gain_sems.at[n], here.at(f=f_))
    add_to(nparts.at[f], nrecv[0], nrecv[1], nrecv[2])
    for k in (1, 2, 3):
        links.send(("gain_z", k), nparts.at[f], nrecv.at[k + 2], gain_sems.at[k + 2], here.at(z=zk[k]))
    due("t5")
    for k in (1, 2, 3):
        links.arrived(qrecv3.at[k - 1], recv_sems.at[18, k - 1], here.at(z=zk[k]))
    small_total = qsend[0].astype(F32)
    for k in range(3):
        small_total = small_total + qrecv3[k].astype(F32)
    qsend[0] = small_total.astype(BF)
    links.send("small_core", qsend.at[0], qrecvc, core_sems.at[3], core)
    due("t6")
    for k in (1, 2, 3):
        links.arrived(nrecv.at[k + 2], gain_sems.at[k + 2], here.at(z=zk[k]))
    gain_total = nparts[f].astype(F32)
    for k in (3, 4, 5):
        gain_total = gain_total + nrecv[k].astype(F32)
    nback[...] = gain_total.astype(BF)
    links.send("gain_core", nback, nrecv.at[6], gain_sems.at[6], core)
    for k in (1, 2, 3):
        links.arrived(srecv3.at[k - 1], recv_sems.at[17, k - 1], here.at(z=zk[k]))
    total = state_part(f)[...].astype(F32)
    for k in range(3):
        total = total + srecv3[k].astype(F32)
    back = halfr.at[pl.ds(0, depth), pl.ds(512, 128)]
    back[...] = total.astype(BF)
    links.send("state_back", back, srecvc, core_sems.at[4], core)
    due("t7")
    gain_row = iota((SMALL, GW), 0) == 23
    links.arrived(qrecvc, core_sems.at[3], core)
    links.arrived(nrecv.at[6], gain_sems.at[6], core)
    gsmall_ref[...] = jnp.where(gain_row, gain_total[0:1, :], small_total)
    gother_ref[...] = jnp.where(gain_row, nrecv[6][0:1, :].astype(F32), qrecvc[...].astype(F32))
    links.arrived(srecvc, core_sems.at[4], core)
    rest = srecvc[...].astype(F32)
    gstate_ref[...] = jnp.concatenate([jnp.where(here.c == 0, total, rest), jnp.where(here.c == 0, rest, total)], 1)
    for side in range(2):
        loads[1, side].wait()
    results[staged[-1]].wait()
    links.finish(core_sems.at[0], core)


def block_call(model, hidden, *args):
    rows = hidden.shape[0]
    depth = model // 4
    any_ = pl.BlockSpec(memory_space=pl.ANY)
    sds = jax.ShapeDtypeStruct
    block = (GW, GW)
    part = (depth, 128)
    small = (SMALL, GW)

    def v(kind, *shape):
        return pltpu.VMEM(shape, kind)

    return pl.pallas_call(
        functools.partial(block_kernel, model),
        out_shape=(
            sds((rows, model), BF), sds((rows, model), BF),
            sds((model, SEQ), BF), sds((4, model, 2 * GW), BF), sds((4, SEQ, 2 * GW), F32), sds((4, CH, 128, GW), BF),
            sds(block, F32), sds(block, F32), sds(block, F32), sds((depth, 256), F32), sds(small, F32), sds(small, F32),
        ),
        in_specs=[any_] * 5 + [vm()] * (len(args) - 4),
        out_specs=tuple([any_] * 9 + [vm()] * 3),
        scratch_shapes=[
            v(BF, SEQ, model), v(BF, SEQ, model), v(BF, 4, model, 2 * GW), v(BF, 4, GW, model),
            v(F32, 2, SEQ + 8, 2 * GW), v(F32, SEQ, 2 * GW), v(BF, model, SEQ), v(BF, 4, SEQ, GW), v(BF, CH, 128, GW),
            v(BF, SEQ, 2 * GW), v(BF, 4, 2, GW, GW), v(BF, 4, GW, GW), v(BF, 3, 3, GW, GW), v(F32, GW, GW),
            v(BF, *small), v(BF, 4, 4, *small), v(BF, 4, depth, 256), v(F32, SEQ + 8, 256),
            v(F32, SEQ, 128), v(F32, SEQ, 128), v(F32, SEQ, 128), v(F32, CH, L),
            v(BF, SEQ, 256), v(BF, CH, 256, L), v(F32, CH, L, L), v(F32, 2, SEQ, 128), v(F32, 4, CH, 8, L),
            v(F32, 4, 8, GW), v(F32, 8, 128), v(F32, 8, 256), v(BF, 64, model), v(F32, 8, model), v(F32, 4, 8, GW),
            v(F32, 128, GW),
            v(BF, 4, *part), v(BF, 3, *part), v(BF, 3, *part), v(BF, *part),
            v(BF, 3, 4 * SMALL, GW), v(BF, 3, *small), v(BF, 4, *small), v(BF, *small),
            v(BF, 4, 16, GW), v(BF, 7, 16, GW), v(BF, 16, GW),
            v(BF, SEQ, 128), v(BF, SEQ, 256), v(F32, 4, 8, GW), v(F32, 8, 128), v(F32, 8, 256), v(F32, 128, GW),
            v(F32, CH, L, L), v(F32, SEQ, 256),
            pltpu.SemaphoreType.DMA((144,)),
            pltpu.SemaphoreType.DMA((3, 4, 4)),
            pltpu.SemaphoreType.DMA((7,)),
            pltpu.SemaphoreType.DMA((6,)),
            pltpu.SemaphoreType.DMA((4,)),
            pltpu.SemaphoreType.DMA((19, 4)),
            pltpu.SemaphoreType.DMA((5,)),
            pltpu.SemaphoreType.DMA((4,)),
            pltpu.SemaphoreType.DMA((7,)),
            pltpu.SemaphoreType.DMA((16,)),
            pltpu.SemaphoreType.DMA((4,)),
            pltpu.SemaphoreType.DMA((4,)),
            pltpu.SemaphoreType.DMA((4,)),
            pltpu.SemaphoreType.DMA((8,)),
            pltpu.SemaphoreType.DMA((3,)),
            pltpu.SemaphoreType.DMA((5,)),
            pltpu.SemaphoreType.REGULAR,
            pltpu.SemaphoreType.REGULAR,
            pltpu.SemaphoreType.REGULAR,
            pltpu.SemaphoreType.REGULAR,
        ],
        compiler_params=pltpu.CompilerParams(vmem_limit_bytes=VMEM_LIMIT, collective_id=1, has_side_effects=True),
        name="whole_block",
    )(hidden, *args)


def exact(values, places):
    return sum(mm(part, places, ((1,), (1,))) for part in split3(values))


def finish_kernel(layer_in, hidden_in, gate_in, inner_in, out_in, state_in, own_ref, other_ref,
                  layer_out, hidden_out, gain_out, gate_out, inner_out, state_out, step_out, conv_out, shift_out, cst_out,
                  cst_shift_out, offset_out, rate_out, skip_out, inner_gain_out, out_out, sems):
    pairs = [(layer_in, layer_out), (hidden_in, hidden_out), (gate_in, gate_out), (inner_in, inner_out), (out_in, out_out),
             (state_in, state_out)]
    copies = [pltpu.make_async_copy(a, b, sems.at[n]) for n, (a, b) in enumerate(pairs)]
    for copy in copies:
        copy.start()
    f, core = lax.axis_index("fsdp"), lax.axis_index("core")
    own, other = own_ref[...], other_ref[...]
    shared = own + other
    gain_out[...] = shared[23:24].reshape(GW)
    step_out[...] = own[:GH]
    unit = conv_out.shape[2]
    heads = iota((8, GW), 1) >> 6 == iota((8, GW), 0)
    rows = [jnp.where(heads, own[r : r + 1], 0.0) for r in range(16, 22)]
    picked = exact(jnp.concatenate(rows, 0), own_block(f, unit, unit))
    for k in range(K):
        conv_out[:, k : k + 1, :] = picked[8 * k : 8 * k + GH].reshape(GH, 1, unit)
    shift_out[...] = picked[8 * K : 8 * K + GH]
    inner_gain_out[...] = picked[8 * K + 8 : 8 * K + 8 + GH]
    size = cst_out.shape[1]
    states = exact(shared[24:32], at_block(f, size, size))
    cst_out[...] = states[:K]
    cst_shift_out[...] = states[K : K + 1].reshape(size)
    place, lane = iota((16, GW), 0), iota((16, GW), 1)
    lower = ((lane == 16 * f + place) & (place < GH)).astype(BF)
    upper = ((lane == 16 * f + place - GH) & (place >= GH) & (place < 2 * GH)).astype(BF)
    first = jnp.where(core == 0, own[24:32], other[24:32])
    second = jnp.where(core == 0, other[24:32], own[24:32])
    per_head = exact(first, lower) + exact(second, upper)
    rate_out[...] = per_head[5:6, : 2 * GH].reshape(2 * GH)
    offset_out[...] = per_head[6:7, : 2 * GH].reshape(2 * GH)
    skip_out[...] = per_head[7:8, : 2 * GH].reshape(2 * GH)
    for copy in copies:
        copy.wait()


def finish_call(*args):
    any_ = pl.BlockSpec(memory_space=pl.ANY)
    sds = jax.ShapeDtypeStruct
    layer, hidden, gate, inner, out, state = [sds(v.shape, v.dtype) for v in args[:6]]
    return pl.pallas_call(
        finish_kernel,
        out_shape=(
            layer, hidden, sds((GW,), F32), gate, inner, state, sds((GH, GW), F32), sds((GH, K, 16), F32), sds((GH, 16), F32),
            sds((K, 64), F32), sds((64,), F32), sds((2 * GH,), F32), sds((2 * GH,), F32), sds((2 * GH,), F32),
            sds((GH, 16), F32), out,
        ),
        in_specs=[vm()] * 8,
        out_specs=tuple([any_] * 2 + [vm()] + [any_] * 3 + [vm()] * 9 + [any_]),
        scratch_shapes=[pltpu.SemaphoreType.DMA((6,))],
        compiler_params=pltpu.CompilerParams(vmem_limit_bytes=VMEM_LIMIT),
        name="finish",
    )(*args)


def on_device(fsdp, halves, hidden_in, norm_gain, in_gate, in_inner, in_state, in_step, conv_inner, conv_inner_shift,
              conv_state, conv_state_shift, step_offset, log_rate, skip_gain, inner_gain, out_weight, segment_ids,
              grad_out):
    both = ("fsdp", "zz")
    depth, width = in_gate.shape
    model = depth * fsdp
    inner = width * halves
    heads_dev = in_step.shape[1]
    heads = heads_dev * halves
    heads_all = 2 * heads
    unit = conv_inner.shape[2] * fsdp
    inner_all = 2 * inner
    core = lax.axis_index("core")
    zz = lax.axis_index("zz")
    rows = hidden_in.shape[0]

    def swap(x):
        return lax.ppermute(x, "core", [(0, 1), (1, 0)])

    def both_cores(own, other):
        return jnp.where(core == 0, jnp.concatenate([own, other], 0), jnp.concatenate([other, own], 0))

    small = [norm_gain, in_step, conv_inner, conv_inner_shift, conv_state, conv_state_shift, step_offset, log_rate,
             skip_gain, inner_gain]
    flat = jnp.concatenate([v.reshape(-1) for v in small])
    got = lax.all_gather(flat, both, axis=0).reshape(fsdp, halves, -1)
    parts = []
    at = 0
    for v in small:
        parts.append(got[:, :, at : at + v.size].reshape((fsdp, halves) + v.shape))
        at += v.size
    gain_outer = parts[0][:, 0].reshape(model).astype(F32)
    step_cols = parts[1].transpose(0, 2, 1, 3).reshape(model, heads)
    conv_in = parts[2].transpose(2, 1, 3, 0, 4).reshape(K, inner).astype(F32)
    shift_in = parts[3].transpose(1, 2, 0, 3).reshape(1, inner).astype(F32)
    conv_st = parts[4][:, 0].transpose(1, 0, 2).reshape(K, -1).astype(F32)
    shift_st = parts[5][:, 0].reshape(1, -1).astype(F32)
    gain_in = parts[9].transpose(1, 2, 0, 3).reshape(1, inner).astype(F32)

    def my_heads(v):
        return v.reshape(halves, 2, heads_dev)[:, core].reshape(heads).astype(F32)

    offset = my_heads(parts[6][:, 0].reshape(heads_all))
    decay = -jnp.exp(my_heads(parts[7][:, 0].reshape(heads_all)))
    skip = my_heads(parts[8][:, 0].reshape(heads_all))
    state_cols = lax.all_gather(in_state, "fsdp", axis=0, tiled=True)

    def columns(w):
        return lax.all_gather(w, both, axis=0).reshape(fsdp, halves, depth, width).transpose(0, 2, 1, 3).reshape(model, inner)

    inner_cols = columns(in_inner)
    gate_cols = columns(in_gate)
    out_rows = lax.all_gather(out_weight, both, axis=0).reshape(fsdp, halves, width, depth).transpose(1, 2, 0, 3).reshape(inner, model)

    par = jnp.concatenate([conv_in, shift_in, jnp.repeat(skip, unit)[None], gain_in, jnp.zeros((1, inner), F32)], 0)
    convst = jnp.concatenate([conv_st, shift_st, jnp.zeros((3, 256), F32)], 0)
    head = jnp.pad(jnp.stack([offset, decay]), ((0, 6), (0, 128 - heads)))
    decay_g = jnp.pad(decay.reshape(heads // GH, 1, GH), ((0, 0), (0, 7), (0, 128 - GH)))

    docs = lax.dynamic_slice_in_dim(segment_ids, zz * SEQ, SEQ)
    blocks = docs.reshape(CH, L)
    prior = jnp.concatenate([jnp.full((1,), -1, docs.dtype), blocks[:-1, -1]])
    masks = [docs, (blocks == prior[:, None]).reshape(SEQ), (blocks == blocks[:, -1:]).reshape(SEQ)]
    for k in range(1, K):
        masks.append(jnp.concatenate([jnp.zeros((k,), bool), docs[k:] == docs[:-k]]))
    for k in range(1, K):
        masks.append(jnp.concatenate([docs[k:] == docs[:-k], jnp.zeros((k,), bool)]))
    tok = jnp.pad(jnp.stack([m.astype(F32) for m in masks], 1), ((0, 0), (0, 128 - len(masks))))
    row = jnp.broadcast_to(blocks.astype(F32)[:, None, :], (CH, 8, L))

    hidden_all = both_cores(hidden_in, swap(hidden_in)).astype(F32)
    cot_all = both_cores(grad_out, swap(grad_out))
    inv_rms = lax.rsqrt(jnp.mean(hidden_all * hidden_all, -1, keepdims=True) + EPSILON)
    normed = (hidden_all * inv_rms * gain_outer).astype(BF)
    small_cols = jnp.concatenate([state_cols, jnp.pad(step_cols, ((0, 0), (0, 128 - heads)))], 1)
    pre_small = mm(normed, small_cols)
    state_pre = pre_small[:, :256]
    step_pre = pre_small[:, 256:]
    inner_pre = mm(normed, inner_cols)
    gate_pre = mm(normed, gate_cols)
    bc, bct, gs, pack, cumt = prep(state_pre, step_pre, tok, row, convst, head)
    gated, states, ss = fwd(inner_pre, gate_pre, par, tok, bc, bct, gs, pack, cumt)
    ss_own = jnp.sum(ss, -1)
    squares = ss_own + swap(ss_own)
    inner_inv = lax.rsqrt(squares / inner_all + EPSILON)[:, None]
    normed_inner = (gated * inner_inv * gain_in).astype(BF)
    mixed = mm(normed_inner, out_rows)

    def to_own(x):
        own = lax.dynamic_slice_in_dim(x, core * rows, rows)
        other = lax.dynamic_slice_in_dim(x, (1 - core) * rows, rows)
        return own + swap(other.astype(BF)).astype(F32)

    layer_out = (hidden_in.astype(F32) + to_own(mixed)).astype(BF)
    grad_out_part = mm(normed_inner, cot_all, ((0,), (0,)))
    d_inner = mm(cot_all, out_rows, ((1,), (1,)))
    grad_gain_in = jnp.sum(d_inner * gated * inner_inv, 0)
    prod_own = jnp.sum(gated * d_inner * gain_in, -1)
    products = prod_own + swap(prod_own)
    inv_pack = jnp.pad(
        jnp.stack([inner_inv[:, 0], inner_inv[:, 0] ** 3 * products / inner_all], 1), ((0, 0), (0, 126))
    )
    d_gate, d_pre, d_step, d_state, pgrad, hgrad, sgrad = bwd(
        inner_pre, gate_pre, d_inner, par, tok, inv_pack, bc, bct, gs, pack, cumt, states, decay_g, state_pre, convst, row
    )
    d_step = d_step.astype(BF)
    d_small = jnp.concatenate([d_state, d_step], 1)
    d_normed = to_own(
        mm(d_gate, gate_cols, ((1,), (1,))) + mm(d_pre, inner_cols, ((1,), (1,))) + mm(d_small, small_cols, ((1,), (1,)))
    )
    hidden = hidden_in.astype(F32)
    inv_own = lax.dynamic_slice_in_dim(inv_rms, core * rows, rows)
    grad_gain_outer = jnp.sum(d_normed * hidden * inv_own, 0)
    weighted_back = d_normed * gain_outer
    d_hidden = inv_own * weighted_back - hidden * inv_own**3 * jnp.mean(hidden * weighted_back, -1, keepdims=True)
    grad_hidden = (grad_out.astype(F32) + d_hidden).astype(BF)

    def scatter_columns(g):
        g = g.astype(BF).reshape(fsdp, depth, halves, width).transpose(0, 2, 1, 3).reshape(fsdp * halves, depth, width)
        return lax.psum_scatter(g, both, scatter_dimension=0).astype(F32)

    grad_gate = scatter_columns(mm(normed, d_gate, ((0,), (0,))))
    grad_inner = scatter_columns(mm(normed, d_pre, ((0,), (0,))))
    grad_small = mm(normed, d_small, ((0,), (0,)))
    grad_out_weight = grad_out_part.astype(BF).reshape(halves, width, fsdp, depth).transpose(2, 0, 1, 3)
    grad_out_weight = lax.psum_scatter(
        grad_out_weight.reshape(fsdp * halves, width, depth), both, scatter_dimension=0
    ).astype(F32)
    grad_state = lax.psum_scatter(grad_small[:, :256].astype(BF), "fsdp", scatter_dimension=0, tiled=True)
    grad_state = lax.psum(grad_state, ("zz", "core")).astype(F32)

    own_heads = [
        grad_small[:, 256 : 256 + heads].reshape(fsdp, depth, halves, heads_dev).transpose(0, 2, 1, 3),
        pgrad[:K].reshape(K, halves, heads_dev, fsdp, -1).transpose(3, 1, 0, 2, 4),
        pgrad[K].reshape(halves, heads_dev, fsdp, -1).transpose(2, 0, 1, 3),
        grad_gain_in.reshape(halves, heads_dev, fsdp, -1).transpose(2, 0, 1, 3),
    ]
    sizes = [v.shape[2:] for v in own_heads]
    stacked = jnp.concatenate([v.reshape(fsdp * halves, -1) for v in own_heads], 1)
    mine = lax.psum_scatter(stacked, both, scatter_dimension=0)
    outs = []
    at = 0
    for s in sizes:
        n = 1
        for d in s:
            n *= d
        outs.append(mine[at : at + n].reshape(s))
        at += n
    grad_step, grad_conv_in, grad_conv_in_shift, grad_gain_inner = outs

    def place(v):
        v = v.reshape(halves, 1, heads_dev)
        zero = jnp.zeros_like(v)
        return jnp.where(core == 0, jnp.concatenate([v, zero], 1), jnp.concatenate([zero, v], 1)).reshape(heads_all)

    skip_sum = jnp.sum(pgrad[P_SKIP].reshape(heads, unit), 1)
    shared = [grad_gain_outer.reshape(fsdp, depth), sgrad[:K].reshape(K, fsdp, -1).transpose(1, 0, 2), sgrad[K].reshape(fsdp, -1)]
    shared += [place(v).reshape(fsdp, -1) for v in (hgrad[1, :heads], hgrad[0, :heads], skip_sum)]
    sizes = [v.shape[1:] for v in shared]
    stacked = jnp.concatenate([v.reshape(fsdp, -1) for v in shared], 1)
    mine = lax.psum(stacked, ("fsdp", "zz", "core"))
    mine = lax.dynamic_index_in_dim(mine, lax.axis_index("fsdp"), keepdims=False)
    outs = []
    at = 0
    for s in sizes:
        n = 1
        for d in s:
            n *= d
        outs.append(mine[at : at + n].reshape(s))
        at += n
    grad_norm_gain, grad_conv_st, grad_conv_st_shift, grad_offset, grad_rate, grad_skip = outs
    return (layer_out, grad_hidden, grad_norm_gain, grad_gate, grad_inner, grad_state, grad_step, grad_conv_in,
            grad_conv_in_shift, grad_conv_st, grad_conv_st_shift, grad_offset, grad_rate, grad_skip, grad_gain_inner,
            grad_out_weight)


def on_chip(hidden_in, norm_gain, in_gate, in_inner, in_state, in_step, conv_inner, conv_inner_shift, conv_state,
            conv_state_shift, step_offset, log_rate, skip_gain, inner_gain, out_weight, segment_ids, grad_out):
    model = in_gate.shape[0] * 4
    result = block_call(
        model, hidden_in, grad_out, in_inner, in_gate, out_weight, in_state, norm_gain, in_step.T,
        conv_inner.transpose(1, 0, 2), conv_inner_shift, inner_gain, conv_state, conv_state_shift, step_offset, log_rate,
        skip_gain, segment_ids.reshape(-1, L),
    )
    layer_out, grad_hidden, g_inner, g_gate, g_out, g_state, own, other = result[:2] + result[6:]
    outs = list(finish_call(layer_out, grad_hidden, g_gate, g_inner, g_out, g_state, own, other))
    outs[6] = outs[6].T
    outs[7] = outs[7].transpose(1, 0, 2)
    return tuple(outs)


def solution(mesh):
    fsdp = mesh.shape["fsdp"]
    halves = mesh.shape["tensor"] // 2
    fine = jax.sharding.Mesh(mesh.devices.reshape(fsdp, halves, 2), ("fsdp", "zz", "core"))
    tensor = ("zz", "core")
    tokens = P(("fsdp", "zz", "core"), None)
    grid = P("fsdp", tensor)
    heads = P(tensor, "fsdp")
    return jax.shard_map(
        on_chip if (fsdp, halves) == (4, 4) else functools.partial(on_device, fsdp, halves),
        mesh=fine,
        in_specs=(
            tokens, P("fsdp"), grid, grid, P("fsdp", None), grid, P(None, tensor, "fsdp"), heads, P(None, "fsdp"),
            P("fsdp"), P("fsdp"), P("fsdp"), P("fsdp"), heads, heads, P("fsdp"), tokens,
        ),
        out_specs=(
            tokens, tokens, P("fsdp"), grid, grid, P("fsdp", None), grid, P(None, tensor, "fsdp"), heads,
            P(None, "fsdp"), P("fsdp"), P("fsdp"), P("fsdp"), P("fsdp"), heads, heads,
        ),
        check_vma=False,
    )
```

```python
import functools

import jax
import jax.numpy as jnp
from jax import lax
from jax.sharding import PartitionSpec as P
from jax.experimental import pallas as pl
from jax.experimental.pallas import tpu as pltpu

SEQ = 1024
L = 128
CH = SEQ // L
K = 4
GH = 6
GW = 384
EPSILON = 1e-05
LOG2E = 1.4426950408889634
F32 = jnp.float32
BF = jnp.bfloat16
ST, CU, EE, FF, SG = 0, 8, 16, 24, 32


def mm(a, b, dims=((1,), (0,))):
    return lax.dot_general(a, b, (dims, ((), ())), preferred_element_type=F32)


def split2(x):
    hi = x.astype(BF)
    return hi, (x - hi.astype(F32)).astype(BF)


def split3(x):
    hi = x.astype(BF)
    rest = x - hi.astype(F32)
    mid = rest.astype(BF)
    return hi, mid, (rest - mid.astype(F32)).astype(BF)


def sigmoid(v):
    return 1.0 / (1.0 + jnp.exp(-v))


def back_conv_input(window, k):
    return window[8 - k : 8 - k + L]


def prep_body(state_ref, step_ref, tok_ref, row_ref, convst_ref, head_ref,
              bc_ref, bct_ref, g_ref, pack_ref, cumt_ref, pad_ref):
    pad_ref[pl.ds(0, 8), :] = jnp.zeros((8, 256), F32)
    pad_ref[pl.ds(8, SEQ), :] = state_ref[...]
    lane = lax.broadcasted_iota(jnp.int32, (L, L), 1)
    sub = lax.broadcasted_iota(jnp.int32, (L, L), 0)
    tri = (sub >= lane).astype(BF)
    offset = head_ref[0:1, :]
    decay = head_ref[1:2, :]
    taps = [convst_ref[k : k + 1, :] for k in range(K)]
    shift = convst_ref[K : K + 1, :]

    def chunk(c, _):
        base = pl.multiple_of(c * L, L)
        rows = pl.ds(base, L)
        tok = tok_ref[rows, :]
        window = pad_ref[pl.ds(base, L + 8), :]
        total = shift + taps[K - 1] * back_conv_input(window, 0)
        for k in range(1, K):
            total = total + taps[K - 1 - k] * (back_conv_input(window, k) * tok[:, 2 + k : 3 + k])
        act = total * sigmoid(total)
        low = act.astype(BF)
        bc_ref[rows, :] = low
        bct_ref[c] = jnp.concatenate([act[:, :128].T, act[:, 128:].T], 0).astype(BF)
        scores = mm(low[:, 128:], low[:, :128], ((1,), (1,)))
        same = (tok[:, 0:1] == row_ref[c][0:1, :]) & (sub >= lane)
        g_ref[c] = jnp.where(same, scores, 0.0)
        v = step_ref[rows, :] + offset
        steps = jnp.maximum(v, 0.0) + jnp.log1p(jnp.exp(-jnp.abs(v)))
        logs = steps * (decay * LOG2E)
        hi, mid, lo = split3(logs)
        cum = mm(tri, hi) + mm(tri, mid) + mm(tri, lo)
        last = cum[L - 1 : L, :]
        enter = jnp.exp2(cum) * tok[:, 1:2]
        leave = jnp.exp2(last - cum) * tok[:, 2:3]
        sig = sigmoid(v)
        cumt = cum.T
        zeros = jnp.zeros((L, 2), F32)
        for g in range(4):
            part = slice(GH * g, GH * g + GH)
            pieces = []
            for values in (steps, cum, enter, leave, sig):
                pieces += [values[:, part], zeros]
            pieces.append(jnp.zeros((L, 88), F32))
            pack_ref[g, rows, :] = jnp.concatenate(pieces, 1)
            cumt_ref[g, c] = jnp.concatenate([cumt[part, :], jnp.zeros((2, L), F32)], 0)
        return 0

    lax.fori_loop(0, CH, chunk, 0)


def vm(*shape):
    return pl.BlockSpec(memory_space=pltpu.VMEM)


def prep(state_pre, step_pre, tok, row, convst, head):
    return pl.pallas_call(
        prep_body,
        out_shape=(
            jax.ShapeDtypeStruct((SEQ, 256), BF),
            jax.ShapeDtypeStruct((CH, 256, L), BF),
            jax.ShapeDtypeStruct((CH, L, L), F32),
            jax.ShapeDtypeStruct((4, SEQ, 128), F32),
            jax.ShapeDtypeStruct((4, CH, 8, L), F32),
        ),
        in_specs=[vm()] * 6,
        out_specs=[vm()] * 5,
        scratch_shapes=[pltpu.VMEM((SEQ + 8, 256), F32)],
        compiler_params=pltpu.CompilerParams(vmem_limit_bytes=56 * 2**20),
        name="prep",
    )(state_pre, step_pre, tok, row, convst, head)


def pair_lanes(pack, first, q):
    lane = lax.broadcasted_iota(jnp.int32, (pack.shape[0], 128), 1)
    a = pack[:, first + 2 * q : first + 2 * q + 1]
    b = pack[:, first + 2 * q + 1 : first + 2 * q + 2]
    return jnp.where(lane < 64, a, b)


def spread(pack, first):
    return jnp.concatenate([pair_lanes(pack, first, q) for q in range(3)], 1)


def block_diag(x):
    lane = lax.broadcasted_iota(jnp.int32, x.shape, 1)
    zero = jnp.zeros_like(x)
    return jnp.concatenate([jnp.where(lane < 64, x, zero), jnp.where(lane < 64, zero, x)], 0)


def decay_kernel(pack, cumt, h):
    return jnp.exp2(jnp.minimum(pack[:, CU + h : CU + h + 1] - cumt[h : h + 1, :], 0.0))


def conv_of(window, tok, par):
    total = par[K : K + 1, :] + par[K - 1 : K, :] * back_conv_input(window, 0)
    for k in range(1, K):
        total = total + par[K - 1 - k : K - k, :] * (back_conv_input(window, k) * tok[:, 2 + k : 3 + k])
    return total


P_SHIFT, P_SKIP, P_GAIN = 4, 5, 6


def fwd_body(inner_ref, gate_ref, par_ref, tok_ref, bc_ref, bct_ref, g_ref, pack_ref, cumt_ref,
             gated_ref, states_ref, ss_ref, pad_ref, st_ref):
    pad_ref[pl.ds(0, 8), :] = jnp.zeros((8, GW), F32)
    pad_ref[pl.ds(8, SEQ), :] = inner_ref[...]
    st_ref[...] = jnp.zeros_like(st_ref)
    par = par_ref[...]

    @pl.when(pl.program_id(0) == 0)
    def _():
        ss_ref[...] = jnp.zeros_like(ss_ref)

    def chunk(c, _):
        base = pl.multiple_of(c * L, L)
        rows = pl.ds(base, L)
        tok = tok_ref[rows, :]
        u = conv_of(pad_ref[pl.ds(base, L + 8), :], tok, par)
        act = u * sigmoid(u)
        pack = pack_ref[0, rows, :]
        cumt = cumt_ref[0, c]
        g = g_ref[c]
        weighted = act * spread(pack, ST)
        low = weighted.astype(BF)
        enter = spread(pack, EE)
        state = st_ref[...]
        low_state = state.astype(BF)
        states_ref[0, c] = low_state
        y = mm(bc_ref[rows, 128:], low_state) * enter
        locals_ = []
        for q in range(3):
            kernels = [(g * decay_kernel(pack, cumt, 2 * q + e)).astype(BF) for e in range(2)]
            locals_.append(mm(jnp.concatenate(kernels, 1), block_diag(low[:, 128 * q : 128 * q + 128])))
        y = y + jnp.concatenate(locals_, 1)
        out = weighted * spread(pack, FF)
        st_ref[...] = enter[L - 1 : L, :] * state + mm(bct_ref[c, pl.ds(0, 128), :], out.astype(BF))
        ssd = y + par[P_SKIP : P_SKIP + 1, :] * act
        gate = gate_ref[rows, :]
        gated = ssd * (gate * sigmoid(gate))
        gated_ref[rows, :] = gated
        sq = gated * gated
        ss_ref[rows, :] += sq[:, :128] + sq[:, 128:256] + sq[:, 256:]
        return 0

    lax.fori_loop(0, CH, chunk, 0)


def whole_spec(shape):
    return pl.BlockSpec(shape, lambda g: (0,) * len(shape))


def fwd(inner_pre, gate_pre, par, tok, bc, bct, gs, pack, cumt):
    cols = pl.BlockSpec((SEQ, GW), lambda g: (0, g))
    return pl.pallas_call(
        fwd_body,
        grid=(4,),
        out_shape=(
            jax.ShapeDtypeStruct((SEQ, 4 * GW), F32),
            jax.ShapeDtypeStruct((4, CH, 128, GW), BF),
            jax.ShapeDtypeStruct((SEQ, 128), F32),
        ),
        in_specs=[
            cols, cols, pl.BlockSpec((8, GW), lambda g: (0, g)),
            whole_spec((SEQ, 128)), whole_spec((SEQ, 256)), whole_spec((CH, 256, L)), whole_spec((CH, L, L)),
            pl.BlockSpec((1, SEQ, 128), lambda g: (g, 0, 0)),
            pl.BlockSpec((1, CH, 8, L), lambda g: (g, 0, 0, 0)),
        ],
        out_specs=(
            cols,
            pl.BlockSpec((1, CH, 128, GW), lambda g: (g, 0, 0, 0)),
            whole_spec((SEQ, 128)),
        ),
        scratch_shapes=[pltpu.VMEM((SEQ + 8, GW), F32), pltpu.VMEM((128, GW), F32)],
        compiler_params=pltpu.CompilerParams(vmem_limit_bytes=56 * 2**20),
        name="mixer_forward",
    )(inner_pre, gate_pre, par, tok, bc, bct, gs, pack, cumt)


def bwd_body(inner_ref, gate_ref, dinner_ref, par_ref, tok_ref, inv_ref, bc_ref, bct_ref, g_ref, pack_ref,
             cumt_ref, states_ref, decay_ref, state_pre_ref, convst_ref, row_ref,
             dgate_ref, dpre_ref, dstep_ref, dstate_ref, pgrad_ref, hgrad_ref, sgrad_ref,
             pad_ref, rt_ref, dg_ref, dbc_ref, spad_ref):
    group = pl.program_id(0)
    pad_ref[pl.ds(0, 8), :] = jnp.zeros((8, GW), F32)
    pad_ref[pl.ds(8, SEQ), :] = inner_ref[...]
    rt_ref[...] = jnp.zeros_like(rt_ref)
    pgrad_ref[...] = jnp.zeros_like(pgrad_ref)
    par = par_ref[...]
    decay = decay_ref[0]

    @pl.when(group == 0)
    def _():
        dg_ref[...] = jnp.zeros_like(dg_ref)
        dbc_ref[...] = jnp.zeros_like(dbc_ref)
        dstep_ref[...] = jnp.zeros_like(dstep_ref)
        hgrad_ref[...] = jnp.zeros_like(hgrad_ref)

    lane = lax.broadcasted_iota(jnp.int32, (L, L), 1)
    sub = lax.broadcasted_iota(jnp.int32, (L, L), 0)
    upper = (sub <= lane).astype(BF)
    per_head = (lax.broadcasted_iota(jnp.int32, (GW, 128), 0) >> 6
                == lax.broadcasted_iota(jnp.int32, (GW, 128), 1)).astype(BF)

    def head_sums(x):
        hi, lo = split2(x)
        return mm(hi, per_head) + mm(lo, per_head)

    def chunk(step, later):
        c = CH - 1 - step
        base = pl.multiple_of(c * L, L)
        rows = pl.ds(base, L)
        tok = tok_ref[rows, :]
        window = pad_ref[pl.ds(base, L + 8), :]
        u = conv_of(window, tok, par)
        su = sigmoid(u)
        act = u * su
        pack = pack_ref[0, rows, :]
        cumt = cumt_ref[0, c]
        g = g_ref[c]
        steps = spread(pack, ST)
        enter = spread(pack, EE)
        leave = spread(pack, FF)
        weighted = act * steps
        low = weighted.astype(BF)
        low_state = states_ref[0, c]
        bmat = bc_ref[rows, :128]
        cmat = bc_ref[rows, 128:]
        diags = [block_diag(low[:, 128 * q : 128 * q + 128]) for q in range(3)]
        decays = [decay_kernel(pack, cumt, h) for h in range(GH)]
        kernels = [jnp.concatenate([(g * decays[2 * q + e]).astype(BF) for e in range(2)], 1) for q in range(3)]
        y = mm(cmat, low_state) * enter + jnp.concatenate([mm(kernels[q], diags[q]) for q in range(3)], 1)
        skip = par[P_SKIP : P_SKIP + 1, :]
        ssd = y + skip * act
        gate = gate_ref[rows, :]
        sg = sigmoid(gate)
        silu = gate * sg
        scaled = dinner_ref[rows, :] * par[P_GAIN : P_GAIN + 1, :]
        inv = inv_ref[rows, :]
        d_gated = inv[:, 0:1] * scaled - (ssd * silu) * inv[:, 1:2]
        dy = d_gated * silu
        dgate_ref[rows, :] = (d_gated * ssd * sg * (1.0 + gate * (1.0 - sg))).astype(BF)
        dy_low = dy.astype(BF)
        dy_in = (dy * enter).astype(BF)
        rt = rt_ref[...]
        rt_low = rt.astype(BF)
        carried = mm(bmat, rt_low) * leave
        pieces = []
        d_scores = jnp.zeros((L, L), F32)
        for q in range(3):
            dq = dy_low[:, 128 * q : 128 * q + 128]
            dm = mm(dq, diags[q], ((1,), (1,)))
            d_scores = d_scores + dm[:, :L] * decays[2 * q] + dm[:, L:] * decays[2 * q + 1]
            both = mm(kernels[q], dq, ((0,), (0,)))
            pieces.append(jnp.where(lane < 64, both[:L], both[L:]))
        d_weighted = jnp.concatenate(pieces, 1) + carried
        dg_ref[c] += d_scores
        out = (weighted * leave).astype(BF)
        dbc_ref[rows, 128:] += mm(dy_in, low_state, ((1,), (1,)))
        dbc_ref[rows, :128] += mm(out, rt_low, ((1,), (1,)))
        keep = enter[L - 1 : L, :]
        low32 = low.astype(F32)
        d_cum = head_sums(dy_low.astype(F32) * y - low32 * d_weighted)
        at_end = jnp.sum(low32 * carried, 0, keepdims=True) + keep * jnp.sum(rt * low_state.astype(F32), 0, keepdims=True)
        d_last = head_sums(jnp.concatenate([at_end, jnp.zeros((7, GW), F32)], 0))[0:1, :]
        hi, mid, lo = split3(d_cum)
        d_log = mm(upper, hi) + mm(upper, mid) + mm(upper, lo) + d_last
        rt_ref[...] = keep * rt + mm(bct_ref[c, pl.ds(128, 128), :], dy_in)
        d_step = head_sums(act * d_weighted) + decay[0:1, :] * d_log
        heads = lane < GH
        d_step_pre = jnp.where(heads, d_step * jnp.roll(pack, -SG, 1), 0.0)
        dstep_ref[rows, :] += pltpu.roll(d_step_pre, GH * group, 1)
        rate = jnp.sum(jnp.where(heads, pack, 0.0) * d_log, 0, keepdims=True) * decay[0:1, :]
        offs = jnp.sum(d_step_pre, 0, keepdims=True)
        hgrad_ref[0:1, :] += pltpu.roll(jnp.concatenate([rate, jnp.zeros((7, 128), F32)], 0), GH * group, 1)[0:1]
        hgrad_ref[1:2, :] += pltpu.roll(jnp.concatenate([offs, jnp.zeros((7, 128), F32)], 0), GH * group, 1)[0:1]
        d_act = skip * dy + steps * d_weighted
        du = d_act * su * (1.0 + u * (1.0 - su))
        pgrad_ref[K : K + 1, :] += jnp.sum(du, 0, keepdims=True)
        pgrad_ref[P_SKIP : P_SKIP + 1, :] += jnp.sum(dy * act, 0, keepdims=True)
        for k in range(K):
            moved = back_conv_input(window, k)
            if k:
                moved = moved * tok[:, 2 + k : 3 + k]
            pgrad_ref[K - 1 - k : K - k, :] += jnp.sum(du * moved, 0, keepdims=True)
        ahead = jnp.concatenate([du, later], 0)
        d_pre = par[K - 1 : K, :] * du
        for k in range(1, K):
            d_pre = d_pre + par[K - 1 - k : K - k, :] * (ahead[k : k + L] * tok[:, 5 + k : 6 + k])
        dpre_ref[rows, :] = d_pre.astype(BF)
        return du[:8]

    lax.fori_loop(0, CH, chunk, jnp.zeros((8, GW), F32))

    @pl.when(group == pl.num_programs(0) - 1)
    def _():
        spad_ref[pl.ds(0, 8), :] = jnp.zeros((8, 256), F32)
        spad_ref[pl.ds(8, SEQ), :] = state_pre_ref[...]
        sgrad_ref[...] = jnp.zeros_like(sgrad_ref)
        cst = convst_ref[...]

        def last(step, later):
            c = CH - 1 - step
            base = pl.multiple_of(c * L, L)
            rows = pl.ds(base, L)
            tok = tok_ref[rows, :]
            same = (tok[:, 0:1] == row_ref[c][0:1, :]) & (sub >= lane)
            ds = jnp.where(same, dg_ref[c], 0.0).astype(BF)
            d_c = dbc_ref[rows, 128:] + mm(ds, bc_ref[rows, :128])
            d_b = dbc_ref[rows, :128] + mm(ds, bc_ref[rows, 128:], ((0,), (0,)))
            window = spad_ref[pl.ds(base, L + 8), :]
            w = conv_of(window, tok, cst)
            sw = sigmoid(w)
            dw = jnp.concatenate([d_b, d_c], 1) * (sw * (1.0 + w * (1.0 - sw)))
            sgrad_ref[K : K + 1, :] += jnp.sum(dw, 0, keepdims=True)
            for k in range(K):
                moved = back_conv_input(window, k)
                if k:
                    moved = moved * tok[:, 2 + k : 3 + k]
                sgrad_ref[K - 1 - k : K - k, :] += jnp.sum(dw * moved, 0, keepdims=True)
            ahead = jnp.concatenate([dw, later], 0)
            d_pre = cst[K - 1 : K, :] * dw
            for k in range(1, K):
                d_pre = d_pre + cst[K - 1 - k : K - k, :] * (ahead[k : k + L] * tok[:, 5 + k : 6 + k])
            dstate_ref[rows, :] = d_pre.astype(BF)
            return dw[:8]

        lax.fori_loop(0, CH, last, jnp.zeros((8, 256), F32))


def bwd(inner_pre, gate_pre, d_inner, par, tok, inv, bc, bct, gs, pack, cumt, states, decay, state_pre, convst, row):
    cols = pl.BlockSpec((SEQ, GW), lambda g: (0, g))
    pcol = pl.BlockSpec((8, GW), lambda g: (0, g))
    return pl.pallas_call(
        bwd_body,
        grid=(4,),
        out_shape=(
            jax.ShapeDtypeStruct((SEQ, 4 * GW), BF),
            jax.ShapeDtypeStruct((SEQ, 4 * GW), BF),
            jax.ShapeDtypeStruct((SEQ, 128), F32),
            jax.ShapeDtypeStruct((SEQ, 256), BF),
            jax.ShapeDtypeStruct((8, 4 * GW), F32),
            jax.ShapeDtypeStruct((8, 128), F32),
            jax.ShapeDtypeStruct((8, 256), F32),
        ),
        in_specs=[
            cols, cols, cols, pcol,
            whole_spec((SEQ, 128)), whole_spec((SEQ, 128)), whole_spec((SEQ, 256)), whole_spec((CH, 256, L)),
            whole_spec((CH, L, L)),
            pl.BlockSpec((1, SEQ, 128), lambda g: (g, 0, 0)),
            pl.BlockSpec((1, CH, 8, L), lambda g: (g, 0, 0, 0)),
            pl.BlockSpec((1, CH, 128, GW), lambda g: (g, 0, 0, 0)),
            pl.BlockSpec((1, 8, 128), lambda g: (g, 0, 0)),
            whole_spec((SEQ, 256)), whole_spec((8, 256)), whole_spec((CH, 8, L)),
        ],
        out_specs=(
            cols, cols, whole_spec((SEQ, 128)), whole_spec((SEQ, 256)), pcol, whole_spec((8, 128)), whole_spec((8, 256)),
        ),
        scratch_shapes=[
            pltpu.VMEM((SEQ + 8, GW), F32),
            pltpu.VMEM((128, GW), F32),
            pltpu.VMEM((CH, L, L), F32),
            pltpu.VMEM((SEQ, 256), F32),
            pltpu.VMEM((SEQ + 8, 256), F32),
        ],
        compiler_params=pltpu.CompilerParams(vmem_limit_bytes=56 * 2**20),
        name="mixer_backward",
    )(inner_pre, gate_pre, d_inner, par, tok, inv, bc, bct, gs, pack, cumt, states, decay, state_pre, convst, row)


def prep_chunks(state_ref, step_ref, tok_ref, row_ref, convst_ref, head_ref,
                bc_ref, bct_ref, g_ref, pack_ref, cumt_ref):
    lane = lax.broadcasted_iota(jnp.int32, (L, L), 1)
    sub = lax.broadcasted_iota(jnp.int32, (L, L), 0)
    tri = (sub >= lane).astype(BF)
    offset = head_ref[0:1, :]
    decay = head_ref[1:2, :]
    convst = convst_ref[...]

    def chunk(c, _):
        base = pl.multiple_of(c * L, L)
        rows = pl.ds(base, L)
        tok = tok_ref[rows, :]
        total = conv_of(state_ref[pl.ds(base, L + 8), :], tok, convst)
        act = total * sigmoid(total)
        low = act.astype(BF)
        bc_ref[rows, :] = low
        bct_ref[c] = jnp.concatenate([act[:, :128].T, act[:, 128:].T], 0).astype(BF)
        scores = mm(low[:, 128:], low[:, :128], ((1,), (1,)))
        same = (tok[:, 0:1] == row_ref[pl.ds(c, 1), :]) & (sub >= lane)
        g_ref[c] = jnp.where(same, scores, 0.0)
        v = step_ref[rows, :] + offset
        steps = jnp.maximum(v, 0.0) + jnp.log1p(jnp.exp(-jnp.abs(v)))
        logs = steps * (decay * LOG2E)
        hi, mid, lo = split3(logs)
        cum = mm(tri, hi) + mm(tri, mid) + mm(tri, lo)
        last = cum[L - 1 : L, :]
        enter = jnp.exp2(cum) * tok[:, 1:2]
        leave = jnp.exp2(last - cum) * tok[:, 2:3]
        sig = sigmoid(v)
        cumt = cum.T
        for g in range(4):
            cumt_ref[g, c] = cumt[16 * g : 16 * g + 8, :]
        for g in range(2):
            pieces = []
            for part in (slice(32 * g, 32 * g + 8), slice(32 * g + 16, 32 * g + 24)):
                pieces += [values[:, part] for values in (steps, cum, enter, leave, sig)] + [jnp.zeros((L, 24), F32)]
            pack_ref[g, rows, :] = jnp.concatenate(pieces, 1)
        return 0

    lax.fori_loop(0, CH, chunk, 0)


def spread_masks(tok):
    return [jnp.broadcast_to(tok[:, i : i + 1], (L, 128)) for i in range(3, 9)]


def pair_conv(window, masks, par):
    total = par[K : K + 1, :] + par[K - 1 : K, :] * back_conv_input(window, 0)
    moved = [back_conv_input(window, 0)]
    for k in range(1, K):
        moved.append(back_conv_input(window, k) * masks[k - 1])
        total = total + par[K - 1 - k : K - k, :] * moved[k]
    return total, moved


def fwd_chunks(group, tick, pre_ref, par_ref, tok_ref, bc_ref, bct_ref, g_ref, pack_ref, cumt_ref,
               gated_ref, states_ref, ss_ref, st_ref):
    st_ref[...] = jnp.zeros_like(st_ref)

    def chunk(c, _):
        tick(c)
        base = pl.multiple_of(c * L, L)
        rows = pl.ds(base, L)
        masks = spread_masks(tok_ref[rows, :])
        pack = pack_ref[rows, :]
        if group % 2:
            pack = pltpu.roll(pack, 64, 1)
        cumt = cumt_ref[c]
        g = g_ref[c]
        squares = jnp.zeros((L, 128), F32)
        for q in range(3):
            lanes = pl.ds(128 * q, 128)
            par = par_ref[:, lanes]
            u, _ = pair_conv(pre_ref[pl.ds(base, L + 8), lanes], masks, par)
            act = u * sigmoid(u)
            weighted = act * pair_lanes(pack, ST, q)
            kernels = [(g * decay_kernel(pack, cumt, 2 * q + e)).astype(BF) for e in range(2)]
            y = mm(jnp.concatenate(kernels, 1), block_diag(weighted.astype(BF)))
            enter = pair_lanes(pack, EE, q)
            state = st_ref[:, lanes]
            low_state = state.astype(BF)
            states_ref[c, :, lanes] = low_state
            y = y + mm(bc_ref[rows, 128:], low_state) * enter
            out = (weighted * pair_lanes(pack, FF, q)).astype(BF)
            st_ref[:, lanes] = enter[L - 1 : L, :] * state + mm(bct_ref[c, pl.ds(0, 128), :], out)
            ssd = y + par[P_SKIP : P_SKIP + 1, :] * act
            gate = pre_ref[pl.ds(base + 8, L), pl.ds(GW + 128 * q, 128)]
            gated = ssd * (gate * sigmoid(gate))
            gated_ref[rows, lanes] = gated.astype(BF)
            squares = squares + gated * gated
        ss_ref[rows, :] += squares
        return 0

    lax.fori_loop(0, CH, chunk, 0)


def bwd_chunks(group, z_k, tick, pre_ref, dinner_ref, par_ref, tok_ref, bc_ref, bct_ref, g_ref, pack_ref,
               cumt_ref, states_ref, hpar_ref, dcat_ref, dstep_ref, pgrad_ref, hgrad_ref, rt_ref, dg_ref, dbc_ref):
    rt_ref[...] = jnp.zeros_like(rt_ref)
    pgrad_ref[...] = jnp.zeros_like(pgrad_ref)
    decay = pltpu.roll(hpar_ref[...], (128 - 16 * group) % 128, 1)[1:2, :]
    lane = lax.broadcasted_iota(jnp.int32, (L, L), 1)
    sub = lax.broadcasted_iota(jnp.int32, (L, L), 0)
    upper = (sub <= lane).astype(BF)
    heads = lane < GH
    per_head = (lax.broadcasted_iota(jnp.int32, (GW, 128), 0) >> 6
                == lax.broadcasted_iota(jnp.int32, (GW, 128), 1)).astype(BF)

    def chunk(step, later):
        tick(step)
        c = CH - 1 - step
        base = pl.multiple_of(c * L, L)
        rows = pl.ds(base, L)
        tok = tok_ref[rows, :]
        masks = spread_masks(tok)
        inv = jnp.broadcast_to(tok[:, T_INV : T_INV + 1], (L, 128))
        inv_back = jnp.broadcast_to(tok[:, T_BACK : T_BACK + 1], (L, 128))
        pack = pack_ref[rows, :]
        if group % 2:
            pack = pltpu.roll(pack, 64, 1)
        cumt = cumt_ref[c]
        g = g_ref[c]
        d_scores = jnp.zeros((L, L), F32)
        to_sum = []
        d_c = dbc_ref[rows, 128:]
        d_b = dbc_ref[rows, :128]
        heads_of_pair = []
        for q in range(3):
            lanes = pl.ds(128 * q, 128)
            gate_lanes = pl.ds(GW + 128 * q, 128)
            par = par_ref[:, lanes]
            u, moved = pair_conv(pre_ref[pl.ds(base, L + 8), lanes], masks, par)
            su = sigmoid(u)
            act = u * su
            steps = pair_lanes(pack, ST, q)
            weighted = act * steps
            low = weighted.astype(BF)
            diag = block_diag(low)
            decays = [decay_kernel(pack, cumt, 2 * q + e) for e in range(2)]
            kernels = jnp.concatenate([(g * d).astype(BF) for d in decays], 1)
            enter = pair_lanes(pack, EE, q)
            low_state = states_ref[c, :, lanes]
            y = mm(bc_ref[rows, 128:], low_state) * enter + mm(kernels, diag)
            skip = par[P_SKIP : P_SKIP + 1, :]
            ssd = y + skip * act
            gate = pre_ref[pl.ds(base + 8, L), gate_lanes]
            sg = sigmoid(gate)
            silu = gate * sg
            scaled = dinner_ref[rows, lanes].astype(F32) * par[P_GAIN : P_GAIN + 1, :]
            d_gated = inv * scaled - (ssd * silu) * inv_back
            dy = d_gated * silu
            dcat_ref[rows, gate_lanes] = (d_gated * ssd * (sg + silu * (1.0 - sg))).astype(BF)
            dy_low = dy.astype(BF)
            dy_in = (dy * enter).astype(BF)
            d_c = d_c + mm(dy_in, low_state, ((1,), (1,)))
            dm = mm(dy_low, diag, ((1,), (1,)))
            d_scores = d_scores + dm[:, :L] * decays[0] + dm[:, L:] * decays[1]
            both = mm(kernels, dy_low, ((0,), (0,)))
            rt = rt_ref[:, lanes]
            rt_low = rt.astype(BF)
            leave = pair_lanes(pack, FF, q)
            carried = mm(bc_ref[rows, :128], rt_low) * leave
            d_weighted = jnp.where(lane < 64, both[:L], both[L:]) + carried
            d_b = d_b + mm((weighted * leave).astype(BF), rt_low, ((1,), (1,)))
            keep = enter[L - 1 : L, :]
            rt_ref[:, lanes] = keep * rt + mm(bct_ref[c, pl.ds(128, 128), :], dy_in)
            low32 = low.astype(F32)
            at_end = jnp.sum(low32 * carried, 0, keepdims=True)
            at_end = at_end + keep * jnp.sum(rt * low_state.astype(F32), 0, keepdims=True)
            cum_high, cum_low = split2(dy_low.astype(F32) * y - low32 * d_weighted)
            end_high, end_low = split2(jnp.concatenate([at_end, jnp.zeros((7, 128), F32)], 0))
            ends = jnp.concatenate([end_high, end_low], 0)
            to_sum.append(jnp.concatenate([cum_high, cum_low, (act * d_weighted).astype(BF), ends], 0))
            d_act = skip * dy + steps * d_weighted
            du = d_act * (su + act * (1.0 - su))
            pgrad_ref[K : K + 1, lanes] += jnp.sum(du, 0, keepdims=True)
            pgrad_ref[P_SKIP : P_SKIP + 1, lanes] += jnp.sum(dy * act, 0, keepdims=True)
            ahead = jnp.concatenate([du, later[:, 128 * q : 128 * q + 128]], 0)
            d_pre = par[K - 1 : K, :] * du
            for k in range(K):
                pgrad_ref[K - 1 - k : K - k, lanes] += jnp.sum(du * moved[k], 0, keepdims=True)
                if k:
                    d_pre = d_pre + par[K - 1 - k : K - k, :] * (ahead[k : k + L] * masks[2 + k])
            dcat_ref[rows, lanes] = d_pre.astype(BF)
            heads_of_pair.append(du[:8])
        dg_ref[c] += d_scores
        dbc_ref[rows, 128:] = d_c
        dbc_ref[rows, :128] = d_b
        sums = mm(jnp.concatenate(to_sum, 1), per_head)
        d_last = sums[3 * L : 3 * L + 1] + sums[3 * L + 8 : 3 * L + 9]
        hi, mid, lo = split3(sums[:L] + sums[L : 2 * L])
        parts = hi.astype(F32) + pltpu.roll(mid.astype(F32), 8, 1) + pltpu.roll(lo.astype(F32), 16, 1)
        d_log = mm(upper, parts.astype(BF))
        d_log = d_log + pltpu.roll(d_log, 120, 1) + pltpu.roll(d_log, 112, 1) + d_last
        d_step = sums[2 * L : 3 * L] + decay * d_log
        d_step_pre = jnp.where(heads, d_step * pltpu.roll(pack, 128 - SG, 1), 0.0)
        dstep_ref[rows, :] += pltpu.roll(d_step_pre, 16 * group, 1).astype(BF)
        rate = jnp.sum(jnp.where(heads, pack, 0.0) * d_log, 0, keepdims=True) * decay
        offs = jnp.sum(d_step_pre, 0, keepdims=True)
        hgrad_ref[0:1, :] += pltpu.roll(jnp.concatenate([rate, jnp.zeros((7, 128), F32)], 0), 16 * z_k, 1)[0:1]
        hgrad_ref[1:2, :] += pltpu.roll(jnp.concatenate([offs, jnp.zeros((7, 128), F32)], 0), 16 * z_k, 1)[0:1]
        return jnp.concatenate(heads_of_pair, 1)

    lax.fori_loop(0, CH, chunk, jnp.zeros((8, GW), F32))


def state_chunks(statepre_ref, cst_ref, tok_ref, row_ref, bc_ref, dg_ref, dbc_ref, dstate_ref, sgrad_ref):
    sgrad_ref[...] = jnp.zeros_like(sgrad_ref)
    cst = cst_ref[...]
    lane = lax.broadcasted_iota(jnp.int32, (L, L), 1)
    sub = lax.broadcasted_iota(jnp.int32, (L, L), 0)

    def last(step, later):
        c = CH - 1 - step
        base = pl.multiple_of(c * L, L)
        rows = pl.ds(base, L)
        tok = tok_ref[rows, :]
        same = (tok[:, 0:1] == row_ref[pl.ds(c, 1), :]) & (sub >= lane)
        ds = jnp.where(same, dg_ref[c], 0.0).astype(BF)
        d_c = dbc_ref[rows, 128:] + mm(ds, bc_ref[rows, :128])
        d_b = dbc_ref[rows, :128] + mm(ds, bc_ref[rows, 128:], ((0,), (0,)))
        window = statepre_ref[pl.ds(base, L + 8), :]
        w = conv_of(window, tok, cst)
        sw = sigmoid(w)
        dw = jnp.concatenate([d_b, d_c], 1) * (sw * (1.0 + w * (1.0 - sw)))
        sgrad_ref[K : K + 1, :] += jnp.sum(dw, 0, keepdims=True)
        for k in range(K):
            moved = back_conv_input(window, k)
            if k:
                moved = moved * tok[:, 2 + k : 3 + k]
            sgrad_ref[K - 1 - k : K - k, :] += jnp.sum(dw * moved, 0, keepdims=True)
        ahead = jnp.concatenate([dw, later], 0)
        d_pre = cst[K - 1 : K, :] * dw
        for k in range(1, K):
            d_pre = d_pre + cst[K - 1 - k : K - k, :] * (ahead[k : k + L] * tok[:, 5 + k : 6 + k])
        dstate_ref[rows, :] = d_pre.astype(BF)
        return dw[:8]

    lax.fori_loop(0, CH, last, jnp.zeros((8, 256), F32))


MESH = pl.DeviceIdType.MESH
VMEM_LIMIT = 63 * 2**20
R_GAIN, R_CONV, R_SHIFT, R_INNER, R_OFF, R_RATE, R_SKIP, R_CST = 6, 7, 11, 12, 13, 14, 15, 16
SMALL = 32


class Links:
    def __init__(self, send_sems):
        self.send_sems = send_sems
        self.number = {}
        self.like = {}
        self.ended = set()

    def send(self, name, src, dst, recv_sem, device, like=None):
        at = self.number.setdefault(name, len(self.number))
        self.like[name] = src if like is None else like
        pltpu.make_async_remote_copy(
            src_ref=src, dst_ref=dst, send_sem=self.send_sems.at[at], recv_sem=recv_sem,
            device_id=device, device_id_type=MESH,
        ).start()

    def arrived(self, dst, recv_sem, device):
        pltpu.make_async_remote_copy(
            src_ref=dst, dst_ref=dst, send_sem=self.send_sems.at[0], recv_sem=recv_sem,
            device_id=device, device_id_type=MESH,
        ).wait_recv()

    def left(self, name, recv_sem, device):
        self.ended.add(name)
        like = self.like[name]
        pltpu.make_async_remote_copy(
            src_ref=like, dst_ref=like, send_sem=self.send_sems.at[self.number[name]], recv_sem=recv_sem,
            device_id=device, device_id_type=MESH,
        ).wait_send()

    def finish(self, recv_sem, device):
        for name in self.number:
            if name not in self.ended:
                self.left(name, recv_sem, device)


OUT_MAIN = 256


class Place:
    def __init__(self):
        self.f = lax.axis_index("fsdp")
        self.z = lax.axis_index("zz")
        self.c = lax.axis_index("core")
        f, c = self.f, self.c
        y, x = f // 2, f % 2
        by_x = y * 2 + 1 - x
        by_y = (1 - y) * 2 + x
        self.f2 = by_x * (1 - c) + by_y * c
        self.f3 = by_y * (1 - c) + by_x * c
        self.f4 = 3 - f
        z_low, z_high = self.z % 2, self.z // 2
        self.zk = [((z_high + k // 2) % 2) * 2 + (z_low + k % 2) % 2 for k in range(4)]

    def at(self, f=None, z=None, c=None):
        return (self.f if f is None else f, self.z if z is None else z, self.c if c is None else c)

    def near(self):
        devices = [self.at(z=self.zk[k]) for k in (1, 2, 3)]
        return devices + [self.at(f=self.f2), self.at(f=self.f3), self.at(f=self.f4), self.at(c=1 - self.c)]

    def greet(self):
        for device in self.near():
            pl.semaphore_signal(pltpu.get_barrier_semaphore(), inc=1, device_id=device, device_id_type=MESH)

    def greeted(self):
        pl.semaphore_wait(pltpu.get_barrier_semaphore(), len(self.near()))


def piece(inout_ref, out_ref, m, f, z):
    depth = out_ref.shape[2] // 4
    at = pl.ds(pl.multiple_of(f * depth, depth), depth)
    if m == 2:
        return out_ref.at[z, pl.ds(0, OUT_MAIN), at]
    return inout_ref.at[z, at, pl.ds(m * GW, GW)]


def iota(shape, dim):
    return lax.broadcasted_iota(jnp.int32, shape, dim)


def own_block(f, rows, unit):
    return ((iota((rows, GW), 1) & 63) == f * unit + iota((rows, GW), 0)).astype(BF)


def at_block(f, rows, size):
    row = iota((rows, GW), 0)
    return ((iota((rows, GW), 1) == f * size + row) & (row < size)).astype(BF)


def spread_units(values, place):
    rows = mm(values, place)
    return jnp.sum(jnp.where((iota(rows.shape, 1) >> 6) == iota(rows.shape, 0), rows, 0.0), 0, keepdims=True)


def small_block(f, refs):
    norm, step, conv, shift, gain, cst, cst_shift, offset, rate, skip = [r[...].astype(F32) for r in refs]
    units = own_block(f, conv.shape[2], conv.shape[2])
    states = at_block(f, cst.shape[1], cst.shape[1])
    heads = at_block(f, 16, 12)
    rows = [step, norm.reshape(1, -1)]
    rows += [spread_units(conv[:, k].astype(BF), units) for k in range(K)]
    rows += [spread_units(shift.astype(BF), units), spread_units(gain.astype(BF), units)]
    per_head = jnp.concatenate([v.reshape(1, -1) for v in (offset, rate, skip)], 0)
    per_head = jnp.concatenate([per_head, jnp.zeros((3, 16 - per_head.shape[1]), F32)], 1)
    rows.append(mm(per_head.astype(BF), heads))
    rows.append(mm(cst.astype(BF), states))
    rows.append(mm(cst_shift.reshape(1, -1).astype(BF), states))
    rows.append(jnp.zeros((SMALL - 21, GW), F32))
    return jnp.concatenate(rows, 0).astype(BF)


def token_masks(docs, tok_ref):
    lane, sub = iota((CH, L), 1), iota((CH, L), 0)
    masks = [docs, jnp.where((sub > 0) & (docs == pltpu.roll(docs, 1, 0)[:, L - 1 : L]), 1.0, 0.0)]
    masks.append(jnp.where(docs == docs[:, L - 1 : L], 1.0, 0.0))
    for k in range(1, K):
        moved = pltpu.roll(docs, k, 1)
        before = jnp.where(lane < k, pltpu.roll(moved, 1, 0), moved)
        masks.append(jnp.where((before == docs) & ((sub > 0) | (lane >= k)), 1.0, 0.0))
    for k in range(1, K):
        moved = pltpu.roll(docs, L - k, 1)
        after = jnp.where(lane >= L - k, pltpu.roll(moved, CH - 1, 0), moved)
        masks.append(jnp.where((after == docs) & ((sub < CH - 1) | (lane < L - k)), 1.0, 0.0))
    for c in range(CH):
        rows = [m[c : c + 1, :] for m in masks] + [jnp.zeros((128 - len(masks), L), F32)]
        tok_ref[pl.ds(c * L, L), :] = jnp.concatenate(rows, 0).T


ORDER = (3, 2, 1, 0)
ROWS = 128
SCHEDULE = {
    "s1": [("second", 0, 0)],
    "s2": [("second", 1, 0), ("first", 0, 1)],
    "s5": [("second", 0, 1), ("first", 1, 1)],
    "m07": [("second", 1, 1), ("first", 0, 2)],
    "m10": [("second", 0, 2), ("first", 1, 2)],
    "p2": [("second", 1, 2), ("first", 0, 3)],
    "m20": [("second", 0, 3), ("first", 1, 3)],
    "p3": [("second", 1, 3), ("first", 2, 0)],
    "m30": [("second", 2, 0), ("first", 2, 1)],
    "m37": [("second", 2, 1), ("first", 2, 2)],
    "b00": [("second", 2, 2), ("first", 2, 3)],
    "b11": [("second", 2, 3), ("s1", 0), ("s1", 1)],
    "b21": [("s1", 2)],
    "b31": [("s1", 3)],
    "x1": [("s2", 0)],
    "g01": [("s3", 0), ("s2", 1)],
    "g05": [("s3", 1)],
    "g06": [("s2", 2)],
    "h01": [("s3", 2), ("s2", 3)],
    "g13": [("s2", 4), ("last", 3)],
    "g17": [("s3", 4)],
    "h10": [("s2", 5)],
    "h12": [("s3", 5)],
    "g23": [("s2", 6)],
    "g27": [("s3", 6)],
    "h20": [("s2", 7)],
    "h22": [("s3", 7)],
    "g33": [("s2", 8)],
    "g37": [("s3", 8)],
    "h30": [("s2", 9)],
    "t0": [("s3", 9)],
    "t1": [("s2", 10)],
    "t2": [("last", 10)],
    "t4": [("s2", 11)],
    "t7": [("last", 11)],
}
T_INV, T_BACK = 16, 17


def block_kernel(model, hid_ref, cot_ref, w0_ref, w1_ref, w2_ref, wst_ref, norm_ref, step_ref, conv_ref, shift_ref, gain_ref,
                 cvst_ref, cvst_shift_ref, offset_ref, rate_ref, skip_ref, seg_ref,
                 layer_out, hidden_out, normt_hbm, win_hbm, pre_hbm, states_hbm,
                 ginner_out, ggate_out, gout_out, gstate_ref, gsmall_ref, gother_ref,
                 hall, call, win, wout, pre, accr, flip, gated, states, halfr, recv1, recv2, recv3, stage,
                 small_ref, sbuf, stbuf, statepre_ref, ss_ref, ssr_ref, tok_ref, docs_ref,
                 bc_ref, bct_ref, g_ref, pack_ref, cumt_ref, par_ref, hpar_ref, cst_ref, stw_ref, gains_ref, gaingrad_ref, st_ref,
                 srecv, srecv1, srecv3, srecvc, qrecv1, qrecv3, qsend, qrecvc, nparts, nrecv, nback,
                 dstep, dstate, pgrad, hgrad, sgrad, rt_ref, dg_ref, dbc_ref,
                 sends, recvs, small_recvs, state_recvs, core_recvs, recv_sems, core_sems, state_sems, gain_sems, rest_sems,
                 outs_sem, pre_sem, state_sem, own_sem, load_sems, stage_sem, hid_sem, credit, free_out, free_core, free_half):
    stepre_ref = pr_ref = ss_ref
    dcat = hall.at[:, pl.ds(0, 2 * GW)]
    here = Place()
    z, zk = here.z, here.zk
    rows_own = hid_ref.shape[0]
    wide = 2 * GW
    depth = model // 4
    links = Links(sends)
    shards = [w0_ref, w1_ref, w2_ref.at[pl.ds(0, OUT_MAIN)]]
    outs = []

    def put(src, dst):
        copy = pltpu.make_async_copy(src, dst, outs_sem.at[len(outs)])
        copy.start()
        outs.append(copy)

    here.greet()
    small_ref[...] = small_block(
        here.f, (norm_ref, step_ref, conv_ref, shift_ref, gain_ref, cvst_ref, cvst_shift_ref, offset_ref, rate_ref, skip_ref)
    )
    here.greeted()
    mine = pl.ds(pl.multiple_of(here.c * rows_own, rows_own), rows_own)
    other = pl.ds(pl.multiple_of((1 - here.c) * rows_own, rows_own), rows_own)
    core = here.at(c=1 - here.c)
    one_block = recv2.at[0]
    like = [one_block, one_block, recv2.at[0, pl.ds(0, OUT_MAIN)]]
    for k in (1, 2, 3):
        links.send(("small", k), small_ref, sbuf.at[here.f, z], small_recvs.at[k], here.at(z=zk[k]))
    links.send("hidden", hid_ref, hall.at[mine], core_recvs.at[0], core)

    def recv_sem(m, f, z_):
        return recvs.at[m, f, z_]

    def push_z(m):
        for k in (1, 2, 3):
            links.send(("z", m, k), shards[m], piece(win, wout, m, here.f, z), recv_sem(m, here.f, z), here.at(z=zk[k]))

    def first(m, k):
        dst = piece(win, wout, m, here.f, zk[k])
        src = shards[m] if k == 0 else dst
        if k:
            links.arrived(dst, recv_sem(m, here.f, zk[k]), here.at(z=zk[k]))
        links.send(("first", m, k, 2), src, dst, recv_sem(m, here.f, zk[k]), here.at(f=here.f2), like[m])
        links.send(("first", m, k, 3), src, dst, recv_sem(m, here.f, zk[k]), here.at(f=here.f3), like[m])

    def second(m, k):
        src = piece(win, wout, m, here.f2, zk[k])
        links.arrived(src, recv_sem(m, here.f2, zk[k]), here.at(f=here.f2))
        links.send(("second", m, k), src, src, recv_sem(m, here.f2, zk[k]), here.at(f=here.f3), like[m])

    def third(m, k):
        for f in (here.f3, here.f4):
            src = piece(win, wout, m, f, zk[k])
            links.arrived(src, recv_sem(m, f, zk[k]), here.at(f=here.f3))

    rest = pl.ds(OUT_MAIN, GW - OUT_MAIN)

    def rest_of(f):
        return wout.at[z, rest, pl.ds(pl.multiple_of(f * depth, depth), depth)]

    def rest_first():
        for n, f in enumerate((here.f2, here.f3)):
            links.send(("rest", n), w2_ref.at[rest], rest_of(here.f), rest_sems.at[n], here.at(f=f))

    def rest_second():
        links.arrived(rest_of(here.f2), rest_sems.at[0], here.at(f=here.f2))
        links.send(("rest", 2), rest_of(here.f2), rest_of(here.f2), rest_sems.at[2], here.at(f=here.f3))

    def rest_third():
        links.arrived(rest_of(here.f3), rest_sems.at[1], here.at(f=here.f3))
        links.arrived(rest_of(here.f4), rest_sems.at[2], here.at(f=here.f3))
        own_copies[2].wait()
        for k in (1, 2, 3):
            links.send(("rest", 2 + k), wout.at[z, rest], wout.at[z, rest], rest_sems.at[2 + k], here.at(z=zk[k]))

    events = {"first": first, "second": second}

    def due(slot):
        for name, *what in SCHEDULE.get(slot, ()):
            events[name](*what)

    def ticker(prefix):
        def tick(step):
            for at in range(CH):
                if prefix + str(at) in SCHEDULE:
                    pl.when(step == at)(functools.partial(due, prefix + str(at)))

        return tick

    def state_of(f, part):
        return stbuf.at[f, :, part]

    push_z(0)
    links.send("cot", cot_ref, call.at[mine], core_recvs.at[1], core)
    own_copies = [pltpu.make_async_copy(shards[m], piece(win, wout, m, here.f, z), own_sem.at[m]) for m in range(2)]
    own_out = wout.at[z, :, pl.ds(pl.multiple_of(here.f * depth, depth), depth)]
    own_copies.append(pltpu.make_async_copy(w2_ref, own_out, own_sem.at[2]))
    own_copies.append(pltpu.make_async_copy(cot_ref, call.at[mine], own_sem.at[3]))
    own_copies.append(pltpu.make_async_copy(hid_ref, hall.at[mine], hid_sem.at[4]))
    for copy in own_copies:
        copy.start()
    sbuf[here.f, z] = small_ref[...]
    stbuf[here.f] = wst_ref[...]
    docs = seg_ref[pl.ds(pl.multiple_of(z * CH, CH), CH), :].astype(F32)
    docs_ref[...] = docs
    token_masks(docs, tok_ref)
    for k in (1, 2, 3):
        links.arrived(sbuf.at[here.f, zk[k]], small_recvs.at[k], here.at(z=zk[k]))
    links.send(("small", 4), sbuf.at[here.f], sbuf.at[here.f], small_recvs.at[4], here.at(f=here.f2))
    links.send(("small", 5), sbuf.at[here.f], sbuf.at[here.f], small_recvs.at[5], here.at(f=here.f3))
    half_state = pl.ds(pl.multiple_of(here.c * 128, 128), 128)
    rest_state = pl.ds(pl.multiple_of(128 - here.c * 128, 128), 128)
    links.send(("state", 0), wst_ref.at[:, half_state], state_of(here.f, half_state), state_recvs.at[0], here.at(f=here.f2))
    links.send(("state", 1), wst_ref.at[:, half_state], state_of(here.f, half_state), state_recvs.at[1], here.at(f=here.f3))
    first(0, 0)
    push_z(1)
    links.arrived(sbuf.at[here.f2], small_recvs.at[4], here.at(f=here.f2))
    links.send(("small", 6), sbuf.at[here.f2], sbuf.at[here.f2], small_recvs.at[6], here.at(f=here.f3))
    links.arrived(state_of(here.f2, half_state), state_recvs.at[0], here.at(f=here.f2))
    links.send(("state", 2), state_of(here.f2, half_state), state_of(here.f2, half_state), state_recvs.at[2], here.at(f=here.f3))
    links.send(("state", 3), state_of(here.f2, half_state), state_of(here.f2, half_state), state_recvs.at[3], core)
    first(1, 0)
    rest_first()
    push_z(2)
    due("s0")
    links.arrived(sbuf.at[here.f3], small_recvs.at[5], here.at(f=here.f3))
    links.arrived(sbuf.at[here.f4], small_recvs.at[6], here.at(f=here.f3))

    shared = sum(sbuf[f, 0].astype(F32) for f in range(4))
    gain_outer = jnp.concatenate([sbuf[f, 0][R_GAIN : R_GAIN + 1, :].astype(F32) for f in range(4)], 1)
    gains_ref[...] = jnp.broadcast_to(gain_outer, (8, model))
    cst_ref[...] = jnp.concatenate([shared[R_CST : R_CST + 5, :256], jnp.zeros((3, 256), F32)], 0)
    lane8 = lax.broadcasted_iota(jnp.int32, (8, 128), 1)
    heads8 = jnp.concatenate([shared[R_OFF : R_SKIP + 1, :128], jnp.zeros((5, 128), F32)], 0)
    own_heads = jnp.zeros((8, 128), F32)
    spread_heads = (lax.broadcasted_iota(jnp.int32, (128, GW), 1) >> 6
                    == lax.broadcasted_iota(jnp.int32, (128, GW), 0)).astype(BF)
    stw_ref[...] = jnp.zeros_like(stw_ref)
    for k in range(4):
        turned = pltpu.roll(heads8, 128 - (2 * zk[k] + here.c) * GH, 1)
        own_heads = own_heads + pltpu.roll(jnp.where(lane8 < GH, turned, 0.0), 16 * k, 1)
        group = sum(sbuf[f, zk[k]].astype(F32) for f in range(4))
        skips = mm(turned.astype(BF), spread_heads)[2:3, :]
        par_ref[k] = jnp.concatenate(
            [group[R_CONV : R_CONV + 5], skips, group[R_INNER : R_INNER + 1], jnp.zeros((1, GW), F32)], 0
        )
        for f in range(4):
            block = sbuf[f, zk[k]][:16].astype(F32)
            keep = lax.broadcasted_iota(jnp.int32, block.shape, 0) < GH
            stw_ref[pl.ds(16 * k, 16), pl.ds(depth * f, depth)] = jnp.where(keep, block, 0.0).astype(BF)
    decay = -jnp.exp(own_heads[1:2, :])
    hpar_ref[...] = jnp.concatenate([own_heads[0:1], decay, own_heads[2:3], jnp.zeros((5, 128), F32)], 0)

    due("s1")
    rest_second()
    own_copies[4].wait()
    links.arrived(hall.at[other], core_recvs.at[0], core)

    def norm(i, _):
        rows = pl.ds(pl.multiple_of(i * L, L), L)
        x = hall[rows, :].astype(F32)
        inv = lax.rsqrt(jnp.sum(x * x, 1, keepdims=True) / model + EPSILON)
        hall[rows, :] = (x * inv * gain_outer).astype(BF)
        return 0

    lax.fori_loop(0, SEQ // L, norm, 0)
    due("s2")
    links.arrived(state_of(here.f3, half_state), state_recvs.at[1], here.at(f=here.f3))
    links.send(("state", 4), state_of(here.f3, half_state), state_of(here.f3, half_state), state_recvs.at[4], core)
    links.arrived(state_of(here.f4, half_state), state_recvs.at[2], here.at(f=here.f3))
    links.send(("state", 5), state_of(here.f4, half_state), state_of(here.f4, half_state), state_recvs.at[5], core)
    for n, f in ((3, here.f3), (4, here.f2), (5, here.f4)):
        links.arrived(state_of(f, rest_state), state_recvs.at[n], core)

    TILE = 256
    WIDE_TILE = 512

    def project_small(i, _):
        rows = pl.ds(pl.multiple_of(i * TILE, TILE), TILE)
        total = jnp.zeros((TILE, 256), F32)
        for f in range(4):
            total = total + mm(hall[rows, pl.ds(depth * f, depth)], stbuf[f])
        statepre_ref[pl.ds(pl.multiple_of(i * TILE + 8, 8), TILE), :] = total
        steps = mm(hall[rows, :], stw_ref[...], ((1,), (1,)))
        stepre_ref[rows, :] = jnp.concatenate([steps, jnp.zeros((TILE, 64), F32)], 1)
        return 0

    statepre_ref[pl.ds(0, 8), :] = jnp.zeros((8, 256), F32)
    lax.fori_loop(0, SEQ // TILE, project_small, 0)

    due("s3")

    def turn(i, _):
        for half in range(2):
            lanes = pl.ds(pl.multiple_of(i * 256 + half * 128, 128), 128)
            flip[lanes, :] = hall[:, lanes].T
        return 0

    lax.fori_loop(0, model // 256, turn, 0)
    TURNED = len(outs)
    put(flip, normt_hbm)
    due("s4")
    rest_third()
    prep_chunks(statepre_ref, stepre_ref, tok_ref, docs_ref, cst_ref, hpar_ref, bc_ref, bct_ref, g_ref, pack_ref, cumt_ref)
    due("s5")
    links.arrived(call.at[other], core_recvs.at[1], core)
    for copy in (own_copies[0], own_copies[1], own_copies[3]):
        copy.wait()
    ss_ref[...] = jnp.zeros_like(ss_ref)
    for slot in range(2):
        pre[slot, pl.ds(0, 8), :] = jnp.zeros((8, 2 * GW), F32)
    pre_copies = []
    state_copies = []
    for k in range(4):
        due("p%d" % k)
        third(0, k)
        third(1, k)
        slot = k % 2
        if k >= 2:
            pre_copies[k - 2].wait()

        def project(i, _, slot=slot, k=k):
            rows = pl.ds(pl.multiple_of(i * WIDE_TILE, WIDE_TILE), WIDE_TILE)
            to = pl.ds(pl.multiple_of(i * WIDE_TILE + 8, 8), WIDE_TILE)
            pre[slot, to, :] = mm(hall[rows, :], win[zk[k]])
            return 0

        lax.fori_loop(0, SEQ // WIDE_TILE, project, 0)
        copy = pltpu.make_async_copy(pre.at[slot, pl.ds(8, SEQ)], pre_hbm.at[k], pre_sem.at[k])
        copy.start()
        pre_copies.append(copy)
        put(win.at[zk[k]], win_hbm.at[k])
        if k:
            state_copies[k - 1].wait()
        fwd_chunks(k, ticker("m%d" % k), pre.at[slot], par_ref.at[k], tok_ref, bc_ref, bct_ref, g_ref, pack_ref.at[k // 2], cumt_ref.at[k],
                   gated.at[k], states, ss_ref, st_ref)
        copy = pltpu.make_async_copy(states, states_hbm.at[k], state_sem.at[k])
        copy.start()
        state_copies.append(copy)
    for copy in pre_copies[2:] + state_copies[3:]:
        copy.wait()

    links.send("squares", ss_ref, ssr_ref, core_recvs.at[2], core)
    due("n0")
    links.arrived(ssr_ref, core_recvs.at[2], core)
    inner_all = 2 * 4 * GW

    def inner_norm(i, _):
        rows = pl.ds(pl.multiple_of(i * L, L), L)
        total = jnp.sum(ss_ref[rows, :] + ssr_ref[rows, :], 1, keepdims=True)
        inv = lax.rsqrt(total / inner_all + EPSILON)
        tok_ref[rows, :] = jnp.where(iota((L, 128), 1) == T_INV, inv, tok_ref[rows, :])
        for k in range(4):
            gain = par_ref[k, P_GAIN : P_GAIN + 1, :]
            low = (gated[k, rows, :].astype(F32) * inv * gain).astype(BF)
            hall[rows, pl.ds(k * GW, GW)] = low
            flip[pl.ds(k * GW, GW), rows] = low.T
        pr_ref[rows, :] = jnp.zeros((L, 128), F32)
        return 0

    links.left("squares", core_recvs.at[0], core)
    for copy in outs:
        copy.wait()
    lax.fori_loop(0, SEQ // L, inner_norm, 0)
    pl.semaphore_signal(free_core, inc=1, device_id=core, device_id_type=MESH)
    f, f2, f3, f4 = here.f, here.f2, here.f3, here.f4
    for m in (0, 1):
        for k in range(4):
            for name in (("first", m, k, 2), ("first", m, k, 3), ("second", m, k)):
                links.left(name, core_recvs.at[0], core)
    loads = {}

    def load(name, src, dst, sem):
        copy = pltpu.make_async_copy(src, dst, load_sems.at[sem])
        copy.start()
        loads[name] = copy

    accl = pre.at[0, pl.ds(8, SEQ)]

    def slot_of(u):
        return (u % 6) // 2, u % 2

    def part(u, f_):
        at, side = slot_of(u)
        return win.at[at, pl.ds(pl.multiple_of(f_ * depth, depth), depth), pl.ds(side * GW, GW)]

    def landing(u, n):
        if u < 4:
            return recv1.at[u, n]
        n += 2 * (u - 4)
        return wout.at[n // 4, :, pl.ds((n % 4) * GW, GW)]

    def s1(u):
        for n, f_ in enumerate((f3, f4)):
            links.send(("s1", u, n), part(u, f_), landing(u, n), recv_sems.at[u, n], here.at(f=f3), one_block)

    units = [(k, 2) for k in ORDER] + [(k, m) for k in ORDER for m in (0, 1)]

    def add_into(dst, src):
        rows, width = dst.shape

        def body(i, _):
            at = pl.ds(pl.multiple_of(i * ROWS, ROWS), ROWS)
            dst[at, :] = (dst[at, :].astype(F32) + src[at, :].astype(F32)).astype(dst.dtype)
            return 0

        lax.fori_loop(0, rows // ROWS, body, 0)

    def s2(u):
        links.arrived(landing(u, 1), recv_sems.at[u, 1], here.at(f=f3))
        add_into(part(u, f2), landing(u, 1))
        if u >= 4:
            pl.semaphore_wait(credit, 1)
        links.send(("s2", u), part(u, f2), recv2.at[u % 4], recv_sems.at[u, 2], here.at(f=f2), one_block)
        links.arrived(landing(u, 0), recv_sems.at[u, 0], here.at(f=f3))
        add_into(part(u, f), landing(u, 0))

    def give_credit(u):
        if u < 8:
            pl.semaphore_signal(credit, inc=1, device_id=here.at(f=f2), device_id_type=MESH)

    outs = {0: ginner_out, 1: ggate_out, 2: gout_out}
    results = [pltpu.make_async_copy(stage, outs[m], stage_sem.at[m]) for m in range(3)]
    staged = []

    def s3(u):
        k, m = units[u]
        links.arrived(recv2.at[u % 4], recv_sems.at[u, 2], here.at(f=f2))
        add_into(part(u, f), recv2.at[u % 4])
        give_credit(u)
        links.send(("s3", u), part(u, f), recv3.at[m, k - 1], recv_sems.at[12 + m, k - 1], here.at(z=zk[k]), one_block)

    def last_sum(u):
        k, m = units[u]
        links.arrived(recv2.at[u % 4], recv_sems.at[u, 2], here.at(f=f2))
        for j in (1, 2, 3):
            links.arrived(recv3.at[m, j - 1], recv_sems.at[12 + m, j - 1], here.at(z=zk[j]))
        own = part(u, f)
        if staged:
            results[staged[-1]].wait()

        def body(i, _):
            at = pl.ds(pl.multiple_of(i * ROWS, ROWS), ROWS)
            total = own[at, :].astype(F32) + recv2[u % 4, at, :].astype(F32)
            for j in range(3):
                total = total + recv3[m, j, at, :].astype(F32)
            stage[at, :] = total
            return 0

        lax.fori_loop(0, GW // ROWS, body, 0)
        give_credit(u)
        staged.append(m)
        results[m].start()

    events.update({"s1": s1, "s2": s2, "s3": s3, "last": last_sum})

    def grad_out(i):
        k = ORDER[i]
        at, side = slot_of(i)

        def columns_of(f_, _):
            lanes = pl.ds(pl.multiple_of(f_ * depth, depth), depth)
            total = mm(flip[pl.ds(k * GW, GW), :], call[:, lanes])
            win[at, lanes, pl.ds(side * GW, GW)] = total.astype(BF)
            return 0

        lax.fori_loop(0, 4, columns_of, 0)

    hid_copies = []
    for side in range(2):
        src = hid_ref.at[:, pl.ds(side * wide, wide)]
        hid_copies.append(pltpu.make_async_copy(src, halfr.at[pl.ds(side * rows_own, rows_own)], hid_sem.at[side]))
        hid_copies[-1].start()
    due("n1")
    for k in range(4):
        due("b%d0" % k)
        grad_out(k)
        due("b%d1" % k)
        third(2, k)
        if k:
            links.arrived(wout.at[zk[k], rest], rest_sems.at[2 + k], here.at(z=zk[k]))
        gaingrad_ref[k] = jnp.zeros((8, GW), F32)

        def back(i, _, k=k):
            rows = pl.ds(pl.multiple_of(i * WIDE_TILE, WIDE_TILE), WIDE_TILE)
            d = mm(call[rows, :], wout[zk[k]], ((1,), (1,)))
            both = d * gated[k, rows, :].astype(F32)
            gated[k, rows, :] = d.astype(BF)
            gaingrad_ref[k, 0:1, :] += jnp.sum(both * tok_ref[rows, T_INV : T_INV + 1], 0, keepdims=True)
            both = both * par_ref[k, P_GAIN : P_GAIN + 1, :]
            pr_ref[rows, :] += both[:, :128] + both[:, 128:256] + both[:, 256:]
            return 0

        lax.fori_loop(0, SEQ // WIDE_TILE, back, 0)
    pl.semaphore_wait(free_core, 1)
    links.send("products", pr_ref, ssr_ref, core_recvs.at[3], core)
    due("x0")
    load("normt", normt_hbm, flip, 0)
    load(("win", 0), win_hbm.at[ORDER[0]], win.at[3], 1)

    def mix_rows(i, _):
        rows = pl.ds(pl.multiple_of(i * WIDE_TILE, WIDE_TILE), WIDE_TILE)
        for acc, first_lane in ((accl, 0), (accr, wide)):
            acc[rows, :] = sum(mm(hall[rows, pl.ds(k * GW, GW)], wout[zk[k], :, pl.ds(first_lane, wide)]) for k in range(4))
        return 0

    lax.fori_loop(0, SEQ // WIDE_TILE, mix_rows, 0)
    due("x1")
    half = hall.at[:, pl.ds(0, wide)]
    halves = [halfr, hall.at[:, pl.ds(wide, wide)]]

    def exchange(n):
        def body(j, _):
            src = pl.ds(pl.multiple_of((1 - here.c) * rows_own + j * ROWS, ROWS), ROWS)
            half[pl.ds(pl.multiple_of(j * ROWS, ROWS), ROWS), :] = accl[src, :].astype(BF)
            half[pl.ds(pl.multiple_of(rows_own + j * ROWS, ROWS), ROWS), :] = accr[src, :].astype(BF)
            return 0

        lax.fori_loop(0, rows_own // ROWS, body, 0)
        links.send(("half", n), half, halves[n], core_sems.at[n], core)

    def received(n):
        links.arrived(halves[n], core_sems.at[n], core)

    def places(j):
        own = pl.ds(pl.multiple_of(here.c * rows_own + j * ROWS, ROWS), ROWS)
        at = pl.ds(pl.multiple_of(j * ROWS, ROWS), ROWS)
        below = pl.ds(pl.multiple_of(rows_own + j * ROWS, ROWS), ROWS)
        return own, at, below

    def summed(n, j):
        own, at, below = places(j)
        left = accl[own, :] + halves[n][at, :].astype(F32)
        right = accr[own, :] + halves[n][below, :].astype(F32)
        return own, at, below, jnp.concatenate([left, right], 1)

    def store(n, at, below, values):
        halves[n][at, :] = values[:, :wide].astype(BF)
        halves[n][below, :] = values[:, wide:].astype(BF)

    def give(n, out, sem):
        for side in range(2):
            load((n, side), halves[n].at[pl.ds(side * rows_own, rows_own)], out.at[:, pl.ds(side * wide, wide)], sem + side)

    def add_hidden(j, _):
        own, at, below = places(j)
        accl[own, :] = accl[own, :] + halfr[at, :].astype(F32)
        accr[own, :] = accr[own, :] + halfr[below, :].astype(F32)
        return 0

    for copy in hid_copies:
        copy.wait()
    lax.fori_loop(0, rows_own // ROWS, add_hidden, 0)
    pl.semaphore_signal(free_half, inc=1, device_id=core, device_id_type=MESH)
    pl.semaphore_wait(free_half, 1)
    exchange(0)
    due("x2")
    links.arrived(ssr_ref, core_recvs.at[3], core)

    def scale(i, _):
        rows = pl.ds(pl.multiple_of(i * L, L), L)
        total = jnp.sum(pr_ref[rows, :] + ssr_ref[rows, :], 1, keepdims=True)
        tok = tok_ref[rows, :]
        inv = tok[:, T_INV : T_INV + 1]
        tok_ref[rows, :] = jnp.where(iota((L, 128), 1) == T_BACK, inv * inv * inv * (total / inner_all), tok)
        return 0

    lax.fori_loop(0, SEQ // L, scale, 0)
    for k in range(4):
        for name in (("first", 2, k, 2), ("first", 2, k, 3), ("second", 2, k)):
            links.left(name, core_recvs.at[0], core)
    for n in range(6):
        links.left(("rest", n), core_recvs.at[0], core)
    pl.semaphore_signal(free_out, inc=1, device_id=here.at(f=f3), device_id_type=MESH)
    links.left(("half", 0), core_sems.at[0], core)
    hgrad[...] = jnp.zeros_like(hgrad)
    dg_ref[...] = jnp.zeros_like(dg_ref)
    dbc_ref[...] = jnp.zeros_like(dbc_ref)
    dstep[...] = jnp.zeros_like(dstep)
    def to_normed(fresh, j, _):
        at = pl.ds(pl.multiple_of(j * WIDE_TILE, WIDE_TILE), WIDE_TILE)
        for acc, first_row in ((accl, 0), (accr, wide)):
            total = mm(dcat[at, :], win[3, pl.ds(first_row, wide), :], ((1,), (1,)))
            acc[at, :] = total if fresh else acc[at, :] + total
        return 0

    for i, k in enumerate(ORDER):
        if i:
            for name in ("pre", "states"):
                loads[name, i].wait()

        bwd_chunks(k, zk[k], ticker("g%d" % i), pre.at[1], gated.at[k], par_ref.at[k], tok_ref, bc_ref, bct_ref, g_ref,
                   pack_ref.at[k // 2], cumt_ref.at[k], states, hpar_ref, dcat, dstep, pgrad.at[k], hgrad, rt_ref, dg_ref, dbc_ref)
        if i < 3:
            load(("pre", i + 1), pre_hbm.at[ORDER[i + 1]], pre.at[1, pl.ds(8, SEQ)], 2)
            load(("states", i + 1), states_hbm.at[ORDER[i + 1]], states, 3)
        else:
            loads[0, 0].wait()
            loads[0, 1].wait()
        u = 4 + 2 * i
        due("h%d0" % i)
        if u >= 6:
            for n in (u - 6, u - 5):
                for name in (("s1", n, 0), ("s1", n, 1), ("s2", n), ("s3", n)):
                    if name in links.number:
                        links.left(name, core_sems.at[0], here.at(c=1 - here.c))

        if i == 0:
            loads["normt"].wait()
            pl.semaphore_wait(free_out, 1)

        def grads(j, _, u=u):
            at = pl.ds(pl.multiple_of(j * depth, depth), depth)
            win[slot_of(u)[0], at, :] = mm(flip[at, :], dcat[...]).astype(BF)
            return 0

        lax.fori_loop(0, 4, grads, 0)
        s1(u)
        s1(u + 1)
        if i == 0:
            received(0)

            def layer(j, _):
                own, at, below, total = summed(0, j)
                store(0, at, below, total)
                return 0

            lax.fori_loop(0, rows_own // ROWS, layer, 0)
            give(0, layer_out, 4)
        due("h%d1" % i)
        if i < 3:
            loads["win", i].wait()
            lax.fori_loop(0, SEQ // WIDE_TILE, functools.partial(to_normed, i == 0), 0)
            load(("win", i + 1), win_hbm.at[ORDER[i + 1]], win.at[3], 1)
            due("h%d2" % i)

    last_tokens = []
    for k in range(4):
        src = hid_ref.at[:, pl.ds(k * GW, GW)]
        last_tokens.append(pltpu.make_async_copy(src, gated.at[k, pl.ds(0, rows_own)], hid_sem.at[k]))
        last_tokens[-1].start()
    state_chunks(statepre_ref, cst_ref, tok_ref, docs_ref, bc_ref, dg_ref, dbc_ref, dstate, sgrad)
    due("t0")

    def state_part(f_, n=0):
        at = pl.ds(pl.multiple_of((f_ % 2) * depth, depth), depth)
        return halfr.at[at, pl.ds(pl.multiple_of((f_ // 2) * 256 + n * 128, 128), 128)]

    def small_part(f_):
        at = pl.ds(pl.multiple_of(2 * depth + (f_ // 2) * 4 * SMALL, 4 * SMALL), 4 * SMALL)
        return halfr.at[at, pl.ds(pl.multiple_of((f_ % 2) * GW, GW), GW)]

    def add_to(ref, *others):
        total = ref[...].astype(F32)
        for other in others:
            total = total + other.astype(F32)
        ref[...] = total.astype(BF)
        return total

    for f_ in range(4):
        sums = mm(flip[pl.ds(f_ * depth, depth), :], dstate[...])
        lower, upper = sums[:, :128], sums[:, 128:]
        state_part(f_)[...] = jnp.where(here.c == 0, lower, upper).astype(BF)
        state_part(f_, 1)[...] = jnp.where(here.c == 0, upper, lower).astype(BF)
        links.send(("state_core", f_), state_part(f_, 1), srecv.at[f_], state_sems.at[f_], core)
    due("t1")
    step_rows = mm(dstep[:, :64], flip[...], ((0,), (1,)))
    zeros = jnp.zeros((1, GW - 256), F32)
    skips = jnp.zeros((8, 128), F32)
    heads_of = (iota((GW, 128), 0) >> 6 == iota((GW, 128), 1)).astype(BF)
    for k in range(4):
        hi, lo = split2(pgrad[k])
        skips = skips + pltpu.roll(mm(hi, heads_of) + mm(lo, heads_of), 16 * zk[k], 1)
    head_rows = jnp.concatenate([hgrad[0:2, :], skips[P_SKIP : P_SKIP + 1, :]], 0)
    head_rows = jnp.concatenate([head_rows, jnp.zeros((3, GW - 128), F32)], 1)
    common = [jnp.zeros((1, GW), F32)]
    common += [jnp.concatenate([sgrad[r : r + 1, :], zeros], 1) for r in range(5)]
    common.append(head_rows)
    for f_ in range(4):
        blocks = []
        for k in range(4):
            own = jnp.concatenate([pgrad[k, 0:5, :], gaingrad_ref[k, 0:1, :], jnp.zeros((1, GW), F32)], 0)
            blocks += [step_rows[16 * k : 16 * k + 16, f_ * depth : (f_ + 1) * depth], own] + common
        small_part(f_)[...] = jnp.concatenate(blocks, 0).astype(BF)
    for n, f_ in enumerate((f2, f3, f4)):
        links.send(("sums", n), small_part(f_), qrecv1.at[n], recv_sems.at[16, n], here.at(f=f_))
    loads["win", 3].wait()
    lax.fori_loop(0, SEQ // WIDE_TILE, functools.partial(to_normed, False), 0)

    def finish_normed(j, _):
        at = pl.ds(pl.multiple_of(j * 256, 256), 256)
        total = mm(dstep[at, :64], stw_ref[...])
        total = total + jnp.concatenate([mm(dstate[at, :], stbuf[f_], ((1,), (1,))) for f_ in range(4)], 1)
        accl[at, :] = accl[at, :] + total[:, :wide]
        accr[at, :] = accr[at, :] + total[:, wide:]
        return 0

    lax.fori_loop(0, SEQ // 256, finish_normed, 0)
    due("t2")
    exchange(1)
    for f_ in range(4):
        links.arrived(srecv.at[f_], state_sems.at[f_], core)
        add_to(state_part(f_), srecv[f_])
    for n, f_ in enumerate((f2, f3, f4)):
        links.send(("state", f"f{n}"), state_part(f_), srecv1.at[n], recv_sems.at[15, n], here.at(f=f_))
    due("t3")
    received(1)
    gain = gains_ref[0:1, :]
    for copy in last_tokens:
        copy.wait()

    def last(j, gain_grad):
        own, at, below, d = summed(1, j)
        x = jnp.concatenate([gated[k, at, :] for k in range(4)], 1).astype(F32)
        inv = lax.rsqrt(jnp.sum(x * x, 1, keepdims=True) / model + EPSILON)
        weighted = d * gain
        mean = jnp.sum(x * weighted, 1, keepdims=True) / model
        d_hidden = inv * weighted - x * (inv * inv * inv * mean)
        store(1, at, below, call[own, :].astype(F32) + d_hidden)
        return gain_grad + jnp.sum(d * x * inv, 0, keepdims=True)

    gain_grad = lax.fori_loop(0, rows_own // ROWS, last, jnp.zeros((1, model), F32))
    give(1, hidden_out, 6)
    for f_ in range(4):
        nparts[f_] = jnp.broadcast_to(gain_grad[:, f_ * depth : (f_ + 1) * depth], (16, GW)).astype(BF)
    for n, f_ in enumerate((f2, f3, f4)):
        links.send(("gain", n), nparts.at[f_], nrecv.at[n], gain_sems.at[n], here.at(f=f_))
    due("t4")
    for n, f_ in enumerate((f2, f3, f4)):
        links.arrived(qrecv1.at[n], recv_sems.at[16, n], here.at(f=f_))
    sums = add_to(small_part(f), qrecv1[0], qrecv1[1], qrecv1[2])
    for k in range(4):
        qsend[k] = sums[k * SMALL : (k + 1) * SMALL].astype(BF)
        if k:
            links.send(("small_z", k), qsend.at[k], qrecv3.at[k - 1], recv_sems.at[18, k - 1], here.at(z=zk[k]))
    for n, f_ in enumerate((f2, f3, f4)):
        links.arrived(srecv1.at[n], recv_sems.at[15, n], here.at(f=f_))
    add_to(state_part(f), srecv1[0], srecv1[1], srecv1[2])
    for k in (1, 2, 3):
        links.send(("state_z", k), state_part(f), srecv3.at[k - 1], recv_sems.at[17, k - 1], here.at(z=zk[k]))
    for n, f_ in enumerate((f2, f3, f4)):
        links.arrived(nrecv.at[n], gain_sems.at[n], here.at(f=f_))
    add_to(nparts.at[f], nrecv[0], nrecv[1], nrecv[2])
    for k in (1, 2, 3):
        links.send(("gain_z", k), nparts.at[f], nrecv.at[k + 2], gain_sems.at[k + 2], here.at(z=zk[k]))
    due("t5")
    for k in (1, 2, 3):
        links.arrived(qrecv3.at[k - 1], recv_sems.at[18, k - 1], here.at(z=zk[k]))
    small_total = qsend[0].astype(F32)
    for k in range(3):
        small_total = small_total + qrecv3[k].astype(F32)
    qsend[0] = small_total.astype(BF)
    links.send("small_core", qsend.at[0], qrecvc, core_sems.at[3], core)
    due("t6")
    for k in (1, 2, 3):
        links.arrived(nrecv.at[k + 2], gain_sems.at[k + 2], here.at(z=zk[k]))
    gain_total = nparts[f].astype(F32)
    for k in (3, 4, 5):
        gain_total = gain_total + nrecv[k].astype(F32)
    nback[...] = gain_total.astype(BF)
    links.send("gain_core", nback, nrecv.at[6], gain_sems.at[6], core)
    for k in (1, 2, 3):
        links.arrived(srecv3.at[k - 1], recv_sems.at[17, k - 1], here.at(z=zk[k]))
    total = state_part(f)[...].astype(F32)
    for k in range(3):
        total = total + srecv3[k].astype(F32)
    back = halfr.at[pl.ds(0, depth), pl.ds(512, 128)]
    back[...] = total.astype(BF)
    links.send("state_back", back, srecvc, core_sems.at[4], core)
    due("t7")
    gain_row = iota((SMALL, GW), 0) == 23
    links.arrived(qrecvc, core_sems.at[3], core)
    links.arrived(nrecv.at[6], gain_sems.at[6], core)
    gsmall_ref[...] = jnp.where(gain_row, gain_total[0:1, :], small_total)
    gother_ref[...] = jnp.where(gain_row, nrecv[6][0:1, :].astype(F32), qrecvc[...].astype(F32))
    links.arrived(srecvc, core_sems.at[4], core)
    rest = srecvc[...].astype(F32)
    gstate_ref[...] = jnp.concatenate([jnp.where(here.c == 0, total, rest), jnp.where(here.c == 0, rest, total)], 1)
    for side in range(2):
        loads[1, side].wait()
    results[staged[-1]].wait()
    links.finish(core_sems.at[0], core)


def block_call(model, hidden, *args):
    rows = hidden.shape[0]
    depth = model // 4
    any_ = pl.BlockSpec(memory_space=pl.ANY)
    sds = jax.ShapeDtypeStruct
    block = (GW, GW)
    part = (depth, 128)
    small = (SMALL, GW)

    def v(kind, *shape):
        return pltpu.VMEM(shape, kind)

    return pl.pallas_call(
        functools.partial(block_kernel, model),
        out_shape=(
            sds((rows, model), BF), sds((rows, model), BF),
            sds((model, SEQ), BF), sds((4, model, 2 * GW), BF), sds((4, SEQ, 2 * GW), F32), sds((4, CH, 128, GW), BF),
            sds(block, F32), sds(block, F32), sds(block, F32), sds((depth, 256), F32), sds(small, F32), sds(small, F32),
        ),
        in_specs=[any_] * 5 + [vm()] * (len(args) - 4),
        out_specs=tuple([any_] * 9 + [vm()] * 3),
        scratch_shapes=[
            v(BF, SEQ, model), v(BF, SEQ, model), v(BF, 4, model, 2 * GW), v(BF, 4, GW, model),
            v(F32, 2, SEQ + 8, 2 * GW), v(F32, SEQ, 2 * GW), v(BF, model, SEQ), v(BF, 4, SEQ, GW), v(BF, CH, 128, GW),
            v(BF, SEQ, 2 * GW), v(BF, 4, 2, GW, GW), v(BF, 4, GW, GW), v(BF, 3, 3, GW, GW), v(F32, GW, GW),
            v(BF, *small), v(BF, 4, 4, *small), v(BF, 4, depth, 256), v(F32, SEQ + 8, 256),
            v(F32, SEQ, 128), v(F32, SEQ, 128), v(F32, SEQ, 128), v(F32, CH, L),
            v(BF, SEQ, 256), v(BF, CH, 256, L), v(F32, CH, L, L), v(F32, 2, SEQ, 128), v(F32, 4, CH, 8, L),
            v(F32, 4, 8, GW), v(F32, 8, 128), v(F32, 8, 256), v(BF, 64, model), v(F32, 8, model), v(F32, 4, 8, GW),
            v(F32, 128, GW),
            v(BF, 4, *part), v(BF, 3, *part), v(BF, 3, *part), v(BF, *part),
            v(BF, 3, 4 * SMALL, GW), v(BF, 3, *small), v(BF, 4, *small), v(BF, *small),
            v(BF, 4, 16, GW), v(BF, 7, 16, GW), v(BF, 16, GW),
            v(BF, SEQ, 128), v(BF, SEQ, 256), v(F32, 4, 8, GW), v(F32, 8, 128), v(F32, 8, 256), v(F32, 128, GW),
            v(F32, CH, L, L), v(F32, SEQ, 256),
            pltpu.SemaphoreType.DMA((144,)),
            pltpu.SemaphoreType.DMA((3, 4, 4)),
            pltpu.SemaphoreType.DMA((7,)),
            pltpu.SemaphoreType.DMA((6,)),
            pltpu.SemaphoreType.DMA((4,)),
            pltpu.SemaphoreType.DMA((19, 4)),
            pltpu.SemaphoreType.DMA((5,)),
            pltpu.SemaphoreType.DMA((4,)),
            pltpu.SemaphoreType.DMA((7,)),
            pltpu.SemaphoreType.DMA((6,)),
            pltpu.SemaphoreType.DMA((16,)),
            pltpu.SemaphoreType.DMA((4,)),
            pltpu.SemaphoreType.DMA((4,)),
            pltpu.SemaphoreType.DMA((4,)),
            pltpu.SemaphoreType.DMA((8,)),
            pltpu.SemaphoreType.DMA((3,)),
            pltpu.SemaphoreType.DMA((5,)),
            pltpu.SemaphoreType.REGULAR,
            pltpu.SemaphoreType.REGULAR,
            pltpu.SemaphoreType.REGULAR,
            pltpu.SemaphoreType.REGULAR,
        ],
        compiler_params=pltpu.CompilerParams(vmem_limit_bytes=VMEM_LIMIT, collective_id=1, has_side_effects=True),
        name="whole_block",
    )(hidden, *args)


def exact(values, places):
    return sum(mm(part, places, ((1,), (1,))) for part in split3(values))


def finish_kernel(layer_in, hidden_in, gate_in, inner_in, out_in, state_in, own_ref, other_ref,
                  layer_out, hidden_out, gain_out, gate_out, inner_out, state_out, step_out, conv_out, shift_out, cst_out,
                  cst_shift_out, offset_out, rate_out, skip_out, inner_gain_out, out_out, sems):
    pairs = [(layer_in, layer_out), (hidden_in, hidden_out), (gate_in, gate_out), (inner_in, inner_out), (out_in, out_out),
             (state_in, state_out)]
    copies = [pltpu.make_async_copy(a, b, sems.at[n]) for n, (a, b) in enumerate(pairs)]
    for copy in copies:
        copy.start()
    f, core = lax.axis_index("fsdp"), lax.axis_index("core")
    own, other = own_ref[...], other_ref[...]
    shared = own + other
    gain_out[...] = shared[23:24].reshape(GW)
    step_out[...] = own[:GH]
    unit = conv_out.shape[2]
    heads = iota((8, GW), 1) >> 6 == iota((8, GW), 0)
    rows = [jnp.where(heads, own[r : r + 1], 0.0) for r in range(16, 22)]
    picked = exact(jnp.concatenate(rows, 0), own_block(f, unit, unit))
    for k in range(K):
        conv_out[:, k : k + 1, :] = picked[8 * k : 8 * k + GH].reshape(GH, 1, unit)
    shift_out[...] = picked[8 * K : 8 * K + GH]
    inner_gain_out[...] = picked[8 * K + 8 : 8 * K + 8 + GH]
    size = cst_out.shape[1]
    states = exact(shared[24:32], at_block(f, size, size))
    cst_out[...] = states[:K]
    cst_shift_out[...] = states[K : K + 1].reshape(size)
    place, lane = iota((16, GW), 0), iota((16, GW), 1)
    lower = ((lane == 16 * f + place) & (place < GH)).astype(BF)
    upper = ((lane == 16 * f + place - GH) & (place >= GH) & (place < 2 * GH)).astype(BF)
    first = jnp.where(core == 0, own[24:32], other[24:32])
    second = jnp.where(core == 0, other[24:32], own[24:32])
    per_head = exact(first, lower) + exact(second, upper)
    rate_out[...] = per_head[5:6, : 2 * GH].reshape(2 * GH)
    offset_out[...] = per_head[6:7, : 2 * GH].reshape(2 * GH)
    skip_out[...] = per_head[7:8, : 2 * GH].reshape(2 * GH)
    for copy in copies:
        copy.wait()


def finish_call(*args):
    any_ = pl.BlockSpec(memory_space=pl.ANY)
    sds = jax.ShapeDtypeStruct
    layer, hidden, gate, inner, out, state = [sds(v.shape, v.dtype) for v in args[:6]]
    return pl.pallas_call(
        finish_kernel,
        out_shape=(
            layer, hidden, sds((GW,), F32), gate, inner, state, sds((GH, GW), F32), sds((GH, K, 16), F32), sds((GH, 16), F32),
            sds((K, 64), F32), sds((64,), F32), sds((2 * GH,), F32), sds((2 * GH,), F32), sds((2 * GH,), F32),
            sds((GH, 16), F32), out,
        ),
        in_specs=[vm()] * 8,
        out_specs=tuple([any_] * 2 + [vm()] + [any_] * 3 + [vm()] * 9 + [any_]),
        scratch_shapes=[pltpu.SemaphoreType.DMA((6,))],
        compiler_params=pltpu.CompilerParams(vmem_limit_bytes=VMEM_LIMIT),
        name="finish",
    )(*args)


def on_device(fsdp, halves, hidden_in, norm_gain, in_gate, in_inner, in_state, in_step, conv_inner, conv_inner_shift,
              conv_state, conv_state_shift, step_offset, log_rate, skip_gain, inner_gain, out_weight, segment_ids,
              grad_out):
    both = ("fsdp", "zz")
    depth, width = in_gate.shape
    model = depth * fsdp
    inner = width * halves
    heads_dev = in_step.shape[1]
    heads = heads_dev * halves
    heads_all = 2 * heads
    unit = conv_inner.shape[2] * fsdp
    inner_all = 2 * inner
    core = lax.axis_index("core")
    zz = lax.axis_index("zz")
    rows = hidden_in.shape[0]

    def swap(x):
        return lax.ppermute(x, "core", [(0, 1), (1, 0)])

    def both_cores(own, other):
        return jnp.where(core == 0, jnp.concatenate([own, other], 0), jnp.concatenate([other, own], 0))

    small = [norm_gain, in_step, conv_inner, conv_inner_shift, conv_state, conv_state_shift, step_offset, log_rate,
             skip_gain, inner_gain]
    flat = jnp.concatenate([v.reshape(-1) for v in small])
    got = lax.all_gather(flat, both, axis=0).reshape(fsdp, halves, -1)
    parts = []
    at = 0
    for v in small:
        parts.append(got[:, :, at : at + v.size].reshape((fsdp, halves) + v.shape))
        at += v.size
    gain_outer = parts[0][:, 0].reshape(model).astype(F32)
    step_cols = parts[1].transpose(0, 2, 1, 3).reshape(model, heads)
    conv_in = parts[2].transpose(2, 1, 3, 0, 4).reshape(K, inner).astype(F32)
    shift_in = parts[3].transpose(1, 2, 0, 3).reshape(1, inner).astype(F32)
    conv_st = parts[4][:, 0].transpose(1, 0, 2).reshape(K, -1).astype(F32)
    shift_st = parts[5][:, 0].reshape(1, -1).astype(F32)
    gain_in = parts[9].transpose(1, 2, 0, 3).reshape(1, inner).astype(F32)

    def my_heads(v):
        return v.reshape(halves, 2, heads_dev)[:, core].reshape(heads).astype(F32)

    offset = my_heads(parts[6][:, 0].reshape(heads_all))
    decay = -jnp.exp(my_heads(parts[7][:, 0].reshape(heads_all)))
    skip = my_heads(parts[8][:, 0].reshape(heads_all))
    state_cols = lax.all_gather(in_state, "fsdp", axis=0, tiled=True)

    def columns(w):
        return lax.all_gather(w, both, axis=0).reshape(fsdp, halves, depth, width).transpose(0, 2, 1, 3).reshape(model, inner)

    inner_cols = columns(in_inner)
    gate_cols = columns(in_gate)
    out_rows = lax.all_gather(out_weight, both, axis=0).reshape(fsdp, halves, width, depth).transpose(1, 2, 0, 3).reshape(inner, model)

    par = jnp.concatenate([conv_in, shift_in, jnp.repeat(skip, unit)[None], gain_in, jnp.zeros((1, inner), F32)], 0)
    convst = jnp.concatenate([conv_st, shift_st, jnp.zeros((3, 256), F32)], 0)
    head = jnp.pad(jnp.stack([offset, decay]), ((0, 6), (0, 128 - heads)))
    decay_g = jnp.pad(decay.reshape(heads // GH, 1, GH), ((0, 0), (0, 7), (0, 128 - GH)))

    docs = lax.dynamic_slice_in_dim(segment_ids, zz * SEQ, SEQ)
    blocks = docs.reshape(CH, L)
    prior = jnp.concatenate([jnp.full((1,), -1, docs.dtype), blocks[:-1, -1]])
    masks = [docs, (blocks == prior[:, None]).reshape(SEQ), (blocks == blocks[:, -1:]).reshape(SEQ)]
    for k in range(1, K):
        masks.append(jnp.concatenate([jnp.zeros((k,), bool), docs[k:] == docs[:-k]]))
    for k in range(1, K):
        masks.append(jnp.concatenate([docs[k:] == docs[:-k], jnp.zeros((k,), bool)]))
    tok = jnp.pad(jnp.stack([m.astype(F32) for m in masks], 1), ((0, 0), (0, 128 - len(masks))))
    row = jnp.broadcast_to(blocks.astype(F32)[:, None, :], (CH, 8, L))

    hidden_all = both_cores(hidden_in, swap(hidden_in)).astype(F32)
    cot_all = both_cores(grad_out, swap(grad_out))
    inv_rms = lax.rsqrt(jnp.mean(hidden_all * hidden_all, -1, keepdims=True) + EPSILON)
    normed = (hidden_all * inv_rms * gain_outer).astype(BF)
    small_cols = jnp.concatenate([state_cols, jnp.pad(step_cols, ((0, 0), (0, 128 - heads)))], 1)
    pre_small = mm(normed, small_cols)
    state_pre = pre_small[:, :256]
    step_pre = pre_small[:, 256:]
    inner_pre = mm(normed, inner_cols)
    gate_pre = mm(normed, gate_cols)
    bc, bct, gs, pack, cumt = prep(state_pre, step_pre, tok, row, convst, head)
    gated, states, ss = fwd(inner_pre, gate_pre, par, tok, bc, bct, gs, pack, cumt)
    ss_own = jnp.sum(ss, -1)
    squares = ss_own + swap(ss_own)
    inner_inv = lax.rsqrt(squares / inner_all + EPSILON)[:, None]
    normed_inner = (gated * inner_inv * gain_in).astype(BF)
    mixed = mm(normed_inner, out_rows)

    def to_own(x):
        own = lax.dynamic_slice_in_dim(x, core * rows, rows)
        other = lax.dynamic_slice_in_dim(x, (1 - core) * rows, rows)
        return own + swap(other.astype(BF)).astype(F32)

    layer_out = (hidden_in.astype(F32) + to_own(mixed)).astype(BF)
    grad_out_part = mm(normed_inner, cot_all, ((0,), (0,)))
    d_inner = mm(cot_all, out_rows, ((1,), (1,)))
    grad_gain_in = jnp.sum(d_inner * gated * inner_inv, 0)
    prod_own = jnp.sum(gated * d_inner * gain_in, -1)
    products = prod_own + swap(prod_own)
    inv_pack = jnp.pad(
        jnp.stack([inner_inv[:, 0], inner_inv[:, 0] ** 3 * products / inner_all], 1), ((0, 0), (0, 126))
    )
    d_gate, d_pre, d_step, d_state, pgrad, hgrad, sgrad = bwd(
        inner_pre, gate_pre, d_inner, par, tok, inv_pack, bc, bct, gs, pack, cumt, states, decay_g, state_pre, convst, row
    )
    d_step = d_step.astype(BF)
    d_small = jnp.concatenate([d_state, d_step], 1)
    d_normed = to_own(
        mm(d_gate, gate_cols, ((1,), (1,))) + mm(d_pre, inner_cols, ((1,), (1,))) + mm(d_small, small_cols, ((1,), (1,)))
    )
    hidden = hidden_in.astype(F32)
    inv_own = lax.dynamic_slice_in_dim(inv_rms, core * rows, rows)
    grad_gain_outer = jnp.sum(d_normed * hidden * inv_own, 0)
    weighted_back = d_normed * gain_outer
    d_hidden = inv_own * weighted_back - hidden * inv_own**3 * jnp.mean(hidden * weighted_back, -1, keepdims=True)
    grad_hidden = (grad_out.astype(F32) + d_hidden).astype(BF)

    def scatter_columns(g):
        g = g.astype(BF).reshape(fsdp, depth, halves, width).transpose(0, 2, 1, 3).reshape(fsdp * halves, depth, width)
        return lax.psum_scatter(g, both, scatter_dimension=0).astype(F32)

    grad_gate = scatter_columns(mm(normed, d_gate, ((0,), (0,))))
    grad_inner = scatter_columns(mm(normed, d_pre, ((0,), (0,))))
    grad_small = mm(normed, d_small, ((0,), (0,)))
    grad_out_weight = grad_out_part.astype(BF).reshape(halves, width, fsdp, depth).transpose(2, 0, 1, 3)
    grad_out_weight = lax.psum_scatter(
        grad_out_weight.reshape(fsdp * halves, width, depth), both, scatter_dimension=0
    ).astype(F32)
    grad_state = lax.psum_scatter(grad_small[:, :256].astype(BF), "fsdp", scatter_dimension=0, tiled=True)
    grad_state = lax.psum(grad_state, ("zz", "core")).astype(F32)

    own_heads = [
        grad_small[:, 256 : 256 + heads].reshape(fsdp, depth, halves, heads_dev).transpose(0, 2, 1, 3),
        pgrad[:K].reshape(K, halves, heads_dev, fsdp, -1).transpose(3, 1, 0, 2, 4),
        pgrad[K].reshape(halves, heads_dev, fsdp, -1).transpose(2, 0, 1, 3),
        grad_gain_in.reshape(halves, heads_dev, fsdp, -1).transpose(2, 0, 1, 3),
    ]
    sizes = [v.shape[2:] for v in own_heads]
    stacked = jnp.concatenate([v.reshape(fsdp * halves, -1) for v in own_heads], 1)
    mine = lax.psum_scatter(stacked, both, scatter_dimension=0)
    outs = []
    at = 0
    for s in sizes:
        n = 1
        for d in s:
            n *= d
        outs.append(mine[at : at + n].reshape(s))
        at += n
    grad_step, grad_conv_in, grad_conv_in_shift, grad_gain_inner = outs

    def place(v):
        v = v.reshape(halves, 1, heads_dev)
        zero = jnp.zeros_like(v)
        return jnp.where(core == 0, jnp.concatenate([v, zero], 1), jnp.concatenate([zero, v], 1)).reshape(heads_all)

    skip_sum = jnp.sum(pgrad[P_SKIP].reshape(heads, unit), 1)
    shared = [grad_gain_outer.reshape(fsdp, depth), sgrad[:K].reshape(K, fsdp, -1).transpose(1, 0, 2), sgrad[K].reshape(fsdp, -1)]
    shared += [place(v).reshape(fsdp, -1) for v in (hgrad[1, :heads], hgrad[0, :heads], skip_sum)]
    sizes = [v.shape[1:] for v in shared]
    stacked = jnp.concatenate([v.reshape(fsdp, -1) for v in shared], 1)
    mine = lax.psum(stacked, ("fsdp", "zz", "core"))
    mine = lax.dynamic_index_in_dim(mine, lax.axis_index("fsdp"), keepdims=False)
    outs = []
    at = 0
    for s in sizes:
        n = 1
        for d in s:
            n *= d
        outs.append(mine[at : at + n].reshape(s))
        at += n
    grad_norm_gain, grad_conv_st, grad_conv_st_shift, grad_offset, grad_rate, grad_skip = outs
    return (layer_out, grad_hidden, grad_norm_gain, grad_gate, grad_inner, grad_state, grad_step, grad_conv_in,
            grad_conv_in_shift, grad_conv_st, grad_conv_st_shift, grad_offset, grad_rate, grad_skip, grad_gain_inner,
            grad_out_weight)


def on_chip(hidden_in, norm_gain, in_gate, in_inner, in_state, in_step, conv_inner, conv_inner_shift, conv_state,
            conv_state_shift, step_offset, log_rate, skip_gain, inner_gain, out_weight, segment_ids, grad_out):
    model = in_gate.shape[0] * 4
    result = block_call(
        model, hidden_in, grad_out, in_inner, in_gate, out_weight, in_state, norm_gain, in_step.T,
        conv_inner.transpose(1, 0, 2), conv_inner_shift, inner_gain, conv_state, conv_state_shift, step_offset, log_rate,
        skip_gain, segment_ids.reshape(-1, L),
    )
    layer_out, grad_hidden, g_inner, g_gate, g_out, g_state, own, other = result[:2] + result[6:]
    outs = list(finish_call(layer_out, grad_hidden, g_gate, g_inner, g_out, g_state, own, other))
    outs[6] = outs[6].T
    outs[7] = outs[7].transpose(1, 0, 2)
    return tuple(outs)


def solution(mesh):
    fsdp = mesh.shape["fsdp"]
    halves = mesh.shape["tensor"] // 2
    fine = jax.sharding.Mesh(mesh.devices.reshape(fsdp, halves, 2), ("fsdp", "zz", "core"))
    tensor = ("zz", "core")
    tokens = P(("fsdp", "zz", "core"), None)
    grid = P("fsdp", tensor)
    heads = P(tensor, "fsdp")
    return jax.shard_map(
        on_chip if (fsdp, halves) == (4, 4) else functools.partial(on_device, fsdp, halves),
        mesh=fine,
        in_specs=(
            tokens, P("fsdp"), grid, grid, P("fsdp", None), grid, P(None, tensor, "fsdp"), heads, P(None, "fsdp"),
            P("fsdp"), P("fsdp"), P("fsdp"), P("fsdp"), heads, heads, P("fsdp"), tokens,
        ),
        out_specs=(
            tokens, tokens, P("fsdp"), grid, grid, P("fsdp", None), grid, P(None, tensor, "fsdp"), heads,
            P(None, "fsdp"), P("fsdp"), P("fsdp"), P("fsdp"), P("fsdp"), heads, heads,
        ),
        check_vma=False,
    )
```
